32 devices in a mesh: dp: 8 (over z, y), chan: 4 (over x, core).
Axes of the slice: x: 2, y: 2, z: 4, core: 2. Of those that a mesh axis runs over, the one named last changes fastest.
Arguments:
- features: bfloat16 [32, 660, 1024], P('dp', 'chan'), may hold values from -6 to 6
- gain1: float32 [660], P('chan'), may hold values from 0.1 to 1.9
- bias1: float32 [660], P('chan'), may hold values from -3 to 3
- weight1: bfloat16 [660, 132], P('chan'), may hold values from -0.25 to 0.25
- gain2: float32 [132], P('chan'), may hold values from 0.1 to 1.9
- bias2: float32 [132], P('chan'), may hold values from -3 to 3
- weight2: bfloat16 [3, 3, 132, 33], P(None, None, 'chan'), may hold values from -0.3125 to 0.3125
- cotangent: bfloat16 [32, 660, 1024], P('dp', 'chan'), may hold values from -6 to 6
- image_side: int32 [32], P('dp'), may hold values from 24 to 32, as said below
- block_slot: int32 [20], replicated, may hold values from 0 to 19, each once
Outputs:
- output: float32 [32, 660, 1024], P('dp', 'chan')
- grad_features: float32 [32, 660, 1024], P('dp', 'chan')
- grad_weight1: float32 [660, 132], P('chan')
- grad_gain1: float32 [660], P('chan')
- grad_bias1: float32 [660], P('chan')
- grad_weight2: float32 [3, 3, 132, 33], P(None, None, 'chan')
- grad_gain2: float32 [132], P('chan')
- grad_bias2: float32 [132], P('chan')
The draws below stay inside these ranges and needn't reach their ends.
Inputs may be any that keep to these rules, and one draw needn't show every extreme that they name: `image_side`: each image's side is 24 or 32; both occur in every draw; its valid pixels are the top-left square of that side. A permutation: block k is stored in channel slot block_slot[k]; the last block is the new one.
All inputs are finite; a program needn't handle non-finite values.
Results may differ from the reference program's by a relative error of at most 0.00089.
Values may be sent and summed in bfloat16 or wider, within the bound.
A program may use at most 64 MiB of HBM per device.

```python
import jax
import jax.numpy as jnp
from jax import lax

GROW = 33
BLOCKS = 20
SIDE = 32
SMALL = 24
IMAGES = 32
CH = 660
BOTTLE = 132


def image_offsets(key, reach):
    offset_key = jax.random.fold_in(key, 5)
    return jax.random.uniform(offset_key, (IMAGES,), jnp.float32, -1.0, 1.0) * reach


def channel_signs(key):
    return jnp.where(jax.random.bernoulli(key, 0.5, (CH,)), 1.0, -1.0).astype(jnp.float32)


def draw_features(key, part):
    reach = 1.8
    offsets = image_offsets(key, reach)
    key = jax.random.fold_in(key, 31)
    sign_key, noise_key = jax.random.split(key)
    signs = channel_signs(sign_key)
    noise = jnp.clip(jax.random.normal(noise_key, (IMAGES, CH, SIDE * SIDE), jnp.float32), -4.0, 4.0)
    values = noise + offsets[:, None, None] * signs[None, :, None]
    return values.astype(jnp.bfloat16)


def draw_cotangent(key, part):
    reach = 1.8
    offsets = image_offsets(key, reach)
    key = jax.random.fold_in(key, 37)
    sign_key, noise_key = jax.random.split(key)
    signs = channel_signs(sign_key)
    noise = jnp.clip(jax.random.normal(noise_key, (IMAGES, CH, SIDE * SIDE), jnp.float32), -4.0, 4.0)
    values = noise + offsets[:, None, None] * signs[None, :, None]
    return values.astype(jnp.bfloat16)


def draw_image_side(key, part):
    key = jax.random.fold_in(key, 11)
    picks = jax.random.randint(key, (IMAGES,), 0, 20)
    large = (picks < 7).astype(jnp.int32)
    large = large.at[0].set(1).at[1].set(0)
    return jnp.where(large == 1, SIDE, SMALL).astype(jnp.int32)


def block_levels(rng, extent, pieces, least, top_value):
    level = 1.0
    for position, shards_of in pieces:
        draws = jax.random.uniform(jax.random.fold_in(jax.random.fold_in(rng, 6), position), (shards_of,), jnp.float32, least / len(pieces), top_value / len(pieces))
        level = level * jnp.repeat(jnp.exp(draws), extent[position] // shards_of).reshape((-1,) + (1,) * (len(extent) - 1 - position))
    return level


def gaussian(stream_key, extent, deviation, limit, cuts=(), held_as=jnp.bfloat16):
    result = jax.random.normal(stream_key, extent, jnp.float32) * deviation
    if len(cuts) > 0:
        result = block_levels(stream_key, extent, cuts, -0.22, 0.18) * result
    return jnp.clip(result, min=-limit, max=limit).astype(held_as)


def setup_inputs(seed: int = 0) -> dict:
    key_of = jax.random.split(jax.random.key(seed), 11)
    return {
        "features": draw_features(jax.random.fold_in(key_of[10], 71), 0),
        "gain1": jnp.clip(1.0 + 0.18 * jax.random.normal(key_of[1], (CH,), jnp.float32), 0.1, 1.9),
        "bias1": gaussian(key_of[2], (CH,), 0.5, 3.0, ((0, 4),), jnp.float32),
        "weight1": gaussian(key_of[3], (CH, BOTTLE), CH ** -0.5, 0.25, ((0, 4),)),
        "gain2": jnp.clip(1.0 + 0.18 * jax.random.normal(key_of[4], (BOTTLE,), jnp.float32), 0.1, 1.9),
        "bias2": gaussian(key_of[5], (BOTTLE,), 0.5, 3.0, ((0, 4),), jnp.float32),
        "weight2": gaussian(key_of[6], (3, 3, BOTTLE, GROW), (3 * BOTTLE) ** -0.5, 0.3125, ((2, 4),)),
        "cotangent": draw_cotangent(jax.random.fold_in(key_of[10], 71), 0),
        "image_side": draw_image_side(jax.random.fold_in(key_of[10], 71), 0),
        "block_slot": jax.random.permutation(key_of[9], BLOCKS).astype(jnp.int32),
    }


@jax.custom_vjp
def low(v):
    return lax.optimization_barrier(v.astype(jnp.bfloat16)).astype(jnp.float32)

@jax.custom_vjp
def low_back(v):
    return v

def low_keep(v):
    return (low(v), None)

def low_pass(kept, grad):
    return (grad,)

def back_keep(v):
    return (v, None)

def back_low(kept, grad):
    return (low(grad),)
low.defvjp(low_keep, low_pass)
low_back.defvjp(back_keep, back_low)
EPS = 1e-05

def smooth(values):
    return values * jax.nn.sigmoid(values)

def normalize(values, pixel_mask, count, gain, bias):
    weighted = values * pixel_mask
    mean = lax.optimization_barrier(jnp.sum(weighted, axis=(0, 2))) / count
    square = lax.optimization_barrier(jnp.sum(weighted * values, axis=(0, 2))) / count
    rstd = lax.rsqrt(square - mean * mean + EPS)
    return (values - mean[:, None]) * rstd[:, None] * gain[:, None] + bias[:, None]

def forward(inputs, gain1, bias1, weight1, gain2, bias2, weight2, pixel_mask, keep, place):
    count = jnp.sum(pixel_mask)
    images = inputs.shape[0]
    pre_one = normalize(inputs, pixel_mask, count, gain1, bias1)
    act_one = low(smooth(pre_one) * pixel_mask * keep[:, None])
    hidden = low_back(jnp.einsum('bcp,cd->bdp', act_one, weight1, precision=lax.Precision.HIGHEST))
    pre_two = normalize(hidden, pixel_mask, count, gain2, bias2)
    act_two = low(smooth(pre_two) * pixel_mask)
    squares = act_two.reshape(images, BOTTLE, SIDE, SIDE)
    conv = lax.conv_general_dilated(squares, weight2, (1, 1), 'SAME', dimension_numbers=('NCHW', 'HWIO', 'NCHW'), precision=lax.Precision.HIGHEST)
    grown = low_back(conv.reshape(images, GROW, SIDE * SIDE) * pixel_mask)
    placed = jnp.einsum('bgp,gc->bcp', grown, place, precision=lax.Precision.HIGHEST)
    return inputs * keep[:, None] + placed

def reference(features, gain1, bias1, weight1, gain2, bias2, weight2, cotangent, image_side, block_slot):
    steps_along = jnp.arange(SIDE, dtype=jnp.int32)
    inside = steps_along[None, :] < image_side[:, None]
    pixel_mask = (inside[:, :, None] & inside[:, None, :]).astype(jnp.float32).reshape(image_side.shape[0], 1, SIDE * SIDE)
    new_slot = block_slot[BLOCKS - 1]
    channel_ids = jnp.arange(CH, dtype=jnp.int32)
    keep = (channel_ids // GROW != new_slot).astype(jnp.float32)
    grow_ids = jnp.arange(GROW, dtype=jnp.int32)
    place = (channel_ids[None, :] == new_slot * GROW + grow_ids[:, None]).astype(jnp.float32)
    primals = (features.astype(jnp.float32), gain1, bias1, weight1.astype(jnp.float32), gain2, bias2, weight2.astype(jnp.float32))

    def apply_layer(inputs, g_one, b_one, w_one, g_two, b_two, w_two):
        return forward(inputs, g_one, b_one, w_one, g_two, b_two, w_two, pixel_mask, keep, place)
    output, pullback = jax.vjp(apply_layer, *primals)
    grads = pullback(cotangent.astype(jnp.float32))
    return (output, grads[0], grads[3], grads[1], grads[2], grads[6], grads[4], grads[5])
```

```python
import functools

import jax
import jax.numpy as jnp
from jax import lax
from jax.experimental import pallas as pl
from jax.experimental.pallas import tpu as pltpu
from jax.sharding import PartitionSpec as P

SIDE = 32
EPS = 1e-05
LANES = 128
TAP = 48
TAPS = 512
OWNERS = 8

MESH = pl.DeviceIdType.MESH
F32 = jnp.float32
BF16 = jnp.bfloat16


def pad_to(size, unit):
    return (size + unit - 1) // unit * unit


def iota(shape, axis):
    return lax.broadcasted_iota(jnp.int32, shape, axis)


def as_row(column):
    n = column.shape[0]
    eye = iota((n, LANES), 0) == iota((n, LANES), 1)
    return jnp.sum(jnp.where(eye, column, 0.0), axis=0, keepdims=True)


def as_column(row, n):
    eye = iota((n, LANES), 0) == iota((n, LANES), 1)
    return jnp.broadcast_to(jnp.sum(jnp.where(eye, row, 0.0), axis=1, keepdims=True), (n, LANES))


def as_rows(values, sizes):
    column = jnp.sum(values, axis=1, keepdims=True)
    rows, start = [], 0
    for size in sizes:
        rows.append(as_row(column[start : start + size]))
        start += size
    return rows


def layer(
    cfg,
    feat_h, cot_h, w1_h, gain1_h, bias1_h, gain2_h, bias2_h, w2_h, side_h, slot_h,
    out_x, out_g, out_w1, out_g1, out_b1, out_w2, out_g2, out_b2,
    feat, cot, w1v, gain1v, bias1v, gain2v, bias2v, w2v, side, slot,
    mask, xb, act, slope, gp1, gact,
    col_a, col_b, col_m, col_k, col_c, sum_a, sum_b, rowbuf,
    w1s, part, rx_a, rx_b, rx_x, hid,
    graw, gsend, grecv, g9, w2blk, w2r, w2b, gsl,
    act2, gp2, back, zbuf, gall, gcur, gha,
    cb, cw, cwr, rsl, fin, w1acc, w2acc,
    ar1, ar2, ar3, ar4,
    load_sem, s1, r1, s2, r2, s3, r3, s4, r4, sx, rxs, sg, rg, sw, rw, sb, rb, sh, rh, so, ro, sc, rc, sr, rr, sa, ra,
):
    n_dp, n_ch, n_img, n_c, n_px, n_d, grow = cfg
    n_dev = n_dp * n_ch
    cp = xb.shape[1]
    dpad = w1s.shape[0]
    d8 = pad_to(n_d, 8)
    tiles = n_px // LANES
    rpc = tiles * n_img
    c_sizes = (LANES, cp - LANES)
    d_sizes = (LANES, d8 - LANES)
    dp = lax.axis_index("dp")
    ch = lax.axis_index("chan")
    me = dp * n_ch + ch
    half = n_ch // 2
    cx, cc = ch // half, lax.rem(ch, half)
    sib = cx * half + (1 - cc)
    xp = (1 - cx) * half + cc
    xs = (1 - cx) * half + (1 - cc)

    def dev_peer(k):
        q = lax.rem(me + k, n_dev)
        return {"dp": q // n_ch, "chan": lax.rem(q, n_ch)}

    def dp_peer(k):
        return {"dp": lax.rem(dp + k, n_dp)}

    def ch_peer(k):
        return {"chan": lax.rem(ch + k, n_ch)}

    loads = [
        pltpu.make_async_copy(h, v, load_sem.at[i])
        for i, (h, v) in enumerate(
            (
                (feat_h, feat), (cot_h, cot), (w1_h, w1v), (gain1_h, gain1v), (bias1_h, bias1v),
                (gain2_h, gain2v), (bias2_h, bias2v), (w2_h, w2v), (side_h, side), (slot_h, slot),
            )
        )
    ]
    for copy in loads:
        copy.start()
    barrier = pltpu.get_barrier_semaphore()

    def greet(k, c):
        pl.semaphore_signal(barrier, inc=1, device_id=dev_peer(k), device_id_type=MESH)
        return c

    lax.fori_loop(1, n_dev, greet, 0)

    def remote(src, dst, send, recv, device):
        return pltpu.make_async_remote_copy(
            src_ref=src, dst_ref=dst, send_sem=send, recv_sem=recv, device_id=device, device_id_type=MESH
        )

    def share_start(slots, mine, count, peer, send, recv):
        def step(k, c):
            remote(slots.at[mine], slots.at[mine], send.at[k], recv.at[k], peer(k)).start()
            return c

        lax.fori_loop(1, count, step, 0)

    def share_wait(slots, mine, count, peer, send, recv):
        def step(k, c):
            remote(slots.at[mine], slots.at[mine], send.at[k], recv.at[k], peer(k)).wait()
            return c

        lax.fori_loop(1, count, step, 0)

    def total(slots):
        if slots.shape[0] <= 32:
            value = slots[0]
            for i in range(1, slots.shape[0]):
                value = value + slots[i]
            return value
        return lax.fori_loop(1, slots.shape[0], lambda i, v: v + slots[i], slots[0])

    for copy in loads[8:]:
        copy.wait()
    lane16 = iota((16, n_px), 1)
    row_of, col_of = lane16 >> 5, lane16 & (SIDE - 1)
    count_here = jnp.int32(0)
    for b in range(n_img):
        s = side[b]
        count_here = count_here + s * s
        mask[b] = jnp.where((row_of < s) & (col_of < s), 1.0, 0.0)
    new_slot = slot[slot.shape[0] - 1]
    per_device = n_c // grow
    slot_of = iota((rpc, LANES), 0) * 0 + new_slot

    n_rows = feat.shape[0]
    out_x[pl.ds(n_rows, out_x.shape[0] - n_rows), :] = jnp.zeros((out_x.shape[0] - n_rows, LANES), F32)
    out_g[pl.ds(n_rows, out_g.shape[0] - n_rows), :] = jnp.zeros((out_g.shape[0] - n_rows, LANES), F32)
    step_rows = 3 * rpc
    loads[0].wait()

    def widen(i, c):
        r = pl.ds(pl.multiple_of(i * step_rows, step_rows), step_rows)
        out_x[r, :] = feat[r, :].astype(F32)
        return c

    lax.fori_loop(0, n_rows // step_rows, widen, 0)

    def relayout(g, c):
        base = g * 16 * rpc
        r = pl.ds(pl.multiple_of(g * 16, 16), 16)
        s_acc = jnp.zeros((16, LANES), F32)
        q_acc = jnp.zeros((16, LANES), F32)
        for b in range(n_img):
            for t in range(tiles):
                k = t * n_img + b
                v = jnp.concatenate(
                    [out_x[pl.ds(base + h * 8 * rpc + k, 8, stride=rpc), :] for h in range(2)], axis=0
                )
                w = v * mask[b, :, t * LANES : (t + 1) * LANES]
                s_acc = s_acc + w
                q_acc = q_acc + w * v
                xb[b, r, t * LANES : (t + 1) * LANES] = v.astype(BF16)
        sum_a[r, :] = s_acc
        sum_b[r, :] = q_acc
        return c

    lax.fori_loop(0, cp // 16, relayout, 0)
    lane1 = iota((1, LANES), 1)
    s0, sq0 = as_rows(sum_a[...], c_sizes), as_rows(sum_b[...], c_sizes)
    ar1[dp, 0:1, :] = s0[0]
    ar1[dp, 1:2, :] = jnp.where(lane1 == LANES - 1, count_here.astype(F32), s0[1])
    ar1[dp, 2:3, :] = sq0[0]
    ar1[dp, 3:4, :] = sq0[1]

    loads[7].wait()
    w2blk[...] = jnp.zeros(w2blk.shape, BF16)
    acc = jnp.zeros((grow, w2blk.shape[1]), F32)
    for t in range(9):
        place = jnp.where(
            iota((grow, w2blk.shape[1]), 1) == iota((grow, w2blk.shape[1]), 0) + t * TAP, 1.0, 0.0
        ).astype(BF16)
        acc = acc + jnp.dot(w2v[t], place, preferred_element_type=F32)
    w2blk[0:grow, :] = acc.astype(BF16)
    loads[5].wait()
    loads[6].wait()
    gsl[ch, 0:1, 0:grow] = gain2v[...]
    gsl[ch, 1:2, 0:grow] = bias2v[...]
    loads[1].wait()

    def widen_cot(i, c):
        r = pl.ds(pl.multiple_of(i * step_rows, step_rows), step_rows)
        out_g[r, :] = cot[r, :].astype(F32)
        return c

    lax.fori_loop(0, n_rows // step_rows, widen_cot, 0)
    graw[...] = jnp.zeros(graw.shape, F32)

    picks = [jnp.where(slot_of == ch * per_device + i, 1.0, 0.0) for i in range(per_device)]

    def pick(i, c):
        v = jnp.zeros((rpc, LANES), F32)
        for k in range(per_device):
            v = v + out_g[pl.ds(pl.multiple_of((k * grow + i) * rpc, rpc), rpc), :] * picks[k]
        graw[pl.ds(pl.multiple_of(i * rpc, rpc), rpc), :] = v
        return c

    lax.fori_loop(0, grow, pick, 0)
    for b in range(n_img):
        for t in range(tiles):
            for h in range(TAP // 16):
                v = jnp.concatenate(
                    [
                        graw[pl.ds((h * 16 + i * 8) * rpc + t * n_img + b, 8, stride=rpc), :]
                        for i in range(2)
                    ],
                    axis=0,
                )
                v = v * mask[b, :, t * LANES : (t + 1) * LANES]
                gsend[b, h * 16 : h * 16 + 16, t * LANES : (t + 1) * LANES] = v.astype(BF16)

    pl.semaphore_wait(barrier, n_dev - 1)
    share_start(ar1, dp, n_dp, dp_peer, s1, r1)
    w2r[ch] = w2blk[...]
    share_start(gsl, ch, n_ch, ch_peer, sb, rb)
    for k in range(1, n_ch):
        to = lax.rem(ch + k, n_ch)
        remote(gsend.at[to], grecv.at[ch], sg.at[k], rg.at[k], {"chan": to}).start()
    share_start(w2r, ch, n_ch, ch_peer, sw, rw)

    loads[2].wait()
    w1s[...] = jnp.zeros(w1s.shape, BF16)
    w1s[0:n_d, 0:n_c] = w1v[...]
    rowbuf[...] = jnp.zeros(rowbuf.shape, F32)
    loads[3].wait()
    loads[4].wait()
    rowbuf[0:1, :] = gain1v[0:1, 0:LANES]
    rowbuf[1:2, 0 : n_c - LANES] = gain1v[0:1, LANES:n_c]
    rowbuf[2:3, :] = bias1v[0:1, 0:LANES]
    rowbuf[3:4, 0 : n_c - LANES] = bias1v[0:1, LANES:n_c]

    share_wait(ar1, dp, n_dp, dp_peer, s1, r1)
    tot1 = total(ar1)
    count = tot1[1:2, LANES - 1 : LANES]
    mean1, rstd1, scale1 = [], [], []
    for i in range(2):
        mean = tot1[i : i + 1] / count
        rstd = lax.rsqrt(tot1[2 + i : 3 + i] / count - mean * mean + EPS)
        here = lane1 + i * LANES
        ids = ch * n_c + here
        first = new_slot * grow
        keep = jnp.where(
            (here < n_c) & ((ids < first) | (ids >= first + grow)), 1.0, 0.0
        )
        scale = rstd * rowbuf[i : i + 1, :]
        shift = rowbuf[2 + i : 3 + i, :] - mean * scale
        size = c_sizes[i]
        r = pl.ds(i * LANES, size)
        col_a[r, :] = as_column(0.5 * scale * keep, size)
        col_b[r, :] = as_column(0.5 * shift * keep, size)
        col_m[r, :] = as_column(mean, size)
        col_k[r, :] = as_column(keep, size)
        mean1.append(mean)
        rstd1.append(rstd)
        scale1.append(scale)

    def partial(j):
        def body(g, c):
            r = pl.ds(pl.multiple_of(g * 16, 16), 16)
            a, b = col_a[r, :], col_b[r, :]
            for t in range(tiles):
                sl = slice(t * LANES, (t + 1) * LANES)
                v = xb[j, r, sl].astype(F32) * a + b
                act[j, r, sl] = ((v * jnp.tanh(v) + v) * mask[j, :, sl]).astype(BF16)
            return c

        lax.fori_loop(0, cp // 16, body, 0)
        part[j] = jnp.dot(w1s[...], act[j], preferred_element_type=F32)

    rows_d = pl.ds(0, d8)
    partial(xs)
    to_sib_a = remote(part.at[xs, rows_d], rx_a.at[rows_d], sx.at[0], rxs.at[0], {"chan": sib})
    to_sib_a.start()
    partial(xp)
    to_sib_a.wait()

    def add_a(g, c):
        r = pl.ds(pl.multiple_of(g * 8, 8), 8)
        part[xp, r, :] = part[xp, r, :] + rx_a[r, :]
        return c

    lax.fori_loop(0, d8 // 8, add_a, 0)
    to_x = remote(part.at[xp, rows_d], rx_x.at[rows_d], sx.at[1], rxs.at[1], {"chan": xp})
    to_x.start()
    partial(sib)
    to_sib_b = remote(part.at[sib, rows_d], rx_b.at[rows_d], sx.at[2], rxs.at[2], {"chan": sib})
    to_sib_b.start()
    partial(ch)

    for k in range(1, n_ch):
        to = lax.rem(ch + k, n_ch)
        remote(gsend.at[to], grecv.at[ch], sg.at[k], rg.at[k], {"chan": to}).wait()
    share_wait(w2r, ch, n_ch, ch_peer, sw, rw)
    share_wait(gsl, ch, n_ch, ch_peer, sb, rb)
    g = gsend[ch].astype(F32)
    for k in range(1, n_ch):
        g = g + grecv[lax.rem(ch + k, n_ch)].astype(F32)
    gcur[...] = g
    px = iota((TAP, n_px), 1)
    py, pxx = px >> 5, px & (SIDE - 1)
    for ky in range(3):
        for kx in range(3):
            shift = (ky - 1) * SIDE + (kx - 1)
            t = ky * 3 + kx
            v = gcur[...]
            if shift != 0:
                v = pltpu.roll(v, shift % n_px, 1)
            ok = None
            for off, pos in ((ky - 1, py), (kx - 1, pxx)):
                if off == 1:
                    test = pos >= 1
                elif off == -1:
                    test = pos <= SIDE - 2
                else:
                    continue
                ok = test if ok is None else ok & test
            if ok is not None:
                v = jnp.where(ok, v, 0.0)
            g9[t * TAP : (t + 1) * TAP, :] = v.astype(BF16)
    acc = jnp.zeros((dpad, w2b.shape[1]), F32)
    for j in range(n_ch):
        rows = iota((dpad, TAP), 0)
        cols = iota((dpad, TAP), 1)
        place = jnp.where((rows == cols + j * grow) & (cols < grow), 1.0, 0.0).astype(BF16)
        acc = acc + jnp.dot(place, w2r[j], preferred_element_type=F32)
    w2b[...] = acc.astype(BF16)
    g9[pl.ds(9 * TAP, TAPS - 9 * TAP), :] = jnp.zeros((TAPS - 9 * TAP, n_px), BF16)
    back[...] = jnp.dot(w2b[...], g9[...], preferred_element_type=F32)
    rows = iota((dpad, LANES), 0)
    cols = iota((dpad, LANES), 1)
    gain2c = jnp.zeros((dpad, 1), F32)
    bias2c = jnp.zeros((dpad, 1), F32)
    for j in range(n_ch):
        place = (rows == cols + j * grow) & (cols < grow)
        gain2c = gain2c + jnp.sum(jnp.where(place, gsl[j, 0:1, :], 0.0), axis=1, keepdims=True)
        bias2c = bias2c + jnp.sum(jnp.where(place, gsl[j, 1:2, :], 0.0), axis=1, keepdims=True)
    col_c[0] = jnp.broadcast_to(gain2c, (dpad, LANES))
    col_c[1] = jnp.broadcast_to(bias2c, (dpad, LANES))

    to_x.wait()
    to_sib_b.wait()
    sum_a[...] = jnp.zeros(sum_a.shape, F32)
    sum_b[...] = jnp.zeros(sum_b.shape, F32)

    def gather(g, c):
        r = pl.ds(pl.multiple_of(g * 8, 8), 8)
        s_acc = jnp.zeros((8, LANES), F32)
        q_acc = jnp.zeros((8, LANES), F32)
        for t in range(tiles):
            sl = slice(t * LANES, (t + 1) * LANES)
            v = (part[ch, r, sl] + rx_b[r, sl]) + rx_x[r, sl]
            hid[r, sl] = v
            s_acc = s_acc + v
            q_acc = q_acc + v * v
        sum_a[r, :] = s_acc
        sum_b[r, :] = q_acc
        return c

    lax.fori_loop(0, d8 // 8, gather, 0)
    hid[pl.ds(d8, dpad - d8), :] = jnp.zeros((dpad - d8, n_px), F32)
    gp2[...] = jnp.zeros(gp2.shape, F32)

    def pack(slots):
        s, q = as_rows(sum_a[0:d8, :], d_sizes), as_rows(sum_b[0:d8, :], d_sizes)
        slots[me, 0:1, :] = s[0]
        slots[me, 1:2, :] = s[1]
        slots[me, 2:3, :] = q[0]
        slots[me, 3:4, :] = q[1]

    def columns_d(row0, row1):
        tail = jnp.zeros((dpad - d8, LANES), F32)
        return jnp.concatenate(
            [as_column(row0, LANES), as_column(row1, d8 - LANES), tail], axis=0
        )

    pack(ar2)
    share_start(ar2, me, n_dev, dev_peer, s2, r2)

    def slopes(j):
        def body(g, c):
            r = pl.ds(pl.multiple_of(g * 16, 16), 16)
            a, b = col_a[r, :], col_b[r, :]
            k = 0.5 * col_k[r, :]
            for t in range(tiles):
                sl = slice(t * LANES, (t + 1) * LANES)
                v = xb[j, r, sl].astype(F32) * a + b
                th = jnp.tanh(v)
                slope[j, r, sl] = ((1.0 + th) * (1.0 + v * (1.0 - th))) * (mask[j, :, sl] * k)
            return c

        lax.fori_loop(0, cp // 16, body, 0)

    for j in range(n_img):
        slopes(j)

    share_wait(ar2, me, n_dev, dev_peer, s2, r2)
    tot2 = total(ar2)
    mean2 = [tot2[i : i + 1] / count for i in range(2)]
    rstd2 = [lax.rsqrt(tot2[2 + i : 3 + i] / count - mean2[i] * mean2[i] + EPS) for i in range(2)]
    mean2c = columns_d(*mean2)
    rstd2c = columns_d(*rstd2)
    scale2c = rstd2c * col_c[0]
    col_c[2] = mean2c
    col_c[3] = rstd2c
    col_c[4] = scale2c
    col_c[5] = 0.5 * scale2c
    col_c[6] = 0.5 * (col_c[1] - mean2c * scale2c)

    def second(g, c):
        r = pl.ds(pl.multiple_of(g * 16, 16), 16)
        a, b, m = col_c[5, r, :], col_c[6, r, :], col_c[2, r, :]
        s_acc = jnp.zeros((16, LANES), F32)
        q_acc = jnp.zeros((16, LANES), F32)
        for t in range(tiles):
            sl = slice(t * LANES, (t + 1) * LANES)
            h = hid[r, sl]
            mk = mask[ch, :, sl]
            v = h * a + b
            th = jnp.tanh(v)
            act2[r, sl] = ((v * th + v) * mk).astype(BF16)
            gp = (0.5 * mk) * ((1.0 + th) * (1.0 + v * (1.0 - th))) * back[r, sl]
            gp2[r, sl] = gp
            s_acc = s_acc + gp
            q_acc = q_acc + gp * (h - m)
        sum_a[r, :] = s_acc
        sum_b[r, :] = q_acc
        return c

    lax.fori_loop(0, dpad // 16, second, 0)
    pack(ar3)
    share_start(ar3, me, n_dev, dev_peer, s3, r3)

    w2acc[...] = lax.dot_general(
        act2[...], g9[...], (((1,), (1,)), ((), ())), preferred_element_type=F32
    )
    cw[...] = jnp.zeros(cw.shape, F32)
    for j in range(n_ch):
        for q in range(20):
            lt, rt = q // 5, q % 5
            cw[j, q // 3, (q % 3) * 8 : (q % 3) * 8 + 8, :] = w2acc[
                j * grow + rt * 8 : j * grow + rt * 8 + 8, lt * LANES : (lt + 1) * LANES
            ]
    for k in range(1, n_ch):
        to = lax.rem(ch + k, n_ch)
        remote(cw.at[to], cwr.at[ch], sc.at[k], rc.at[k], {"chan": to}).start()
    zbuf[...] = lax.dot_general(
        w2b[...], act2[...], (((0,), (0,)), ((), ())), preferred_element_type=F32
    )
    new = jnp.zeros((TAP, n_px), F32)
    for ky in range(3):
        for kx in range(3):
            shift = (ky - 1) * SIDE + (kx - 1)
            t = ky * 3 + kx
            v = zbuf[t * TAP : (t + 1) * TAP, :]
            if shift != 0:
                v = pltpu.roll(v, (-shift) % n_px, 1)
            ok = None
            for off, pos in ((ky - 1, py), (kx - 1, pxx)):
                if off == -1:
                    test = pos >= 1
                elif off == 1:
                    test = pos <= SIDE - 2
                else:
                    continue
                ok = test if ok is None else ok & test
            if ok is not None:
                v = jnp.where(ok, v, 0.0)
            new = new + v
    new = new * jnp.concatenate([mask[ch]] * (TAP // 16), axis=0)
    gall[ch] = new[0 : gall.shape[1]]

    share_wait(ar3, me, n_dev, dev_peer, s3, r3)
    tot3 = total(ar3)
    gain_sum2 = [tot3[2 + i : 3 + i] * rstd2[i] for i in range(2)]
    bias_sum2 = [tot3[i : i + 1] for i in range(2)]
    gain_sum2c = columns_d(*gain_sum2)
    bias_sum2c = columns_d(*bias_sum2)
    col_c[5] = col_c[4] * bias_sum2c / count
    col_c[6] = col_c[4] * col_c[3] * gain_sum2c / count

    def third(g, c):
        r = pl.ds(pl.multiple_of(g * 16, 16), 16)
        c1, c2, c3, m = col_c[4, r, :], col_c[5, r, :], col_c[6, r, :], col_c[2, r, :]
        for t in range(tiles):
            sl = slice(t * LANES, (t + 1) * LANES)
            gha[ch, r, sl] = (
                c1 * gp2[r, sl] - mask[ch, :, sl] * (c2 + c3 * (hid[r, sl] - m))
            ).astype(BF16)
        return c

    lax.fori_loop(0, dpad // 16, third, 0)

    def spread(buf, send, recv):
        to_sib = remote(buf.at[ch], buf.at[ch], send.at[0], recv.at[0], {"chan": sib})
        to_xp = remote(buf.at[ch], buf.at[ch], send.at[1], recv.at[1], {"chan": xp})
        on = remote(buf.at[xp], buf.at[xp], send.at[2], recv.at[2], {"chan": sib})
        return to_sib, to_xp, on

    grad_sib, grad_xp, grad_on = spread(gha, sh, rh)
    grad_xp.start()
    grad_sib.start()
    new_sib, new_xp, new_on = spread(gall, so, ro)
    new_xp.start()
    new_sib.start()
    d_rows, d_cols = iota((dpad, LANES), 0), iota((dpad, LANES), 1)
    here_d = (d_rows == d_cols + ch * grow) & (d_cols < grow)
    out_g2[...] = jnp.sum(jnp.where(here_d, gain_sum2c, 0.0), axis=0, keepdims=True)[:, 0:grow]
    out_b2[...] = jnp.sum(jnp.where(here_d, bias_sum2c, 0.0), axis=0, keepdims=True)[:, 0:grow]

    w1acc[...] = jnp.zeros(w1acc.shape, F32)
    sum_a[...] = jnp.zeros(sum_a.shape, F32)
    sum_b[...] = jnp.zeros(sum_b.shape, F32)

    def weight_grad(j):
        w1acc[0:dpad, 0:cp] = w1acc[0:dpad, 0:cp] + lax.dot_general(
            gha[j], act[j], (((1,), (1,)), ((), ())), preferred_element_type=F32
        )

    def input_grad(j):
        gact[...] = lax.dot_general(
            w1s[...], gha[j], (((0,), (0,)), ((), ())), preferred_element_type=F32
        )

        def body(g, c):
            r = pl.ds(pl.multiple_of(g * 16, 16), 16)
            m = col_m[r, :]
            s_acc, q_acc = sum_a[r, :], sum_b[r, :]
            for t in range(tiles):
                sl = slice(t * LANES, (t + 1) * LANES)
                gp = gact[r, sl] * slope[j, r, sl]
                gp1[j, r, sl] = gp
                s_acc = s_acc + gp
                q_acc = q_acc + gp * (xb[j, r, sl].astype(F32) - m)
            sum_a[r, :] = s_acc
            sum_b[r, :] = q_acc
            return c

        lax.fori_loop(0, cp // 16, body, 0)

    weight_grad(ch)
    input_grad(ch)
    grad_sib.wait()
    weight_grad(sib)
    input_grad(sib)
    grad_xp.wait()
    grad_on.start()
    weight_grad(xp)
    input_grad(xp)
    for k in range(1, n_ch):
        to = lax.rem(ch + k, n_ch)
        remote(cw.at[to], cwr.at[ch], sc.at[k], rc.at[k], {"chan": to}).wait()
    for q in range(OWNERS):
        v = cw[ch, q]
        for k in range(1, n_ch):
            v = v + cwr[lax.rem(ch + k, n_ch), q]
        cb[q, 40:64, :] = v
    grad_on.wait()
    weight_grad(xs)

    for q in range(OWNERS):
        r, h = q % 4, q // 4
        cb[q, 0:40, :] = w1acc[r * 40 : r * 40 + 40, h * LANES : (h + 1) * LANES]
    stride = n_dp // OWNERS
    my_part = dp // stride
    is_owner = lax.rem(dp, stride) == 0

    def part_to(k):
        q = lax.rem(my_part + k, OWNERS)
        return q, q * stride

    def push(k, c):
        q, to = part_to(k)

        @pl.when(to != dp)
        def _():
            remote(cb.at[q], rsl.at[dp], sr.at[k], rr.at[dp], {"dp": to}).start()

        return c

    lax.fori_loop(0, OWNERS, push, 0)
    input_grad(xs)
    s4_, q4_ = as_rows(sum_a[...], c_sizes), as_rows(sum_b[...], c_sizes)
    for i in range(2):
        ar4[dp, i : i + 1, :] = s4_[i]
        ar4[dp, 2 + i : 3 + i, :] = q4_[i]
    share_start(ar4, dp, n_dp, dp_peer, s4, r4)

    def push_wait(k, c):
        q, to = part_to(k)

        @pl.when(to != dp)
        def _():
            remote(cb.at[q], rsl.at[dp], sr.at[k], rr.at[dp], {"dp": to}).wait_send()

        return c

    def pull(k, c):
        src = lax.rem(dp + k, n_dp)
        remote(cb.at[0], rsl.at[src], sr.at[0], rr.at[src], {"dp": src}).wait_recv()
        return c

    @pl.when(is_owner)
    def _():
        lax.fori_loop(1, n_dp, pull, 0)
        v = cb[my_part]
        for k in range(1, n_dp):
            v = v + rsl[lax.rem(dp + k, n_dp)]
        fin[my_part] = v

        def give(k, c):
            remote(fin.at[my_part], fin.at[my_part], sa.at[k], ra.at[my_part], dp_peer(k)).start()
            return c

        lax.fori_loop(1, n_dp, give, 0)

    lax.fori_loop(0, OWNERS, push_wait, 0)

    new_xp.wait()
    new_on.start()
    new_sib.wait()
    new_on.wait()
    for b in range(n_img):
        for t in range(tiles):
            for h in range(gall.shape[1] // 8):
                graw[pl.ds(h * 8 * rpc + t * n_img + b, 8, stride=rpc), :] = gall[
                    b, h * 8 : h * 8 + 8, t * LANES : (t + 1) * LANES
                ]
    for s in range(per_device):
        chosen = slot_of == ch * per_device + s

        def place_new(i, c):
            src = pl.ds(pl.multiple_of(i * rpc, rpc), rpc)
            dst = pl.ds(pl.multiple_of((s * grow + i) * rpc, rpc), rpc)
            out_x[dst, :] = jnp.where(chosen, graw[src, :], out_x[dst, :])
            return c

        lax.fori_loop(0, grow, place_new, 0)

    share_wait(ar4, dp, n_dp, dp_peer, s4, r4)
    tot4 = total(ar4)
    for i in range(2):
        bias_sum = tot4[i : i + 1]
        gain_sum = tot4[2 + i : 3 + i] * rstd1[i]
        size = c_sizes[i]
        r = pl.ds(i * LANES, size)
        k1 = -scale1[i] * rstd1[i] * gain_sum / count
        k0 = -scale1[i] * bias_sum / count - k1 * mean1[i]
        col_a[r, :] = as_column(scale1[i], size)
        col_b[r, :] = as_column(k0, size)
        col_m[r, :] = as_column(k1, size)
        width = min(LANES, n_c - i * LANES)
        out_g1[0:1, i * LANES : i * LANES + width] = gain_sum[:, 0:width]
        out_b1[0:1, i * LANES : i * LANES + width] = bias_sum[:, 0:width]

    def last(g, c):
        base = g * 16 * rpc
        r = pl.ds(pl.multiple_of(g * 16, 16), 16)
        a, k0, k1, keep = col_a[r, :], col_b[r, :], col_m[r, :], col_k[r, :]
        for b in range(n_img):
            for t in range(tiles):
                sl = slice(t * LANES, (t + 1) * LANES)
                v = a * gp1[b, r, sl] + mask[b, :, sl] * (k0 + k1 * xb[b, r, sl].astype(F32))
                for h in range(2):
                    at = pl.ds(base + h * 8 * rpc + t * n_img + b, 8, stride=rpc)
                    out_g[at, :] = out_g[at, :] * keep[h * 8 : h * 8 + 8] + v[h * 8 : h * 8 + 8]
        return c

    lax.fori_loop(0, cp // 16, last, 0)

    @pl.when(is_owner)
    def _():
        def gave(k, c):
            remote(fin.at[my_part], fin.at[my_part], sa.at[k], ra.at[my_part], dp_peer(k)).wait_send()
            return c

        lax.fori_loop(1, n_dp, gave, 0)

    def take(q, c):
        @pl.when(q * stride != dp)
        def _():
            remote(fin.at[q], fin.at[q], sa.at[0], ra.at[q], {"dp": q * stride}).wait_recv()

        return c

    lax.fori_loop(0, OWNERS, take, 0)
    for q in range(OWNERS):
        r, h = q % 4, q // 4
        height = min(40, n_d - r * 40)
        width = min(LANES, n_c - h * LANES)
        out_w1[r * 40 : r * 40 + height, h * LANES : h * LANES + width] = fin[q, 0:height, 0:width]
    for q in range(20):
        lt, rt = q // 5, q % 5
        w2acc[rt * 8 : rt * 8 + 8, lt * LANES : (lt + 1) * LANES] = fin[
            q // 3, 40 + (q % 3) * 8 : 48 + (q % 3) * 8, :
        ]
    v = w2acc[0:40, :]
    for t in range(9):
        u = v if t == 0 else pltpu.roll(v, TAPS - t * TAP, 1)
        out_w2[t] = u[0:grow, 0:grow]


def finish(n_rows, *refs):
    n = (len(refs) - 1) // 2
    sem = refs[-1]
    copies = []
    for i in range(n):
        src, dst = refs[i], refs[n + i]
        if i < 2:
            src = src.at[pl.ds(0, n_rows)]
        copies.append(pltpu.make_async_copy(src, dst, sem.at[i]))
    for copy in copies:
        copy.start()
    for copy in copies:
        copy.wait()


def flat(values):
    n, c, p = values.shape
    return (
        values.transpose(1, 0, 2).reshape(c, n, p // LANES, LANES).transpose(0, 2, 1, 3).reshape(-1, LANES)
    )


def unflat(rows, n, c, p):
    return rows.reshape(c, p // LANES, n, LANES).transpose(0, 2, 1, 3).reshape(c, n, p).transpose(1, 0, 2)


def on_device(
    n_dp, n_ch, features, gain1, bias1, weight1, gain2, bias2, weight2, cotangent, image_side, block_slot
):
    n_img, n_c, n_px = features.shape
    n_d = weight1.shape[1]
    grow = weight2.shape[3]
    cp = pad_to(n_c, 16)
    dpad = pad_to(n_d, 16)
    d8 = pad_to(n_d, 8)
    rpc = n_px // LANES * n_img
    n_rows, n_pad = n_c * rpc, cp * rpc
    n_dev = n_dp * n_ch
    cfg = (n_dp, n_ch, n_img, n_c, n_px, n_d, grow)
    args = (
        flat(features),
        flat(cotangent),
        weight1.T,
        gain1.reshape(1, -1),
        bias1.reshape(1, -1),
        gain2.reshape(1, -1),
        bias2.reshape(1, -1),
        weight2.reshape(9, grow, grow),
        image_side,
        block_slot,
    )
    args = [pltpu.with_memory_space_constraint(v, pltpu.HBM) for v in args]
    sd = jax.ShapeDtypeStruct
    in_vmem = pl.BlockSpec(memory_space=pltpu.VMEM)
    in_hbm = pl.BlockSpec(memory_space=pltpu.HBM)
    dma = pltpu.SemaphoreType.DMA
    v = pltpu.VMEM
    scratch = [
        v((n_rows, LANES), BF16), v((n_rows, LANES), BF16), v((n_d, n_c), BF16),
        v((1, n_c), F32), v((1, n_c), F32), v((1, grow), F32), v((1, grow), F32),
        v((9, grow, grow), BF16), pltpu.SMEM(image_side.shape, jnp.int32), pltpu.SMEM(block_slot.shape, jnp.int32),
        v((n_img, 16, n_px), F32),
        v((n_img, cp, n_px), BF16), v((n_img, cp, n_px), BF16),
        v((n_img, cp, n_px), F32), v((n_img, cp, n_px), F32), v((cp, n_px), F32),
        v((cp, LANES), F32), v((cp, LANES), F32), v((cp, LANES), F32), v((cp, LANES), F32),
        v((7, dpad, LANES), F32), v((cp, LANES), F32), v((cp, LANES), F32), v((8, LANES), F32),
        v((dpad, cp), BF16), v((n_img, dpad, n_px), F32),
        v((dpad, n_px), F32), v((dpad, n_px), F32), v((dpad, n_px), F32), v((dpad, n_px), F32),
        v((TAP * rpc, LANES), F32), v((n_ch, TAP, n_px), BF16), v((n_ch, TAP, n_px), BF16),
        v((TAPS, n_px), BF16), v((TAP, TAPS), BF16), v((n_ch, TAP, TAPS), BF16), v((dpad, TAPS), BF16),
        v((n_ch, 2, LANES), F32),
        v((dpad, n_px), BF16), v((dpad, n_px), F32), v((dpad, n_px), F32), v((TAPS, n_px), F32),
        v((n_ch, 40, n_px), F32), v((TAP, n_px), F32), v((n_ch, dpad, n_px), BF16),
        v((OWNERS, 64, LANES), F32), v((n_ch, OWNERS, 24, LANES), F32), v((n_ch, OWNERS, 24, LANES), F32),
        v((n_dp, 64, LANES), F32), v((OWNERS, 64, LANES), F32), v((160, 256), F32), v((dpad, TAPS), F32),
        v((n_dp, 4, LANES), F32), v((n_dev, 4, LANES), F32), v((n_dev, 4, LANES), F32), v((n_dp, 4, LANES), F32),
        dma((10,)),
        dma((n_dp,)), dma((n_dp,)), dma((n_dev,)), dma((n_dev,)), dma((n_dev,)), dma((n_dev,)), dma((n_dp,)), dma((n_dp,)),
        dma((3,)), dma((3,)), dma((n_ch,)), dma((n_ch,)), dma((n_ch,)), dma((n_ch,)), dma((n_ch,)), dma((n_ch,)),
        dma((3,)), dma((3,)), dma((3,)), dma((3,)), dma((n_ch,)), dma((n_ch,)),
        dma((OWNERS,)), dma((n_dp,)), dma((n_dp,)), dma((OWNERS,)),
    ]
    out_shape = (
        sd((n_pad, LANES), F32), sd((n_pad, LANES), F32), sd((n_d, n_c), F32),
        sd((1, n_c), F32), sd((1, n_c), F32), sd((9, grow, grow), F32), sd((1, grow), F32), sd((1, grow), F32),
    )
    outs = pl.pallas_call(
        functools.partial(layer, cfg),
        out_shape=out_shape,
        in_specs=[in_hbm] * len(args),
        out_specs=(in_vmem,) * len(out_shape),
        scratch_shapes=scratch,
        compiler_params=pltpu.CompilerParams(
            collective_id=0, has_side_effects=True, vmem_limit_bytes=40 << 20
        ),
    )(*args)
    final = (sd((n_rows, LANES), F32),) * 2 + out_shape[2:]
    o = pl.pallas_call(
        functools.partial(finish, n_rows),
        out_shape=final,
        in_specs=[in_vmem] * len(final),
        out_specs=(in_hbm,) * len(final),
        scratch_shapes=[dma((len(final),))],
        compiler_params=pltpu.CompilerParams(vmem_limit_bytes=8 << 20),
    )(*outs)
    return (
        unflat(o[0], n_img, n_c, n_px),
        unflat(o[1], n_img, n_c, n_px),
        o[2].T,
        o[3].reshape(-1),
        o[4].reshape(-1),
        o[5].reshape(3, 3, grow, grow),
        o[6].reshape(-1),
        o[7].reshape(-1),
    )


def solution(mesh):
    in_specs = (
        P("dp", "chan", None),
        P("chan"),
        P("chan"),
        P("chan", None),
        P("chan"),
        P("chan"),
        P(None, None, "chan", None),
        P("dp", "chan", None),
        P("dp"),
        P(),
    )
    out_specs = (
        P("dp", "chan", None),
        P("dp", "chan", None),
        P("chan", None),
        P("chan"),
        P("chan"),
        P(None, None, "chan", None),
        P("chan"),
        P("chan"),
    )
    body = functools.partial(on_device, mesh.shape["dp"], mesh.shape["chan"])
    return jax.shard_map(body, mesh=mesh, in_specs=in_specs, out_specs=out_specs, check_vma=False)
```

```python
import functools

import jax
import jax.numpy as jnp
from jax import lax
from jax.experimental import pallas as pl
from jax.experimental.pallas import tpu as pltpu
from jax.sharding import PartitionSpec as P

SIDE = 32
EPS = 1e-05
LANES = 128
TAP = 48
TAPS = 512
PIECES = 4
OWNERS = 8

MESH = pl.DeviceIdType.MESH
F32 = jnp.float32
BF16 = jnp.bfloat16


def pad_to(size, unit):
    return (size + unit - 1) // unit * unit


def iota(shape, axis):
    return lax.broadcasted_iota(jnp.int32, shape, axis)


def as_row(column):
    n = column.shape[0]
    eye = iota((n, LANES), 0) == iota((n, LANES), 1)
    return jnp.sum(jnp.where(eye, column, 0.0), axis=0, keepdims=True)


def as_column(row, n):
    eye = iota((n, LANES), 0) == iota((n, LANES), 1)
    return jnp.broadcast_to(jnp.sum(jnp.where(eye, row, 0.0), axis=1, keepdims=True), (n, LANES))


def as_rows(values, sizes):
    column = jnp.sum(values, axis=1, keepdims=True)
    rows, start = [], 0
    for size in sizes:
        rows.append(as_row(column[start : start + size]))
        start += size
    return rows


def layer(
    cfg,
    feat_h, cot_h, w1_h, gain1_h, bias1_h, gain2_h, bias2_h, w2_h, side_h, slot_h,
    out_x, out_g, out_w1, out_g1, out_b1, out_w2, out_g2, out_b2,
    feat, cot, w1v, gain1v, bias1v, gain2v, bias2v, w2v, side, slot,
    mask, mask_raw, xb, act, slope, gp1, gact,
    col_a, col_b, col_m, col_k, col_c, sum_a, sum_b, rowbuf,
    w1s, part, rx_a, rx_b, rx_x, hid,
    graw, gsend, gsx, gpair, grx, gcur, g9, w2blk, w2r, w2b, gsl,
    act2, gp2, back, zbuf, gall, gha,
    cw, cwr, cwx, cb, rsl, fin, w1acc, w2acc,
    ar1, ar2, ar3, ar4,
    load_sem, s1, r1, s2, r2, s3, r3, s4, r4, sx, rxs, sp, rp, sq, rq, sg, rg, sw, rw, sb, rb, sh, rh, so, ro, sc, rc, sr, rr, sa, ra,
):
    n_dp, n_ch, n_img, n_c, n_px, n_d, grow = cfg
    n_dev = n_dp * n_ch
    cp = xb.shape[1]
    dpad = w1s.shape[0]
    d8 = pad_to(n_d, 8)
    tiles = n_px // LANES
    rpc = tiles * n_img
    c_sizes = (LANES, cp - LANES)
    d_sizes = (LANES, d8 - LANES)
    dp = lax.axis_index("dp")
    ch = lax.axis_index("chan")
    me = dp * n_ch + ch
    half = n_ch // 2
    cx, cc = ch // half, lax.rem(ch, half)
    sib = cx * half + (1 - cc)
    xp = (1 - cx) * half + cc
    xs = (1 - cx) * half + (1 - cc)

    def dev_peer(k):
        q = lax.rem(me + k, n_dev)
        return {"dp": q // n_ch, "chan": lax.rem(q, n_ch)}

    def dp_peer(k):
        return {"dp": lax.rem(dp + k, n_dp)}

    def ch_peer(k):
        return {"chan": lax.rem(ch + k, n_ch)}

    loads = [
        pltpu.make_async_copy(h, v, load_sem.at[i])
        for i, (h, v) in enumerate(
            (
                (feat_h, feat), (cot_h, cot), (w1_h, w1v), (gain1_h, gain1v), (bias1_h, bias1v),
                (gain2_h, gain2v), (bias2_h, bias2v), (w2_h, w2v), (side_h, side), (slot_h, slot),
            )
        )
    ]
    for copy in loads:
        copy.start()
    barrier = pltpu.get_barrier_semaphore()

    def greet(k, c):
        pl.semaphore_signal(barrier, inc=1, device_id=dev_peer(k), device_id_type=MESH)
        return c

    lax.fori_loop(1, n_dev, greet, 0)

    def remote(src, dst, send, recv, device):
        return pltpu.make_async_remote_copy(
            src_ref=src, dst_ref=dst, send_sem=send, recv_sem=recv, device_id=device, device_id_type=MESH
        )

    def share_start(slots, mine, count, peer, send, recv):
        def step(k, c):
            remote(slots.at[mine], slots.at[mine], send.at[k], recv.at[k], peer(k)).start()
            return c

        lax.fori_loop(1, count, step, 0)

    def share_wait(slots, mine, count, peer, send, recv):
        def step(k, c):
            remote(slots.at[mine], slots.at[mine], send.at[k], recv.at[k], peer(k)).wait()
            return c

        lax.fori_loop(1, count, step, 0)

    def total(slots):
        if slots.shape[0] <= 32:
            value = slots[0]
            for i in range(1, slots.shape[0]):
                value = value + slots[i]
            return value
        return lax.fori_loop(1, slots.shape[0], lambda i, v: v + slots[i], slots[0])

    for copy in loads[8:]:
        copy.wait()
    lane16 = iota((16, n_px), 1)
    row_of, col_of = lane16 >> 5, lane16 & (SIDE - 1)
    count_here = jnp.int32(0)
    for b in range(n_img):
        s = side[b]
        count_here = count_here + s * s
        mask[b] = jnp.where((row_of < s) & (col_of < s), 1.0, 0.0)
    new_slot = slot[slot.shape[0] - 1]
    per_device = n_c // grow
    slot_of = iota((rpc, LANES), 0) * 0 + new_slot

    n_rows = feat.shape[0]
    out_x[pl.ds(n_rows, out_x.shape[0] - n_rows), :] = jnp.zeros((out_x.shape[0] - n_rows, LANES), F32)
    out_g[pl.ds(n_rows, out_g.shape[0] - n_rows), :] = jnp.zeros((out_g.shape[0] - n_rows, LANES), F32)
    step_rows = 3 * rpc
    loads[0].wait()

    def widen(i, c):
        r = pl.ds(pl.multiple_of(i * step_rows, step_rows), step_rows)
        out_x[r, :] = feat[r, :].astype(F32)
        return c

    lax.fori_loop(0, n_rows // step_rows, widen, 0)

    def relayout(g, c):
        base = g * 16 * rpc
        r = pl.ds(pl.multiple_of(g * 16, 16), 16)
        s_acc = jnp.zeros((16, LANES), F32)
        q_acc = jnp.zeros((16, LANES), F32)
        for b in range(n_img):
            for t in range(tiles):
                k = t * n_img + b
                v = jnp.concatenate(
                    [out_x[pl.ds(base + h * 8 * rpc + k, 8, stride=rpc), :] for h in range(2)], axis=0
                )
                w = v * mask[b, :, t * LANES : (t + 1) * LANES]
                s_acc = s_acc + w
                q_acc = q_acc + w * v
                xb[b, r, t * LANES : (t + 1) * LANES] = v.astype(BF16)
        sum_a[r, :] = s_acc
        sum_b[r, :] = q_acc
        return c

    lax.fori_loop(0, cp // 16, relayout, 0)
    lane1 = iota((1, LANES), 1)
    s0, sq0 = as_rows(sum_a[...], c_sizes), as_rows(sum_b[...], c_sizes)
    ar1[dp, 0:1, :] = s0[0]
    ar1[dp, 1:2, :] = jnp.where(lane1 == LANES - 1, count_here.astype(F32), s0[1])
    ar1[dp, 2:3, :] = sq0[0]
    ar1[dp, 3:4, :] = sq0[1]

    loads[7].wait()
    w2blk[...] = jnp.zeros(w2blk.shape, BF16)
    acc = jnp.zeros((grow, w2blk.shape[1]), F32)
    for t in range(9):
        place = jnp.where(
            iota((grow, w2blk.shape[1]), 1) == iota((grow, w2blk.shape[1]), 0) + t * TAP, 1.0, 0.0
        ).astype(BF16)
        acc = acc + jnp.dot(w2v[t], place, preferred_element_type=F32)
    w2blk[0:grow, :] = acc.astype(BF16)
    loads[5].wait()
    loads[6].wait()
    gsl[ch, 0:1, 0:grow] = gain2v[...]
    gsl[ch, 1:2, 0:grow] = bias2v[...]
    w2r[ch] = w2blk[...]

    pl.semaphore_wait(barrier, n_dev - 1)
    share_start(ar1, dp, n_dp, dp_peer, s1, r1)
    share_start(gsl, ch, n_ch, ch_peer, sb, rb)
    share_start(w2r, ch, n_ch, ch_peer, sw, rw)

    loads[1].wait()
    graw[...] = jnp.zeros(graw.shape, F32)
    picks = [jnp.where(slot_of == ch * per_device + i, 1.0, 0.0) for i in range(per_device)]

    def pick(i, c):
        v = jnp.zeros((rpc, LANES), F32)
        for k in range(per_device):
            v = v + cot[pl.ds(pl.multiple_of((k * grow + i) * rpc, rpc), rpc), :].astype(F32) * picks[k]
        graw[pl.ds(pl.multiple_of(i * rpc, rpc), rpc), :] = v
        return c

    lax.fori_loop(0, grow, pick, 0)

    def by_image(b):
        for t in range(tiles):
            for h in range(TAP // 16):
                v = jnp.concatenate(
                    [
                        graw[pl.ds((h * 16 + i * 8) * rpc + t * n_img + b, 8, stride=rpc), :]
                        for i in range(2)
                    ],
                    axis=0,
                )
                v = v * mask[b, :, t * LANES : (t + 1) * LANES]
                gsend[b, h * 16 : h * 16 + 16, t * LANES : (t + 1) * LANES] = v.astype(BF16)

    by_image(sib)
    by_image(xs)
    g_sib = [
        remote(gsend.at[sib], gsx.at[0], sg.at[0], rg.at[0], {"chan": sib}),
        remote(gsend.at[xs], gsx.at[1], sg.at[1], rg.at[1], {"chan": sib}),
    ]
    for copy in g_sib:
        copy.start()
    by_image(ch)
    by_image(xp)
    for copy in g_sib:
        copy.wait()
    gpair[0] = (gsend[ch].astype(F32) + gsx[0].astype(F32)).astype(BF16)
    gpair[1] = (gsend[xp].astype(F32) + gsx[1].astype(F32)).astype(BF16)
    g_x = [
        remote(gpair.at[0], grx.at[1], sg.at[2], rg.at[3], {"chan": xp}),
        remote(gpair.at[1], grx.at[0], sg.at[3], rg.at[2], {"chan": xp}),
    ]
    for copy in g_x:
        copy.start()

    loads[2].wait()
    w1s[...] = jnp.zeros(w1s.shape, BF16)
    w1s[0:n_d, 0:n_c] = w1v[...]
    rowbuf[...] = jnp.zeros(rowbuf.shape, F32)
    loads[3].wait()
    loads[4].wait()
    rowbuf[0:1, :] = gain1v[0:1, 0:LANES]
    rowbuf[1:2, 0 : n_c - LANES] = gain1v[0:1, LANES:n_c]
    rowbuf[2:3, :] = bias1v[0:1, 0:LANES]
    rowbuf[3:4, 0 : n_c - LANES] = bias1v[0:1, LANES:n_c]

    share_wait(ar1, dp, n_dp, dp_peer, s1, r1)
    tot1 = total(ar1)
    count = tot1[1:2, LANES - 1 : LANES]
    mean1, rstd1, scale1 = [], [], []
    for i in range(2):
        mean = tot1[i : i + 1] / count
        rstd = lax.rsqrt(tot1[2 + i : 3 + i] / count - mean * mean + EPS)
        here = lane1 + i * LANES
        ids = ch * n_c + here
        first = new_slot * grow
        keep = jnp.where(
            (here < n_c) & ((ids < first) | (ids >= first + grow)), 1.0, 0.0
        )
        scale = rstd * rowbuf[i : i + 1, :]
        shift = rowbuf[2 + i : 3 + i, :] - mean * scale
        size = c_sizes[i]
        r = pl.ds(i * LANES, size)
        col_a[r, :] = as_column(0.5 * scale * keep, size)
        col_b[r, :] = as_column(0.5 * shift * keep, size)
        col_m[r, :] = as_column(mean, size)
        col_k[r, :] = as_column(keep, size)
        mean1.append(mean)
        rstd1.append(rstd)
        scale1.append(scale)

    def partial(j, first, n):
        def body(g, c):
            r = pl.ds(pl.multiple_of(g * 16, 16), 16)
            a, b = col_a[r, :], col_b[r, :]
            for t in range(first, first + n):
                sl = slice(t * LANES, (t + 1) * LANES)
                v = xb[j, r, sl].astype(F32) * a + b
                act[j, r, sl] = ((v * jnp.tanh(v) + v) * mask[j, :, sl]).astype(BF16)
            return c

        lax.fori_loop(0, cp // 16, body, 0)
        sl = slice(first * LANES, (first + n) * LANES)
        part[j, :, sl] = jnp.dot(w1s[...], act[j, :, sl], preferred_element_type=F32)

    rows_d = pl.ds(0, d8)
    span = tiles // PIECES

    def lanes_of(p):
        return pl.ds(p * span * LANES, span * LANES)

    to_x = []
    for p in range(PIECES):
        at = lanes_of(p)
        partial(xs, p * span, span)
        over = remote(part.at[xs, rows_d, at], rx_a.at[rows_d, at], sp.at[p], rp.at[p], {"chan": sib})
        over.start()
        partial(xp, p * span, span)
        over.wait()

        def add_a(g, c):
            r = pl.ds(pl.multiple_of(g * 8, 8), 8)
            part[xp, r, at] = part[xp, r, at] + rx_a[r, at]
            return c

        lax.fori_loop(0, d8 // 8, add_a, 0)
        to_x.append(remote(part.at[xp, rows_d, at], rx_x.at[rows_d, at], sq.at[p], rq.at[p], {"chan": xp}))
        to_x[p].start()
    partial(sib, 0, tiles)
    to_sib_b = remote(part.at[sib, rows_d], rx_b.at[rows_d], sx.at[0], rxs.at[0], {"chan": sib})
    to_sib_b.start()
    partial(ch, 0, tiles)

    for copy in g_x:
        copy.wait()
    share_wait(w2r, ch, n_ch, ch_peer, sw, rw)
    share_wait(gsl, ch, n_ch, ch_peer, sb, rb)
    px = iota((TAP, n_px), 1)
    py, pxx = px >> 5, px & (SIDE - 1)
    for i in range(2):
        gcur[...] = gpair[i].astype(F32) + grx[i].astype(F32)
        for ky in range(3):
            for kx in range(3):
                shift = (ky - 1) * SIDE + (kx - 1)
                t = ky * 3 + kx
                v = gcur[...]
                if shift != 0:
                    v = pltpu.roll(v, shift % n_px, 1)
                ok = None
                for off, pos in ((ky - 1, py), (kx - 1, pxx)):
                    if off == 1:
                        test = pos >= 1
                    elif off == -1:
                        test = pos <= SIDE - 2
                    else:
                        continue
                    ok = test if ok is None else ok & test
                if ok is not None:
                    v = jnp.where(ok, v, 0.0)
                g9[i, t * TAP : (t + 1) * TAP, :] = v.astype(BF16)
        g9[i, pl.ds(9 * TAP, TAPS - 9 * TAP), :] = jnp.zeros((TAPS - 9 * TAP, n_px), BF16)
    acc = jnp.zeros((dpad, w2b.shape[1]), F32)
    for j in range(n_ch):
        rows = iota((dpad, TAP), 0)
        cols = iota((dpad, TAP), 1)
        place = jnp.where((rows == cols + j * grow) & (cols < grow), 1.0, 0.0).astype(BF16)
        acc = acc + jnp.dot(place, w2r[j], preferred_element_type=F32)
    w2b[...] = acc.astype(BF16)
    for i in range(2):
        back[i] = jnp.dot(w2b[...], g9[i], preferred_element_type=F32)
    rows = iota((dpad, LANES), 0)
    cols = iota((dpad, LANES), 1)
    gain2c = jnp.zeros((dpad, 1), F32)
    bias2c = jnp.zeros((dpad, 1), F32)
    for j in range(n_ch):
        place = (rows == cols + j * grow) & (cols < grow)
        gain2c = gain2c + jnp.sum(jnp.where(place, gsl[j, 0:1, :], 0.0), axis=1, keepdims=True)
        bias2c = bias2c + jnp.sum(jnp.where(place, gsl[j, 1:2, :], 0.0), axis=1, keepdims=True)
    col_c[0] = jnp.broadcast_to(gain2c, (dpad, LANES))
    col_c[1] = jnp.broadcast_to(bias2c, (dpad, LANES))

    def slopes(j):
        def body(g, c):
            r = pl.ds(pl.multiple_of(g * 16, 16), 16)
            a, b = col_a[r, :], col_b[r, :]
            k = 0.5 * col_k[r, :]
            for t in range(tiles):
                sl = slice(t * LANES, (t + 1) * LANES)
                v = xb[j, r, sl].astype(F32) * a + b
                th = jnp.tanh(v)
                slope[j, r, sl] = ((1.0 + th) * (1.0 + v * (1.0 - th))) * (mask[j, :, sl] * k)
            return c

        lax.fori_loop(0, cp // 16, body, 0)

    for j in range(n_img):
        slopes(j)

    def widen_cot(i, c):
        r = pl.ds(pl.multiple_of(i * step_rows, step_rows), step_rows)
        out_g[r, :] = cot[r, :].astype(F32)
        return c

    lax.fori_loop(0, n_rows // step_rows, widen_cot, 0)

    to_sib_b.wait()
    sum_a[...] = jnp.zeros(sum_a.shape, F32)
    sum_b[...] = jnp.zeros(sum_b.shape, F32)
    hid[:, d8:dpad, :] = jnp.zeros((2, dpad - d8, n_px), F32)
    gp2[...] = jnp.zeros(gp2.shape, F32)

    def across(p):
        at = lanes_of(p)
        return remote(hid.at[0, rows_d, at], hid.at[1, rows_d, at], sh.at[p], rh.at[p], {"chan": xp})

    for p in range(PIECES):
        to_x[p].wait()

        def gather(g, c):
            r = pl.ds(pl.multiple_of(g * 8, 8), 8)
            s_acc, q_acc = sum_a[r, :], sum_b[r, :]
            for t in range(p * span, (p + 1) * span):
                sl = slice(t * LANES, (t + 1) * LANES)
                v = (part[ch, r, sl] + rx_b[r, sl]) + rx_x[r, sl]
                hid[0, r, sl] = v
                s_acc = s_acc + v
                q_acc = q_acc + v * v
            sum_a[r, :] = s_acc
            sum_b[r, :] = q_acc
            return c

        lax.fori_loop(0, d8 // 8, gather, 0)
        if p == 0:
            across(p).start()

    def pack(slots):
        s, q = as_rows(sum_a[0:d8, :], d_sizes), as_rows(sum_b[0:d8, :], d_sizes)
        slots[me, 0:1, :] = s[0]
        slots[me, 1:2, :] = s[1]
        slots[me, 2:3, :] = q[0]
        slots[me, 3:4, :] = q[1]

    def columns_d(row0, row1):
        tail = jnp.zeros((dpad - d8, LANES), F32)
        return jnp.concatenate(
            [as_column(row0, LANES), as_column(row1, d8 - LANES), tail], axis=0
        )

    pack(ar2)
    share_start(ar2, me, n_dev, dev_peer, s2, r2)
    for p in range(1, PIECES - 1):
        across(p).start()

    share_wait(ar2, me, n_dev, dev_peer, s2, r2)
    tot2 = total(ar2)
    mean2 = [tot2[i : i + 1] / count for i in range(2)]
    rstd2 = [lax.rsqrt(tot2[2 + i : 3 + i] / count - mean2[i] * mean2[i] + EPS) for i in range(2)]
    mean2c = columns_d(*mean2)
    rstd2c = columns_d(*rstd2)
    scale2c = rstd2c * col_c[0]
    col_c[2] = mean2c
    col_c[3] = rstd2c
    col_c[4] = scale2c
    col_c[5] = 0.5 * scale2c
    col_c[6] = 0.5 * (col_c[1] - mean2c * scale2c)

    def second(g, c):
        r = pl.ds(pl.multiple_of(g * 16, 16), 16)
        a, b, m = col_c[5, r, :], col_c[6, r, :], col_c[2, r, :]
        s_acc = jnp.zeros((16, LANES), F32)
        q_acc = jnp.zeros((16, LANES), F32)
        for t in range(tiles):
            sl = slice(t * LANES, (t + 1) * LANES)
            h = hid[0, r, sl]
            mk = mask[ch, :, sl]
            v = h * a + b
            th = jnp.tanh(v)
            act2[r, sl] = ((v * th + v) * mk).astype(BF16)
            gp = (0.5 * mk) * ((1.0 + th) * (1.0 + v * (1.0 - th))) * back[0, r, sl]
            gp2[0, r, sl] = gp
            s_acc = s_acc + gp
            q_acc = q_acc + gp * (h - m)
        sum_a[r, :] = s_acc
        sum_b[r, :] = q_acc
        return c

    lax.fori_loop(0, dpad // 16, second, 0)
    pack(ar3)
    share_start(ar3, me, n_dev, dev_peer, s3, r3)
    across(PIECES - 1).start()

    w2acc[...] = lax.dot_general(
        act2[...], g9[0], (((1,), (1,)), ((), ())), preferred_element_type=F32
    )
    cw[...] = jnp.zeros(cw.shape, F32)
    for j in range(n_ch):
        for q in range(20):
            lt, rt = q // 5, q % 5
            cw[j, q // 3, (q % 3) * 8 : (q % 3) * 8 + 8, :] = w2acc[
                j * grow + rt * 8 : j * grow + rt * 8 + 8, lt * LANES : (lt + 1) * LANES
            ]
    w_sib = [
        remote(cw.at[xs], cwr.at[1], sc.at[0], rc.at[0], {"chan": sib}),
        remote(cw.at[sib], cwr.at[0], sc.at[1], rc.at[1], {"chan": sib}),
    ]
    for copy in w_sib:
        copy.start()

    def second_other(p):
        def body(g, c):
            r = pl.ds(pl.multiple_of(g * 16, 16), 16)
            a, b = col_c[5, r, :], col_c[6, r, :]
            for t in range(p * span, (p + 1) * span):
                sl = slice(t * LANES, (t + 1) * LANES)
                v = hid[1, r, sl] * a + b
                th = jnp.tanh(v)
                gp2[1, r, sl] = (
                    (0.5 * mask[xp, :, sl]) * ((1.0 + th) * (1.0 + v * (1.0 - th))) * back[1, r, sl]
                )
            return c

        lax.fori_loop(0, dpad // 16, body, 0)

    for p in range(PIECES - 1):
        across(p).wait()
        second_other(p)
    for copy in w_sib:
        copy.wait()
    cw[xp] = cw[xp] + cwr[1]
    cw[ch] = cw[ch] + cwr[0]
    w_x = remote(cw.at[xp], cwx, sc.at[2], rc.at[2], {"chan": xp})
    w_x.start()

    zbuf[...] = lax.dot_general(
        w2b[...], act2[...], (((0,), (0,)), ((), ())), preferred_element_type=F32
    )
    new = jnp.zeros((TAP, n_px), F32)
    for ky in range(3):
        for kx in range(3):
            shift = (ky - 1) * SIDE + (kx - 1)
            t = ky * 3 + kx
            v = zbuf[t * TAP : (t + 1) * TAP, :]
            if shift != 0:
                v = pltpu.roll(v, (-shift) % n_px, 1)
            ok = None
            for off, pos in ((ky - 1, py), (kx - 1, pxx)):
                if off == -1:
                    test = pos >= 1
                elif off == 1:
                    test = pos <= SIDE - 2
                else:
                    continue
                ok = test if ok is None else ok & test
            if ok is not None:
                v = jnp.where(ok, v, 0.0)
            new = new + v
    new = new * jnp.concatenate([mask[ch]] * (TAP // 16), axis=0)
    gall[ch] = new[0 : gall.shape[1]]
    new_sib = remote(gall.at[ch], gall.at[ch], so.at[0], ro.at[0], {"chan": sib})
    new_xp = remote(gall.at[ch], gall.at[ch], so.at[1], ro.at[1], {"chan": xp})
    new_on = remote(gall.at[xp], gall.at[xp], so.at[2], ro.at[2], {"chan": sib})
    new_xp.start()
    new_sib.start()

    across(PIECES - 1).wait()
    second_other(PIECES - 1)
    share_wait(ar3, me, n_dev, dev_peer, s3, r3)
    tot3 = total(ar3)
    gain_sum2 = [tot3[2 + i : 3 + i] * rstd2[i] for i in range(2)]
    bias_sum2 = [tot3[i : i + 1] for i in range(2)]
    gain_sum2c = columns_d(*gain_sum2)
    bias_sum2c = columns_d(*bias_sum2)
    col_c[5] = col_c[4] * bias_sum2c / count
    col_c[6] = col_c[4] * col_c[3] * gain_sum2c / count

    def third(i, j):
        def body(g, c):
            r = pl.ds(pl.multiple_of(g * 16, 16), 16)
            c1, c2, c3, m = col_c[4, r, :], col_c[5, r, :], col_c[6, r, :], col_c[2, r, :]
            for t in range(tiles):
                sl = slice(t * LANES, (t + 1) * LANES)
                gha[j, r, sl] = (
                    c1 * gp2[i, r, sl] - mask[j, :, sl] * (c2 + c3 * (hid[i, r, sl] - m))
                ).astype(BF16)
            return c

        lax.fori_loop(0, dpad // 16, body, 0)

    third(0, ch)
    grad_sib = remote(gha.at[ch], gha.at[ch], sx.at[1], rxs.at[1], {"chan": sib})
    grad_sib.start()
    third(1, xp)
    grad_xs = remote(gha.at[xp], gha.at[xp], sx.at[2], rxs.at[2], {"chan": sib})
    grad_xs.start()
    d_rows, d_cols = iota((dpad, LANES), 0), iota((dpad, LANES), 1)
    here_d = (d_rows == d_cols + ch * grow) & (d_cols < grow)
    out_g2[...] = jnp.sum(jnp.where(here_d, gain_sum2c, 0.0), axis=0, keepdims=True)[:, 0:grow]
    out_b2[...] = jnp.sum(jnp.where(here_d, bias_sum2c, 0.0), axis=0, keepdims=True)[:, 0:grow]

    w1acc[...] = jnp.zeros(w1acc.shape, F32)
    sum_a[...] = jnp.zeros(sum_a.shape, F32)
    sum_b[...] = jnp.zeros(sum_b.shape, F32)

    def weight_grad(j):
        w1acc[0:dpad, 0:cp] = w1acc[0:dpad, 0:cp] + lax.dot_general(
            gha[j], act[j], (((1,), (1,)), ((), ())), preferred_element_type=F32
        )

    def input_grad(j):
        gact[...] = lax.dot_general(
            w1s[...], gha[j], (((0,), (0,)), ((), ())), preferred_element_type=F32
        )

        def body(g, c):
            r = pl.ds(pl.multiple_of(g * 16, 16), 16)
            m = col_m[r, :]
            s_acc, q_acc = sum_a[r, :], sum_b[r, :]
            for t in range(tiles):
                sl = slice(t * LANES, (t + 1) * LANES)
                gp = gact[r, sl] * slope[j, r, sl]
                gp1[j, r, sl] = gp
                s_acc = s_acc + gp
                q_acc = q_acc + gp * (xb[j, r, sl].astype(F32) - m)
            sum_a[r, :] = s_acc
            sum_b[r, :] = q_acc
            return c

        lax.fori_loop(0, cp // 16, body, 0)

    weight_grad(ch)
    weight_grad(xp)
    w_x.wait()
    for q in range(OWNERS):
        cb[q, 40:64, :] = cw[ch, q] + cwx[q]
    grad_sib.wait()
    weight_grad(sib)
    grad_xs.wait()
    weight_grad(xs)

    for q in range(OWNERS):
        r, h = q % 4, q // 4
        cb[q, 0:40, :] = w1acc[r * 40 : r * 40 + 40, h * LANES : (h + 1) * LANES]
    stride = n_dp // OWNERS
    my_part = dp // stride
    is_owner = lax.rem(dp, stride) == 0

    def part_to(k):
        q = lax.rem(my_part + k, OWNERS)
        return q, q * stride

    def push(k, c):
        q, to = part_to(k)

        @pl.when(to != dp)
        def _():
            remote(cb.at[q], rsl.at[dp], sr.at[k], rr.at[dp], {"dp": to}).start()

        return c

    lax.fori_loop(0, OWNERS, push, 0)
    for j in range(n_img):
        input_grad(j)
    s4_, q4_ = as_rows(sum_a[...], c_sizes), as_rows(sum_b[...], c_sizes)
    for i in range(2):
        ar4[dp, i : i + 1, :] = s4_[i]
        ar4[dp, 2 + i : 3 + i, :] = q4_[i]
    share_start(ar4, dp, n_dp, dp_peer, s4, r4)

    for i in range(2):
        col_a[pl.ds(i * LANES, c_sizes[i]), :] = as_column(scale1[i], c_sizes[i])
        for b in range(n_img):
            for t in range(tiles // 2):
                u = i * (tiles // 2) + t
                mask_raw[u * n_img + b : u * n_img + b + 1, :] = mask[b, 0:1, u * LANES : (u + 1) * LANES]

    def direct(g, c):
        base = g * 16 * rpc
        r = pl.ds(pl.multiple_of(g * 16, 16), 16)
        a, keep = col_a[r, :], col_k[r, :]
        for b in range(n_img):
            for t in range(tiles):
                v = a * gp1[b, r, t * LANES : (t + 1) * LANES]
                for h in range(2):
                    at = pl.ds(base + h * 8 * rpc + t * n_img + b, 8, stride=rpc)
                    out_g[at, :] = out_g[at, :] * keep[h * 8 : h * 8 + 8] + v[h * 8 : h * 8 + 8]
        return c

    lax.fori_loop(0, cp // 16, direct, 0)

    def push_wait(k, c):
        q, to = part_to(k)

        @pl.when(to != dp)
        def _():
            remote(cb.at[q], rsl.at[dp], sr.at[k], rr.at[dp], {"dp": to}).wait_send()

        return c

    def pull(k, c):
        src = lax.rem(dp + k, n_dp)
        remote(cb.at[0], rsl.at[src], sr.at[0], rr.at[src], {"dp": src}).wait_recv()
        return c

    @pl.when(is_owner)
    def _():
        lax.fori_loop(1, n_dp, pull, 0)
        v = cb[my_part]
        for k in range(1, n_dp):
            v = v + rsl[lax.rem(dp + k, n_dp)]
        fin[my_part] = v

        def give(k, c):
            remote(fin.at[my_part], fin.at[my_part], sa.at[k], ra.at[my_part], dp_peer(k)).start()
            return c

        lax.fori_loop(1, n_dp, give, 0)

    lax.fori_loop(0, OWNERS, push_wait, 0)

    new_xp.wait()
    new_on.start()
    new_sib.wait()
    new_on.wait()
    for b in range(n_img):
        for t in range(tiles):
            for h in range(gall.shape[1] // 8):
                graw[pl.ds(h * 8 * rpc + t * n_img + b, 8, stride=rpc), :] = gall[
                    b, h * 8 : h * 8 + 8, t * LANES : (t + 1) * LANES
                ]
    for s in range(per_device):
        chosen = slot_of == ch * per_device + s

        def place_new(i, c):
            src = pl.ds(pl.multiple_of(i * rpc, rpc), rpc)
            dst = pl.ds(pl.multiple_of((s * grow + i) * rpc, rpc), rpc)
            out_x[dst, :] = jnp.where(chosen, graw[src, :], out_x[dst, :])
            return c

        lax.fori_loop(0, grow, place_new, 0)

    share_wait(ar4, dp, n_dp, dp_peer, s4, r4)
    tot4 = total(ar4)
    for i in range(2):
        bias_sum = tot4[i : i + 1]
        gain_sum = tot4[2 + i : 3 + i] * rstd1[i]
        size = c_sizes[i]
        r = pl.ds(i * LANES, size)
        k1 = -scale1[i] * rstd1[i] * gain_sum / count
        k0 = -scale1[i] * bias_sum / count - k1 * mean1[i]
        col_b[r, :] = as_column(k0, size)
        col_m[r, :] = as_column(k1, size)
        width = min(LANES, n_c - i * LANES)
        out_g1[0:1, i * LANES : i * LANES + width] = gain_sum[:, 0:width]
        out_b1[0:1, i * LANES : i * LANES + width] = bias_sum[:, 0:width]
    mask_of = mask_raw[...]

    def last(i, c):
        for k in range(5):
            row = i * 5 + k
            at = pl.ds(pl.multiple_of(row * rpc, rpc), rpc)
            k0 = jnp.broadcast_to(col_b[pl.ds(row, 1), :], (rpc, LANES))
            k1 = jnp.broadcast_to(col_m[pl.ds(row, 1), :], (rpc, LANES))
            out_g[at, :] = out_g[at, :] + mask_of * (k0 + k1 * out_x[at, :])
        return c

    lax.fori_loop(0, n_c // 5, last, 0)

    @pl.when(is_owner)
    def _():
        def gave(k, c):
            remote(fin.at[my_part], fin.at[my_part], sa.at[k], ra.at[my_part], dp_peer(k)).wait_send()
            return c

        lax.fori_loop(1, n_dp, gave, 0)

    def take(q, c):
        @pl.when(q * stride != dp)
        def _():
            remote(fin.at[q], fin.at[q], sa.at[0], ra.at[q], {"dp": q * stride}).wait_recv()

        return c

    lax.fori_loop(0, OWNERS, take, 0)
    for q in range(OWNERS):
        r, h = q % 4, q // 4
        height = min(40, n_d - r * 40)
        width = min(LANES, n_c - h * LANES)
        out_w1[r * 40 : r * 40 + height, h * LANES : h * LANES + width] = fin[q, 0:height, 0:width]
    for q in range(20):
        lt, rt = q // 5, q % 5
        w2acc[rt * 8 : rt * 8 + 8, lt * LANES : (lt + 1) * LANES] = fin[
            q // 3, 40 + (q % 3) * 8 : 48 + (q % 3) * 8, :
        ]
    v = w2acc[0:40, :]
    for t in range(9):
        u = v if t == 0 else pltpu.roll(v, TAPS - t * TAP, 1)
        out_w2[t] = u[0:grow, 0:grow]


def finish(n_rows, *refs):
    n = (len(refs) - 1) // 2
    sem = refs[-1]
    copies = []
    for i in range(n):
        src, dst = refs[i], refs[n + i]
        if i < 2:
            src = src.at[pl.ds(0, n_rows)]
        copies.append(pltpu.make_async_copy(src, dst, sem.at[i]))
    for copy in copies:
        copy.start()
    for copy in copies:
        copy.wait()


def flat(values):
    n, c, p = values.shape
    return (
        values.transpose(1, 0, 2).reshape(c, n, p // LANES, LANES).transpose(0, 2, 1, 3).reshape(-1, LANES)
    )


def unflat(rows, n, c, p):
    return rows.reshape(c, p // LANES, n, LANES).transpose(0, 2, 1, 3).reshape(c, n, p).transpose(1, 0, 2)


def on_device(
    n_dp, n_ch, features, gain1, bias1, weight1, gain2, bias2, weight2, cotangent, image_side, block_slot
):
    n_img, n_c, n_px = features.shape
    n_d = weight1.shape[1]
    grow = weight2.shape[3]
    cp = pad_to(n_c, 16)
    dpad = pad_to(n_d, 16)
    d8 = pad_to(n_d, 8)
    rpc = n_px // LANES * n_img
    n_rows, n_pad = n_c * rpc, cp * rpc
    n_dev = n_dp * n_ch
    cfg = (n_dp, n_ch, n_img, n_c, n_px, n_d, grow)
    args = (
        flat(features),
        flat(cotangent),
        weight1.T,
        gain1.reshape(1, -1),
        bias1.reshape(1, -1),
        gain2.reshape(1, -1),
        bias2.reshape(1, -1),
        weight2.reshape(9, grow, grow),
        image_side,
        block_slot,
    )
    args = [pltpu.with_memory_space_constraint(v, pltpu.HBM) for v in args]
    sd = jax.ShapeDtypeStruct
    in_vmem = pl.BlockSpec(memory_space=pltpu.VMEM)
    in_hbm = pl.BlockSpec(memory_space=pltpu.HBM)
    dma = pltpu.SemaphoreType.DMA
    v = pltpu.VMEM
    scratch = [
        v((n_rows, LANES), BF16), v((n_rows, LANES), BF16), v((n_d, n_c), BF16),
        v((1, n_c), F32), v((1, n_c), F32), v((1, grow), F32), v((1, grow), F32),
        v((9, grow, grow), BF16), pltpu.SMEM(image_side.shape, jnp.int32), pltpu.SMEM(block_slot.shape, jnp.int32),
        v((n_img, 16, n_px), F32), v((rpc, LANES), F32),
        v((n_img, cp, n_px), BF16), v((n_img, cp, n_px), BF16),
        v((n_img, cp, n_px), F32), v((n_img, cp, n_px), F32), v((cp, n_px), F32),
        v((cp, LANES), F32), v((cp, LANES), F32), v((cp, LANES), F32), v((cp, LANES), F32),
        v((7, dpad, LANES), F32), v((cp, LANES), F32), v((cp, LANES), F32), v((8, LANES), F32),
        v((dpad, cp), BF16), v((n_img, dpad, n_px), F32),
        v((dpad, n_px), F32), v((dpad, n_px), F32), v((dpad, n_px), F32), v((2, dpad, n_px), F32),
        v((TAP * rpc, LANES), F32), v((n_ch, TAP, n_px), BF16),
        v((2, TAP, n_px), BF16), v((2, TAP, n_px), BF16), v((2, TAP, n_px), BF16), v((TAP, n_px), F32),
        v((2, TAPS, n_px), BF16), v((TAP, TAPS), BF16), v((n_ch, TAP, TAPS), BF16), v((dpad, TAPS), BF16),
        v((n_ch, 2, LANES), F32),
        v((dpad, n_px), BF16), v((2, dpad, n_px), F32), v((2, dpad, n_px), F32), v((TAPS, n_px), F32),
        v((n_ch, 40, n_px), F32), v((n_ch, dpad, n_px), BF16),
        v((n_ch, OWNERS, 24, LANES), F32), v((2, OWNERS, 24, LANES), F32), v((OWNERS, 24, LANES), F32),
        v((OWNERS, 64, LANES), F32),
        v((n_dp, 64, LANES), F32), v((OWNERS, 64, LANES), F32), v((160, 256), F32), v((dpad, TAPS), F32),
        v((n_dp, 4, LANES), F32), v((n_dev, 4, LANES), F32), v((n_dev, 4, LANES), F32), v((n_dp, 4, LANES), F32),
        dma((10,)),
        dma((n_dp,)), dma((n_dp,)), dma((n_dev,)), dma((n_dev,)), dma((n_dev,)), dma((n_dev,)), dma((n_dp,)), dma((n_dp,)),
        dma((3,)), dma((3,)), dma((PIECES,)), dma((PIECES,)), dma((PIECES,)), dma((PIECES,)),
        dma((4,)), dma((4,)), dma((n_ch,)), dma((n_ch,)), dma((n_ch,)), dma((n_ch,)),
        dma((PIECES,)), dma((PIECES,)), dma((3,)), dma((3,)), dma((3,)), dma((3,)),
        dma((OWNERS,)), dma((n_dp,)), dma((n_dp,)), dma((OWNERS,)),
    ]
    out_shape = (
        sd((n_pad, LANES), F32), sd((n_pad, LANES), F32), sd((n_d, n_c), F32),
        sd((1, n_c), F32), sd((1, n_c), F32), sd((9, grow, grow), F32), sd((1, grow), F32), sd((1, grow), F32),
    )
    outs = pl.pallas_call(
        functools.partial(layer, cfg),
        out_shape=out_shape,
        in_specs=[in_hbm] * len(args),
        out_specs=(in_vmem,) * len(out_shape),
        scratch_shapes=scratch,
        compiler_params=pltpu.CompilerParams(
            collective_id=0, has_side_effects=True, vmem_limit_bytes=40 << 20
        ),
    )(*args)
    final = (sd((n_rows, LANES), F32),) * 2 + out_shape[2:]
    o = pl.pallas_call(
        functools.partial(finish, n_rows),
        out_shape=final,
        in_specs=[in_vmem] * len(final),
        out_specs=(in_hbm,) * len(final),
        scratch_shapes=[dma((len(final),))],
        compiler_params=pltpu.CompilerParams(vmem_limit_bytes=8 << 20),
    )(*outs)
    return (
        unflat(o[0], n_img, n_c, n_px),
        unflat(o[1], n_img, n_c, n_px),
        o[2].T,
        o[3].reshape(-1),
        o[4].reshape(-1),
        o[5].reshape(3, 3, grow, grow),
        o[6].reshape(-1),
        o[7].reshape(-1),
    )


def solution(mesh):
    in_specs = (
        P("dp", "chan", None),
        P("chan"),
        P("chan"),
        P("chan", None),
        P("chan"),
        P("chan"),
        P(None, None, "chan", None),
        P("dp", "chan", None),
        P("dp"),
        P(),
    )
    out_specs = (
        P("dp", "chan", None),
        P("dp", "chan", None),
        P("chan", None),
        P("chan"),
        P("chan"),
        P(None, None, "chan", None),
        P("chan"),
        P("chan"),
    )
    body = functools.partial(on_device, mesh.shape["dp"], mesh.shape["chan"])
    return jax.shard_map(body, mesh=mesh, in_specs=in_specs, out_specs=out_specs, check_vma=False)
```

```python
import functools

import jax
import jax.numpy as jnp
from jax import lax
from jax.experimental import pallas as pl
from jax.experimental.pallas import tpu as pltpu
from jax.sharding import PartitionSpec as P

SIDE = 32
EPS = 1e-05
LANES = 128
TAP = 48
TAPS = 512
PIECES = 4
OWNERS = 8

MESH = pl.DeviceIdType.MESH
F32 = jnp.float32
BF16 = jnp.bfloat16


def pad_to(size, unit):
    return (size + unit - 1) // unit * unit


def iota(shape, axis):
    return lax.broadcasted_iota(jnp.int32, shape, axis)


def as_row(column):
    n = column.shape[0]
    eye = iota((n, LANES), 0) == iota((n, LANES), 1)
    return jnp.sum(jnp.where(eye, column, 0.0), axis=0, keepdims=True)


def as_column(row, n):
    eye = iota((n, LANES), 0) == iota((n, LANES), 1)
    return jnp.broadcast_to(jnp.sum(jnp.where(eye, row, 0.0), axis=1, keepdims=True), (n, LANES))


def as_rows(values, sizes):
    column = jnp.sum(values, axis=1, keepdims=True)
    rows, start = [], 0
    for size in sizes:
        rows.append(as_row(column[start : start + size]))
        start += size
    return rows


def layer(
    cfg,
    feat_h, cot_h, w1_h, gain1_h, bias1_h, gain2_h, bias2_h, w2_h, side_h, slot_h,
    out_x, out_g, out_w1, out_g1, out_b1, out_w2, out_g2, out_b2,
    feat, cot, w1v, gain1v, bias1v, gain2v, bias2v, w2v, side, slot,
    mask, mask_raw, base, xb, act, slope, gp1, gact,
    col_a, col_b, col_m, col_k, col_c, sum_a, sum_b, rowbuf,
    w1s, part, rx_a, rx_b, rx_x, hid,
    graw, gsend, gsx, gpair, grx, gcur, g9, w2blk, w2r, w2b, gsl,
    act2, gp2, back, zbuf, gall, gha,
    cw, cwr, cwx, cb, coded, rsl, fin, w1acc, w2acc,
    ar1, ar2, ar3, ar4,
    load_sem, s1, r1, s2, r2, s3, r3, s4, r4, sx, rxs, sp, rp, sq, rq, sg, rg, sw, rw, sb, rb, sh, rh, so, ro, sc, rc, sr, rr, sa, ra,
):
    n_dp, n_ch, n_img, n_c, n_px, n_d, grow = cfg
    n_dev = n_dp * n_ch
    cp = xb.shape[1]
    dpad = w1s.shape[0]
    d8 = pad_to(n_d, 8)
    tiles = n_px // LANES
    rpc = tiles * n_img
    c_sizes = (LANES, cp - LANES)
    d_sizes = (LANES, d8 - LANES)
    dp = lax.axis_index("dp")
    ch = lax.axis_index("chan")
    me = dp * n_ch + ch
    half = n_ch // 2
    cx, cc = ch // half, lax.rem(ch, half)
    sib = cx * half + (1 - cc)
    xp = (1 - cx) * half + cc
    xs = (1 - cx) * half + (1 - cc)

    def dev_peer(k):
        q = lax.rem(me + k, n_dev)
        return {"dp": q // n_ch, "chan": lax.rem(q, n_ch)}

    def dp_peer(k):
        return {"dp": lax.rem(dp + k, n_dp)}

    def ch_peer(k):
        return {"chan": lax.rem(ch + k, n_ch)}

    loads = [
        pltpu.make_async_copy(h, v, load_sem.at[i])
        for i, (h, v) in enumerate(
            (
                (feat_h, feat), (cot_h, cot), (w1_h, w1v), (gain1_h, gain1v), (bias1_h, bias1v),
                (gain2_h, gain2v), (bias2_h, bias2v), (w2_h, w2v), (side_h, side), (slot_h, slot),
            )
        )
    ]
    for copy in loads:
        copy.start()
    barrier = pltpu.get_barrier_semaphore()

    def greet(k, c):
        pl.semaphore_signal(barrier, inc=1, device_id=dev_peer(k), device_id_type=MESH)
        return c

    lax.fori_loop(1, n_dev, greet, 0)

    def remote(src, dst, send, recv, device):
        return pltpu.make_async_remote_copy(
            src_ref=src, dst_ref=dst, send_sem=send, recv_sem=recv, device_id=device, device_id_type=MESH
        )

    def share_start(slots, mine, count, peer, send, recv):
        def step(k, c):
            remote(slots.at[mine], slots.at[mine], send.at[k], recv.at[k], peer(k)).start()
            return c

        lax.fori_loop(1, count, step, 0)

    def share_wait(slots, mine, count, peer, send, recv):
        def step(k, c):
            remote(slots.at[mine], slots.at[mine], send.at[k], recv.at[k], peer(k)).wait()
            return c

        lax.fori_loop(1, count, step, 0)

    def total(slots):
        if slots.shape[0] <= 32:
            value = slots[0]
            for i in range(1, slots.shape[0]):
                value = value + slots[i]
            return value
        return lax.fori_loop(1, slots.shape[0], lambda i, v: v + slots[i], slots[0])

    for copy in loads[8:]:
        copy.wait()
    lane16 = iota((16, n_px), 1)
    row_of, col_of = lane16 >> 5, lane16 & (SIDE - 1)
    count_here = jnp.int32(0)
    for b in range(n_img):
        s = side[b]
        count_here = count_here + s * s
        mask[b] = jnp.where((row_of < s) & (col_of < s), 1.0, 0.0)
    new_slot = slot[slot.shape[0] - 1]
    per_device = n_c // grow
    slot_of = iota((rpc, LANES), 0) * 0 + new_slot

    n_rows = feat.shape[0]
    out_x[pl.ds(n_rows, out_x.shape[0] - n_rows), :] = jnp.zeros((out_x.shape[0] - n_rows, LANES), F32)
    out_g[pl.ds(n_rows, out_g.shape[0] - n_rows), :] = jnp.zeros((out_g.shape[0] - n_rows, LANES), F32)
    step_rows = 3 * rpc
    loads[0].wait()

    def widen(i, c):
        r = pl.ds(pl.multiple_of(i * step_rows, step_rows), step_rows)
        out_x[r, :] = feat[r, :].astype(F32)
        return c

    lax.fori_loop(0, n_rows // step_rows, widen, 0)

    def relayout(g, c):
        base = g * 16 * rpc
        r = pl.ds(pl.multiple_of(g * 16, 16), 16)
        s_acc = jnp.zeros((16, LANES), F32)
        q_acc = jnp.zeros((16, LANES), F32)
        for b in range(n_img):
            for t in range(tiles):
                k = t * n_img + b
                v = jnp.concatenate(
                    [out_x[pl.ds(base + h * 8 * rpc + k, 8, stride=rpc), :] for h in range(2)], axis=0
                )
                w = v * mask[b, :, t * LANES : (t + 1) * LANES]
                s_acc = s_acc + w
                q_acc = q_acc + w * v
                xb[b, r, t * LANES : (t + 1) * LANES] = v.astype(BF16)
        sum_a[r, :] = s_acc
        sum_b[r, :] = q_acc
        return c

    lax.fori_loop(0, cp // 16, relayout, 0)
    lane1 = iota((1, LANES), 1)
    s0, sq0 = as_rows(sum_a[...], c_sizes), as_rows(sum_b[...], c_sizes)
    ar1[dp, 0:1, :] = s0[0]
    ar1[dp, 1:2, :] = jnp.where(lane1 == LANES - 1, count_here.astype(F32), s0[1])
    ar1[dp, 2:3, :] = sq0[0]
    ar1[dp, 3:4, :] = sq0[1]

    loads[7].wait()
    w2blk[...] = jnp.zeros(w2blk.shape, BF16)
    acc = jnp.zeros((grow, w2blk.shape[1]), F32)
    for t in range(9):
        place = jnp.where(
            iota((grow, w2blk.shape[1]), 1) == iota((grow, w2blk.shape[1]), 0) + t * TAP, 1.0, 0.0
        ).astype(BF16)
        acc = acc + jnp.dot(w2v[t], place, preferred_element_type=F32)
    w2blk[0:grow, :] = acc.astype(BF16)
    loads[5].wait()
    loads[6].wait()
    gsl[ch, 0:1, 0:grow] = gain2v[...]
    gsl[ch, 1:2, 0:grow] = bias2v[...]
    w2r[ch] = w2blk[...]

    loads[1].wait()
    graw[...] = jnp.zeros(graw.shape, F32)
    picks = [jnp.where(slot_of == ch * per_device + i, 1.0, 0.0) for i in range(per_device)]

    def pick(i, c):
        v = jnp.zeros((rpc, LANES), F32)
        for k in range(per_device):
            v = v + cot[pl.ds(pl.multiple_of((k * grow + i) * rpc, rpc), rpc), :].astype(F32) * picks[k]
        graw[pl.ds(pl.multiple_of(i * rpc, rpc), rpc), :] = v
        return c

    lax.fori_loop(0, grow, pick, 0)

    def by_image(b):
        for t in range(tiles):
            for h in range(TAP // 16):
                v = jnp.concatenate(
                    [
                        graw[pl.ds((h * 16 + i * 8) * rpc + t * n_img + b, 8, stride=rpc), :]
                        for i in range(2)
                    ],
                    axis=0,
                )
                v = v * mask[b, :, t * LANES : (t + 1) * LANES]
                gsend[b, h * 16 : h * 16 + 16, t * LANES : (t + 1) * LANES] = v.astype(BF16)

    by_image(sib)
    by_image(xs)
    loads[2].wait()
    w1s[...] = jnp.zeros(w1s.shape, BF16)
    w1s[0:n_d, 0:n_c] = w1v[...]
    rowbuf[...] = jnp.zeros(rowbuf.shape, F32)
    loads[3].wait()
    loads[4].wait()
    rowbuf[0:1, :] = gain1v[0:1, 0:LANES]
    rowbuf[1:2, 0 : n_c - LANES] = gain1v[0:1, LANES:n_c]
    rowbuf[2:3, :] = bias1v[0:1, 0:LANES]
    rowbuf[3:4, 0 : n_c - LANES] = bias1v[0:1, LANES:n_c]

    pl.semaphore_wait(barrier, n_dev - 1)
    share_start(ar1, dp, n_dp, dp_peer, s1, r1)
    share_start(gsl, ch, n_ch, ch_peer, sb, rb)
    share_start(w2r, ch, n_ch, ch_peer, sw, rw)

    by_image(ch)
    by_image(xp)
    g_sib = [
        remote(gsend.at[sib], gsx.at[0], sg.at[0], rg.at[0], {"chan": sib}),
        remote(gsend.at[xs], gsx.at[1], sg.at[1], rg.at[1], {"chan": sib}),
    ]
    for copy in g_sib:
        copy.start()
    for copy in g_sib:
        copy.wait()
    gpair[0] = (gsend[ch].astype(F32) + gsx[0].astype(F32)).astype(BF16)
    gpair[1] = (gsend[xp].astype(F32) + gsx[1].astype(F32)).astype(BF16)
    g_x = [
        remote(gpair.at[0], grx.at[1], sg.at[2], rg.at[3], {"chan": xp}),
        remote(gpair.at[1], grx.at[0], sg.at[3], rg.at[2], {"chan": xp}),
    ]
    for copy in g_x:
        copy.start()

    share_wait(ar1, dp, n_dp, dp_peer, s1, r1)
    tot1 = total(ar1)
    count = tot1[1:2, LANES - 1 : LANES]
    mean1, rstd1, scale1 = [], [], []
    for i in range(2):
        mean = tot1[i : i + 1] / count
        rstd = lax.rsqrt(tot1[2 + i : 3 + i] / count - mean * mean + EPS)
        here = lane1 + i * LANES
        ids = ch * n_c + here
        first = new_slot * grow
        keep = jnp.where(
            (here < n_c) & ((ids < first) | (ids >= first + grow)), 1.0, 0.0
        )
        scale = rstd * rowbuf[i : i + 1, :]
        shift = rowbuf[2 + i : 3 + i, :] - mean * scale
        size = c_sizes[i]
        r = pl.ds(i * LANES, size)
        col_a[r, :] = as_column(0.5 * scale * keep, size)
        col_b[r, :] = as_column(0.5 * shift * keep, size)
        col_m[r, :] = as_column(mean, size)
        col_k[r, :] = as_column(keep, size)
        mean1.append(mean)
        rstd1.append(rstd)
        scale1.append(scale)

    def partial(j, first, n):
        def body(g, c):
            r = pl.ds(pl.multiple_of(g * 16, 16), 16)
            a, b = col_a[r, :], col_b[r, :]
            for t in range(first, first + n):
                sl = slice(t * LANES, (t + 1) * LANES)
                v = xb[j, r, sl].astype(F32) * a + b
                act[j, r, sl] = ((v * jnp.tanh(v) + v) * mask[j, :, sl]).astype(BF16)
            return c

        lax.fori_loop(0, cp // 16, body, 0)
        sl = slice(first * LANES, (first + n) * LANES)
        part[j, :, sl] = jnp.dot(w1s[...], act[j, :, sl], preferred_element_type=F32)

    rows_d = pl.ds(0, d8)
    span = tiles // PIECES

    def lanes_of(p):
        return pl.ds(p * span * LANES, span * LANES)

    to_x = []
    for p in range(PIECES):
        at = lanes_of(p)
        partial(xs, p * span, span)
        over = remote(part.at[xs, rows_d, at], rx_a.at[rows_d, at], sp.at[p], rp.at[p], {"chan": sib})
        over.start()
        partial(xp, p * span, span)
        over.wait()

        def add_a(g, c):
            r = pl.ds(pl.multiple_of(g * 8, 8), 8)
            part[xp, r, at] = part[xp, r, at] + rx_a[r, at]
            return c

        lax.fori_loop(0, d8 // 8, add_a, 0)
        to_x.append(remote(part.at[xp, rows_d, at], rx_x.at[rows_d, at], sq.at[p], rq.at[p], {"chan": xp}))
        to_x[p].start()
    partial(sib, 0, tiles)
    to_sib_b = remote(part.at[sib, rows_d], rx_b.at[rows_d], sx.at[0], rxs.at[0], {"chan": sib})
    to_sib_b.start()
    partial(ch, 0, tiles)

    for copy in g_x:
        copy.wait()
    share_wait(w2r, ch, n_ch, ch_peer, sw, rw)
    share_wait(gsl, ch, n_ch, ch_peer, sb, rb)
    px = iota((TAP, n_px), 1)
    py, pxx = px >> 5, px & (SIDE - 1)
    for i in range(2):
        gcur[...] = gpair[i].astype(F32) + grx[i].astype(F32)
        for ky in range(3):
            for kx in range(3):
                shift = (ky - 1) * SIDE + (kx - 1)
                t = ky * 3 + kx
                v = gcur[...]
                if shift != 0:
                    v = pltpu.roll(v, shift % n_px, 1)
                ok = None
                for off, pos in ((ky - 1, py), (kx - 1, pxx)):
                    if off == 1:
                        test = pos >= 1
                    elif off == -1:
                        test = pos <= SIDE - 2
                    else:
                        continue
                    ok = test if ok is None else ok & test
                if ok is not None:
                    v = jnp.where(ok, v, 0.0)
                g9[i, t * TAP : (t + 1) * TAP, :] = v.astype(BF16)
        g9[i, pl.ds(9 * TAP, TAPS - 9 * TAP), :] = jnp.zeros((TAPS - 9 * TAP, n_px), BF16)
    acc = jnp.zeros((dpad, w2b.shape[1]), F32)
    for j in range(n_ch):
        rows = iota((dpad, TAP), 0)
        cols = iota((dpad, TAP), 1)
        place = jnp.where((rows == cols + j * grow) & (cols < grow), 1.0, 0.0).astype(BF16)
        acc = acc + jnp.dot(place, w2r[j], preferred_element_type=F32)
    w2b[...] = acc.astype(BF16)
    for i in range(2):
        back[i] = jnp.dot(w2b[...], g9[i], preferred_element_type=F32)
    rows = iota((dpad, LANES), 0)
    cols = iota((dpad, LANES), 1)
    gain2c = jnp.zeros((dpad, 1), F32)
    bias2c = jnp.zeros((dpad, 1), F32)
    for j in range(n_ch):
        place = (rows == cols + j * grow) & (cols < grow)
        gain2c = gain2c + jnp.sum(jnp.where(place, gsl[j, 0:1, :], 0.0), axis=1, keepdims=True)
        bias2c = bias2c + jnp.sum(jnp.where(place, gsl[j, 1:2, :], 0.0), axis=1, keepdims=True)
    col_c[0] = jnp.broadcast_to(gain2c, (dpad, LANES))
    col_c[1] = jnp.broadcast_to(bias2c, (dpad, LANES))

    def slopes(j):
        def body(g, c):
            r = pl.ds(pl.multiple_of(g * 16, 16), 16)
            a, b = col_a[r, :], col_b[r, :]
            k = 0.5 * col_k[r, :]
            for t in range(tiles):
                sl = slice(t * LANES, (t + 1) * LANES)
                v = xb[j, r, sl].astype(F32) * a + b
                th = jnp.tanh(v)
                slope[j, r, sl] = ((1.0 + th) * (1.0 + v * (1.0 - th))) * (mask[j, :, sl] * k)
            return c

        lax.fori_loop(0, cp // 16, body, 0)

    for j in range(n_img):
        slopes(j)

    def widen_cot(i, c):
        r = pl.ds(pl.multiple_of(i * step_rows, step_rows), step_rows)
        k = [jnp.broadcast_to(col_k[pl.ds(i * 3 + n, 1), :], (rpc, LANES)) for n in range(3)]
        base[r, :] = cot[r, :].astype(F32) * jnp.concatenate(k, axis=0)
        return c

    lax.fori_loop(0, n_rows // step_rows, widen_cot, 0)

    to_sib_b.wait()
    sum_a[...] = jnp.zeros(sum_a.shape, F32)
    sum_b[...] = jnp.zeros(sum_b.shape, F32)
    hid[:, d8:dpad, :] = jnp.zeros((2, dpad - d8, n_px), F32)
    gp2[...] = jnp.zeros(gp2.shape, F32)

    def across(p):
        at = lanes_of(p)
        return remote(hid.at[0, rows_d, at], hid.at[1, rows_d, at], sh.at[p], rh.at[p], {"chan": xp})

    for p in range(PIECES):
        to_x[p].wait()

        def gather(g, c):
            r = pl.ds(pl.multiple_of(g * 8, 8), 8)
            s_acc, q_acc = sum_a[r, :], sum_b[r, :]
            for t in range(p * span, (p + 1) * span):
                sl = slice(t * LANES, (t + 1) * LANES)
                v = (part[ch, r, sl] + rx_b[r, sl]) + rx_x[r, sl]
                hid[0, r, sl] = v
                s_acc = s_acc + v
                q_acc = q_acc + v * v
            sum_a[r, :] = s_acc
            sum_b[r, :] = q_acc
            return c

        lax.fori_loop(0, d8 // 8, gather, 0)
        if p == 0:
            across(p).start()

    def pack(slots):
        s, q = as_rows(sum_a[0:d8, :], d_sizes), as_rows(sum_b[0:d8, :], d_sizes)
        slots[me, 0:1, :] = s[0]
        slots[me, 1:2, :] = s[1]
        slots[me, 2:3, :] = q[0]
        slots[me, 3:4, :] = q[1]

    def columns_d(row0, row1):
        tail = jnp.zeros((dpad - d8, LANES), F32)
        return jnp.concatenate(
            [as_column(row0, LANES), as_column(row1, d8 - LANES), tail], axis=0
        )

    pack(ar2)
    share_start(ar2, me, n_dev, dev_peer, s2, r2)
    for p in range(1, PIECES - 1):
        across(p).start()

    share_wait(ar2, me, n_dev, dev_peer, s2, r2)
    tot2 = total(ar2)
    mean2 = [tot2[i : i + 1] / count for i in range(2)]
    rstd2 = [lax.rsqrt(tot2[2 + i : 3 + i] / count - mean2[i] * mean2[i] + EPS) for i in range(2)]
    mean2c = columns_d(*mean2)
    rstd2c = columns_d(*rstd2)
    scale2c = rstd2c * col_c[0]
    col_c[2] = mean2c
    col_c[3] = rstd2c
    col_c[4] = scale2c
    col_c[5] = 0.5 * scale2c
    col_c[6] = 0.5 * (col_c[1] - mean2c * scale2c)

    def second(g, c):
        r = pl.ds(pl.multiple_of(g * 16, 16), 16)
        a, b, m = col_c[5, r, :], col_c[6, r, :], col_c[2, r, :]
        s_acc = jnp.zeros((16, LANES), F32)
        q_acc = jnp.zeros((16, LANES), F32)
        for t in range(tiles):
            sl = slice(t * LANES, (t + 1) * LANES)
            h = hid[0, r, sl]
            mk = mask[ch, :, sl]
            v = h * a + b
            th = jnp.tanh(v)
            act2[r, sl] = ((v * th + v) * mk).astype(BF16)
            gp = (0.5 * mk) * ((1.0 + th) * (1.0 + v * (1.0 - th))) * back[0, r, sl]
            gp2[0, r, sl] = gp
            s_acc = s_acc + gp
            q_acc = q_acc + gp * (h - m)
        sum_a[r, :] = s_acc
        sum_b[r, :] = q_acc
        return c

    lax.fori_loop(0, dpad // 16, second, 0)
    pack(ar3)
    share_start(ar3, me, n_dev, dev_peer, s3, r3)
    across(PIECES - 1).start()

    w2acc[...] = lax.dot_general(
        act2[...], g9[0], (((1,), (1,)), ((), ())), preferred_element_type=F32
    )
    for j in range(n_ch):
        for lt in range(4):
            sl = slice(lt * LANES, (lt + 1) * LANES)
            cw[j, lt * 32 : lt * 32 + 32, :] = w2acc[j * grow : j * grow + 32, sl]
            cw[j, 128 + lt : 129 + lt, :] = w2acc[j * grow + 32 : j * grow + 33, sl]
        cw[j, 132:136, :] = jnp.zeros((4, LANES), F32)
    w_sib = [
        remote(cw.at[xs], cwr.at[1], sc.at[0], rc.at[0], {"chan": sib}),
        remote(cw.at[sib], cwr.at[0], sc.at[1], rc.at[1], {"chan": sib}),
    ]
    for copy in w_sib:
        copy.start()

    def second_other(p):
        def body(g, c):
            r = pl.ds(pl.multiple_of(g * 16, 16), 16)
            a, b = col_c[5, r, :], col_c[6, r, :]
            for t in range(p * span, (p + 1) * span):
                sl = slice(t * LANES, (t + 1) * LANES)
                v = hid[1, r, sl] * a + b
                th = jnp.tanh(v)
                gp2[1, r, sl] = (
                    (0.5 * mask[xp, :, sl]) * ((1.0 + th) * (1.0 + v * (1.0 - th))) * back[1, r, sl]
                )
            return c

        lax.fori_loop(0, dpad // 16, body, 0)

    across(0).wait()
    second_other(0)
    for copy in w_sib:
        copy.wait()
    cw[xp] = cw[xp] + cwr[1]
    cw[ch] = cw[ch] + cwr[0]
    w_x = remote(cw.at[xp], cwx, sc.at[2], rc.at[2], {"chan": xp})
    w_x.start()
    for p in range(1, PIECES - 1):
        across(p).wait()
        second_other(p)

    zbuf[...] = lax.dot_general(
        w2b[...], act2[...], (((0,), (0,)), ((), ())), preferred_element_type=F32
    )
    new = jnp.zeros((TAP, n_px), F32)
    for ky in range(3):
        for kx in range(3):
            shift = (ky - 1) * SIDE + (kx - 1)
            t = ky * 3 + kx
            v = zbuf[t * TAP : (t + 1) * TAP, :]
            if shift != 0:
                v = pltpu.roll(v, (-shift) % n_px, 1)
            ok = None
            for off, pos in ((ky - 1, py), (kx - 1, pxx)):
                if off == -1:
                    test = pos >= 1
                elif off == 1:
                    test = pos <= SIDE - 2
                else:
                    continue
                ok = test if ok is None else ok & test
            if ok is not None:
                v = jnp.where(ok, v, 0.0)
            new = new + v
    new = new * jnp.concatenate([mask[ch]] * (TAP // 16), axis=0)
    gall[ch] = new[0 : gall.shape[1]]
    new_sib = remote(gall.at[ch], gall.at[ch], so.at[0], ro.at[0], {"chan": sib})
    new_xp = remote(gall.at[ch], gall.at[ch], so.at[1], ro.at[1], {"chan": xp})
    new_on = remote(gall.at[xp], gall.at[xp], so.at[2], ro.at[2], {"chan": sib})
    new_xp.start()
    new_sib.start()

    share_wait(ar3, me, n_dev, dev_peer, s3, r3)
    tot3 = total(ar3)
    gain_sum2 = [tot3[2 + i : 3 + i] * rstd2[i] for i in range(2)]
    bias_sum2 = [tot3[i : i + 1] for i in range(2)]
    gain_sum2c = columns_d(*gain_sum2)
    bias_sum2c = columns_d(*bias_sum2)
    col_c[7] = col_c[4] * bias_sum2c / count
    col_c[8] = col_c[4] * col_c[3] * gain_sum2c / count

    def third(i, j):
        def body(g, c):
            r = pl.ds(pl.multiple_of(g * 16, 16), 16)
            c1, c2, c3, m = col_c[4, r, :], col_c[7, r, :], col_c[8, r, :], col_c[2, r, :]
            for t in range(tiles):
                sl = slice(t * LANES, (t + 1) * LANES)
                gha[j, r, sl] = (
                    c1 * gp2[i, r, sl] - mask[j, :, sl] * (c2 + c3 * (hid[i, r, sl] - m))
                ).astype(BF16)
            return c

        lax.fori_loop(0, dpad // 16, body, 0)

    third(0, ch)
    grad_sib = remote(gha.at[ch], gha.at[ch], sx.at[1], rxs.at[1], {"chan": sib})
    grad_sib.start()
    across(PIECES - 1).wait()
    second_other(PIECES - 1)
    third(1, xp)
    grad_xs = remote(gha.at[xp], gha.at[xp], sx.at[2], rxs.at[2], {"chan": sib})
    grad_xs.start()
    d_rows, d_cols = iota((dpad, LANES), 0), iota((dpad, LANES), 1)
    here_d = (d_rows == d_cols + ch * grow) & (d_cols < grow)
    out_g2[...] = jnp.sum(jnp.where(here_d, gain_sum2c, 0.0), axis=0, keepdims=True)[:, 0:grow]
    out_b2[...] = jnp.sum(jnp.where(here_d, bias_sum2c, 0.0), axis=0, keepdims=True)[:, 0:grow]

    w1acc[...] = jnp.zeros(w1acc.shape, F32)
    sum_a[...] = jnp.zeros(sum_a.shape, F32)
    sum_b[...] = jnp.zeros(sum_b.shape, F32)

    def weight_grad(j):
        w1acc[0:dpad, 0:cp] = w1acc[0:dpad, 0:cp] + lax.dot_general(
            gha[j], act[j], (((1,), (1,)), ((), ())), preferred_element_type=F32
        )

    def input_grad(j):
        gact[...] = lax.dot_general(
            w1s[...], gha[j], (((0,), (0,)), ((), ())), preferred_element_type=F32
        )

        def body(g, c):
            r = pl.ds(pl.multiple_of(g * 16, 16), 16)
            m = col_m[r, :]
            s_acc, q_acc = sum_a[r, :], sum_b[r, :]
            for t in range(tiles):
                sl = slice(t * LANES, (t + 1) * LANES)
                gp = gact[r, sl] * slope[j, r, sl]
                gp1[j, r, sl] = gp
                s_acc = s_acc + gp
                q_acc = q_acc + gp * (xb[j, r, sl].astype(F32) - m)
            sum_a[r, :] = s_acc
            sum_b[r, :] = q_acc
            return c

        lax.fori_loop(0, cp // 16, body, 0)

    weight_grad(ch)
    weight_grad(xp)
    w_x.wait()
    grad_sib.wait()
    weight_grad(sib)
    input_grad(ch)
    grad_xs.wait()
    weight_grad(xs)

    for r in range(17):
        cb[r // 5, r % 5 * 8 : r % 5 * 8 + 8, :] = w1acc[r * 8 : r * 8 + 8, 0:LANES]
    for k in range(6):
        v = w1acc[k * 8 : k * 8 + 8, LANES : 2 * LANES]
        for i in range(1, 3):
            v = v + pltpu.roll(w1acc[i * 48 + k * 8 : i * 48 + k * 8 + 8, LANES : 2 * LANES], 40 * i, 1)
        r = 17 + k
        cb[r // 5, r % 5 * 8 : r % 5 * 8 + 8, :] = v
    for k in range(17):
        r = 23 + k
        cb[r // 5, r % 5 * 8 : r % 5 * 8 + 8, :] = cw[ch, k * 8 : k * 8 + 8, :] + cwx[k * 8 : k * 8 + 8, :]

    def encode(v):
        top = jnp.maximum(jnp.max(jnp.abs(v), axis=0, keepdims=True), 1e-30)
        power = jnp.floor(jnp.log2(top) + 1.0001)
        q = jnp.clip(jnp.round(v * jnp.exp2(15.0 - power)), -32767.0, 32767.0).astype(jnp.int32)
        low = jnp.concatenate([q[24:40], jnp.broadcast_to(power.astype(jnp.int32), (8, LANES))], axis=0)
        return (q[0:24] << 16) | (low & 0xFFFF)

    def decode(w):
        high, low = w >> 16, (w << 16) >> 16
        scale = jnp.exp2(low[16:24].astype(F32) - 15.0)
        q = jnp.concatenate([high, low[0:16]], axis=0).astype(F32)
        return q * jnp.concatenate([scale] * 5, axis=0)

    for q in range(OWNERS):
        coded[q] = encode(cb[q])
    stride = n_dp // OWNERS
    my_part = dp // stride
    is_owner = lax.rem(dp, stride) == 0

    def part_to(k):
        q = lax.rem(my_part + k, OWNERS)
        return q, q * stride

    def push(k, c):
        q, to = part_to(k)

        @pl.when(to != dp)
        def _():
            remote(coded.at[q], rsl.at[dp], sr.at[k], rr.at[dp], {"dp": to}).start()

        return c

    lax.fori_loop(0, OWNERS, push, 0)
    for j in (xp, sib, xs):
        input_grad(j)
    s4_, q4_ = as_rows(sum_a[...], c_sizes), as_rows(sum_b[...], c_sizes)
    for i in range(2):
        ar4[dp, i : i + 1, :] = s4_[i]
        ar4[dp, 2 + i : 3 + i, :] = q4_[i]
    share_start(ar4, dp, n_dp, dp_peer, s4, r4)

    def scatter(g, c):
        first = g * 16 * rpc
        r = pl.ds(pl.multiple_of(g * 16, 16), 16)
        for b in range(n_img):
            for t in range(tiles):
                v = gp1[b, r, t * LANES : (t + 1) * LANES]
                for h in range(2):
                    at = pl.ds(first + h * 8 * rpc + t * n_img + b, 8, stride=rpc)
                    out_g[at, :] = v[h * 8 : h * 8 + 8]
        return c

    lax.fori_loop(0, cp // 16, scatter, 0)

    def push_wait(k, c):
        q, to = part_to(k)

        @pl.when(to != dp)
        def _():
            remote(coded.at[q], rsl.at[dp], sr.at[k], rr.at[dp], {"dp": to}).wait_send()

        return c

    def pull(k, c):
        src = lax.rem(dp + k, n_dp)
        remote(coded.at[0], rsl.at[src], sr.at[0], rr.at[src], {"dp": src}).wait_recv()
        return c

    @pl.when(is_owner)
    def _():
        lax.fori_loop(1, n_dp, pull, 0)
        v = cb[my_part]
        for k in range(1, n_dp):
            v = v + decode(rsl[lax.rem(dp + k, n_dp)])
        fin[my_part] = encode(v)

        def give(k, c):
            remote(fin.at[my_part], fin.at[my_part], sa.at[k], ra.at[my_part], dp_peer(k)).start()
            return c

        lax.fori_loop(1, n_dp, give, 0)

    lax.fori_loop(0, OWNERS, push_wait, 0)

    for i in range(2):
        col_a[pl.ds(i * LANES, c_sizes[i]), :] = as_column(scale1[i], c_sizes[i])
        for b in range(n_img):
            for t in range(tiles // 2):
                u = i * (tiles // 2) + t
                mask_raw[u * n_img + b : u * n_img + b + 1, :] = mask[b, 0:1, u * LANES : (u + 1) * LANES]

    new_xp.wait()
    new_on.start()
    new_sib.wait()
    new_on.wait()
    for b in range(n_img):
        for t in range(tiles):
            for h in range(gall.shape[1] // 8):
                graw[pl.ds(h * 8 * rpc + t * n_img + b, 8, stride=rpc), :] = gall[
                    b, h * 8 : h * 8 + 8, t * LANES : (t + 1) * LANES
                ]
    for s in range(per_device):
        chosen = slot_of == ch * per_device + s

        def place_new(i, c):
            src = pl.ds(pl.multiple_of(i * rpc, rpc), rpc)
            dst = pl.ds(pl.multiple_of((s * grow + i) * rpc, rpc), rpc)
            out_x[dst, :] = jnp.where(chosen, graw[src, :], out_x[dst, :])
            return c

        lax.fori_loop(0, grow, place_new, 0)

    share_wait(ar4, dp, n_dp, dp_peer, s4, r4)
    tot4 = total(ar4)
    for i in range(2):
        bias_sum = tot4[i : i + 1]
        gain_sum = tot4[2 + i : 3 + i] * rstd1[i]
        size = c_sizes[i]
        r = pl.ds(i * LANES, size)
        k1 = -scale1[i] * rstd1[i] * gain_sum / count
        k0 = -scale1[i] * bias_sum / count - k1 * mean1[i]
        col_b[r, :] = as_column(k0, size)
        col_m[r, :] = as_column(k1, size)
        width = min(LANES, n_c - i * LANES)
        out_g1[0:1, i * LANES : i * LANES + width] = gain_sum[:, 0:width]
        out_b1[0:1, i * LANES : i * LANES + width] = bias_sum[:, 0:width]
    mask_of = mask_raw[...]

    def last(i, c):
        for k in range(5):
            row = i * 5 + k
            at = pl.ds(pl.multiple_of(row * rpc, rpc), rpc)
            k0 = jnp.broadcast_to(col_b[pl.ds(row, 1), :], (rpc, LANES))
            k1 = jnp.broadcast_to(col_m[pl.ds(row, 1), :], (rpc, LANES))
            a = jnp.broadcast_to(col_a[pl.ds(row, 1), :], (rpc, LANES))
            out_g[at, :] = base[at, :] + a * out_g[at, :] + mask_of * (k0 + k1 * out_x[at, :])
        return c

    lax.fori_loop(0, n_c // 5, last, 0)

    @pl.when(is_owner)
    def _():
        def gave(k, c):
            remote(fin.at[my_part], fin.at[my_part], sa.at[k], ra.at[my_part], dp_peer(k)).wait_send()
            return c

        lax.fori_loop(1, n_dp, gave, 0)

    def take(q, c):
        @pl.when(q * stride != dp)
        def _():
            remote(fin.at[q], fin.at[q], sa.at[0], ra.at[q], {"dp": q * stride}).wait_recv()

        return c

    lax.fori_loop(0, OWNERS, take, 0)
    for q in range(OWNERS):
        cb[q] = decode(fin[q])
    for r in range(17):
        height = min(8, n_d - r * 8)
        out_w1[r * 8 : r * 8 + height, 0:LANES] = cb[r // 5, r % 5 * 8 : r % 5 * 8 + height, :]
    for k in range(6):
        r = 17 + k
        v = cb[r // 5, r % 5 * 8 : r % 5 * 8 + 8, :]
        for i in range(3):
            row = i * 48 + k * 8
            height = min(8, n_d - row)
            if height > 0:
                u = v if i == 0 else pltpu.roll(v, LANES - 40 * i, 1)
                out_w1[row : row + height, LANES:n_c] = u[0:height, 0 : n_c - LANES]
    for k in range(17):
        r = 23 + k
        v = cb[r // 5, r % 5 * 8 : r % 5 * 8 + 8, :]
        if k < 16:
            w2acc[k % 4 * 8 : k % 4 * 8 + 8, k // 4 * LANES : (k // 4 + 1) * LANES] = v
        else:
            for lt in range(4):
                w2acc[32:33, lt * LANES : (lt + 1) * LANES] = v[lt : lt + 1]
    v = w2acc[0:40, :]
    for t in range(9):
        u = v if t == 0 else pltpu.roll(v, TAPS - t * TAP, 1)
        out_w2[t] = u[0:grow, 0:grow]


def finish(n_rows, *refs):
    n = (len(refs) - 1) // 2
    sem = refs[-1]
    copies = []
    for i in range(n):
        src, dst = refs[i], refs[n + i]
        if i < 2:
            src = src.at[pl.ds(0, n_rows)]
        copies.append(pltpu.make_async_copy(src, dst, sem.at[i]))
    for copy in copies:
        copy.start()
    for copy in copies:
        copy.wait()


def flat(values):
    n, c, p = values.shape
    return (
        values.transpose(1, 0, 2).reshape(c, n, p // LANES, LANES).transpose(0, 2, 1, 3).reshape(-1, LANES)
    )


def unflat(rows, n, c, p):
    return rows.reshape(c, p // LANES, n, LANES).transpose(0, 2, 1, 3).reshape(c, n, p).transpose(1, 0, 2)


def on_device(
    n_dp, n_ch, features, gain1, bias1, weight1, gain2, bias2, weight2, cotangent, image_side, block_slot
):
    n_img, n_c, n_px = features.shape
    n_d = weight1.shape[1]
    grow = weight2.shape[3]
    cp = pad_to(n_c, 16)
    dpad = pad_to(n_d, 16)
    d8 = pad_to(n_d, 8)
    rpc = n_px // LANES * n_img
    n_rows, n_pad = n_c * rpc, cp * rpc
    n_dev = n_dp * n_ch
    cfg = (n_dp, n_ch, n_img, n_c, n_px, n_d, grow)
    args = (
        flat(features),
        flat(cotangent),
        weight1.T,
        gain1.reshape(1, -1),
        bias1.reshape(1, -1),
        gain2.reshape(1, -1),
        bias2.reshape(1, -1),
        weight2.reshape(9, grow, grow),
        image_side,
        block_slot,
    )
    args = [pltpu.with_memory_space_constraint(v, pltpu.HBM) for v in args]
    sd = jax.ShapeDtypeStruct
    in_vmem = pl.BlockSpec(memory_space=pltpu.VMEM)
    in_hbm = pl.BlockSpec(memory_space=pltpu.HBM)
    dma = pltpu.SemaphoreType.DMA
    v = pltpu.VMEM
    scratch = [
        v((n_rows, LANES), BF16), v((n_rows, LANES), BF16), v((n_d, n_c), BF16),
        v((1, n_c), F32), v((1, n_c), F32), v((1, grow), F32), v((1, grow), F32),
        v((9, grow, grow), BF16), pltpu.SMEM(image_side.shape, jnp.int32), pltpu.SMEM(block_slot.shape, jnp.int32),
        v((n_img, 16, n_px), F32), v((rpc, LANES), F32), v((n_rows, LANES), F32),
        v((n_img, cp, n_px), BF16), v((n_img, cp, n_px), BF16),
        v((n_img, cp, n_px), F32), v((n_img, cp, n_px), F32), v((cp, n_px), F32),
        v((cp, LANES), F32), v((cp, LANES), F32), v((cp, LANES), F32), v((cp, LANES), F32),
        v((9, dpad, LANES), F32), v((cp, LANES), F32), v((cp, LANES), F32), v((8, LANES), F32),
        v((dpad, cp), BF16), v((n_img, dpad, n_px), F32),
        v((dpad, n_px), F32), v((dpad, n_px), F32), v((dpad, n_px), F32), v((2, dpad, n_px), F32),
        v((TAP * rpc, LANES), F32), v((n_ch, TAP, n_px), BF16),
        v((2, TAP, n_px), BF16), v((2, TAP, n_px), BF16), v((2, TAP, n_px), BF16), v((TAP, n_px), F32),
        v((2, TAPS, n_px), BF16), v((TAP, TAPS), BF16), v((n_ch, TAP, TAPS), BF16), v((dpad, TAPS), BF16),
        v((n_ch, 2, LANES), F32),
        v((dpad, n_px), BF16), v((2, dpad, n_px), F32), v((2, dpad, n_px), F32), v((TAPS, n_px), F32),
        v((n_ch, 40, n_px), F32), v((n_ch, dpad, n_px), BF16),
        v((n_ch, 136, LANES), F32), v((2, 136, LANES), F32), v((136, LANES), F32),
        v((OWNERS, 40, LANES), F32), v((OWNERS, 24, LANES), jnp.int32),
        v((n_dp, 24, LANES), jnp.int32), v((OWNERS, 24, LANES), jnp.int32), v((dpad, 256), F32), v((dpad, TAPS), F32),
        v((n_dp, 4, LANES), F32), v((n_dev, 4, LANES), F32), v((n_dev, 4, LANES), F32), v((n_dp, 4, LANES), F32),
        dma((10,)),
        dma((n_dp,)), dma((n_dp,)), dma((n_dev,)), dma((n_dev,)), dma((n_dev,)), dma((n_dev,)), dma((n_dp,)), dma((n_dp,)),
        dma((3,)), dma((3,)), dma((PIECES,)), dma((PIECES,)), dma((PIECES,)), dma((PIECES,)),
        dma((4,)), dma((4,)), dma((n_ch,)), dma((n_ch,)), dma((n_ch,)), dma((n_ch,)),
        dma((PIECES,)), dma((PIECES,)), dma((3,)), dma((3,)), dma((3,)), dma((3,)),
        dma((OWNERS,)), dma((n_dp,)), dma((n_dp,)), dma((OWNERS,)),
    ]
    out_shape = (
        sd((n_pad, LANES), F32), sd((n_pad, LANES), F32), sd((n_d, n_c), F32),
        sd((1, n_c), F32), sd((1, n_c), F32), sd((9, grow, grow), F32), sd((1, grow), F32), sd((1, grow), F32),
    )
    outs = pl.pallas_call(
        functools.partial(layer, cfg),
        out_shape=out_shape,
        in_specs=[in_hbm] * len(args),
        out_specs=(in_vmem,) * len(out_shape),
        scratch_shapes=scratch,
        compiler_params=pltpu.CompilerParams(
            collective_id=0, has_side_effects=True, vmem_limit_bytes=40 << 20
        ),
    )(*args)
    final = (sd((n_rows, LANES), F32),) * 2 + out_shape[2:]
    o = pl.pallas_call(
        functools.partial(finish, n_rows),
        out_shape=final,
        in_specs=[in_vmem] * len(final),
        out_specs=(in_hbm,) * len(final),
        scratch_shapes=[dma((len(final),))],
        compiler_params=pltpu.CompilerParams(vmem_limit_bytes=8 << 20),
    )(*outs)
    return (
        unflat(o[0], n_img, n_c, n_px),
        unflat(o[1], n_img, n_c, n_px),
        o[2].T,
        o[3].reshape(-1),
        o[4].reshape(-1),
        o[5].reshape(3, 3, grow, grow),
        o[6].reshape(-1),
        o[7].reshape(-1),
    )


def solution(mesh):
    in_specs = (
        P("dp", "chan", None),
        P("chan"),
        P("chan"),
        P("chan", None),
        P("chan"),
        P("chan"),
        P(None, None, "chan", None),
        P("dp", "chan", None),
        P("dp"),
        P(),
    )
    out_specs = (
        P("dp", "chan", None),
        P("dp", "chan", None),
        P("chan", None),
        P("chan"),
        P("chan"),
        P(None, None, "chan", None),
        P("chan"),
        P("chan"),
    )
    body = functools.partial(on_device, mesh.shape["dp"], mesh.shape["chan"])
    return jax.shard_map(body, mesh=mesh, in_specs=in_specs, out_specs=out_specs, check_vma=False)
```

```python
import functools

import jax
import jax.numpy as jnp
from jax import lax
from jax.experimental import pallas as pl
from jax.experimental.pallas import tpu as pltpu
from jax.sharding import PartitionSpec as P

SIDE = 32
EPS = 1e-05
LANES = 128
TAP = 48
TAPS = 512
PIECES = 4
LEVELS = 1048000.0
OWNERS = 8

MESH = pl.DeviceIdType.MESH
F32 = jnp.float32
BF16 = jnp.bfloat16


def pad_to(size, unit):
    return (size + unit - 1) // unit * unit


def iota(shape, axis):
    return lax.broadcasted_iota(jnp.int32, shape, axis)


def as_row(column):
    n = column.shape[0]
    eye = iota((n, LANES), 0) == iota((n, LANES), 1)
    return jnp.sum(jnp.where(eye, column, 0.0), axis=0, keepdims=True)


def as_column(row, n):
    eye = iota((n, LANES), 0) == iota((n, LANES), 1)
    return jnp.broadcast_to(jnp.sum(jnp.where(eye, row, 0.0), axis=1, keepdims=True), (n, LANES))


def as_rows(values, sizes):
    column = jnp.sum(values, axis=1, keepdims=True)
    rows, start = [], 0
    for size in sizes:
        rows.append(as_row(column[start : start + size]))
        start += size
    return rows


def layer(
    cfg,
    feat_h, cot_h, w1_h, gain1_h, bias1_h, gain2_h, bias2_h, w2_h, side_h, slot_h,
    out_x, out_g, out_w1, out_g1, out_b1, out_w2, out_g2, out_b2,
    feat, cot, w1v, gain1v, bias1v, gain2v, bias2v, w2v, side, slot,
    mask, mask_raw, base, xb, act, slope, gp1, gact,
    col_a, col_b, col_m, col_k, col_c, sum_a, sum_b, rowbuf,
    w1s, part, rx_a, rx_b, hid, row_top, row_scale, tops_h,
    px_out, px_in, tx_out, tx_in, ph_out, ph_in, th_out, th_in,
    graw, gsend, gsx, gpair, grx, gcur, g9, w2blk, w2r, w2b, gsl,
    act2, gp2, back, zbuf, gall, gha,
    cw, cwr, cwx, cb, coded, rsl, fin, w1acc, w2acc,
    ar1, ar2, ar3, ar4,
    load_sem, s1, r1, s2, r2, s3, r3, s4, r4, sx, rxs, sp, rp, sq, rq, sg, rg, sw, rw, sb, rb, sh, rh, so, ro, sc, rc, sr, rr, sa, ra,
):
    n_dp, n_ch, n_img, n_c, n_px, n_d, grow = cfg
    n_dev = n_dp * n_ch
    cp = xb.shape[1]
    dpad = w1s.shape[0]
    d8 = pad_to(n_d, 8)
    tiles = n_px // LANES
    rpc = tiles * n_img
    c_sizes = (LANES, cp - LANES)
    d_sizes = (LANES, d8 - LANES)
    dp = lax.axis_index("dp")
    ch = lax.axis_index("chan")
    me = dp * n_ch + ch
    half = n_ch // 2
    cx, cc = ch // half, lax.rem(ch, half)
    sib = cx * half + (1 - cc)
    xp = (1 - cx) * half + cc
    xs = (1 - cx) * half + (1 - cc)

    def dev_peer(k):
        q = lax.rem(me + k, n_dev)
        return {"dp": q // n_ch, "chan": lax.rem(q, n_ch)}

    def dp_peer(k):
        return {"dp": lax.rem(dp + k, n_dp)}

    def ch_peer(k):
        return {"chan": lax.rem(ch + k, n_ch)}

    loads = [
        pltpu.make_async_copy(h, v, load_sem.at[i])
        for i, (h, v) in enumerate(
            (
                (feat_h, feat), (cot_h, cot), (w1_h, w1v), (gain1_h, gain1v), (bias1_h, bias1v),
                (gain2_h, gain2v), (bias2_h, bias2v), (w2_h, w2v), (side_h, side), (slot_h, slot),
            )
        )
    ]
    for copy in loads:
        copy.start()
    barrier = pltpu.get_barrier_semaphore()

    def greet(k, c):
        pl.semaphore_signal(barrier, inc=1, device_id=dev_peer(k), device_id_type=MESH)
        return c

    lax.fori_loop(1, n_dev, greet, 0)

    def remote(src, dst, send, recv, device):
        return pltpu.make_async_remote_copy(
            src_ref=src, dst_ref=dst, send_sem=send, recv_sem=recv, device_id=device, device_id_type=MESH
        )

    def share_start(slots, mine, count, peer, send, recv):
        def step(k, c):
            remote(slots.at[mine], slots.at[mine], send.at[k], recv.at[k], peer(k)).start()
            return c

        lax.fori_loop(1, count, step, 0)

    def share_wait(slots, mine, count, peer, send, recv):
        def step(k, c):
            remote(slots.at[mine], slots.at[mine], send.at[k], recv.at[k], peer(k)).wait()
            return c

        lax.fori_loop(1, count, step, 0)

    def total(slots):
        if slots.shape[0] <= 32:
            value = slots[0]
            for i in range(1, slots.shape[0]):
                value = value + slots[i]
            return value
        return lax.fori_loop(1, slots.shape[0], lambda i, v: v + slots[i], slots[0])

    for copy in loads[8:]:
        copy.wait()
    lane16 = iota((16, n_px), 1)
    row_of, col_of = lane16 >> 5, lane16 & (SIDE - 1)
    count_here = jnp.int32(0)
    for b in range(n_img):
        s = side[b]
        count_here = count_here + s * s
        mask[b] = jnp.where((row_of < s) & (col_of < s), 1.0, 0.0)
    new_slot = slot[slot.shape[0] - 1]
    per_device = n_c // grow
    slot_of = iota((rpc, LANES), 0) * 0 + new_slot

    n_rows = feat.shape[0]
    out_x[pl.ds(n_rows, out_x.shape[0] - n_rows), :] = jnp.zeros((out_x.shape[0] - n_rows, LANES), F32)
    out_g[pl.ds(n_rows, out_g.shape[0] - n_rows), :] = jnp.zeros((out_g.shape[0] - n_rows, LANES), F32)
    step_rows = 3 * rpc
    loads[0].wait()

    def widen(i, c):
        r = pl.ds(pl.multiple_of(i * step_rows, step_rows), step_rows)
        out_x[r, :] = feat[r, :].astype(F32)
        return c

    lax.fori_loop(0, n_rows // step_rows, widen, 0)

    def relayout(g, c):
        base = g * 16 * rpc
        r = pl.ds(pl.multiple_of(g * 16, 16), 16)
        s_acc = jnp.zeros((16, LANES), F32)
        q_acc = jnp.zeros((16, LANES), F32)
        for b in range(n_img):
            for t in range(tiles):
                k = t * n_img + b
                v = jnp.concatenate(
                    [out_x[pl.ds(base + h * 8 * rpc + k, 8, stride=rpc), :] for h in range(2)], axis=0
                )
                w = v * mask[b, :, t * LANES : (t + 1) * LANES]
                s_acc = s_acc + w
                q_acc = q_acc + w * v
                xb[b, r, t * LANES : (t + 1) * LANES] = v.astype(BF16)
        sum_a[r, :] = s_acc
        sum_b[r, :] = q_acc
        return c

    lax.fori_loop(0, cp // 16, relayout, 0)
    lane1 = iota((1, LANES), 1)
    s0, sq0 = as_rows(sum_a[...], c_sizes), as_rows(sum_b[...], c_sizes)
    ar1[dp, 0:1, :] = s0[0]
    ar1[dp, 1:2, :] = jnp.where(lane1 == LANES - 1, count_here.astype(F32), s0[1])
    ar1[dp, 2:3, :] = sq0[0]
    ar1[dp, 3:4, :] = sq0[1]

    loads[7].wait()
    w2blk[...] = jnp.zeros(w2blk.shape, BF16)
    acc = jnp.zeros((grow, w2blk.shape[1]), F32)
    for t in range(9):
        place = jnp.where(
            iota((grow, w2blk.shape[1]), 1) == iota((grow, w2blk.shape[1]), 0) + t * TAP, 1.0, 0.0
        ).astype(BF16)
        acc = acc + jnp.dot(w2v[t], place, preferred_element_type=F32)
    w2blk[0:grow, :] = acc.astype(BF16)
    loads[5].wait()
    loads[6].wait()
    gsl[ch, 0:1, 0:grow] = gain2v[...]
    gsl[ch, 1:2, 0:grow] = bias2v[...]
    w2r[ch] = w2blk[...]

    loads[1].wait()
    graw[...] = jnp.zeros(graw.shape, F32)
    picks = [jnp.where(slot_of == ch * per_device + i, 1.0, 0.0) for i in range(per_device)]

    def pick(i, c):
        v = jnp.zeros((rpc, LANES), F32)
        for k in range(per_device):
            v = v + cot[pl.ds(pl.multiple_of((k * grow + i) * rpc, rpc), rpc), :].astype(F32) * picks[k]
        graw[pl.ds(pl.multiple_of(i * rpc, rpc), rpc), :] = v
        return c

    lax.fori_loop(0, grow, pick, 0)

    def by_image(b):
        for t in range(tiles):
            for h in range(TAP // 16):
                v = jnp.concatenate(
                    [
                        graw[pl.ds((h * 16 + i * 8) * rpc + t * n_img + b, 8, stride=rpc), :]
                        for i in range(2)
                    ],
                    axis=0,
                )
                v = v * mask[b, :, t * LANES : (t + 1) * LANES]
                gsend[b, h * 16 : h * 16 + 16, t * LANES : (t + 1) * LANES] = v.astype(BF16)

    by_image(sib)
    by_image(xs)
    loads[2].wait()
    w1s[...] = jnp.zeros(w1s.shape, BF16)
    w1s[0:n_d, 0:n_c] = w1v[...]
    rowbuf[...] = jnp.zeros(rowbuf.shape, F32)
    loads[3].wait()
    loads[4].wait()
    rowbuf[0:1, :] = gain1v[0:1, 0:LANES]
    rowbuf[1:2, 0 : n_c - LANES] = gain1v[0:1, LANES:n_c]
    rowbuf[2:3, :] = bias1v[0:1, 0:LANES]
    rowbuf[3:4, 0 : n_c - LANES] = bias1v[0:1, LANES:n_c]

    pl.semaphore_wait(barrier, n_dev - 1)
    share_start(ar1, dp, n_dp, dp_peer, s1, r1)
    share_start(gsl, ch, n_ch, ch_peer, sb, rb)
    share_start(w2r, ch, n_ch, ch_peer, sw, rw)

    by_image(ch)
    by_image(xp)
    g_sib = [
        remote(gsend.at[sib], gsx.at[0], sg.at[0], rg.at[0], {"chan": sib}),
        remote(gsend.at[xs], gsx.at[1], sg.at[1], rg.at[1], {"chan": sib}),
    ]
    for copy in g_sib:
        copy.start()
    for copy in g_sib:
        copy.wait()
    gpair[0] = (gsend[ch].astype(F32) + gsx[0].astype(F32)).astype(BF16)
    gpair[1] = (gsend[xp].astype(F32) + gsx[1].astype(F32)).astype(BF16)
    g_x = [
        remote(gpair.at[0], grx.at[1], sg.at[2], rg.at[3], {"chan": xp}),
        remote(gpair.at[1], grx.at[0], sg.at[3], rg.at[2], {"chan": xp}),
    ]
    for copy in g_x:
        copy.start()

    share_wait(ar1, dp, n_dp, dp_peer, s1, r1)
    tot1 = total(ar1)
    count = tot1[1:2, LANES - 1 : LANES]
    mean1, rstd1, scale1 = [], [], []
    for i in range(2):
        mean = tot1[i : i + 1] / count
        rstd = lax.rsqrt(tot1[2 + i : 3 + i] / count - mean * mean + EPS)
        here = lane1 + i * LANES
        ids = ch * n_c + here
        first = new_slot * grow
        keep = jnp.where(
            (here < n_c) & ((ids < first) | (ids >= first + grow)), 1.0, 0.0
        )
        scale = rstd * rowbuf[i : i + 1, :]
        shift = rowbuf[2 + i : 3 + i, :] - mean * scale
        size = c_sizes[i]
        r = pl.ds(i * LANES, size)
        col_a[r, :] = as_column(0.5 * scale * keep, size)
        col_b[r, :] = as_column(0.5 * shift * keep, size)
        col_m[r, :] = as_column(mean, size)
        col_k[r, :] = as_column(keep, size)
        mean1.append(mean)
        rstd1.append(rstd)
        scale1.append(scale)

    def partial(j, first, n):
        def body(g, c):
            r = pl.ds(pl.multiple_of(g * 16, 16), 16)
            a, b = col_a[r, :], col_b[r, :]
            for t in range(first, first + n):
                sl = slice(t * LANES, (t + 1) * LANES)
                v = xb[j, r, sl].astype(F32) * a + b
                act[j, r, sl] = ((v * jnp.tanh(v) + v) * mask[j, :, sl]).astype(BF16)
            return c

        lax.fori_loop(0, cp // 16, body, 0)
        sl = slice(first * LANES, (first + n) * LANES)
        part[j, :, sl] = jnp.dot(w1s[...], act[j, :, sl], preferred_element_type=F32)

    rows_d = pl.ds(0, d8)
    span = tiles // PIECES

    def lanes_of(p):
        return pl.ds(p * span * LANES, span * LANES)

    def tiles_of(p):
        return [slice(t * LANES, (t + 1) * LANES) for t in range(p * span, (p + 1) * span)]

    blocks, rest = d8 // 24, d8 // 24 * 24

    def code(read, p, words, tops):
        top = jnp.maximum(jnp.max(row_top[...], axis=1, keepdims=True), 1e-30)
        tops[p, 0:1, :] = as_row(top[0:LANES])
        tops[p, 1:2, :] = as_row(top[LANES:d8])
        row_scale[...] = jnp.broadcast_to(LEVELS / top, (d8, LANES))

        def quantized(first, n, sl):
            r = pl.ds(pl.multiple_of(first, 8), n)
            return jnp.round(read(r, sl) * row_scale[r, :]).astype(jnp.int32)

        def block(i, c):
            for sl in tiles_of(p):
                q0, q1, q2 = (quantized(i * 24 + k * 8, 8, sl) for k in range(3))
                words[pl.ds(pl.multiple_of(i * 16, 8), 8), sl] = (q0 << 11) | ((q2 >> 10) & 0x7FF)
                words[pl.ds(pl.multiple_of(i * 16 + 8, 8), 8), sl] = (q1 << 11) | (q2 & 0x3FF)
            return c

        lax.fori_loop(0, blocks, block, 0)
        for sl in tiles_of(p):
            words[blocks * 16 : blocks * 16 + d8 - rest, sl] = quantized(rest, d8 - rest, sl)

    def unscale(tops, p):
        top = jnp.concatenate([as_column(tops[p, 0:1, :], LANES), as_column(tops[p, 1:2, :], d8 - LANES)], axis=0)
        row_scale[...] = top * (1.0 / LEVELS)

    def uncode(write, p, words):
        def put(first, n, sl, q):
            r = pl.ds(pl.multiple_of(first, 8), n)
            write(r, sl, q.astype(F32) * row_scale[r, :])

        def block(i, c):
            for sl in tiles_of(p):
                w0 = words[pl.ds(pl.multiple_of(i * 16, 8), 8), sl]
                w1 = words[pl.ds(pl.multiple_of(i * 16 + 8, 8), 8), sl]
                put(i * 24, 8, sl, w0 >> 11)
                put(i * 24 + 8, 8, sl, w1 >> 11)
                put(i * 24 + 16, 8, sl, (((w0 << 21) >> 21) << 10) | (w1 & 0x3FF))
            return c

        lax.fori_loop(0, blocks, block, 0)
        for sl in tiles_of(p):
            put(rest, d8 - rest, sl, words[blocks * 16 : blocks * 16 + d8 - rest, sl])

    def top_of(values):
        value = jnp.abs(values[0])
        for other in values[1:]:
            value = jnp.maximum(value, jnp.abs(other))
        return value

    to_x = []
    for p in range(PIECES):
        at = lanes_of(p)
        partial(xs, p * span, span)
        over = remote(part.at[xs, rows_d, at], rx_a.at[rows_d, at], sp.at[p], rp.at[p], {"chan": sib})
        over.start()
        partial(xp, p * span, span)
        over.wait()

        def add_a(g, c):
            r = pl.ds(pl.multiple_of(g * 8, 8), 8)
            values = [part[xp, r, sl] + rx_a[r, sl] for sl in tiles_of(p)]
            for sl, v in zip(tiles_of(p), values):
                part[xp, r, sl] = v
            row_top[r, :] = top_of(values)
            return c

        lax.fori_loop(0, d8 // 8, add_a, 0)
        code(lambda r, sl: part[xp, r, sl], p, px_out, tx_out)
        copies = [
            remote(tx_out.at[p], tx_in.at[p], sq.at[0, p], rq.at[0, p], {"chan": xp}),
            remote(px_out.at[:, at], px_in.at[:, at], sq.at[1, p], rq.at[1, p], {"chan": xp}),
        ]
        for copy in copies:
            copy.start()
        to_x.append(copies)
    partial(sib, 0, tiles)
    to_sib_b = remote(part.at[sib, rows_d], rx_b.at[rows_d], sx.at[0], rxs.at[0], {"chan": sib})
    to_sib_b.start()
    partial(ch, 0, tiles)

    for copy in g_x:
        copy.wait()
    share_wait(w2r, ch, n_ch, ch_peer, sw, rw)
    share_wait(gsl, ch, n_ch, ch_peer, sb, rb)
    px = iota((TAP, n_px), 1)
    py, pxx = px >> 5, px & (SIDE - 1)
    for i in range(2):
        gcur[...] = gpair[i].astype(F32) + grx[i].astype(F32)
        for ky in range(3):
            for kx in range(3):
                shift = (ky - 1) * SIDE + (kx - 1)
                t = ky * 3 + kx
                v = gcur[...]
                if shift != 0:
                    v = pltpu.roll(v, shift % n_px, 1)
                ok = None
                for off, pos in ((ky - 1, py), (kx - 1, pxx)):
                    if off == 1:
                        test = pos >= 1
                    elif off == -1:
                        test = pos <= SIDE - 2
                    else:
                        continue
                    ok = test if ok is None else ok & test
                if ok is not None:
                    v = jnp.where(ok, v, 0.0)
                g9[i, t * TAP : (t + 1) * TAP, :] = v.astype(BF16)
        g9[i, pl.ds(9 * TAP, TAPS - 9 * TAP), :] = jnp.zeros((TAPS - 9 * TAP, n_px), BF16)
    acc = jnp.zeros((dpad, w2b.shape[1]), F32)
    for j in range(n_ch):
        rows = iota((dpad, TAP), 0)
        cols = iota((dpad, TAP), 1)
        place = jnp.where((rows == cols + j * grow) & (cols < grow), 1.0, 0.0).astype(BF16)
        acc = acc + jnp.dot(place, w2r[j], preferred_element_type=F32)
    w2b[...] = acc.astype(BF16)
    for i in range(2):
        back[i] = jnp.dot(w2b[...], g9[i], preferred_element_type=F32)
    rows = iota((dpad, LANES), 0)
    cols = iota((dpad, LANES), 1)
    gain2c = jnp.zeros((dpad, 1), F32)
    bias2c = jnp.zeros((dpad, 1), F32)
    for j in range(n_ch):
        place = (rows == cols + j * grow) & (cols < grow)
        gain2c = gain2c + jnp.sum(jnp.where(place, gsl[j, 0:1, :], 0.0), axis=1, keepdims=True)
        bias2c = bias2c + jnp.sum(jnp.where(place, gsl[j, 1:2, :], 0.0), axis=1, keepdims=True)
    col_c[0] = jnp.broadcast_to(gain2c, (dpad, LANES))
    col_c[1] = jnp.broadcast_to(bias2c, (dpad, LANES))

    def slopes(j):
        def body(g, c):
            r = pl.ds(pl.multiple_of(g * 16, 16), 16)
            a, b = col_a[r, :], col_b[r, :]
            k = 0.5 * col_k[r, :]
            for t in range(tiles):
                sl = slice(t * LANES, (t + 1) * LANES)
                v = xb[j, r, sl].astype(F32) * a + b
                th = jnp.tanh(v)
                slope[j, r, sl] = ((1.0 + th) * (1.0 + v * (1.0 - th))) * (mask[j, :, sl] * k)
            return c

        lax.fori_loop(0, cp // 16, body, 0)

    for j in range(n_img):
        slopes(j)

    def widen_cot(i, c):
        r = pl.ds(pl.multiple_of(i * step_rows, step_rows), step_rows)
        k = [jnp.broadcast_to(col_k[pl.ds(i * 3 + n, 1), :], (rpc, LANES)) for n in range(3)]
        base[r, :] = cot[r, :].astype(F32) * jnp.concatenate(k, axis=0)
        return c

    lax.fori_loop(0, n_rows // step_rows, widen_cot, 0)

    to_sib_b.wait()
    sum_a[...] = jnp.zeros(sum_a.shape, F32)
    sum_b[...] = jnp.zeros(sum_b.shape, F32)
    hid[:, d8:dpad, :] = jnp.zeros((2, dpad - d8, n_px), F32)
    gp2[...] = jnp.zeros(gp2.shape, F32)

    def across(p):
        at = lanes_of(p)
        return [
            remote(th_out.at[p], th_in.at[p], sh.at[0, p], rh.at[0, p], {"chan": xp}),
            remote(ph_out.at[:, at], ph_in.at[:, at], sh.at[1, p], rh.at[1, p], {"chan": xp}),
        ]

    def start_across(p):
        for copy in across(p):
            copy.start()

    for p in range(PIECES):
        for copy in to_x[p]:
            copy.wait()
        unscale(tx_in, p)

        def gather(r, sl, v):
            hid[0, r, sl] = (part[ch, r, sl] + rx_b[r, sl]) + v

        uncode(gather, p, px_in)

        def sums(g, c):
            r = pl.ds(pl.multiple_of(g * 8, 8), 8)
            s_acc, q_acc = sum_a[r, :], sum_b[r, :]
            values = [hid[0, r, sl] for sl in tiles_of(p)]
            for v in values:
                s_acc = s_acc + v
                q_acc = q_acc + v * v
            sum_a[r, :] = s_acc
            sum_b[r, :] = q_acc
            tops_h[p, r, :] = top_of(values)
            return c

        lax.fori_loop(0, d8 // 8, sums, 0)
        if p == 0:
            row_top[...] = tops_h[p]
            code(lambda r, sl: hid[0, r, sl], p, ph_out, th_out)
            start_across(p)

    def pack(slots):
        s, q = as_rows(sum_a[0:d8, :], d_sizes), as_rows(sum_b[0:d8, :], d_sizes)
        slots[me, 0:1, :] = s[0]
        slots[me, 1:2, :] = s[1]
        slots[me, 2:3, :] = q[0]
        slots[me, 3:4, :] = q[1]

    def columns_d(row0, row1):
        tail = jnp.zeros((dpad - d8, LANES), F32)
        return jnp.concatenate(
            [as_column(row0, LANES), as_column(row1, d8 - LANES), tail], axis=0
        )

    pack(ar2)
    share_start(ar2, me, n_dev, dev_peer, s2, r2)
    for p in range(1, PIECES):
        row_top[...] = tops_h[p]
        code(lambda r, sl: hid[0, r, sl], p, ph_out, th_out)
        if p < PIECES - 1:
            start_across(p)

    share_wait(ar2, me, n_dev, dev_peer, s2, r2)
    tot2 = total(ar2)
    mean2 = [tot2[i : i + 1] / count for i in range(2)]
    rstd2 = [lax.rsqrt(tot2[2 + i : 3 + i] / count - mean2[i] * mean2[i] + EPS) for i in range(2)]
    mean2c = columns_d(*mean2)
    rstd2c = columns_d(*rstd2)
    scale2c = rstd2c * col_c[0]
    col_c[2] = mean2c
    col_c[3] = rstd2c
    col_c[4] = scale2c
    col_c[5] = 0.5 * scale2c
    col_c[6] = 0.5 * (col_c[1] - mean2c * scale2c)

    def second(g, c):
        r = pl.ds(pl.multiple_of(g * 16, 16), 16)
        a, b, m = col_c[5, r, :], col_c[6, r, :], col_c[2, r, :]
        s_acc = jnp.zeros((16, LANES), F32)
        q_acc = jnp.zeros((16, LANES), F32)
        for t in range(tiles):
            sl = slice(t * LANES, (t + 1) * LANES)
            h = hid[0, r, sl]
            mk = mask[ch, :, sl]
            v = h * a + b
            th = jnp.tanh(v)
            act2[r, sl] = ((v * th + v) * mk).astype(BF16)
            gp = (0.5 * mk) * ((1.0 + th) * (1.0 + v * (1.0 - th))) * back[0, r, sl]
            gp2[0, r, sl] = gp
            s_acc = s_acc + gp
            q_acc = q_acc + gp * (h - m)
        sum_a[r, :] = s_acc
        sum_b[r, :] = q_acc
        return c

    lax.fori_loop(0, dpad // 16, second, 0)
    pack(ar3)
    share_start(ar3, me, n_dev, dev_peer, s3, r3)
    start_across(PIECES - 1)

    w2acc[...] = lax.dot_general(
        act2[...], g9[0], (((1,), (1,)), ((), ())), preferred_element_type=F32
    )
    for j in range(n_ch):
        for lt in range(4):
            sl = slice(lt * LANES, (lt + 1) * LANES)
            cw[j, lt * 32 : lt * 32 + 32, :] = w2acc[j * grow : j * grow + 32, sl]
            cw[j, 128 + lt : 129 + lt, :] = w2acc[j * grow + 32 : j * grow + 33, sl]
        cw[j, 132:136, :] = jnp.zeros((4, LANES), F32)
    w_sib = [
        remote(cw.at[xs], cwr.at[1], sc.at[0], rc.at[0], {"chan": sib}),
        remote(cw.at[sib], cwr.at[0], sc.at[1], rc.at[1], {"chan": sib}),
    ]
    for copy in w_sib:
        copy.start()

    def second_other(p):
        for copy in across(p):
            copy.wait()
        unscale(th_in, p)

        def keep_hidden(r, sl, v):
            hid[1, r, sl] = v

        uncode(keep_hidden, p, ph_in)

        def body(g, c):
            r = pl.ds(pl.multiple_of(g * 16, 16), 16)
            a, b = col_c[5, r, :], col_c[6, r, :]
            for t in range(p * span, (p + 1) * span):
                sl = slice(t * LANES, (t + 1) * LANES)
                v = hid[1, r, sl] * a + b
                th = jnp.tanh(v)
                gp2[1, r, sl] = (
                    (0.5 * mask[xp, :, sl]) * ((1.0 + th) * (1.0 + v * (1.0 - th))) * back[1, r, sl]
                )
            return c

        lax.fori_loop(0, dpad // 16, body, 0)

    second_other(0)
    for copy in w_sib:
        copy.wait()
    cw[xp] = cw[xp] + cwr[1]
    cw[ch] = cw[ch] + cwr[0]
    w_x = remote(cw.at[xp], cwx, sc.at[2], rc.at[2], {"chan": xp})
    w_x.start()
    for p in range(1, PIECES - 1):
        second_other(p)

    zbuf[...] = lax.dot_general(
        w2b[...], act2[...], (((0,), (0,)), ((), ())), preferred_element_type=F32
    )
    new = jnp.zeros((TAP, n_px), F32)
    for ky in range(3):
        for kx in range(3):
            shift = (ky - 1) * SIDE + (kx - 1)
            t = ky * 3 + kx
            v = zbuf[t * TAP : (t + 1) * TAP, :]
            if shift != 0:
                v = pltpu.roll(v, (-shift) % n_px, 1)
            ok = None
            for off, pos in ((ky - 1, py), (kx - 1, pxx)):
                if off == -1:
                    test = pos >= 1
                elif off == 1:
                    test = pos <= SIDE - 2
                else:
                    continue
                ok = test if ok is None else ok & test
            if ok is not None:
                v = jnp.where(ok, v, 0.0)
            new = new + v
    new = new * jnp.concatenate([mask[ch]] * (TAP // 16), axis=0)
    gall[ch] = new[0 : gall.shape[1]]
    new_sib = remote(gall.at[ch], gall.at[ch], so.at[0], ro.at[0], {"chan": sib})
    new_xp = remote(gall.at[ch], gall.at[ch], so.at[1], ro.at[1], {"chan": xp})
    new_on = remote(gall.at[xp], gall.at[xp], so.at[2], ro.at[2], {"chan": sib})
    new_xp.start()
    new_sib.start()

    share_wait(ar3, me, n_dev, dev_peer, s3, r3)
    tot3 = total(ar3)
    gain_sum2 = [tot3[2 + i : 3 + i] * rstd2[i] for i in range(2)]
    bias_sum2 = [tot3[i : i + 1] for i in range(2)]
    gain_sum2c = columns_d(*gain_sum2)
    bias_sum2c = columns_d(*bias_sum2)
    col_c[7] = col_c[4] * bias_sum2c / count
    col_c[8] = col_c[4] * col_c[3] * gain_sum2c / count

    def third(i, j):
        def body(g, c):
            r = pl.ds(pl.multiple_of(g * 16, 16), 16)
            c1, c2, c3, m = col_c[4, r, :], col_c[7, r, :], col_c[8, r, :], col_c[2, r, :]
            for t in range(tiles):
                sl = slice(t * LANES, (t + 1) * LANES)
                gha[j, r, sl] = (
                    c1 * gp2[i, r, sl] - mask[j, :, sl] * (c2 + c3 * (hid[i, r, sl] - m))
                ).astype(BF16)
            return c

        lax.fori_loop(0, dpad // 16, body, 0)

    third(0, ch)
    grad_sib = remote(gha.at[ch], gha.at[ch], sx.at[1], rxs.at[1], {"chan": sib})
    grad_sib.start()
    second_other(PIECES - 1)
    third(1, xp)
    grad_xs = remote(gha.at[xp], gha.at[xp], sx.at[2], rxs.at[2], {"chan": sib})
    grad_xs.start()
    d_rows, d_cols = iota((dpad, LANES), 0), iota((dpad, LANES), 1)
    here_d = (d_rows == d_cols + ch * grow) & (d_cols < grow)
    out_g2[...] = jnp.sum(jnp.where(here_d, gain_sum2c, 0.0), axis=0, keepdims=True)[:, 0:grow]
    out_b2[...] = jnp.sum(jnp.where(here_d, bias_sum2c, 0.0), axis=0, keepdims=True)[:, 0:grow]

    w1acc[...] = jnp.zeros(w1acc.shape, F32)
    sum_a[...] = jnp.zeros(sum_a.shape, F32)
    sum_b[...] = jnp.zeros(sum_b.shape, F32)

    def weight_grad(j):
        w1acc[0:dpad, 0:cp] = w1acc[0:dpad, 0:cp] + lax.dot_general(
            gha[j], act[j], (((1,), (1,)), ((), ())), preferred_element_type=F32
        )

    def input_grad(j):
        gact[...] = lax.dot_general(
            w1s[...], gha[j], (((0,), (0,)), ((), ())), preferred_element_type=F32
        )

        def body(g, c):
            r = pl.ds(pl.multiple_of(g * 16, 16), 16)
            m = col_m[r, :]
            s_acc, q_acc = sum_a[r, :], sum_b[r, :]
            for t in range(tiles):
                sl = slice(t * LANES, (t + 1) * LANES)
                gp = gact[r, sl] * slope[j, r, sl]
                gp1[j, r, sl] = gp
                s_acc = s_acc + gp
                q_acc = q_acc + gp * (xb[j, r, sl].astype(F32) - m)
            sum_a[r, :] = s_acc
            sum_b[r, :] = q_acc
            return c

        lax.fori_loop(0, cp // 16, body, 0)

    weight_grad(ch)
    weight_grad(xp)
    w_x.wait()
    grad_sib.wait()
    weight_grad(sib)
    input_grad(ch)
    grad_xs.wait()
    weight_grad(xs)

    for r in range(17):
        cb[r // 5, r % 5 * 8 : r % 5 * 8 + 8, :] = w1acc[r * 8 : r * 8 + 8, 0:LANES]
    for k in range(6):
        v = w1acc[k * 8 : k * 8 + 8, LANES : 2 * LANES]
        for i in range(1, 3):
            v = v + pltpu.roll(w1acc[i * 48 + k * 8 : i * 48 + k * 8 + 8, LANES : 2 * LANES], 40 * i, 1)
        r = 17 + k
        cb[r // 5, r % 5 * 8 : r % 5 * 8 + 8, :] = v
    for k in range(17):
        r = 23 + k
        cb[r // 5, r % 5 * 8 : r % 5 * 8 + 8, :] = cw[ch, k * 8 : k * 8 + 8, :] + cwx[k * 8 : k * 8 + 8, :]

    def encode(v):
        top = jnp.maximum(jnp.max(jnp.abs(v), axis=0, keepdims=True), 1e-30)
        power = jnp.floor(jnp.log2(top) + 1.0001)
        q = jnp.clip(jnp.round(v * jnp.exp2(15.0 - power)), -32767.0, 32767.0).astype(jnp.int32)
        low = jnp.concatenate([q[24:40], jnp.broadcast_to(power.astype(jnp.int32), (8, LANES))], axis=0)
        return (q[0:24] << 16) | (low & 0xFFFF)

    def decode(w):
        high, low = w >> 16, (w << 16) >> 16
        scale = jnp.exp2(low[16:24].astype(F32) - 15.0)
        q = jnp.concatenate([high, low[0:16]], axis=0).astype(F32)
        return q * jnp.concatenate([scale] * 5, axis=0)

    for q in range(OWNERS):
        coded[q] = encode(cb[q])
    stride = n_dp // OWNERS
    my_part = dp // stride
    is_owner = lax.rem(dp, stride) == 0

    def part_to(k):
        q = lax.rem(my_part + k, OWNERS)
        return q, q * stride

    def push(k, c):
        q, to = part_to(k)

        @pl.when(to != dp)
        def _():
            remote(coded.at[q], rsl.at[dp], sr.at[k], rr.at[dp], {"dp": to}).start()

        return c

    lax.fori_loop(0, OWNERS, push, 0)
    for j in (xp, sib, xs):
        input_grad(j)
    s4_, q4_ = as_rows(sum_a[...], c_sizes), as_rows(sum_b[...], c_sizes)
    for i in range(2):
        ar4[dp, i : i + 1, :] = s4_[i]
        ar4[dp, 2 + i : 3 + i, :] = q4_[i]
    share_start(ar4, dp, n_dp, dp_peer, s4, r4)

    def scatter(g, c):
        first = g * 16 * rpc
        r = pl.ds(pl.multiple_of(g * 16, 16), 16)
        for b in range(n_img):
            for t in range(tiles):
                v = gp1[b, r, t * LANES : (t + 1) * LANES]
                for h in range(2):
                    at = pl.ds(first + h * 8 * rpc + t * n_img + b, 8, stride=rpc)
                    out_g[at, :] = v[h * 8 : h * 8 + 8]
        return c

    lax.fori_loop(0, cp // 16, scatter, 0)

    def push_wait(k, c):
        q, to = part_to(k)

        @pl.when(to != dp)
        def _():
            remote(coded.at[q], rsl.at[dp], sr.at[k], rr.at[dp], {"dp": to}).wait_send()

        return c

    def pull(k, c):
        src = lax.rem(dp + k, n_dp)
        remote(coded.at[0], rsl.at[src], sr.at[0], rr.at[src], {"dp": src}).wait_recv()
        return c

    @pl.when(is_owner)
    def _():
        lax.fori_loop(1, n_dp, pull, 0)
        v = cb[my_part]
        for k in range(1, n_dp):
            v = v + decode(rsl[lax.rem(dp + k, n_dp)])
        fin[my_part] = encode(v)

        def give(k, c):
            remote(fin.at[my_part], fin.at[my_part], sa.at[k], ra.at[my_part], dp_peer(k)).start()
            return c

        lax.fori_loop(1, n_dp, give, 0)

    lax.fori_loop(0, OWNERS, push_wait, 0)

    for i in range(2):
        col_a[pl.ds(i * LANES, c_sizes[i]), :] = as_column(scale1[i], c_sizes[i])
        for b in range(n_img):
            for t in range(tiles // 2):
                u = i * (tiles // 2) + t
                mask_raw[u * n_img + b : u * n_img + b + 1, :] = mask[b, 0:1, u * LANES : (u + 1) * LANES]

    new_xp.wait()
    new_on.start()
    new_sib.wait()
    new_on.wait()
    for b in range(n_img):
        for t in range(tiles):
            for h in range(gall.shape[1] // 8):
                graw[pl.ds(h * 8 * rpc + t * n_img + b, 8, stride=rpc), :] = gall[
                    b, h * 8 : h * 8 + 8, t * LANES : (t + 1) * LANES
                ]
    for s in range(per_device):
        chosen = slot_of == ch * per_device + s

        def place_new(i, c):
            src = pl.ds(pl.multiple_of(i * rpc, rpc), rpc)
            dst = pl.ds(pl.multiple_of((s * grow + i) * rpc, rpc), rpc)
            out_x[dst, :] = jnp.where(chosen, graw[src, :], out_x[dst, :])
            return c

        lax.fori_loop(0, grow, place_new, 0)

    share_wait(ar4, dp, n_dp, dp_peer, s4, r4)
    tot4 = total(ar4)
    for i in range(2):
        bias_sum = tot4[i : i + 1]
        gain_sum = tot4[2 + i : 3 + i] * rstd1[i]
        size = c_sizes[i]
        r = pl.ds(i * LANES, size)
        k1 = -scale1[i] * rstd1[i] * gain_sum / count
        k0 = -scale1[i] * bias_sum / count - k1 * mean1[i]
        col_b[r, :] = as_column(k0, size)
        col_m[r, :] = as_column(k1, size)
        width = min(LANES, n_c - i * LANES)
        out_g1[0:1, i * LANES : i * LANES + width] = gain_sum[:, 0:width]
        out_b1[0:1, i * LANES : i * LANES + width] = bias_sum[:, 0:width]
    mask_of = mask_raw[...]

    def last(i, c):
        for k in range(5):
            row = i * 5 + k
            at = pl.ds(pl.multiple_of(row * rpc, rpc), rpc)
            k0 = jnp.broadcast_to(col_b[pl.ds(row, 1), :], (rpc, LANES))
            k1 = jnp.broadcast_to(col_m[pl.ds(row, 1), :], (rpc, LANES))
            a = jnp.broadcast_to(col_a[pl.ds(row, 1), :], (rpc, LANES))
            out_g[at, :] = base[at, :] + a * out_g[at, :] + mask_of * (k0 + k1 * out_x[at, :])
        return c

    lax.fori_loop(0, n_c // 5, last, 0)

    @pl.when(is_owner)
    def _():
        def gave(k, c):
            remote(fin.at[my_part], fin.at[my_part], sa.at[k], ra.at[my_part], dp_peer(k)).wait_send()
            return c

        lax.fori_loop(1, n_dp, gave, 0)

    def take(q, c):
        @pl.when(q * stride != dp)
        def _():
            remote(fin.at[q], fin.at[q], sa.at[0], ra.at[q], {"dp": q * stride}).wait_recv()

        return c

    lax.fori_loop(0, OWNERS, take, 0)
    for q in range(OWNERS):
        cb[q] = decode(fin[q])
    for r in range(17):
        height = min(8, n_d - r * 8)
        out_w1[r * 8 : r * 8 + height, 0:LANES] = cb[r // 5, r % 5 * 8 : r % 5 * 8 + height, :]
    for k in range(6):
        r = 17 + k
        v = cb[r // 5, r % 5 * 8 : r % 5 * 8 + 8, :]
        for i in range(3):
            row = i * 48 + k * 8
            height = min(8, n_d - row)
            if height > 0:
                u = v if i == 0 else pltpu.roll(v, LANES - 40 * i, 1)
                out_w1[row : row + height, LANES:n_c] = u[0:height, 0 : n_c - LANES]
    for k in range(17):
        r = 23 + k
        v = cb[r // 5, r % 5 * 8 : r % 5 * 8 + 8, :]
        if k < 16:
            w2acc[k % 4 * 8 : k % 4 * 8 + 8, k // 4 * LANES : (k // 4 + 1) * LANES] = v
        else:
            for lt in range(4):
                w2acc[32:33, lt * LANES : (lt + 1) * LANES] = v[lt : lt + 1]
    v = w2acc[0:40, :]
    for t in range(9):
        u = v if t == 0 else pltpu.roll(v, TAPS - t * TAP, 1)
        out_w2[t] = u[0:grow, 0:grow]


def finish(n_rows, *refs):
    n = (len(refs) - 1) // 2
    sem = refs[-1]
    copies = []
    for i in range(n):
        src, dst = refs[i], refs[n + i]
        if i < 2:
            src = src.at[pl.ds(0, n_rows)]
        copies.append(pltpu.make_async_copy(src, dst, sem.at[i]))
    for copy in copies:
        copy.start()
    for copy in copies:
        copy.wait()


def flat(values):
    n, c, p = values.shape
    return (
        values.transpose(1, 0, 2).reshape(c, n, p // LANES, LANES).transpose(0, 2, 1, 3).reshape(-1, LANES)
    )


def unflat(rows, n, c, p):
    return rows.reshape(c, p // LANES, n, LANES).transpose(0, 2, 1, 3).reshape(c, n, p).transpose(1, 0, 2)


def on_device(
    n_dp, n_ch, features, gain1, bias1, weight1, gain2, bias2, weight2, cotangent, image_side, block_slot
):
    n_img, n_c, n_px = features.shape
    n_d = weight1.shape[1]
    grow = weight2.shape[3]
    cp = pad_to(n_c, 16)
    dpad = pad_to(n_d, 16)
    d8 = pad_to(n_d, 8)
    rpc = n_px // LANES * n_img
    n_rows, n_pad = n_c * rpc, cp * rpc
    n_dev = n_dp * n_ch
    words = d8 // 24 * 16 + d8 % 24
    cfg = (n_dp, n_ch, n_img, n_c, n_px, n_d, grow)
    args = (
        flat(features),
        flat(cotangent),
        weight1.T,
        gain1.reshape(1, -1),
        bias1.reshape(1, -1),
        gain2.reshape(1, -1),
        bias2.reshape(1, -1),
        weight2.reshape(9, grow, grow),
        image_side,
        block_slot,
    )
    args = [pltpu.with_memory_space_constraint(v, pltpu.HBM) for v in args]
    sd = jax.ShapeDtypeStruct
    in_vmem = pl.BlockSpec(memory_space=pltpu.VMEM)
    in_hbm = pl.BlockSpec(memory_space=pltpu.HBM)
    dma = pltpu.SemaphoreType.DMA
    v = pltpu.VMEM
    scratch = [
        v((n_rows, LANES), BF16), v((n_rows, LANES), BF16), v((n_d, n_c), BF16),
        v((1, n_c), F32), v((1, n_c), F32), v((1, grow), F32), v((1, grow), F32),
        v((9, grow, grow), BF16), pltpu.SMEM(image_side.shape, jnp.int32), pltpu.SMEM(block_slot.shape, jnp.int32),
        v((n_img, 16, n_px), F32), v((rpc, LANES), F32), v((n_rows, LANES), F32),
        v((n_img, cp, n_px), BF16), v((n_img, cp, n_px), BF16),
        v((n_img, cp, n_px), F32), v((n_img, cp, n_px), F32), v((cp, n_px), F32),
        v((cp, LANES), F32), v((cp, LANES), F32), v((cp, LANES), F32), v((cp, LANES), F32),
        v((9, dpad, LANES), F32), v((cp, LANES), F32), v((cp, LANES), F32), v((8, LANES), F32),
        v((dpad, cp), BF16), v((n_img, dpad, n_px), F32),
        v((dpad, n_px), F32), v((dpad, n_px), F32), v((2, dpad, n_px), F32),
        v((d8, LANES), F32), v((d8, LANES), F32), v((PIECES, d8, LANES), F32),
        v((words, n_px), jnp.int32), v((words, n_px), jnp.int32), v((PIECES, 2, LANES), F32), v((PIECES, 2, LANES), F32),
        v((words, n_px), jnp.int32), v((words, n_px), jnp.int32), v((PIECES, 2, LANES), F32), v((PIECES, 2, LANES), F32),
        v((TAP * rpc, LANES), F32), v((n_ch, TAP, n_px), BF16),
        v((2, TAP, n_px), BF16), v((2, TAP, n_px), BF16), v((2, TAP, n_px), BF16), v((TAP, n_px), F32),
        v((2, TAPS, n_px), BF16), v((TAP, TAPS), BF16), v((n_ch, TAP, TAPS), BF16), v((dpad, TAPS), BF16),
        v((n_ch, 2, LANES), F32),
        v((dpad, n_px), BF16), v((2, dpad, n_px), F32), v((2, dpad, n_px), F32), v((TAPS, n_px), F32),
        v((n_ch, 40, n_px), F32), v((n_ch, dpad, n_px), BF16),
        v((n_ch, 136, LANES), F32), v((2, 136, LANES), F32), v((136, LANES), F32),
        v((OWNERS, 40, LANES), F32), v((OWNERS, 24, LANES), jnp.int32),
        v((n_dp, 24, LANES), jnp.int32), v((OWNERS, 24, LANES), jnp.int32), v((dpad, 256), F32), v((dpad, TAPS), F32),
        v((n_dp, 4, LANES), F32), v((n_dev, 4, LANES), F32), v((n_dev, 4, LANES), F32), v((n_dp, 4, LANES), F32),
        dma((10,)),
        dma((n_dp,)), dma((n_dp,)), dma((n_dev,)), dma((n_dev,)), dma((n_dev,)), dma((n_dev,)), dma((n_dp,)), dma((n_dp,)),
        dma((3,)), dma((3,)), dma((PIECES,)), dma((PIECES,)), dma((2, PIECES)), dma((2, PIECES)),
        dma((4,)), dma((4,)), dma((n_ch,)), dma((n_ch,)), dma((n_ch,)), dma((n_ch,)),
        dma((2, PIECES)), dma((2, PIECES)), dma((3,)), dma((3,)), dma((3,)), dma((3,)),
        dma((OWNERS,)), dma((n_dp,)), dma((n_dp,)), dma((OWNERS,)),
    ]
    out_shape = (
        sd((n_pad, LANES), F32), sd((n_pad, LANES), F32), sd((n_d, n_c), F32),
        sd((1, n_c), F32), sd((1, n_c), F32), sd((9, grow, grow), F32), sd((1, grow), F32), sd((1, grow), F32),
    )
    outs = pl.pallas_call(
        functools.partial(layer, cfg),
        out_shape=out_shape,
        in_specs=[in_hbm] * len(args),
        out_specs=(in_vmem,) * len(out_shape),
        scratch_shapes=scratch,
        compiler_params=pltpu.CompilerParams(
            collective_id=0, has_side_effects=True, vmem_limit_bytes=40 << 20
        ),
    )(*args)
    final = (sd((n_rows, LANES), F32),) * 2 + out_shape[2:]
    o = pl.pallas_call(
        functools.partial(finish, n_rows),
        out_shape=final,
        in_specs=[in_vmem] * len(final),
        out_specs=(in_hbm,) * len(final),
        scratch_shapes=[dma((len(final),))],
        compiler_params=pltpu.CompilerParams(vmem_limit_bytes=8 << 20),
    )(*outs)
    return (
        unflat(o[0], n_img, n_c, n_px),
        unflat(o[1], n_img, n_c, n_px),
        o[2].T,
        o[3].reshape(-1),
        o[4].reshape(-1),
        o[5].reshape(3, 3, grow, grow),
        o[6].reshape(-1),
        o[7].reshape(-1),
    )


def solution(mesh):
    in_specs = (
        P("dp", "chan", None),
        P("chan"),
        P("chan"),
        P("chan", None),
        P("chan"),
        P("chan"),
        P(None, None, "chan", None),
        P("dp", "chan", None),
        P("dp"),
        P(),
    )
    out_specs = (
        P("dp", "chan", None),
        P("dp", "chan", None),
        P("chan", None),
        P("chan"),
        P("chan"),
        P(None, None, "chan", None),
        P("chan"),
        P("chan"),
    )
    body = functools.partial(on_device, mesh.shape["dp"], mesh.shape["chan"])
    return jax.shard_map(body, mesh=mesh, in_specs=in_specs, out_specs=out_specs, check_vma=False)
```

```python
import functools

import jax
import jax.numpy as jnp
from jax import lax
from jax.experimental import pallas as pl
from jax.experimental.pallas import tpu as pltpu
from jax.sharding import PartitionSpec as P

SIDE = 32
EPS = 1e-05
LANES = 128
TAP = 48
TAPS = 512
SPANS = (1, 2, 3, 2)
PIECES = len(SPANS)
AHEAD = 2
LEVELS = 1048000.0
OWNERS = 8

MESH = pl.DeviceIdType.MESH
F32 = jnp.float32
BF16 = jnp.bfloat16


def pad_to(size, unit):
    return (size + unit - 1) // unit * unit


def iota(shape, axis):
    return lax.broadcasted_iota(jnp.int32, shape, axis)


def as_row(column):
    n = column.shape[0]
    eye = iota((n, LANES), 0) == iota((n, LANES), 1)
    return jnp.sum(jnp.where(eye, column, 0.0), axis=0, keepdims=True)


def as_column(row, n):
    eye = iota((n, LANES), 0) == iota((n, LANES), 1)
    return jnp.broadcast_to(jnp.sum(jnp.where(eye, row, 0.0), axis=1, keepdims=True), (n, LANES))


def as_rows(values, sizes):
    column = jnp.sum(values, axis=1, keepdims=True)
    rows, start = [], 0
    for size in sizes:
        rows.append(as_row(column[start : start + size]))
        start += size
    return rows


def layer(
    cfg,
    feat_h, cot_h, w1_h, gain1_h, bias1_h, gain2_h, bias2_h, w2_h, side_h, slot_h,
    out_x, out_g, out_w1, out_g1, out_b1, out_w2, out_g2, out_b2, out_new, out_slot,
    feat, cot, w1v, gain1v, bias1v, gain2v, bias2v, w2v, side, slot,
    mask, mask_raw, base, xb, act, slope, gp1, gact,
    col_a, col_b, col_m, col_k, col_c, sum_a, sum_b, sums_s, sums_q, rowbuf,
    w1s, part, rx_a, rx_b, hid, row_top, row_scale, tops_h,
    px_out, px_in, tx_out, tx_in, ph_out, ph_in, th_out, th_in,
    graw, gsend, gsx, gpair, grx, gcur, g9, w2blk, w2r, w2b, gsl,
    act2, gp2, back, zbuf, gall, gha,
    cw, cwr, cwx, cb, coded, rsl, fin, w1acc, w2acc,
    ar1, ar2, ar3, ar4,
    load_sem, s1, r1, s2, r2, s3, r3, s4, r4, sx, rxs, sp, rp, sq, rq, sg, rg, sw, rw, sb, rb, sh, rh, st, rt, so, ro, sc, rc, sr, rr, sa, ra,
):
    n_dp, n_ch, n_img, n_c, n_px, n_d, grow = cfg
    n_dev = n_dp * n_ch
    cp = xb.shape[1]
    dpad = w1s.shape[0]
    d8 = pad_to(n_d, 8)
    tiles = n_px // LANES
    rpc = tiles * n_img
    c_sizes = (LANES, cp - LANES)
    d_sizes = (LANES, d8 - LANES)
    dp = lax.axis_index("dp")
    ch = lax.axis_index("chan")
    me = dp * n_ch + ch
    half = n_ch // 2
    cx, cc = ch // half, lax.rem(ch, half)
    sib = cx * half + (1 - cc)
    xp = (1 - cx) * half + cc
    xs = (1 - cx) * half + (1 - cc)

    def dev_peer(k):
        q = me ^ k
        return {"dp": q // n_ch, "chan": lax.rem(q, n_ch)}

    def dp_peer(k):
        return {"dp": dp ^ k}

    def ch_peer(k):
        return {"chan": ch ^ k}

    def far_first(count, step):
        if count <= 32:
            for k in range(count - 1, 0, -1):
                step(k)
        else:

            def body(i, c):
                step(count - 1 - i)
                return c

            lax.fori_loop(0, count - 1, body, 0)

    loads = [
        pltpu.make_async_copy(h, v, load_sem.at[i])
        for i, (h, v) in enumerate(
            (
                (feat_h, feat), (cot_h, cot), (w1_h, w1v), (gain1_h, gain1v), (bias1_h, bias1v),
                (gain2_h, gain2v), (bias2_h, bias2v), (w2_h, w2v), (side_h, side), (slot_h, slot),
            )
        )
    ]
    for copy in loads:
        copy.start()
    barrier = pltpu.get_barrier_semaphore()

    def greet(k):
        pl.semaphore_signal(barrier, inc=1, device_id=dev_peer(k), device_id_type=MESH)

    far_first(n_dev, greet)

    def remote(src, dst, send, recv, device):
        return pltpu.make_async_remote_copy(
            src_ref=src, dst_ref=dst, send_sem=send, recv_sem=recv, device_id=device, device_id_type=MESH
        )

    def share_start(slots, mine, count, peer, send, recv):
        def step(k):
            remote(slots.at[mine], slots.at[mine], send.at[k], recv.at[k], peer(k)).start()

        far_first(count, step)

    def share_wait(slots, mine, count, peer, send, recv):
        def step(k):
            remote(slots.at[mine], slots.at[mine], send.at[k], recv.at[k], peer(k)).wait()

        far_first(count, step)

    def total(slots):
        if slots.shape[0] <= 32:
            value = slots[0]
            for i in range(1, slots.shape[0]):
                value = value + slots[i]
            return value
        return lax.fori_loop(1, slots.shape[0], lambda i, v: v + slots[i], slots[0])

    for copy in loads[8:]:
        copy.wait()
    row_r, lane_r = iota((rpc, LANES), 0), iota((rpc, LANES), 1)
    tile_of, image_of = row_r // n_img, row_r % n_img
    count_here = jnp.int32(0)
    side_of = jnp.zeros((rpc, LANES), jnp.int32)
    for b in range(n_img):
        count_here = count_here + side[b] * side[b]
        side_of = jnp.where(image_of == b, side[b], side_of)
    pixel_of = tile_of * LANES + lane_r
    mask_raw[...] = jnp.where((pixel_of // SIDE < side_of) & (pixel_of % SIDE < side_of), 1.0, 0.0)
    mask_of = mask_raw[...]
    n_rows = feat.shape[0]
    loads[0].wait()

    def halves(v):
        while v.shape[0] > 8:
            n = v.shape[0] // 2
            v = v[0:n] + v[n:]
        return v

    def first_sums(i, c):
        for k in range(5):
            row = i * 5 + k
            v = feat[pl.ds(pl.multiple_of(row * rpc, rpc), rpc), :].astype(F32)
            w = v * mask_of
            at = pl.ds(pl.multiple_of(row * 8, 8), 8)
            sums_s[at, :] = halves(w)
            sums_q[at, :] = halves(w * v)
        return c

    lax.fori_loop(0, n_c // 5, first_sums, 0)
    sums_s[n_c * 8 : cp * 8, :] = jnp.zeros(((cp - n_c) * 8, LANES), F32)
    sums_q[n_c * 8 : cp * 8, :] = jnp.zeros(((cp - n_c) * 8, LANES), F32)

    def first_fold(g, c):
        for src, dst in ((sums_s, sum_a), (sums_q, sum_b)):
            v = src[pl.ds(g * 64, 8, stride=8), :]
            for k in range(1, 8):
                v = v + src[pl.ds(g * 64 + k, 8, stride=8), :]
            dst[pl.ds(pl.multiple_of(g * 8, 8), 8), :] = v
        return c

    lax.fori_loop(0, cp // 8, first_fold, 0)
    lane1 = iota((1, LANES), 1)
    s0, sq0 = as_rows(sum_a[...], c_sizes), as_rows(sum_b[...], c_sizes)
    ar1[dp, 0:1, :] = s0[0]
    ar1[dp, 1:2, :] = jnp.where(lane1 == LANES - 1, count_here.astype(F32), s0[1])
    ar1[dp, 2:3, :] = sq0[0]
    ar1[dp, 3:4, :] = sq0[1]

    pl.semaphore_wait(barrier, n_dev - 1)
    share_start(ar1, dp, n_dp, dp_peer, s1, r1)

    new_slot = slot[slot.shape[0] - 1]
    per_device = n_c // grow
    slot_of = iota((rpc, LANES), 0) * 0 + new_slot
    loads[1].wait()
    graw[grow * rpc : TAP * rpc, :] = jnp.zeros(((TAP - grow) * rpc, LANES), F32)
    picks = [jnp.where(slot_of == ch * per_device + i, mask_of, 0.0) for i in range(per_device)]

    def pick(i, c):
        v = jnp.zeros((rpc, LANES), F32)
        for k in range(per_device):
            v = v + cot[pl.ds(pl.multiple_of((k * grow + i) * rpc, rpc), rpc), :].astype(F32) * picks[k]
        graw[pl.ds(pl.multiple_of(i * rpc, rpc), rpc), :] = v
        return c

    lax.fori_loop(0, grow, pick, 0)

    def by_image(b):
        for t in range(tiles):
            for h in range(TAP // 16):
                v = jnp.concatenate(
                    [
                        graw[pl.ds((h * 16 + i * 8) * rpc + t * n_img + b, 8, stride=rpc), :]
                        for i in range(2)
                    ],
                    axis=0,
                )
                gsend[b, h * 16 : h * 16 + 16, t * LANES : (t + 1) * LANES] = v.astype(BF16)

    by_image(sib)
    by_image(xs)
    g_sib = [
        remote(gsend.at[sib], gsx.at[0], sg.at[0], rg.at[0], {"chan": sib}),
        remote(gsend.at[xs], gsx.at[1], sg.at[1], rg.at[1], {"chan": sib}),
    ]
    for copy in g_sib:
        copy.start()
    by_image(ch)
    by_image(xp)

    for copy in g_sib:
        copy.wait()
    gpair[0] = (gsend[ch].astype(F32) + gsx[0].astype(F32)).astype(BF16)
    gpair[1] = (gsend[xp].astype(F32) + gsx[1].astype(F32)).astype(BF16)
    g_x = [
        remote(gpair.at[0], grx.at[1], sg.at[2], rg.at[3], {"chan": xp}),
        remote(gpair.at[1], grx.at[0], sg.at[3], rg.at[2], {"chan": xp}),
    ]
    for copy in g_x:
        copy.start()

    loads[7].wait()
    w2blk[...] = jnp.zeros(w2blk.shape, BF16)
    acc = jnp.zeros((grow, w2blk.shape[1]), F32)
    for t in range(9):
        place = jnp.where(
            iota((grow, w2blk.shape[1]), 1) == iota((grow, w2blk.shape[1]), 0) + t * TAP, 1.0, 0.0
        ).astype(BF16)
        acc = acc + jnp.dot(w2v[t], place, preferred_element_type=F32)
    w2blk[0:grow, :] = acc.astype(BF16)
    loads[5].wait()
    loads[6].wait()
    gsl[ch, 0:1, 0:grow] = gain2v[...]
    gsl[ch, 1:2, 0:grow] = bias2v[...]
    w2r[ch] = w2blk[...]

    w_near = remote(w2r.at[ch], w2r.at[ch], sw.at[0], rw.at[0], {"chan": sib})
    w_far = remote(w2r.at[ch], w2r.at[ch], sw.at[1], rw.at[1], {"chan": xp})
    w_on = remote(w2r.at[xp], w2r.at[xp], sw.at[2], rw.at[2], {"chan": sib})
    w_far.start()
    w_near.start()
    share_start(gsl, ch, n_ch, ch_peer, sb, rb)

    lane16 = iota((16, n_px), 1)
    row_of, col_of = lane16 >> 5, lane16 & (SIDE - 1)
    for b in range(n_img):
        mask[b] = jnp.where((row_of < side[b]) & (col_of < side[b]), 1.0, 0.0)

    out_x[pl.ds(n_rows, out_x.shape[0] - n_rows), :] = jnp.zeros((out_x.shape[0] - n_rows, LANES), F32)
    out_g[pl.ds(n_rows, out_g.shape[0] - n_rows), :] = jnp.zeros((out_g.shape[0] - n_rows, LANES), F32)
    step_rows = 3 * rpc

    def widen(i, c):
        r = pl.ds(pl.multiple_of(i * step_rows, step_rows), step_rows)
        out_x[r, :] = feat[r, :].astype(F32)
        return c

    lax.fori_loop(0, n_rows // step_rows, widen, 0)

    def relayout(g, c):
        base_row = g * 16 * rpc
        r = pl.ds(pl.multiple_of(g * 16, 16), 16)
        for b in range(n_img):
            for t in range(tiles):
                k = t * n_img + b
                v = jnp.concatenate(
                    [out_x[pl.ds(base_row + h * 8 * rpc + k, 8, stride=rpc), :] for h in range(2)], axis=0
                )
                xb[b, r, t * LANES : (t + 1) * LANES] = v.astype(BF16)
        return c

    lax.fori_loop(0, cp // 16, relayout, 0)
    loads[2].wait()
    w1s[...] = jnp.zeros(w1s.shape, BF16)
    w1s[0:n_d, 0:n_c] = w1v[...]
    rowbuf[...] = jnp.zeros(rowbuf.shape, F32)
    loads[3].wait()
    loads[4].wait()
    rowbuf[0:1, :] = gain1v[0:1, 0:LANES]
    rowbuf[1:2, 0 : n_c - LANES] = gain1v[0:1, LANES:n_c]
    rowbuf[2:3, :] = bias1v[0:1, 0:LANES]
    rowbuf[3:4, 0 : n_c - LANES] = bias1v[0:1, LANES:n_c]


    share_wait(ar1, dp, n_dp, dp_peer, s1, r1)
    tot1 = total(ar1)
    count = tot1[1:2, LANES - 1 : LANES]
    mean1, rstd1, scale1, keep1 = [], [], [], []
    for i in range(2):
        mean = tot1[i : i + 1] / count
        rstd = lax.rsqrt(tot1[2 + i : 3 + i] / count - mean * mean + EPS)
        here = lane1 + i * LANES
        ids = ch * n_c + here
        first = new_slot * grow
        keep = jnp.where(
            (here < n_c) & ((ids < first) | (ids >= first + grow)), 1.0, 0.0
        )
        scale = rstd * rowbuf[i : i + 1, :]
        shift = rowbuf[2 + i : 3 + i, :] - mean * scale
        size = c_sizes[i]
        r = pl.ds(i * LANES, size)
        col_a[r, :] = as_column(0.5 * scale * keep, size)
        col_b[r, :] = as_column(0.5 * shift * keep, size)
        mean1.append(mean)
        keep1.append(keep)
        rstd1.append(rstd)
        scale1.append(scale)

    def partial(j, first, n):
        def body(g, c):
            r = pl.ds(pl.multiple_of(g * 16, 16), 16)
            a, b = col_a[r, :], col_b[r, :]
            for t in range(first, first + n):
                sl = slice(t * LANES, (t + 1) * LANES)
                v = xb[j, r, sl].astype(F32) * a + b
                act[j, r, sl] = ((v * jnp.tanh(v) + v) * mask[j, :, sl]).astype(BF16)
            return c

        lax.fori_loop(0, cp // 16, body, 0)
        sl = slice(first * LANES, (first + n) * LANES)
        part[j, :, sl] = jnp.dot(w1s[...], act[j, :, sl], preferred_element_type=F32)

    rows_d = pl.ds(0, d8)
    unit = tiles // sum(SPANS)
    edges = [sum(SPANS[:p]) * unit for p in range(PIECES + 1)]

    def lanes_of(p):
        return pl.ds(edges[p] * LANES, (edges[p + 1] - edges[p]) * LANES)

    def tiles_of(p):
        return [slice(t * LANES, (t + 1) * LANES) for t in range(edges[p], edges[p + 1])]

    blocks, rest = d8 // 24, d8 // 24 * 24

    def code(read, p, words, tops):
        top = jnp.maximum(jnp.max(row_top[...], axis=1, keepdims=True), 1e-30)
        tops[p, 0:1, :] = as_row(top[0:LANES])
        tops[p, 1:2, :] = as_row(top[LANES:d8])
        row_scale[...] = jnp.broadcast_to(LEVELS / top, (d8, LANES))

        def quantized(first, n, sl):
            r = pl.ds(pl.multiple_of(first, 8), n)
            return jnp.round(read(r, sl) * row_scale[r, :]).astype(jnp.int32)

        def block(i, c):
            for sl in tiles_of(p):
                q0, q1, q2 = (quantized(i * 24 + k * 8, 8, sl) for k in range(3))
                words[pl.ds(pl.multiple_of(i * 16, 8), 8), sl] = (q0 << 11) | ((q2 >> 10) & 0x7FF)
                words[pl.ds(pl.multiple_of(i * 16 + 8, 8), 8), sl] = (q1 << 11) | (q2 & 0x3FF)
            return c

        lax.fori_loop(0, blocks, block, 0)
        for sl in tiles_of(p):
            words[blocks * 16 : blocks * 16 + d8 - rest, sl] = quantized(rest, d8 - rest, sl)

    def unscale(tops, p):
        top = jnp.concatenate([as_column(tops[p, 0:1, :], LANES), as_column(tops[p, 1:2, :], d8 - LANES)], axis=0)
        row_scale[...] = top * (1.0 / LEVELS)

    def uncode(write, p, words):
        def put(first, n, sl, q):
            r = pl.ds(pl.multiple_of(first, 8), n)
            write(r, sl, q.astype(F32) * row_scale[r, :])

        def block(i, c):
            for sl in tiles_of(p):
                w0 = words[pl.ds(pl.multiple_of(i * 16, 8), 8), sl]
                w1 = words[pl.ds(pl.multiple_of(i * 16 + 8, 8), 8), sl]
                put(i * 24, 8, sl, w0 >> 11)
                put(i * 24 + 8, 8, sl, w1 >> 11)
                put(i * 24 + 16, 8, sl, (((w0 << 21) >> 21) << 10) | (w1 & 0x3FF))
            return c

        lax.fori_loop(0, blocks, block, 0)
        for sl in tiles_of(p):
            put(rest, d8 - rest, sl, words[blocks * 16 : blocks * 16 + d8 - rest, sl])

    def top_of(values):
        value = jnp.abs(values[0])
        for other in values[1:]:
            value = jnp.maximum(value, jnp.abs(other))
        return value

    def piece_of(j, p):
        partial(j, edges[p], edges[p + 1] - edges[p])

    def over(p):
        at = lanes_of(p)
        return remote(part.at[xs, rows_d, at], rx_a.at[rows_d, at], sp.at[p], rp.at[p], {"chan": sib})

    to_x = []
    piece_of(xs, 0)
    over(0).start()
    piece_of(xp, 0)
    for p in range(PIECES):
        if p + 1 < PIECES:
            piece_of(xs, p + 1)
            over(p + 1).start()
        over(p).wait()

        def add_a(g, c):
            r = pl.ds(pl.multiple_of(g * 8, 8), 8)
            values = [part[xp, r, sl] + rx_a[r, sl] for sl in tiles_of(p)]
            for sl, v in zip(tiles_of(p), values):
                part[xp, r, sl] = v
            row_top[r, :] = top_of(values)
            return c

        lax.fori_loop(0, d8 // 8, add_a, 0)
        code(lambda r, sl: part[xp, r, sl], p, px_out, tx_out)
        at = lanes_of(p)
        copies = [
            remote(tx_out.at[p], tx_in.at[p], sq.at[0, p], rq.at[0, p], {"chan": xp}),
            remote(px_out.at[:, at], px_in.at[:, at], sq.at[1, p], rq.at[1, p], {"chan": xp}),
        ]
        for copy in copies:
            copy.start()
        to_x.append(copies)
        if p + 1 < PIECES:
            piece_of(xp, p + 1)
    for i in range(2):
        r = pl.ds(i * LANES, c_sizes[i])
        col_m[r, :] = as_column(mean1[i], c_sizes[i])
        col_k[r, :] = as_column(keep1[i], c_sizes[i])
    w_far.wait()
    w_on.start()
    partial(sib, 0, tiles)
    to_sib_b = remote(part.at[sib, rows_d], rx_b.at[rows_d], sx.at[0], rxs.at[0], {"chan": sib})
    to_sib_b.start()
    partial(ch, 0, tiles)

    for copy in g_x:
        copy.wait()
    w_near.wait()
    w_on.wait()
    share_wait(gsl, ch, n_ch, ch_peer, sb, rb)
    px = iota((TAP, n_px), 1)
    py, pxx = px >> 5, px & (SIDE - 1)
    for i in range(2):
        gcur[...] = gpair[i].astype(F32) + grx[i].astype(F32)
        for ky in range(3):
            for kx in range(3):
                shift = (ky - 1) * SIDE + (kx - 1)
                t = ky * 3 + kx
                v = gcur[...]
                if shift != 0:
                    v = pltpu.roll(v, shift % n_px, 1)
                ok = None
                for off, pos in ((ky - 1, py), (kx - 1, pxx)):
                    if off == 1:
                        test = pos >= 1
                    elif off == -1:
                        test = pos <= SIDE - 2
                    else:
                        continue
                    ok = test if ok is None else ok & test
                if ok is not None:
                    v = jnp.where(ok, v, 0.0)
                g9[i, t * TAP : (t + 1) * TAP, :] = v.astype(BF16)
        g9[i, pl.ds(9 * TAP, TAPS - 9 * TAP), :] = jnp.zeros((TAPS - 9 * TAP, n_px), BF16)
    acc = jnp.zeros((dpad, w2b.shape[1]), F32)
    for j in range(n_ch):
        rows = iota((dpad, TAP), 0)
        cols = iota((dpad, TAP), 1)
        place = jnp.where((rows == cols + j * grow) & (cols < grow), 1.0, 0.0).astype(BF16)
        acc = acc + jnp.dot(place, w2r[j], preferred_element_type=F32)
    w2b[...] = acc.astype(BF16)
    for i in range(2):
        back[i] = jnp.dot(w2b[...], g9[i], preferred_element_type=F32)
    rows = iota((dpad, LANES), 0)
    cols = iota((dpad, LANES), 1)
    gain2c = jnp.zeros((dpad, 1), F32)
    bias2c = jnp.zeros((dpad, 1), F32)
    for j in range(n_ch):
        place = (rows == cols + j * grow) & (cols < grow)
        gain2c = gain2c + jnp.sum(jnp.where(place, gsl[j, 0:1, :], 0.0), axis=1, keepdims=True)
        bias2c = bias2c + jnp.sum(jnp.where(place, gsl[j, 1:2, :], 0.0), axis=1, keepdims=True)
    col_c[0] = jnp.broadcast_to(gain2c, (dpad, LANES))
    col_c[1] = jnp.broadcast_to(bias2c, (dpad, LANES))

    to_sib_b.wait()
    sum_a[...] = jnp.zeros(sum_a.shape, F32)
    sum_b[...] = jnp.zeros(sum_b.shape, F32)
    hid[:, d8:dpad, :] = jnp.zeros((2, dpad - d8, n_px), F32)
    gp2[...] = jnp.zeros(gp2.shape, F32)

    def across(p):
        at = lanes_of(p)
        return [
            remote(th_out.at[p], th_in.at[p], sh.at[0, p], rh.at[0, p], {"chan": xp}),
            remote(ph_out.at[:, at], ph_in.at[:, at], sh.at[1, p], rh.at[1, p], {"chan": xp}),
        ]

    def start_across(p):
        for copy in across(p):
            copy.start()

    for p in range(PIECES):
        for copy in to_x[p]:
            copy.wait()
        unscale(tx_in, p)

        def gather(r, sl, v):
            hid[0, r, sl] = (part[ch, r, sl] + rx_b[r, sl]) + v

        uncode(gather, p, px_in)

        def sums(g, c):
            r = pl.ds(pl.multiple_of(g * 8, 8), 8)
            s_acc, q_acc = sum_a[r, :], sum_b[r, :]
            values = [hid[0, r, sl] for sl in tiles_of(p)]
            for v in values:
                s_acc = s_acc + v
                q_acc = q_acc + v * v
            sum_a[r, :] = s_acc
            sum_b[r, :] = q_acc
            tops_h[p, r, :] = top_of(values)
            return c

        lax.fori_loop(0, d8 // 8, sums, 0)
        if p < AHEAD:
            row_top[...] = tops_h[p]
            code(lambda r, sl: hid[0, r, sl], p, ph_out, th_out)
            start_across(p)

    def pack(slots):
        s, q = as_rows(sum_a[0:d8, :], d_sizes), as_rows(sum_b[0:d8, :], d_sizes)
        slots[me, 0:1, :] = s[0]
        slots[me, 1:2, :] = s[1]
        slots[me, 2:3, :] = q[0]
        slots[me, 3:4, :] = q[1]

    def columns_d(row0, row1):
        tail = jnp.zeros((dpad - d8, LANES), F32)
        return jnp.concatenate(
            [as_column(row0, LANES), as_column(row1, d8 - LANES), tail], axis=0
        )

    pack(ar2)
    share_start(ar2, me, n_dev, dev_peer, s2, r2)
    for p in range(AHEAD, PIECES):
        row_top[...] = tops_h[p]
        code(lambda r, sl: hid[0, r, sl], p, ph_out, th_out)
        start_across(p)

    def slopes(j):
        def body(g, c):
            r = pl.ds(pl.multiple_of(g * 16, 16), 16)
            a, b = col_a[r, :], col_b[r, :]
            k = 0.5 * col_k[r, :]
            for t in range(tiles):
                sl = slice(t * LANES, (t + 1) * LANES)
                v = xb[j, r, sl].astype(F32) * a + b
                th = jnp.tanh(v)
                slope[j, r, sl] = ((1.0 + th) * (1.0 + v * (1.0 - th))) * (mask[j, :, sl] * k)
            return c

        lax.fori_loop(0, cp // 16, body, 0)

    for j in range(n_img):
        slopes(j)

    def widen_cot(i, c):
        r = pl.ds(pl.multiple_of(i * step_rows, step_rows), step_rows)
        k = [jnp.broadcast_to(col_k[pl.ds(i * 3 + n, 1), :], (rpc, LANES)) for n in range(3)]
        base[r, :] = cot[r, :].astype(F32) * jnp.concatenate(k, axis=0)
        return c

    lax.fori_loop(0, n_rows // step_rows, widen_cot, 0)

    share_wait(ar2, me, n_dev, dev_peer, s2, r2)
    tot2 = total(ar2)
    mean2 = [tot2[i : i + 1] / count for i in range(2)]
    rstd2 = [lax.rsqrt(tot2[2 + i : 3 + i] / count - mean2[i] * mean2[i] + EPS) for i in range(2)]
    mean2c = columns_d(*mean2)
    rstd2c = columns_d(*rstd2)
    scale2c = rstd2c * col_c[0]
    col_c[2] = mean2c
    col_c[3] = rstd2c
    col_c[4] = scale2c
    col_c[5] = 0.5 * scale2c
    col_c[6] = 0.5 * (col_c[1] - mean2c * scale2c)

    def second(g, c):
        r = pl.ds(pl.multiple_of(g * 16, 16), 16)
        a, b, m = col_c[5, r, :], col_c[6, r, :], col_c[2, r, :]
        s_acc = jnp.zeros((16, LANES), F32)
        q_acc = jnp.zeros((16, LANES), F32)
        for t in range(tiles):
            sl = slice(t * LANES, (t + 1) * LANES)
            h = hid[0, r, sl]
            mk = mask[ch, :, sl]
            v = h * a + b
            th = jnp.tanh(v)
            act2[r, sl] = ((v * th + v) * mk).astype(BF16)
            gp = (0.5 * mk) * ((1.0 + th) * (1.0 + v * (1.0 - th))) * back[0, r, sl]
            gp2[0, r, sl] = gp
            s_acc = s_acc + gp
            q_acc = q_acc + gp * (h - m)
        sum_a[r, :] = s_acc
        sum_b[r, :] = q_acc
        return c

    lax.fori_loop(0, dpad // 16, second, 0)
    pack(ar3)
    share_start(ar3, me, n_dev, dev_peer, s3, r3)

    w2acc[...] = lax.dot_general(
        act2[...], g9[0], (((1,), (1,)), ((), ())), preferred_element_type=F32
    )
    for j in range(n_ch):
        for lt in range(4):
            sl = slice(lt * LANES, (lt + 1) * LANES)
            cw[j, lt * 32 : lt * 32 + 32, :] = w2acc[j * grow : j * grow + 32, sl]
            cw[j, 128 + lt : 129 + lt, :] = w2acc[j * grow + 32 : j * grow + 33, sl]
        cw[j, 132:136, :] = jnp.zeros((4, LANES), F32)
    w_sib = [
        remote(cw.at[xs], cwr.at[1], sc.at[0], rc.at[0], {"chan": sib}),
        remote(cw.at[sib], cwr.at[0], sc.at[1], rc.at[1], {"chan": sib}),
    ]
    for copy in w_sib:
        copy.start()

    def second_other(p):
        for copy in across(p):
            copy.wait()
        unscale(th_in, p)

        def keep_hidden(r, sl, v):
            hid[1, r, sl] = v

        uncode(keep_hidden, p, ph_in)

        def body(g, c):
            r = pl.ds(pl.multiple_of(g * 16, 16), 16)
            a, b = col_c[5, r, :], col_c[6, r, :]
            for sl in tiles_of(p):
                v = hid[1, r, sl] * a + b
                th = jnp.tanh(v)
                gp2[1, r, sl] = (
                    (0.5 * mask[xp, :, sl]) * ((1.0 + th) * (1.0 + v * (1.0 - th))) * back[1, r, sl]
                )
            return c

        lax.fori_loop(0, dpad // 16, body, 0)

    zbuf[...] = lax.dot_general(
        w2b[...], act2[...], (((0,), (0,)), ((), ())), preferred_element_type=F32
    )
    new = jnp.zeros((TAP, n_px), F32)
    for ky in range(3):
        for kx in range(3):
            shift = (ky - 1) * SIDE + (kx - 1)
            t = ky * 3 + kx
            v = zbuf[t * TAP : (t + 1) * TAP, :]
            if shift != 0:
                v = pltpu.roll(v, (-shift) % n_px, 1)
            ok = None
            for off, pos in ((ky - 1, py), (kx - 1, pxx)):
                if off == -1:
                    test = pos >= 1
                elif off == 1:
                    test = pos <= SIDE - 2
                else:
                    continue
                ok = test if ok is None else ok & test
            if ok is not None:
                v = jnp.where(ok, v, 0.0)
            new = new + v
    new = new * jnp.concatenate([mask[ch]] * (TAP // 16), axis=0)
    gall[ch] = new[0 : gall.shape[1]]
    for copy in w_sib:
        copy.wait()
    cw[xp] = cw[xp] + cwr[1]
    cw[ch] = cw[ch] + cwr[0]
    w_x = remote(cw.at[xp], cwx, sc.at[2], rc.at[2], {"chan": xp})
    w_x.start()
    new_sib = remote(gall.at[ch], gall.at[ch], so.at[0], ro.at[0], {"chan": sib})
    new_xp = remote(gall.at[ch], gall.at[ch], so.at[1], ro.at[1], {"chan": xp})
    new_on = remote(gall.at[xp], gall.at[xp], so.at[2], ro.at[2], {"chan": sib})
    new_xp.start()
    new_sib.start()
    for p in range(PIECES):
        second_other(p)

    share_wait(ar3, me, n_dev, dev_peer, s3, r3)
    tot3 = total(ar3)
    gain_sum2 = [tot3[2 + i : 3 + i] * rstd2[i] for i in range(2)]
    bias_sum2 = [tot3[i : i + 1] for i in range(2)]
    gain_sum2c = columns_d(*gain_sum2)
    bias_sum2c = columns_d(*bias_sum2)
    col_c[7] = col_c[4] * bias_sum2c / count
    col_c[8] = col_c[4] * col_c[3] * gain_sum2c / count

    def third(i, j, k):
        def body(g, c):
            r = pl.ds(pl.multiple_of(g * 16, 16), 16)
            c1, c2, c3, m = col_c[4, r, :], col_c[7, r, :], col_c[8, r, :], col_c[2, r, :]
            for sl in [slice(t * LANES, (t + 1) * LANES) for t in range(k * tiles // 2, (k + 1) * tiles // 2)]:
                gha[j, r, sl] = (
                    c1 * gp2[i, r, sl] - mask[j, :, sl] * (c2 + c3 * (hid[i, r, sl] - m))
                ).astype(BF16)
            return c

        lax.fori_loop(0, dpad // 16, body, 0)

    grads = []
    for i, j in ((0, ch), (1, xp)):
        for k in range(2):
            third(i, j, k)
            at = pl.ds(k * (n_px // 2), n_px // 2)
            copy = remote(gha.at[j, :, at], gha.at[j, :, at], st.at[i, k], rt.at[i, k], {"chan": sib})
            copy.start()
            grads.append(copy)
    d_rows, d_cols = iota((dpad, LANES), 0), iota((dpad, LANES), 1)
    here_d = (d_rows == d_cols + ch * grow) & (d_cols < grow)
    out_g2[...] = jnp.sum(jnp.where(here_d, gain_sum2c, 0.0), axis=0, keepdims=True)[:, 0:grow]
    out_b2[...] = jnp.sum(jnp.where(here_d, bias_sum2c, 0.0), axis=0, keepdims=True)[:, 0:grow]

    w1acc[...] = jnp.zeros(w1acc.shape, F32)
    sum_a[...] = jnp.zeros(sum_a.shape, F32)
    sum_b[...] = jnp.zeros(sum_b.shape, F32)

    def weight_grad(j, k=None):
        at = slice(0, n_px) if k is None else slice(k * (n_px // 2), (k + 1) * (n_px // 2))
        w1acc[0:dpad, 0:cp] = w1acc[0:dpad, 0:cp] + lax.dot_general(
            gha[j, :, at], act[j, :, at], (((1,), (1,)), ((), ())), preferred_element_type=F32
        )

    def input_grad(j):
        gact[...] = lax.dot_general(
            w1s[...], gha[j], (((0,), (0,)), ((), ())), preferred_element_type=F32
        )

        def body(g, c):
            r = pl.ds(pl.multiple_of(g * 16, 16), 16)
            m = col_m[r, :]
            s_acc, q_acc = sum_a[r, :], sum_b[r, :]
            for t in range(tiles):
                sl = slice(t * LANES, (t + 1) * LANES)
                gp = gact[r, sl] * slope[j, r, sl]
                gp1[j, r, sl] = gp
                s_acc = s_acc + gp
                q_acc = q_acc + gp * (xb[j, r, sl].astype(F32) - m)
            sum_a[r, :] = s_acc
            sum_b[r, :] = q_acc
            return c

        lax.fori_loop(0, cp // 16, body, 0)

    weight_grad(ch)
    weight_grad(xp)
    w_x.wait()
    input_grad(ch)
    for i, j in ((0, sib), (1, xs)):
        for k in range(2):
            grads[2 * i + k].wait()
            weight_grad(j, k)

    for r in range(17):
        cb[r // 5, r % 5 * 8 : r % 5 * 8 + 8, :] = w1acc[r * 8 : r * 8 + 8, 0:LANES]
    for k in range(6):
        v = w1acc[k * 8 : k * 8 + 8, LANES : 2 * LANES]
        for i in range(1, 3):
            v = v + pltpu.roll(w1acc[i * 48 + k * 8 : i * 48 + k * 8 + 8, LANES : 2 * LANES], 40 * i, 1)
        r = 17 + k
        cb[r // 5, r % 5 * 8 : r % 5 * 8 + 8, :] = v
    for k in range(17):
        r = 23 + k
        cb[r // 5, r % 5 * 8 : r % 5 * 8 + 8, :] = cw[ch, k * 8 : k * 8 + 8, :] + cwx[k * 8 : k * 8 + 8, :]

    def encode(v):
        top = jnp.maximum(jnp.max(jnp.abs(v), axis=0, keepdims=True), 1e-30)
        power = jnp.floor(jnp.log2(top) + 1.0001)
        q = jnp.clip(jnp.round(v * jnp.exp2(15.0 - power)), -32767.0, 32767.0).astype(jnp.int32)
        low = jnp.concatenate([q[24:40], jnp.broadcast_to(power.astype(jnp.int32), (8, LANES))], axis=0)
        return (q[0:24] << 16) | (low & 0xFFFF)

    def decode(w):
        high, low = w >> 16, (w << 16) >> 16
        scale = jnp.exp2(low[16:24].astype(F32) - 15.0)
        q = jnp.concatenate([high, low[0:16]], axis=0).astype(F32)
        return q * jnp.concatenate([scale] * 5, axis=0)

    for q in range(OWNERS):
        coded[q] = encode(cb[q])
    stride = n_dp // OWNERS
    my_part = dp // stride
    is_owner = lax.rem(dp, stride) == 0

    def part_to(k):
        q = my_part ^ (OWNERS - 1 - k)
        return q, q * stride

    def push(k, c):
        q, to = part_to(k)

        @pl.when(to != dp)
        def _():
            remote(coded.at[q], rsl.at[dp], sr.at[k], rr.at[dp], {"dp": to}).start()

        return c

    lax.fori_loop(0, OWNERS, push, 0)
    for j in (xp, sib, xs):
        input_grad(j)
    s4_, q4_ = as_rows(sum_a[...], c_sizes), as_rows(sum_b[...], c_sizes)
    for i in range(2):
        ar4[dp, i : i + 1, :] = s4_[i]
        ar4[dp, 2 + i : 3 + i, :] = q4_[i]
    share_start(ar4, dp, n_dp, dp_peer, s4, r4)
    new_xp.wait()
    new_on.start()

    def scatter(g, c):
        first = g * 16 * rpc
        r = pl.ds(pl.multiple_of(g * 16, 16), 16)
        for b in range(n_img):
            for t in range(tiles):
                v = gp1[b, r, t * LANES : (t + 1) * LANES]
                for h in range(2):
                    at = pl.ds(first + h * 8 * rpc + t * n_img + b, 8, stride=rpc)
                    out_g[at, :] = v[h * 8 : h * 8 + 8]
        return c

    lax.fori_loop(0, 5, scatter, 0)

    def push_wait(k, c):
        q, to = part_to(k)

        @pl.when(to != dp)
        def _():
            remote(coded.at[q], rsl.at[dp], sr.at[k], rr.at[dp], {"dp": to}).wait_send()

        return c

    def pull(k, c):
        src = lax.rem(dp + k, n_dp)
        remote(coded.at[0], rsl.at[src], sr.at[0], rr.at[src], {"dp": src}).wait_recv()
        return c

    @pl.when(is_owner)
    def _():
        lax.fori_loop(1, n_dp, pull, 0)
        v = cb[my_part]
        for k in range(1, n_dp):
            v = v + decode(rsl[lax.rem(dp + k, n_dp)])
        fin[my_part] = encode(v)

        def give(k):
            remote(fin.at[my_part], fin.at[my_part], sa.at[k], ra.at[my_part], dp_peer(k)).start()

        far_first(n_dp, give)

    lax.fori_loop(0, OWNERS, push_wait, 0)
    lax.fori_loop(5, cp // 16, scatter, 0)

    for i in range(2):
        col_a[pl.ds(i * LANES, c_sizes[i]), :] = as_column(scale1[i], c_sizes[i])

    new_sib.wait()
    new_on.wait()
    for b in range(n_img):
        for t in range(tiles):
            for h in range(gall.shape[1] // 8):
                out_new[pl.ds(h * 8 * rpc + t * n_img + b, 8, stride=rpc), :] = gall[
                    b, h * 8 : h * 8 + 8, t * LANES : (t + 1) * LANES
                ]
    out_slot[...] = (slot_of - ch * per_device)[0:8].astype(F32)

    share_wait(ar4, dp, n_dp, dp_peer, s4, r4)
    tot4 = total(ar4)
    for i in range(2):
        bias_sum = tot4[i : i + 1]
        gain_sum = tot4[2 + i : 3 + i] * rstd1[i]
        size = c_sizes[i]
        r = pl.ds(i * LANES, size)
        k1 = -scale1[i] * rstd1[i] * gain_sum / count
        k0 = -scale1[i] * bias_sum / count - k1 * mean1[i]
        col_b[r, :] = as_column(k0, size)
        col_m[r, :] = as_column(k1, size)
        width = min(LANES, n_c - i * LANES)
        out_g1[0:1, i * LANES : i * LANES + width] = gain_sum[:, 0:width]
        out_b1[0:1, i * LANES : i * LANES + width] = bias_sum[:, 0:width]
    mask_of = mask_raw[...]

    def last(i, c):
        for k in range(5):
            row = i * 5 + k
            at = pl.ds(pl.multiple_of(row * rpc, rpc), rpc)
            k0 = jnp.broadcast_to(col_b[pl.ds(row, 1), :], (rpc, LANES))
            k1 = jnp.broadcast_to(col_m[pl.ds(row, 1), :], (rpc, LANES))
            a = jnp.broadcast_to(col_a[pl.ds(row, 1), :], (rpc, LANES))
            out_g[at, :] = base[at, :] + a * out_g[at, :] + mask_of * (k0 + k1 * out_x[at, :])
        return c

    lax.fori_loop(0, n_c // 5, last, 0)

    @pl.when(is_owner)
    def _():
        def gave(k, c):
            remote(fin.at[my_part], fin.at[my_part], sa.at[k], ra.at[my_part], dp_peer(k)).wait_send()
            return c

        lax.fori_loop(1, n_dp, gave, 0)

    def take(q, c):
        @pl.when(q * stride != dp)
        def _():
            remote(fin.at[q], fin.at[q], sa.at[0], ra.at[q], {"dp": q * stride}).wait_recv()

        return c

    lax.fori_loop(0, OWNERS, take, 0)
    for q in range(OWNERS):
        cb[q] = decode(fin[q])
    for r in range(17):
        height = min(8, n_d - r * 8)
        out_w1[r * 8 : r * 8 + height, 0:LANES] = cb[r // 5, r % 5 * 8 : r % 5 * 8 + height, :]
    for k in range(6):
        r = 17 + k
        v = cb[r // 5, r % 5 * 8 : r % 5 * 8 + 8, :]
        for i in range(3):
            row = i * 48 + k * 8
            height = min(8, n_d - row)
            if height > 0:
                u = v if i == 0 else pltpu.roll(v, LANES - 40 * i, 1)
                out_w1[row : row + height, LANES:n_c] = u[0:height, 0 : n_c - LANES]
    for k in range(17):
        r = 23 + k
        v = cb[r // 5, r % 5 * 8 : r % 5 * 8 + 8, :]
        if k < 16:
            w2acc[k % 4 * 8 : k % 4 * 8 + 8, k // 4 * LANES : (k // 4 + 1) * LANES] = v
        else:
            for lt in range(4):
                w2acc[32:33, lt * LANES : (lt + 1) * LANES] = v[lt : lt + 1]
    v = w2acc[0:40, :]
    for t in range(9):
        u = v if t == 0 else pltpu.roll(v, TAPS - t * TAP, 1)
        out_w2[t] = u[0:grow, 0:grow]


def finish(n_rows, grow_rows, *refs):
    n = (len(refs) - 3) // 2
    new, slot = refs[n : n + 2]
    outs, sem = refs[n + 2 : -1], refs[-1]
    segments = n_rows // grow_rows
    copies = [pltpu.make_async_copy(refs[1].at[pl.ds(0, n_rows)], outs[1], sem.at[1])]
    copies += [pltpu.make_async_copy(refs[i], outs[i], sem.at[i]) for i in range(2, n)]
    for copy in copies:
        copy.start()
    here = jnp.max(slot[...])
    for k in range(segments):
        at = pl.ds(k * grow_rows, grow_rows)
        kept = pltpu.make_async_copy(refs[0].at[at], outs[0].at[at], sem.at[n + k])
        grown = pltpu.make_async_copy(new.at[pl.ds(0, grow_rows)], outs[0].at[at], sem.at[n + k])
        pl.when(here == k)(grown.start)
        pl.when(here != k)(kept.start)
        copies.append(kept)
    for copy in copies:
        copy.wait()


def flat(values):
    n, c, p = values.shape
    return (
        values.transpose(1, 0, 2).reshape(c, n, p // LANES, LANES).transpose(0, 2, 1, 3).reshape(-1, LANES)
    )


def unflat(rows, n, c, p):
    return rows.reshape(c, p // LANES, n, LANES).transpose(0, 2, 1, 3).reshape(c, n, p).transpose(1, 0, 2)


def on_device(
    n_dp, n_ch, features, gain1, bias1, weight1, gain2, bias2, weight2, cotangent, image_side, block_slot
):
    n_img, n_c, n_px = features.shape
    n_d = weight1.shape[1]
    grow = weight2.shape[3]
    cp = pad_to(n_c, 16)
    dpad = pad_to(n_d, 16)
    d8 = pad_to(n_d, 8)
    rpc = n_px // LANES * n_img
    n_rows, n_pad = n_c * rpc, cp * rpc
    n_dev = n_dp * n_ch
    words = d8 // 24 * 16 + d8 % 24
    cfg = (n_dp, n_ch, n_img, n_c, n_px, n_d, grow)
    args = (
        flat(features),
        flat(cotangent),
        weight1.T,
        gain1.reshape(1, -1),
        bias1.reshape(1, -1),
        gain2.reshape(1, -1),
        bias2.reshape(1, -1),
        weight2.reshape(9, grow, grow),
        image_side,
        block_slot,
    )
    args = [pltpu.with_memory_space_constraint(v, pltpu.HBM) for v in args]
    sd = jax.ShapeDtypeStruct
    in_vmem = pl.BlockSpec(memory_space=pltpu.VMEM)
    in_hbm = pl.BlockSpec(memory_space=pltpu.HBM)
    dma = pltpu.SemaphoreType.DMA
    v = pltpu.VMEM
    scratch = [
        v((n_rows, LANES), BF16), v((n_rows, LANES), BF16), v((n_d, n_c), BF16),
        v((1, n_c), F32), v((1, n_c), F32), v((1, grow), F32), v((1, grow), F32),
        v((9, grow, grow), BF16), pltpu.SMEM(image_side.shape, jnp.int32), pltpu.SMEM(block_slot.shape, jnp.int32),
        v((n_img, 16, n_px), F32), v((rpc, LANES), F32), v((n_rows, LANES), F32),
        v((n_img, cp, n_px), BF16), v((n_img, cp, n_px), BF16),
        v((n_img, cp, n_px), F32), v((n_img, cp, n_px), F32), v((cp, n_px), F32),
        v((cp, LANES), F32), v((cp, LANES), F32), v((cp, LANES), F32), v((cp, LANES), F32),
        v((9, dpad, LANES), F32), v((cp, LANES), F32), v((cp, LANES), F32),
        v((cp * 8, LANES), F32), v((cp * 8, LANES), F32), v((8, LANES), F32),
        v((dpad, cp), BF16), v((n_img, dpad, n_px), F32),
        v((dpad, n_px), F32), v((dpad, n_px), F32), v((2, dpad, n_px), F32),
        v((d8, LANES), F32), v((d8, LANES), F32), v((PIECES, d8, LANES), F32),
        v((words, n_px), jnp.int32), v((words, n_px), jnp.int32), v((PIECES, 2, LANES), F32), v((PIECES, 2, LANES), F32),
        v((words, n_px), jnp.int32), v((words, n_px), jnp.int32), v((PIECES, 2, LANES), F32), v((PIECES, 2, LANES), F32),
        v((TAP * rpc, LANES), F32), v((n_ch, TAP, n_px), BF16),
        v((2, TAP, n_px), BF16), v((2, TAP, n_px), BF16), v((2, TAP, n_px), BF16), v((TAP, n_px), F32),
        v((2, TAPS, n_px), BF16), v((TAP, TAPS), BF16), v((n_ch, TAP, TAPS), BF16), v((dpad, TAPS), BF16),
        v((n_ch, 2, LANES), F32),
        v((dpad, n_px), BF16), v((2, dpad, n_px), F32), v((2, dpad, n_px), F32), v((TAPS, n_px), F32),
        v((n_ch, 40, n_px), F32), v((n_ch, dpad, n_px), BF16),
        v((n_ch, 136, LANES), F32), v((2, 136, LANES), F32), v((136, LANES), F32),
        v((OWNERS, 40, LANES), F32), v((OWNERS, 24, LANES), jnp.int32),
        v((n_dp, 24, LANES), jnp.int32), v((OWNERS, 24, LANES), jnp.int32), v((dpad, 256), F32), v((dpad, TAPS), F32),
        v((n_dp, 4, LANES), F32), v((n_dev, 4, LANES), F32), v((n_dev, 4, LANES), F32), v((n_dp, 4, LANES), F32),
        dma((10,)),
        dma((n_dp,)), dma((n_dp,)), dma((n_dev,)), dma((n_dev,)), dma((n_dev,)), dma((n_dev,)), dma((n_dp,)), dma((n_dp,)),
        dma((3,)), dma((3,)), dma((PIECES,)), dma((PIECES,)), dma((2, PIECES)), dma((2, PIECES)),
        dma((4,)), dma((4,)), dma((n_ch,)), dma((n_ch,)), dma((n_ch,)), dma((n_ch,)),
        dma((2, PIECES)), dma((2, PIECES)), dma((2, 2)), dma((2, 2)), dma((3,)), dma((3,)), dma((3,)), dma((3,)),
        dma((OWNERS,)), dma((n_dp,)), dma((n_dp,)), dma((OWNERS,)),
    ]
    out_shape = (
        sd((n_pad, LANES), F32), sd((n_pad, LANES), F32), sd((n_d, n_c), F32),
        sd((1, n_c), F32), sd((1, n_c), F32), sd((9, grow, grow), F32), sd((1, grow), F32), sd((1, grow), F32),
        sd((40 * rpc, LANES), F32), sd((8, LANES), F32),
    )
    outs = pl.pallas_call(
        functools.partial(layer, cfg),
        out_shape=out_shape,
        in_specs=[in_hbm] * len(args),
        out_specs=(in_vmem,) * len(out_shape),
        scratch_shapes=scratch,
        compiler_params=pltpu.CompilerParams(
            collective_id=0, has_side_effects=True, vmem_limit_bytes=40 << 20
        ),
    )(*args)
    final = (sd((n_rows, LANES), F32),) * 2 + out_shape[2:-2]
    o = pl.pallas_call(
        functools.partial(finish, n_rows, grow * rpc),
        out_shape=final,
        in_specs=[in_vmem] * len(outs),
        out_specs=(in_hbm,) * len(final),
        scratch_shapes=[dma((len(final) + n_c // grow,))],
        compiler_params=pltpu.CompilerParams(vmem_limit_bytes=8 << 20),
    )(*outs)
    return (
        unflat(o[0], n_img, n_c, n_px),
        unflat(o[1], n_img, n_c, n_px),
        o[2].T,
        o[3].reshape(-1),
        o[4].reshape(-1),
        o[5].reshape(3, 3, grow, grow),
        o[6].reshape(-1),
        o[7].reshape(-1),
    )


def solution(mesh):
    in_specs = (
        P("dp", "chan", None),
        P("chan"),
        P("chan"),
        P("chan", None),
        P("chan"),
        P("chan"),
        P(None, None, "chan", None),
        P("dp", "chan", None),
        P("dp"),
        P(),
    )
    out_specs = (
        P("dp", "chan", None),
        P("dp", "chan", None),
        P("chan", None),
        P("chan"),
        P("chan"),
        P(None, None, "chan", None),
        P("chan"),
        P("chan"),
    )
    body = functools.partial(on_device, mesh.shape["dp"], mesh.shape["chan"])
    return jax.shard_map(body, mesh=mesh, in_specs=in_specs, out_specs=out_specs, check_vma=False)
```

```python
import functools

import jax
import jax.numpy as jnp
from jax import lax
from jax.experimental import pallas as pl
from jax.experimental.pallas import tpu as pltpu
from jax.sharding import PartitionSpec as P

SIDE = 32
EPS = 1e-05
LANES = 128
TAP = 48
TAPS = 512
SPANS = (1, 2, 3, 2)
PIECES = len(SPANS)
AHEAD = 2
LEVELS = 524000.0
OWNERS = 8

MESH = pl.DeviceIdType.MESH
F32 = jnp.float32
BF16 = jnp.bfloat16


def pad_to(size, unit):
    return (size + unit - 1) // unit * unit


def iota(shape, axis):
    return lax.broadcasted_iota(jnp.int32, shape, axis)


def as_row(column):
    n = column.shape[0]
    eye = iota((n, LANES), 0) == iota((n, LANES), 1)
    return jnp.sum(jnp.where(eye, column, 0.0), axis=0, keepdims=True)


def as_column(row, n):
    eye = iota((n, LANES), 0) == iota((n, LANES), 1)
    return jnp.broadcast_to(jnp.sum(jnp.where(eye, row, 0.0), axis=1, keepdims=True), (n, LANES))


def as_rows(values, sizes):
    column = jnp.sum(values, axis=1, keepdims=True)
    rows, start = [], 0
    for size in sizes:
        rows.append(as_row(column[start : start + size]))
        start += size
    return rows


def layer(
    cfg,
    feat_h, cot_h, w1_h, gain1_h, bias1_h, gain2_h, bias2_h, w2_h, side_h, slot_h,
    out_x, out_g, out_w1, out_g1, out_b1, out_w2, out_g2, out_b2, out_new, out_slot,
    feat, cot, w1v, gain1v, bias1v, gain2v, bias2v, w2v, side, slot,
    mask, mask_raw, base, xb, act, slope, gp1, gact,
    col_a, col_b, col_m, col_k, col_c, sum_a, sum_b, sums_s, sums_q, rowbuf,
    w1s, part, rx_a, rx_b, hid, row_top, row_scale, tops_h,
    px_out, px_in, tx_out, tx_in, ph_out, ph_in, th_out, th_in,
    graw, gsend, gsx, gpair, grx, gcur, g9, w2pad, w2wide, w2r, w2b, gsl,
    act2, gp2, back, zbuf, gall, gha,
    cw, cwr, cwx, cb, coded, rsl, fin, w1acc, w2acc,
    ar1, ar2, ar3, ar4,
    load_sem, s1, r1, s2, r2, s3, r3, s4, r4, sx, rxs, sp, rp, sq, rq, sg, rg, sw, rw, sb, rb, sh, rh, st, rt, so, ro, sc, rc, sr, rr, sa, ra,
):
    n_dp, n_ch, n_img, n_c, n_px, n_d, grow = cfg
    n_dev = n_dp * n_ch
    cp = xb.shape[1]
    dpad = w1s.shape[0]
    d8 = pad_to(n_d, 8)
    tiles = n_px // LANES
    rpc = tiles * n_img
    c_sizes = (LANES, cp - LANES)
    d_sizes = (LANES, d8 - LANES)
    dp = lax.axis_index("dp")
    ch = lax.axis_index("chan")
    me = dp * n_ch + ch
    half = n_ch // 2
    cx, cc = ch // half, lax.rem(ch, half)
    sib = cx * half + (1 - cc)
    xp = (1 - cx) * half + cc
    xs = (1 - cx) * half + (1 - cc)

    def dev_peer(k):
        q = me ^ k
        return {"dp": q // n_ch, "chan": lax.rem(q, n_ch)}

    def dp_peer(k):
        return {"dp": dp ^ k}

    def ch_peer(k):
        return {"chan": ch ^ k}

    def far_first(count, step):
        if count <= 32:
            for k in range(count - 1, 0, -1):
                step(k)
        else:

            def body(i, c):
                step(count - 1 - i)
                return c

            lax.fori_loop(0, count - 1, body, 0)

    loads = {
        i: pltpu.make_async_copy(h, v, load_sem.at[i])
        for i, (h, v) in enumerate(
            (
                (cot_h, cot), (w1_h, w1v), (gain1_h, gain1v), (bias1_h, bias1v),
                (gain2_h, gain2v), (bias2_h, bias2v), (w2_h, w2v), (side_h, side), (slot_h, slot),
            ),
            1,
        )
    }
    third_rows = feat.shape[0] // 3
    feat_parts = [
        pltpu.make_async_copy(
            feat_h.at[pl.ds(k * third_rows, third_rows)], feat.at[pl.ds(k * third_rows, third_rows)], load_sem.at[10 + k]
        )
        for k in range(3)
    ]
    for copy in [loads[8], loads[9], *feat_parts, *(loads[i] for i in range(1, 8))]:
        copy.start()
    barrier = pltpu.get_barrier_semaphore()

    def greet(k):
        pl.semaphore_signal(barrier, inc=1, device_id=dev_peer(k), device_id_type=MESH)

    far_first(n_dev, greet)

    def remote(src, dst, send, recv, device):
        return pltpu.make_async_remote_copy(
            src_ref=src, dst_ref=dst, send_sem=send, recv_sem=recv, device_id=device, device_id_type=MESH
        )

    def share_start(slots, mine, count, peer, send, recv):
        def step(k):
            remote(slots.at[mine], slots.at[mine], send.at[k], recv.at[k], peer(k)).start()

        far_first(count, step)

    def share_wait(slots, mine, count, peer, send, recv):
        def step(k):
            remote(slots.at[mine], slots.at[mine], send.at[k], recv.at[k], peer(k)).wait()

        far_first(count, step)

    def total(slots):
        if slots.shape[0] <= 32:
            value = slots[0]
            for i in range(1, slots.shape[0]):
                value = value + slots[i]
            return value
        return lax.fori_loop(1, slots.shape[0], lambda i, v: v + slots[i], slots[0])

    loads[8].wait()
    loads[9].wait()
    row_r, lane_r = iota((rpc, LANES), 0), iota((rpc, LANES), 1)
    tile_of, image_of = row_r // n_img, row_r % n_img
    count_here = jnp.int32(0)
    side_of = jnp.zeros((rpc, LANES), jnp.int32)
    for b in range(n_img):
        count_here = count_here + side[b] * side[b]
        side_of = jnp.where(image_of == b, side[b], side_of)
    pixel_of = tile_of * LANES + lane_r
    mask_raw[...] = jnp.where((pixel_of // SIDE < side_of) & (pixel_of % SIDE < side_of), 1.0, 0.0)
    mask_of = mask_raw[...]
    n_rows = feat.shape[0]

    def halves(v):
        while v.shape[0] > 8:
            n = v.shape[0] // 2
            v = v[0:n] + v[n:]
        return v

    def first_sums(i, c):
        for k in range(5):
            row = i * 5 + k
            v = feat[pl.ds(pl.multiple_of(row * rpc, rpc), rpc), :].astype(F32)
            w = v * mask_of
            at = pl.ds(pl.multiple_of(row * 8, 8), 8)
            sums_s[at, :] = halves(w)
            sums_q[at, :] = halves(w * v)
        return c

    for k in range(3):
        feat_parts[k].wait()
        lax.fori_loop(n_c // 15 * k, n_c // 15 * (k + 1), first_sums, 0)
    sums_s[n_c * 8 : cp * 8, :] = jnp.zeros(((cp - n_c) * 8, LANES), F32)
    sums_q[n_c * 8 : cp * 8, :] = jnp.zeros(((cp - n_c) * 8, LANES), F32)

    def first_fold(g, c):
        for src, dst in ((sums_s, sum_a), (sums_q, sum_b)):
            v = src[pl.ds(g * 64, 8, stride=8), :]
            for k in range(1, 8):
                v = v + src[pl.ds(g * 64 + k, 8, stride=8), :]
            dst[pl.ds(pl.multiple_of(g * 8, 8), 8), :] = v
        return c

    lax.fori_loop(0, cp // 8, first_fold, 0)
    lane1 = iota((1, LANES), 1)
    s0, sq0 = as_rows(sum_a[...], c_sizes), as_rows(sum_b[...], c_sizes)
    ar1[dp, 0:1, :] = s0[0]
    ar1[dp, 1:2, :] = jnp.where(lane1 == LANES - 1, count_here.astype(F32), s0[1])
    ar1[dp, 2:3, :] = sq0[0]
    ar1[dp, 3:4, :] = sq0[1]

    pl.semaphore_wait(barrier, n_dev - 1)
    share_start(ar1, dp, n_dp, dp_peer, s1, r1)

    new_slot = slot[slot.shape[0] - 1]
    per_device = n_c // grow
    slot_of = iota((rpc, LANES), 0) * 0 + new_slot
    loads[1].wait()
    graw[grow * rpc : TAP * rpc, :] = jnp.zeros(((TAP - grow) * rpc, LANES), F32)
    picks = [jnp.where(slot_of == ch * per_device + i, mask_of, 0.0) for i in range(per_device)]

    def pick(i, c):
        v = jnp.zeros((rpc, LANES), F32)
        for k in range(per_device):
            v = v + cot[pl.ds(pl.multiple_of((k * grow + i) * rpc, rpc), rpc), :].astype(F32) * picks[k]
        graw[pl.ds(pl.multiple_of(i * rpc, rpc), rpc), :] = v
        return c

    lax.fori_loop(0, grow, pick, 0)

    def by_image(b):
        for t in range(tiles):
            for h in range(TAP // 16):
                v = jnp.concatenate(
                    [
                        graw[pl.ds((h * 16 + i * 8) * rpc + t * n_img + b, 8, stride=rpc), :]
                        for i in range(2)
                    ],
                    axis=0,
                )
                gsend[b, h * 16 : h * 16 + 16, t * LANES : (t + 1) * LANES] = v.astype(BF16)

    by_image(sib)
    by_image(xs)
    g_sib = [
        remote(gsend.at[sib], gsx.at[0], sg.at[0], rg.at[0], {"chan": sib}),
        remote(gsend.at[xs], gsx.at[1], sg.at[1], rg.at[1], {"chan": sib}),
    ]
    for copy in g_sib:
        copy.start()
    by_image(ch)
    by_image(xp)

    lane16 = iota((16, n_px), 1)
    row_of, col_of = lane16 >> 5, lane16 & (SIDE - 1)
    for b in range(n_img):
        mask[b] = jnp.where((row_of < side[b]) & (col_of < side[b]), 1.0, 0.0)

    out_x[pl.ds(n_rows, out_x.shape[0] - n_rows), :] = jnp.zeros((out_x.shape[0] - n_rows, LANES), F32)
    step_rows = 3 * rpc

    def widen(i, c):
        r = pl.ds(pl.multiple_of(i * step_rows, step_rows), step_rows)
        out_x[r, :] = feat[r, :].astype(F32)
        return c

    lax.fori_loop(0, n_rows // step_rows, widen, 0)

    for copy in g_sib:
        copy.wait()
    gpair[0] = (gsend[ch].astype(F32) + gsx[0].astype(F32)).astype(BF16)
    gpair[1] = (gsend[xp].astype(F32) + gsx[1].astype(F32)).astype(BF16)
    g_x = [
        remote(gpair.at[0], grx.at[1], sg.at[2], rg.at[3], {"chan": xp}),
        remote(gpair.at[1], grx.at[0], sg.at[3], rg.at[2], {"chan": xp}),
    ]
    for copy in g_x:
        copy.start()

    def relayout(b):
        def body(g, c):
            r = pl.ds(pl.multiple_of(g * 16, 16), 16)
            for t in range(tiles):
                k = g * 16 * rpc + t * n_img + b
                v = jnp.concatenate([out_x[pl.ds(k + h * 8 * rpc, 8, stride=rpc), :] for h in range(2)], axis=0)
                xb[b, r, t * LANES : (t + 1) * LANES] = v.astype(BF16)
            return c

        lax.fori_loop(0, cp // 16, body, 0)

    relayout(xs)
    relayout(xp)
    loads[7].wait()
    w2pad[...] = jnp.zeros(w2pad.shape, F32)
    w2wide[...] = jnp.zeros(w2wide.shape, F32)
    for t in range(9):
        w2pad[t, 0:grow, 0:grow] = w2v[t].astype(F32)
        tile, off = t * TAP // LANES, t * TAP % LANES
        v = pltpu.roll(w2pad[t], off, 1) if off else w2pad[t]
        lane = iota(v.shape, 1)
        here = slice(tile * LANES, (tile + 1) * LANES)
        w2wide[:, here] = w2wide[:, here] + jnp.where(lane >= off, v, 0.0)
        if off + grow > LANES:
            there = slice((tile + 1) * LANES, (tile + 2) * LANES)
            w2wide[:, there] = w2wide[:, there] + jnp.where(lane < off, v, 0.0)
    w2r[ch] = w2wide[...].astype(BF16)
    loads[5].wait()
    loads[6].wait()
    gsl[ch, 0:1, 0:grow] = gain2v[...]
    gsl[ch, 1:2, 0:grow] = bias2v[...]
    w_near = remote(w2r.at[ch], w2r.at[ch], sw.at[0], rw.at[0], {"chan": sib})
    w_far = remote(w2r.at[ch], w2r.at[ch], sw.at[1], rw.at[1], {"chan": xp})
    w_on = remote(w2r.at[xp], w2r.at[xp], sw.at[2], rw.at[2], {"chan": sib})
    w_far.start()
    w_near.start()
    share_start(gsl, ch, n_ch, ch_peer, sb, rb)

    loads[2].wait()
    w1s[...] = jnp.zeros(w1s.shape, BF16)
    w1s[0:n_d, 0:n_c] = w1v[...]
    rowbuf[...] = jnp.zeros(rowbuf.shape, F32)
    loads[3].wait()
    loads[4].wait()
    rowbuf[0:1, :] = gain1v[0:1, 0:LANES]
    rowbuf[1:2, 0 : n_c - LANES] = gain1v[0:1, LANES:n_c]
    rowbuf[2:3, :] = bias1v[0:1, 0:LANES]
    rowbuf[3:4, 0 : n_c - LANES] = bias1v[0:1, LANES:n_c]


    share_wait(ar1, dp, n_dp, dp_peer, s1, r1)
    tot1 = total(ar1)
    count = tot1[1:2, LANES - 1 : LANES]
    mean1, rstd1, scale1, keep1 = [], [], [], []
    for i in range(2):
        mean = tot1[i : i + 1] / count
        rstd = lax.rsqrt(tot1[2 + i : 3 + i] / count - mean * mean + EPS)
        here = lane1 + i * LANES
        ids = ch * n_c + here
        first = new_slot * grow
        keep = jnp.where(
            (here < n_c) & ((ids < first) | (ids >= first + grow)), 1.0, 0.0
        )
        scale = rstd * rowbuf[i : i + 1, :]
        shift = rowbuf[2 + i : 3 + i, :] - mean * scale
        size = c_sizes[i]
        r = pl.ds(i * LANES, size)
        col_a[r, :] = as_column(0.5 * scale * keep, size)
        col_b[r, :] = as_column(0.5 * shift * keep, size)
        mean1.append(mean)
        keep1.append(keep)
        rstd1.append(rstd)
        scale1.append(scale)

    def partial(j, first, n):
        def body(g, c):
            r = pl.ds(pl.multiple_of(g * 16, 16), 16)
            a, b = col_a[r, :], col_b[r, :]
            for t in range(first, first + n):
                sl = slice(t * LANES, (t + 1) * LANES)
                v = xb[j, r, sl].astype(F32) * a + b
                act[j, r, sl] = ((v * jnp.tanh(v) + v) * mask[j, :, sl]).astype(BF16)
            return c

        lax.fori_loop(0, cp // 16, body, 0)
        sl = slice(first * LANES, (first + n) * LANES)
        part[j, :, sl] = jnp.dot(w1s[...], act[j, :, sl], preferred_element_type=F32)

    rows_d = pl.ds(0, d8)
    unit = tiles // sum(SPANS)
    edges = [sum(SPANS[:p]) * unit for p in range(PIECES + 1)]

    def lanes_of(p):
        return pl.ds(edges[p] * LANES, (edges[p + 1] - edges[p]) * LANES)

    def tiles_of(p):
        return [slice(t * LANES, (t + 1) * LANES) for t in range(edges[p], edges[p + 1])]

    blocks, rest = d8 // 64, d8 // 64 * 64
    plain = blocks * 40

    def code(read, p, words, tops):
        top = jnp.maximum(jnp.max(row_top[...], axis=1, keepdims=True), 1e-30)
        tops[p, 0:1, :] = as_row(top[0:LANES])
        tops[p, 1:2, :] = as_row(top[LANES:d8])
        row_scale[...] = jnp.broadcast_to(LEVELS / top, (d8, LANES))

        def quantized(first, n, sl):
            r = pl.ds(pl.multiple_of(first, 8), n)
            return jnp.round(read(r, sl) * row_scale[r, :]).astype(jnp.int32)

        def block(i, c):
            for t, sl in enumerate(tiles_of(p), edges[p]):
                high = jnp.zeros((8, LANES), jnp.int32)
                for k in range(4):
                    first = quantized(i * 64 + k * 8, 8, sl)
                    second = quantized(i * 64 + 32 + k * 8, 8, sl)
                    words[t, pl.ds(pl.multiple_of(i * 40 + k * 8, 8), 8), :] = (first << 12) | (second & 0xFFF)
                    high = high | (((second >> 12) & 0xFF) << (8 * k))
                words[t, pl.ds(pl.multiple_of(i * 40 + 32, 8), 8), :] = high
            return c

        lax.fori_loop(0, blocks, block, 0)
        for t, sl in enumerate(tiles_of(p), edges[p]):
            words[t, plain : plain + d8 - rest, :] = quantized(rest, d8 - rest, sl)

    def unscale(tops, p):
        top = jnp.concatenate([as_column(tops[p, 0:1, :], LANES), as_column(tops[p, 1:2, :], d8 - LANES)], axis=0)
        row_scale[...] = top * (1.0 / LEVELS)

    def uncode(write, p, words):
        def put(first, n, sl, q):
            r = pl.ds(pl.multiple_of(first, 8), n)
            write(r, sl, q.astype(F32) * row_scale[r, :])

        def block(i, c):
            for t, sl in enumerate(tiles_of(p), edges[p]):
                high = words[t, pl.ds(pl.multiple_of(i * 40 + 32, 8), 8), :]
                for k in range(4):
                    low = words[t, pl.ds(pl.multiple_of(i * 40 + k * 8, 8), 8), :]
                    put(i * 64 + k * 8, 8, sl, low >> 12)
                    put(i * 64 + 32 + k * 8, 8, sl, (((high << (24 - 8 * k)) >> 24) << 12) | (low & 0xFFF))
            return c

        lax.fori_loop(0, blocks, block, 0)
        for t, sl in enumerate(tiles_of(p), edges[p]):
            put(rest, d8 - rest, sl, words[t, plain : plain + d8 - rest, :])

    def top_of(values):
        value = jnp.abs(values[0])
        for other in values[1:]:
            value = jnp.maximum(value, jnp.abs(other))
        return value

    def piece_of(j, p):
        partial(j, edges[p], edges[p + 1] - edges[p])

    def over(p):
        at = lanes_of(p)
        return remote(part.at[xs, rows_d, at], rx_a.at[rows_d, at], sp.at[p], rp.at[p], {"chan": sib})

    to_x = []
    piece_of(xs, 0)
    over(0).start()
    piece_of(xp, 0)
    for p in range(PIECES):
        if p + 1 < PIECES:
            piece_of(xs, p + 1)
            over(p + 1).start()
        over(p).wait()

        def add_a(g, c):
            r = pl.ds(pl.multiple_of(g * 8, 8), 8)
            values = [part[xp, r, sl] + rx_a[r, sl] for sl in tiles_of(p)]
            for sl, v in zip(tiles_of(p), values):
                part[xp, r, sl] = v
            row_top[r, :] = top_of(values)
            return c

        lax.fori_loop(0, d8 // 8, add_a, 0)
        code(lambda r, sl: part[xp, r, sl], p, px_out, tx_out)
        at = pl.ds(edges[p], edges[p + 1] - edges[p])
        copies = [
            remote(tx_out.at[p], tx_in.at[p], sq.at[0, p], rq.at[0, p], {"chan": xp}),
            remote(px_out.at[at], px_in.at[at], sq.at[1, p], rq.at[1, p], {"chan": xp}),
        ]
        for copy in copies:
            copy.start()
        to_x.append(copies)
        if p + 1 < PIECES:
            piece_of(xp, p + 1)
    for i in range(2):
        r = pl.ds(i * LANES, c_sizes[i])
        col_m[r, :] = as_column(mean1[i], c_sizes[i])
        col_k[r, :] = as_column(keep1[i], c_sizes[i])
    relayout(sib)
    relayout(ch)
    partial(sib, 0, tiles)
    to_sib_b = remote(part.at[sib, rows_d], rx_b.at[rows_d], sx.at[0], rxs.at[0], {"chan": sib})
    to_sib_b.start()
    partial(ch, 0, tiles)

    for copy in g_x:
        copy.wait()
    px = iota((TAP, n_px), 1)
    py, pxx = px >> 5, px & (SIDE - 1)
    for i in range(2):
        gcur[...] = gpair[i].astype(F32) + grx[i].astype(F32)
        for ky in range(3):
            for kx in range(3):
                shift = (ky - 1) * SIDE + (kx - 1)
                t = ky * 3 + kx
                v = gcur[...]
                if shift != 0:
                    v = pltpu.roll(v, shift % n_px, 1)
                ok = None
                for off, pos in ((ky - 1, py), (kx - 1, pxx)):
                    if off == 1:
                        test = pos >= 1
                    elif off == -1:
                        test = pos <= SIDE - 2
                    else:
                        continue
                    ok = test if ok is None else ok & test
                if ok is not None:
                    v = jnp.where(ok, v, 0.0)
                g9[i, t * TAP : (t + 1) * TAP, :] = v.astype(BF16)
        g9[i, pl.ds(9 * TAP, TAPS - 9 * TAP), :] = jnp.zeros((TAPS - 9 * TAP, n_px), BF16)
    def slopes(j):
        def body(g, c):
            r = pl.ds(pl.multiple_of(g * 16, 16), 16)
            a, b = col_a[r, :], col_b[r, :]
            k = 0.5 * col_k[r, :]
            for t in range(tiles):
                sl = slice(t * LANES, (t + 1) * LANES)
                v = xb[j, r, sl].astype(F32) * a + b
                th = jnp.tanh(v)
                slope[j, r, sl] = ((1.0 + th) * (1.0 + v * (1.0 - th))) * (mask[j, :, sl] * k)
            return c

        lax.fori_loop(0, cp // 16, body, 0)

    slopes(xs)
    slopes(xp)

    to_sib_b.wait()
    sum_a[...] = jnp.zeros(sum_a.shape, F32)
    sum_b[...] = jnp.zeros(sum_b.shape, F32)
    hid[:, d8:dpad, :] = jnp.zeros((2, dpad - d8, n_px), F32)
    gp2[...] = jnp.zeros(gp2.shape, F32)

    def across(p):
        at = pl.ds(edges[p], edges[p + 1] - edges[p])
        return [
            remote(th_out.at[p], th_in.at[p], sh.at[0, p], rh.at[0, p], {"chan": xp}),
            remote(ph_out.at[at], ph_in.at[at], sh.at[1, p], rh.at[1, p], {"chan": xp}),
        ]

    def start_across(p):
        for copy in across(p):
            copy.start()

    for p in range(PIECES):
        for copy in to_x[p]:
            copy.wait()
        unscale(tx_in, p)

        def gather(r, sl, v):
            hid[0, r, sl] = (part[ch, r, sl] + rx_b[r, sl]) + v

        uncode(gather, p, px_in)

        def sums(g, c):
            r = pl.ds(pl.multiple_of(g * 8, 8), 8)
            s_acc, q_acc = sum_a[r, :], sum_b[r, :]
            values = [hid[0, r, sl] for sl in tiles_of(p)]
            for v in values:
                s_acc = s_acc + v
                q_acc = q_acc + v * v
            sum_a[r, :] = s_acc
            sum_b[r, :] = q_acc
            tops_h[p, r, :] = top_of(values)
            return c

        lax.fori_loop(0, d8 // 8, sums, 0)
        if p < AHEAD:
            row_top[...] = tops_h[p]
            code(lambda r, sl: hid[0, r, sl], p, ph_out, th_out)
            start_across(p)

    def pack(slots):
        s, q = as_rows(sum_a[0:d8, :], d_sizes), as_rows(sum_b[0:d8, :], d_sizes)
        slots[me, 0:1, :] = s[0]
        slots[me, 1:2, :] = s[1]
        slots[me, 2:3, :] = q[0]
        slots[me, 3:4, :] = q[1]

    def columns_d(row0, row1):
        tail = jnp.zeros((dpad - d8, LANES), F32)
        return jnp.concatenate(
            [as_column(row0, LANES), as_column(row1, d8 - LANES), tail], axis=0
        )

    pack(ar2)
    share_start(ar2, me, n_dev, dev_peer, s2, r2)
    for p in range(AHEAD, PIECES):
        row_top[...] = tops_h[p]
        code(lambda r, sl: hid[0, r, sl], p, ph_out, th_out)
        start_across(p)

    w_far.wait()
    w_on.start()
    slopes(sib)
    slopes(ch)
    w_near.wait()
    w_on.wait()
    share_wait(gsl, ch, n_ch, ch_peer, sb, rb)
    acc = jnp.zeros((dpad, w2b.shape[1]), F32)
    for j in range(n_ch):
        rows = iota((dpad, TAP), 0)
        cols = iota((dpad, TAP), 1)
        place = jnp.where((rows == cols + j * grow) & (cols < grow), 1.0, 0.0).astype(BF16)
        acc = acc + jnp.dot(place, w2r[j], preferred_element_type=F32)
    w2b[...] = acc.astype(BF16)
    for i in range(2):
        back[i] = jnp.dot(w2b[...], g9[i], preferred_element_type=F32)
    rows = iota((dpad, LANES), 0)
    cols = iota((dpad, LANES), 1)
    gain2c = jnp.zeros((dpad, 1), F32)
    bias2c = jnp.zeros((dpad, 1), F32)
    for j in range(n_ch):
        place = (rows == cols + j * grow) & (cols < grow)
        gain2c = gain2c + jnp.sum(jnp.where(place, gsl[j, 0:1, :], 0.0), axis=1, keepdims=True)
        bias2c = bias2c + jnp.sum(jnp.where(place, gsl[j, 1:2, :], 0.0), axis=1, keepdims=True)
    col_c[0] = jnp.broadcast_to(gain2c, (dpad, LANES))
    col_c[1] = jnp.broadcast_to(bias2c, (dpad, LANES))

    def widen_cot(i, c):
        r = pl.ds(pl.multiple_of(i * step_rows, step_rows), step_rows)
        k = [jnp.broadcast_to(col_k[pl.ds(i * 3 + n, 1), :], (rpc, LANES)) for n in range(3)]
        base[r, :] = cot[r, :].astype(F32) * jnp.concatenate(k, axis=0)
        return c

    lax.fori_loop(0, n_rows // step_rows, widen_cot, 0)

    share_wait(ar2, me, n_dev, dev_peer, s2, r2)
    tot2 = total(ar2)
    mean2 = [tot2[i : i + 1] / count for i in range(2)]
    rstd2 = [lax.rsqrt(tot2[2 + i : 3 + i] / count - mean2[i] * mean2[i] + EPS) for i in range(2)]
    mean2c = columns_d(*mean2)
    rstd2c = columns_d(*rstd2)
    scale2c = rstd2c * col_c[0]
    col_c[2] = mean2c
    col_c[3] = rstd2c
    col_c[4] = scale2c
    col_c[5] = 0.5 * scale2c
    col_c[6] = 0.5 * (col_c[1] - mean2c * scale2c)

    def second(g, c):
        r = pl.ds(pl.multiple_of(g * 16, 16), 16)
        a, b, m = col_c[5, r, :], col_c[6, r, :], col_c[2, r, :]
        s_acc = jnp.zeros((16, LANES), F32)
        q_acc = jnp.zeros((16, LANES), F32)
        for t in range(tiles):
            sl = slice(t * LANES, (t + 1) * LANES)
            h = hid[0, r, sl]
            mk = mask[ch, :, sl]
            v = h * a + b
            th = jnp.tanh(v)
            act2[r, sl] = ((v * th + v) * mk).astype(BF16)
            gp = (0.5 * mk) * ((1.0 + th) * (1.0 + v * (1.0 - th))) * back[0, r, sl]
            gp2[0, r, sl] = gp
            s_acc = s_acc + gp
            q_acc = q_acc + gp * (h - m)
        sum_a[r, :] = s_acc
        sum_b[r, :] = q_acc
        return c

    lax.fori_loop(0, dpad // 16, second, 0)
    pack(ar3)
    share_start(ar3, me, n_dev, dev_peer, s3, r3)

    w2acc[...] = lax.dot_general(
        act2[...], g9[0], (((1,), (1,)), ((), ())), preferred_element_type=F32
    )
    for j in range(n_ch):
        for lt in range(4):
            sl = slice(lt * LANES, (lt + 1) * LANES)
            cw[j, lt * 32 : lt * 32 + 32, :] = w2acc[j * grow : j * grow + 32, sl]
            cw[j, 128 + lt : 129 + lt, :] = w2acc[j * grow + 32 : j * grow + 33, sl]
        cw[j, 132:136, :] = jnp.zeros((4, LANES), F32)
    w_sib = [
        remote(cw.at[xs], cwr.at[1], sc.at[0], rc.at[0], {"chan": sib}),
        remote(cw.at[sib], cwr.at[0], sc.at[1], rc.at[1], {"chan": sib}),
    ]
    for copy in w_sib:
        copy.start()

    def second_other(p):
        for copy in across(p):
            copy.wait()
        unscale(th_in, p)

        def keep_hidden(r, sl, v):
            hid[1, r, sl] = v

        uncode(keep_hidden, p, ph_in)

        def body(g, c):
            r = pl.ds(pl.multiple_of(g * 16, 16), 16)
            a, b = col_c[5, r, :], col_c[6, r, :]
            for sl in tiles_of(p):
                v = hid[1, r, sl] * a + b
                th = jnp.tanh(v)
                gp2[1, r, sl] = (
                    (0.5 * mask[xp, :, sl]) * ((1.0 + th) * (1.0 + v * (1.0 - th))) * back[1, r, sl]
                )
            return c

        lax.fori_loop(0, dpad // 16, body, 0)

    zbuf[...] = lax.dot_general(
        w2b[...], act2[...], (((0,), (0,)), ((), ())), preferred_element_type=F32
    )
    new = jnp.zeros((TAP, n_px), F32)
    for ky in range(3):
        for kx in range(3):
            shift = (ky - 1) * SIDE + (kx - 1)
            t = ky * 3 + kx
            v = zbuf[t * TAP : (t + 1) * TAP, :]
            if shift != 0:
                v = pltpu.roll(v, (-shift) % n_px, 1)
            ok = None
            for off, pos in ((ky - 1, py), (kx - 1, pxx)):
                if off == -1:
                    test = pos >= 1
                elif off == 1:
                    test = pos <= SIDE - 2
                else:
                    continue
                ok = test if ok is None else ok & test
            if ok is not None:
                v = jnp.where(ok, v, 0.0)
            new = new + v
    new = new * jnp.concatenate([mask[ch]] * (TAP // 16), axis=0)
    gall[ch] = new[0 : gall.shape[1]]
    for copy in w_sib:
        copy.wait()
    cw[xp] = cw[xp] + cwr[1]
    cw[ch] = cw[ch] + cwr[0]
    w_x = remote(cw.at[xp], cwx, sc.at[2], rc.at[2], {"chan": xp})
    w_x.start()
    new_sib = remote(gall.at[ch], gall.at[ch], so.at[0], ro.at[0], {"chan": sib})
    new_xp = remote(gall.at[ch], gall.at[ch], so.at[1], ro.at[1], {"chan": xp})
    new_on = remote(gall.at[xp], gall.at[xp], so.at[2], ro.at[2], {"chan": sib})
    new_xp.start()
    new_sib.start()
    for p in range(PIECES):
        second_other(p)

    share_wait(ar3, me, n_dev, dev_peer, s3, r3)
    tot3 = total(ar3)
    gain_sum2 = [tot3[2 + i : 3 + i] * rstd2[i] for i in range(2)]
    bias_sum2 = [tot3[i : i + 1] for i in range(2)]
    gain_sum2c = columns_d(*gain_sum2)
    bias_sum2c = columns_d(*bias_sum2)
    col_c[7] = col_c[4] * bias_sum2c / count
    col_c[8] = col_c[4] * col_c[3] * gain_sum2c / count

    def third(i, j, k):
        def body(g, c):
            r = pl.ds(pl.multiple_of(g * 16, 16), 16)
            c1, c2, c3, m = col_c[4, r, :], col_c[7, r, :], col_c[8, r, :], col_c[2, r, :]
            for sl in [slice(t * LANES, (t + 1) * LANES) for t in range(k * tiles // 2, (k + 1) * tiles // 2)]:
                gha[j, r, sl] = (
                    c1 * gp2[i, r, sl] - mask[j, :, sl] * (c2 + c3 * (hid[i, r, sl] - m))
                ).astype(BF16)
            return c

        lax.fori_loop(0, dpad // 16, body, 0)

    grads = []
    for i, j in ((0, ch), (1, xp)):
        for k in range(2):
            third(i, j, k)
            at = pl.ds(k * (n_px // 2), n_px // 2)
            copy = remote(gha.at[j, :, at], gha.at[j, :, at], st.at[i, k], rt.at[i, k], {"chan": sib})
            copy.start()
            grads.append(copy)
    d_rows, d_cols = iota((dpad, LANES), 0), iota((dpad, LANES), 1)
    here_d = (d_rows == d_cols + ch * grow) & (d_cols < grow)
    out_g2[...] = jnp.sum(jnp.where(here_d, gain_sum2c, 0.0), axis=0, keepdims=True)[:, 0:grow]
    out_b2[...] = jnp.sum(jnp.where(here_d, bias_sum2c, 0.0), axis=0, keepdims=True)[:, 0:grow]

    w1acc[...] = jnp.zeros(w1acc.shape, F32)
    sum_a[...] = jnp.zeros(sum_a.shape, F32)
    sum_b[...] = jnp.zeros(sum_b.shape, F32)

    def weight_grad(j, k=None):
        at = slice(0, n_px) if k is None else slice(k * (n_px // 2), (k + 1) * (n_px // 2))
        w1acc[0:dpad, 0:cp] = w1acc[0:dpad, 0:cp] + lax.dot_general(
            gha[j, :, at], act[j, :, at], (((1,), (1,)), ((), ())), preferred_element_type=F32
        )

    def input_grad(j):
        gact[...] = lax.dot_general(
            w1s[...], gha[j], (((0,), (0,)), ((), ())), preferred_element_type=F32
        )

        def body(g, c):
            r = pl.ds(pl.multiple_of(g * 16, 16), 16)
            m = col_m[r, :]
            s_acc, q_acc = sum_a[r, :], sum_b[r, :]
            for t in range(tiles):
                sl = slice(t * LANES, (t + 1) * LANES)
                gp = gact[r, sl] * slope[j, r, sl]
                gp1[j, r, sl] = gp
                s_acc = s_acc + gp
                q_acc = q_acc + gp * (xb[j, r, sl].astype(F32) - m)
            sum_a[r, :] = s_acc
            sum_b[r, :] = q_acc
            return c

        lax.fori_loop(0, cp // 16, body, 0)

    weight_grad(ch)
    weight_grad(xp)
    w_x.wait()
    input_grad(ch)
    for i, j in ((0, sib), (1, xs)):
        for k in range(2):
            grads[2 * i + k].wait()
            weight_grad(j, k)

    for r in range(17):
        cb[r // 5, r % 5 * 8 : r % 5 * 8 + 8, :] = w1acc[r * 8 : r * 8 + 8, 0:LANES]
    for k in range(6):
        v = w1acc[k * 8 : k * 8 + 8, LANES : 2 * LANES]
        for i in range(1, 3):
            v = v + pltpu.roll(w1acc[i * 48 + k * 8 : i * 48 + k * 8 + 8, LANES : 2 * LANES], 40 * i, 1)
        r = 17 + k
        cb[r // 5, r % 5 * 8 : r % 5 * 8 + 8, :] = v
    for k in range(17):
        r = 23 + k
        cb[r // 5, r % 5 * 8 : r % 5 * 8 + 8, :] = cw[ch, k * 8 : k * 8 + 8, :] + cwx[k * 8 : k * 8 + 8, :]

    def encode(v):
        top = jnp.maximum(jnp.max(jnp.abs(v), axis=0, keepdims=True), 1e-30)
        power = jnp.floor(jnp.log2(top) + 1.0001)
        q = jnp.clip(jnp.round(v * jnp.exp2(15.0 - power)), -32767.0, 32767.0).astype(jnp.int32)
        low = jnp.concatenate([q[24:40], jnp.broadcast_to(power.astype(jnp.int32), (8, LANES))], axis=0)
        return (q[0:24] << 16) | (low & 0xFFFF)

    def decode(w):
        high, low = w >> 16, (w << 16) >> 16
        scale = jnp.exp2(low[16:24].astype(F32) - 15.0)
        q = jnp.concatenate([high, low[0:16]], axis=0).astype(F32)
        return q * jnp.concatenate([scale] * 5, axis=0)

    for q in range(OWNERS):
        coded[q] = encode(cb[q])
    stride = n_dp // OWNERS
    my_part = dp // stride
    is_owner = lax.rem(dp, stride) == 0

    def part_to(k):
        q = my_part ^ (OWNERS - 1 - k)
        return q, q * stride

    def push(k, c):
        q, to = part_to(k)

        @pl.when(to != dp)
        def _():
            remote(coded.at[q], rsl.at[dp], sr.at[k], rr.at[dp], {"dp": to}).start()

        return c

    lax.fori_loop(0, OWNERS, push, 0)
    for j in (xp, sib, xs):
        input_grad(j)
    s4_, q4_ = as_rows(sum_a[...], c_sizes), as_rows(sum_b[...], c_sizes)
    for i in range(2):
        ar4[dp, i : i + 1, :] = s4_[i]
        ar4[dp, 2 + i : 3 + i, :] = q4_[i]
    share_start(ar4, dp, n_dp, dp_peer, s4, r4)
    new_xp.wait()
    new_on.start()

    def scatter(g, c):
        first = g * 16 * rpc
        r = pl.ds(pl.multiple_of(g * 16, 16), 16)
        for b in range(n_img):
            for t in range(tiles):
                v = gp1[b, r, t * LANES : (t + 1) * LANES]
                for h in range(2):
                    at = pl.ds(first + h * 8 * rpc + t * n_img + b, 8, stride=rpc)
                    out_g[at, :] = v[h * 8 : h * 8 + 8]
        return c

    lax.fori_loop(0, 5, scatter, 0)

    def push_wait(k, c):
        q, to = part_to(k)

        @pl.when(to != dp)
        def _():
            remote(coded.at[q], rsl.at[dp], sr.at[k], rr.at[dp], {"dp": to}).wait_send()

        return c

    def pull(k, c):
        src = lax.rem(dp + k, n_dp)
        remote(coded.at[0], rsl.at[src], sr.at[0], rr.at[src], {"dp": src}).wait_recv()
        return c

    @pl.when(is_owner)
    def _():
        lax.fori_loop(1, n_dp, pull, 0)
        v = cb[my_part]
        for k in range(1, n_dp):
            v = v + decode(rsl[lax.rem(dp + k, n_dp)])
        fin[my_part] = encode(v)

        def give(k):
            remote(fin.at[my_part], fin.at[my_part], sa.at[k], ra.at[my_part], dp_peer(k)).start()

        far_first(n_dp, give)

    lax.fori_loop(0, OWNERS, push_wait, 0)
    lax.fori_loop(5, cp // 16, scatter, 0)

    for i in range(2):
        col_a[pl.ds(i * LANES, c_sizes[i]), :] = as_column(scale1[i], c_sizes[i])

    new_sib.wait()
    new_on.wait()
    for b in range(n_img):
        for t in range(tiles):
            for h in range(gall.shape[1] // 8):
                out_new[pl.ds(h * 8 * rpc + t * n_img + b, 8, stride=rpc), :] = gall[
                    b, h * 8 : h * 8 + 8, t * LANES : (t + 1) * LANES
                ]
    out_slot[...] = (slot_of - ch * per_device)[0:8].astype(F32)

    share_wait(ar4, dp, n_dp, dp_peer, s4, r4)
    tot4 = total(ar4)
    for i in range(2):
        bias_sum = tot4[i : i + 1]
        gain_sum = tot4[2 + i : 3 + i] * rstd1[i]
        size = c_sizes[i]
        r = pl.ds(i * LANES, size)
        k1 = -scale1[i] * rstd1[i] * gain_sum / count
        k0 = -scale1[i] * bias_sum / count - k1 * mean1[i]
        col_b[r, :] = as_column(k0, size)
        col_m[r, :] = as_column(k1, size)
        width = min(LANES, n_c - i * LANES)
        out_g1[0:1, i * LANES : i * LANES + width] = gain_sum[:, 0:width]
        out_b1[0:1, i * LANES : i * LANES + width] = bias_sum[:, 0:width]
    mask_of = mask_raw[...]

    def last(i, c):
        for k in range(5):
            row = i * 5 + k
            at = pl.ds(pl.multiple_of(row * rpc, rpc), rpc)
            k0 = jnp.broadcast_to(col_b[pl.ds(row, 1), :], (rpc, LANES))
            k1 = jnp.broadcast_to(col_m[pl.ds(row, 1), :], (rpc, LANES))
            a = jnp.broadcast_to(col_a[pl.ds(row, 1), :], (rpc, LANES))
            out_g[at, :] = base[at, :] + a * out_g[at, :] + mask_of * (k0 + k1 * out_x[at, :])
        return c

    lax.fori_loop(0, n_c // 5, last, 0)

    @pl.when(is_owner)
    def _():
        def gave(k, c):
            remote(fin.at[my_part], fin.at[my_part], sa.at[k], ra.at[my_part], dp_peer(k)).wait_send()
            return c

        lax.fori_loop(1, n_dp, gave, 0)

    def take(q, c):
        @pl.when(q * stride != dp)
        def _():
            remote(fin.at[q], fin.at[q], sa.at[0], ra.at[q], {"dp": q * stride}).wait_recv()

        return c

    lax.fori_loop(0, OWNERS, take, 0)
    for q in range(OWNERS):
        cb[q] = decode(fin[q])
    for r in range(17):
        height = min(8, n_d - r * 8)
        out_w1[r * 8 : r * 8 + height, 0:LANES] = cb[r // 5, r % 5 * 8 : r % 5 * 8 + height, :]
    for k in range(6):
        r = 17 + k
        v = cb[r // 5, r % 5 * 8 : r % 5 * 8 + 8, :]
        for i in range(3):
            row = i * 48 + k * 8
            height = min(8, n_d - row)
            if height > 0:
                u = v if i == 0 else pltpu.roll(v, LANES - 40 * i, 1)
                out_w1[row : row + height, LANES:n_c] = u[0:height, 0 : n_c - LANES]
    for k in range(17):
        r = 23 + k
        v = cb[r // 5, r % 5 * 8 : r % 5 * 8 + 8, :]
        if k < 16:
            w2acc[k % 4 * 8 : k % 4 * 8 + 8, k // 4 * LANES : (k // 4 + 1) * LANES] = v
        else:
            for lt in range(4):
                w2acc[32:33, lt * LANES : (lt + 1) * LANES] = v[lt : lt + 1]
    v = w2acc[0:40, :]
    for t in range(9):
        u = v if t == 0 else pltpu.roll(v, TAPS - t * TAP, 1)
        out_w2[t] = u[0:grow, 0:grow]


def finish(n_rows, grow_rows, *refs):
    n = (len(refs) - 3) // 2
    new, slot = refs[n : n + 2]
    outs, sem = refs[n + 2 : -1], refs[-1]
    segments = n_rows // grow_rows
    copies = [pltpu.make_async_copy(refs[1].at[pl.ds(0, n_rows)], outs[1], sem.at[1])]
    copies += [pltpu.make_async_copy(refs[i], outs[i], sem.at[i]) for i in range(2, n)]
    for copy in copies:
        copy.start()
    here = jnp.max(slot[...])
    for k in range(segments):
        at = pl.ds(k * grow_rows, grow_rows)
        kept = pltpu.make_async_copy(refs[0].at[at], outs[0].at[at], sem.at[n + k])
        grown = pltpu.make_async_copy(new.at[pl.ds(0, grow_rows)], outs[0].at[at], sem.at[n + k])
        pl.when(here == k)(grown.start)
        pl.when(here != k)(kept.start)
        copies.append(kept)
    for copy in copies:
        copy.wait()


def flat(values):
    n, c, p = values.shape
    return (
        values.transpose(1, 0, 2).reshape(c, n, p // LANES, LANES).transpose(0, 2, 1, 3).reshape(-1, LANES)
    )


def unflat(rows, n, c, p):
    return rows.reshape(c, p // LANES, n, LANES).transpose(0, 2, 1, 3).reshape(c, n, p).transpose(1, 0, 2)


def on_device(
    n_dp, n_ch, features, gain1, bias1, weight1, gain2, bias2, weight2, cotangent, image_side, block_slot
):
    n_img, n_c, n_px = features.shape
    n_d = weight1.shape[1]
    grow = weight2.shape[3]
    cp = pad_to(n_c, 16)
    dpad = pad_to(n_d, 16)
    d8 = pad_to(n_d, 8)
    rpc = n_px // LANES * n_img
    n_rows, n_pad = n_c * rpc, cp * rpc
    n_dev = n_dp * n_ch
    words = d8 // 64 * 40 + d8 % 64
    cfg = (n_dp, n_ch, n_img, n_c, n_px, n_d, grow)
    args = (
        flat(features),
        flat(cotangent),
        weight1.T,
        gain1.reshape(1, -1),
        bias1.reshape(1, -1),
        gain2.reshape(1, -1),
        bias2.reshape(1, -1),
        weight2.reshape(9, grow, grow),
        image_side,
        block_slot,
    )
    args = [pltpu.with_memory_space_constraint(v, pltpu.HBM) for v in args]
    sd = jax.ShapeDtypeStruct
    in_vmem = pl.BlockSpec(memory_space=pltpu.VMEM)
    in_hbm = pl.BlockSpec(memory_space=pltpu.HBM)
    dma = pltpu.SemaphoreType.DMA
    v = pltpu.VMEM
    scratch = [
        v((n_rows, LANES), BF16), v((n_rows, LANES), BF16), v((n_d, n_c), BF16),
        v((1, n_c), F32), v((1, n_c), F32), v((1, grow), F32), v((1, grow), F32),
        v((9, grow, grow), BF16), pltpu.SMEM(image_side.shape, jnp.int32), pltpu.SMEM(block_slot.shape, jnp.int32),
        v((n_img, 16, n_px), F32), v((rpc, LANES), F32), v((n_rows, LANES), F32),
        v((n_img, cp, n_px), BF16), v((n_img, cp, n_px), BF16),
        v((n_img, cp, n_px), F32), v((n_img, cp, n_px), F32), v((cp, n_px), F32),
        v((cp, LANES), F32), v((cp, LANES), F32), v((cp, LANES), F32), v((cp, LANES), F32),
        v((9, dpad, LANES), F32), v((cp, LANES), F32), v((cp, LANES), F32),
        v((cp * 8, LANES), F32), v((cp * 8, LANES), F32), v((8, LANES), F32),
        v((dpad, cp), BF16), v((n_img, dpad, n_px), F32),
        v((dpad, n_px), F32), v((dpad, n_px), F32), v((2, dpad, n_px), F32),
        v((d8, LANES), F32), v((d8, LANES), F32), v((PIECES, d8, LANES), F32),
        v((n_px // LANES, words, LANES), jnp.int32), v((n_px // LANES, words, LANES), jnp.int32), v((PIECES, 2, LANES), F32), v((PIECES, 2, LANES), F32),
        v((n_px // LANES, words, LANES), jnp.int32), v((n_px // LANES, words, LANES), jnp.int32), v((PIECES, 2, LANES), F32), v((PIECES, 2, LANES), F32),
        v((TAP * rpc, LANES), F32), v((n_ch, TAP, n_px), BF16),
        v((2, TAP, n_px), BF16), v((2, TAP, n_px), BF16), v((2, TAP, n_px), BF16), v((TAP, n_px), F32),
        v((2, TAPS, n_px), BF16), v((9, TAP, LANES), F32), v((TAP, TAPS), F32), v((n_ch, TAP, TAPS), BF16), v((dpad, TAPS), BF16),
        v((n_ch, 2, LANES), F32),
        v((dpad, n_px), BF16), v((2, dpad, n_px), F32), v((2, dpad, n_px), F32), v((TAPS, n_px), F32),
        v((n_ch, 40, n_px), F32), v((n_ch, dpad, n_px), BF16),
        v((n_ch, 136, LANES), F32), v((2, 136, LANES), F32), v((136, LANES), F32),
        v((OWNERS, 40, LANES), F32), v((OWNERS, 24, LANES), jnp.int32),
        v((n_dp, 24, LANES), jnp.int32), v((OWNERS, 24, LANES), jnp.int32), v((dpad, 256), F32), v((dpad, TAPS), F32),
        v((n_dp, 4, LANES), F32), v((n_dev, 4, LANES), F32), v((n_dev, 4, LANES), F32), v((n_dp, 4, LANES), F32),
        dma((13,)),
        dma((n_dp,)), dma((n_dp,)), dma((n_dev,)), dma((n_dev,)), dma((n_dev,)), dma((n_dev,)), dma((n_dp,)), dma((n_dp,)),
        dma((3,)), dma((3,)), dma((PIECES,)), dma((PIECES,)), dma((2, PIECES)), dma((2, PIECES)),
        dma((4,)), dma((4,)), dma((n_ch,)), dma((n_ch,)), dma((n_ch,)), dma((n_ch,)),
        dma((2, PIECES)), dma((2, PIECES)), dma((2, 2)), dma((2, 2)), dma((3,)), dma((3,)), dma((3,)), dma((3,)),
        dma((OWNERS,)), dma((n_dp,)), dma((n_dp,)), dma((OWNERS,)),
    ]
    out_shape = (
        sd((n_pad, LANES), F32), sd((n_pad, LANES), F32), sd((n_d, n_c), F32),
        sd((1, n_c), F32), sd((1, n_c), F32), sd((9, grow, grow), F32), sd((1, grow), F32), sd((1, grow), F32),
        sd((40 * rpc, LANES), F32), sd((8, LANES), F32),
    )
    outs = pl.pallas_call(
        functools.partial(layer, cfg),
        out_shape=out_shape,
        in_specs=[in_hbm] * len(args),
        out_specs=(in_vmem,) * len(out_shape),
        scratch_shapes=scratch,
        compiler_params=pltpu.CompilerParams(
            collective_id=0, has_side_effects=True, vmem_limit_bytes=40 << 20
        ),
    )(*args)
    final = (sd((n_rows, LANES), F32),) * 2 + out_shape[2:-2]
    o = pl.pallas_call(
        functools.partial(finish, n_rows, grow * rpc),
        out_shape=final,
        in_specs=[in_vmem] * len(outs),
        out_specs=(in_hbm,) * len(final),
        scratch_shapes=[dma((len(final) + n_c // grow,))],
        compiler_params=pltpu.CompilerParams(vmem_limit_bytes=8 << 20),
    )(*outs)
    return (
        unflat(o[0], n_img, n_c, n_px),
        unflat(o[1], n_img, n_c, n_px),
        o[2].T,
        o[3].reshape(-1),
        o[4].reshape(-1),
        o[5].reshape(3, 3, grow, grow),
        o[6].reshape(-1),
        o[7].reshape(-1),
    )


def solution(mesh):
    in_specs = (
        P("dp", "chan", None),
        P("chan"),
        P("chan"),
        P("chan", None),
        P("chan"),
        P("chan"),
        P(None, None, "chan", None),
        P("dp", "chan", None),
        P("dp"),
        P(),
    )
    out_specs = (
        P("dp", "chan", None),
        P("dp", "chan", None),
        P("chan", None),
        P("chan"),
        P("chan"),
        P(None, None, "chan", None),
        P("chan"),
        P("chan"),
    )
    body = functools.partial(on_device, mesh.shape["dp"], mesh.shape["chan"])
    return jax.shard_map(body, mesh=mesh, in_specs=in_specs, out_specs=out_specs, check_vma=False)
```

```python
import functools

import jax
import jax.numpy as jnp
from jax import lax
from jax.experimental import pallas as pl
from jax.experimental.pallas import tpu as pltpu
from jax.sharding import PartitionSpec as P

SIDE = 32
EPS = 1e-05
LANES = 128
TAP = 48
TAPS = 512
SPANS = (1, 2, 3, 2)
PIECES = len(SPANS)
AHEAD = 2
LEVELS = 524000.0
OWNERS = 8

MESH = pl.DeviceIdType.MESH
F32 = jnp.float32
BF16 = jnp.bfloat16


def pad_to(size, unit):
    return (size + unit - 1) // unit * unit


def iota(shape, axis):
    return lax.broadcasted_iota(jnp.int32, shape, axis)


def as_row(column):
    n = column.shape[0]
    eye = iota((n, LANES), 0) == iota((n, LANES), 1)
    return jnp.sum(jnp.where(eye, column, 0.0), axis=0, keepdims=True)


def as_column(row, n):
    eye = iota((n, LANES), 0) == iota((n, LANES), 1)
    return jnp.broadcast_to(jnp.sum(jnp.where(eye, row, 0.0), axis=1, keepdims=True), (n, LANES))


def as_rows(values, sizes):
    column = jnp.sum(values, axis=1, keepdims=True)
    rows, start = [], 0
    for size in sizes:
        rows.append(as_row(column[start : start + size]))
        start += size
    return rows


def layer(
    cfg,
    feat_h, cot_h, w1_h, gain1_h, bias1_h, gain2_h, bias2_h, w2_h, side_h, slot_h,
    out_x, out_g, out_w1, out_g1, out_b1, out_w2, out_g2, out_b2, out_new, out_slot,
    feat, cot, w1v, gain1v, bias1v, gain2v, bias2v, w2v, side, slot,
    mask, mask_raw, base, xb, act, slope, gp1, gact,
    col_a, col_b, col_m, col_k, col_c, sum_a, sum_b, rowbuf,
    w1s, part, rx_a, rx_b, hid, row_top, row_scale, tops_h,
    px_out, px_in, tx_out, tx_in, ph_out, ph_in, th_out, th_in,
    graw, gsend, gsx, gpair, grx, gcur, g9, w2pad, w2wide, w2r, w2b, gsl,
    act2, gp2, back, zbuf, gall, gha,
    cw, cwr, cwx, cb, coded, rsl, fin, w1acc, w2acc,
    ar1, ar2, ar3, ar4,
    load_sem, s1, r1, s2, r2, s3, r3, s4, r4, sx, rxs, sp, rp, sq, rq, sg, rg, sw, rw, sb, rb, sh, rh, st, rt, so, ro, sc, rc, sr, rr, sa, ra,
):
    n_dp, n_ch, n_img, n_c, n_px, n_d, grow = cfg
    n_dev = n_dp * n_ch
    cp = xb.shape[1]
    dpad = w1s.shape[0]
    d8 = pad_to(n_d, 8)
    tiles = n_px // LANES
    rpc = tiles * n_img
    c_sizes = (LANES, cp - LANES)
    d_sizes = (LANES, d8 - LANES)
    dp = lax.axis_index("dp")
    ch = lax.axis_index("chan")
    me = dp * n_ch + ch
    half = n_ch // 2
    cx, cc = ch // half, lax.rem(ch, half)
    sib = cx * half + (1 - cc)
    xp = (1 - cx) * half + cc
    xs = (1 - cx) * half + (1 - cc)

    def dev_peer(k):
        q = me ^ k
        return {"dp": q // n_ch, "chan": lax.rem(q, n_ch)}

    def dp_peer(k):
        return {"dp": dp ^ k}

    def ch_peer(k):
        return {"chan": ch ^ k}

    def far_first(count, step):
        if count <= 32:
            for k in range(count - 1, 0, -1):
                step(k)
        else:

            def body(i, c):
                step(count - 1 - i)
                return c

            lax.fori_loop(0, count - 1, body, 0)

    loads = {
        i: pltpu.make_async_copy(h, v, load_sem.at[i])
        for i, (h, v) in enumerate(
            (
                (cot_h, cot), (w1_h, w1v), (gain1_h, gain1v), (bias1_h, bias1v),
                (gain2_h, gain2v), (bias2_h, bias2v), (w2_h, w2v), (side_h, side), (slot_h, slot),
            ),
            1,
        )
    }
    feat_groups, feat_parts, start = [], [], 0
    for k in range(3):
        groups = pad_to(n_c, 8) // 8 * (k + 1) // 3 - sum(feat_groups)
        size = min(groups * 8, n_c - start) * rpc
        at = pl.ds(start * rpc, size)
        feat_parts.append(pltpu.make_async_copy(feat_h.at[at], feat.at[at], load_sem.at[10 + k]))
        feat_groups.append(groups)
        start += groups * 8
    for copy in [loads[8], loads[9], *feat_parts, *(loads[i] for i in range(1, 8))]:
        copy.start()
    barrier = pltpu.get_barrier_semaphore()

    def greet(k):
        pl.semaphore_signal(barrier, inc=1, device_id=dev_peer(k), device_id_type=MESH)

    far_first(n_dev, greet)

    def remote(src, dst, send, recv, device):
        return pltpu.make_async_remote_copy(
            src_ref=src, dst_ref=dst, send_sem=send, recv_sem=recv, device_id=device, device_id_type=MESH
        )

    def share_start(slots, mine, count, peer, send, recv):
        def step(k):
            remote(slots.at[mine], slots.at[mine], send.at[k], recv.at[k], peer(k)).start()

        far_first(count, step)

    def share_wait(slots, mine, count, peer, send, recv):
        def step(k):
            remote(slots.at[mine], slots.at[mine], send.at[k], recv.at[k], peer(k)).wait()

        far_first(count, step)

    def total(slots):
        if slots.shape[0] <= 32:
            value = slots[0]
            for i in range(1, slots.shape[0]):
                value = value + slots[i]
            return value
        return lax.fori_loop(1, slots.shape[0], lambda i, v: v + slots[i], slots[0])

    loads[8].wait()
    loads[9].wait()
    row_r, lane_r = iota((rpc, LANES), 0), iota((rpc, LANES), 1)
    tile_of, image_of = row_r // n_img, row_r % n_img
    count_here = jnp.int32(0)
    side_of = jnp.zeros((rpc, LANES), jnp.int32)
    for b in range(n_img):
        count_here = count_here + side[b] * side[b]
        side_of = jnp.where(image_of == b, side[b], side_of)
    pixel_of = tile_of * LANES + lane_r
    mask_raw[...] = jnp.where((pixel_of // SIDE < side_of) & (pixel_of % SIDE < side_of), 1.0, 0.0)
    mask_of = mask_raw[...]
    n_rows = feat.shape[0]

    def halves(v):
        while v.shape[0] > 8:
            n = v.shape[0] // 2
            v = v[0:n] + v[n:]
        return v

    sub = iota((8, LANES), 0)

    def fold(values):
        for d in (4, 2, 1):
            half_n = len(values) // 2
            values = [
                jnp.where((sub & d) == 0, u + pltpu.roll(u, 8 - d, 0), v + pltpu.roll(v, d, 0))
                for u, v in zip(values[:half_n], values[half_n:])
            ]
        return values[0]

    def first_sums(g, c, n=8):
        s, q = [], []
        for k in range(n):
            v = feat[pl.ds(pl.multiple_of((g * 8 + k) * rpc, rpc), rpc), :].astype(F32)
            w = v * mask_of
            s.append(halves(w))
            q.append(halves(w * v))
        none = [jnp.zeros((8, LANES), F32)] * (8 - n)
        at = pl.ds(pl.multiple_of(g * 8, 8), 8)
        sum_a[at, :] = fold(s + none)
        sum_b[at, :] = fold(q + none)
        return c

    whole, done = n_c // 8, 0
    for k, groups in enumerate(feat_groups):
        feat_parts[k].wait()
        lax.fori_loop(done, min(done + groups, whole), first_sums, 0)
        done += groups
    if n_c % 8:
        first_sums(whole, 0, n_c % 8)
    spare = pl.ds(pad_to(n_c, 8), cp - pad_to(n_c, 8))
    sum_a[spare, :] = jnp.zeros((cp - pad_to(n_c, 8), LANES), F32)
    sum_b[spare, :] = jnp.zeros((cp - pad_to(n_c, 8), LANES), F32)
    lane1 = iota((1, LANES), 1)
    s0, sq0 = as_rows(sum_a[...], c_sizes), as_rows(sum_b[...], c_sizes)
    ar1[dp, 0:1, :] = s0[0]
    ar1[dp, 1:2, :] = jnp.where(lane1 == LANES - 1, count_here.astype(F32), s0[1])
    ar1[dp, 2:3, :] = sq0[0]
    ar1[dp, 3:4, :] = sq0[1]

    new_slot = slot[slot.shape[0] - 1]
    per_device = n_c // grow
    slot_of = iota((rpc, LANES), 0) * 0 + new_slot
    loads[1].wait()
    graw[grow * rpc : 40 * rpc, :] = jnp.zeros(((40 - grow) * rpc, LANES), F32)
    picks = [jnp.where(slot_of == ch * per_device + i, mask_of, 0.0) for i in range(per_device)]

    def pick(i, c):
        v = jnp.zeros((rpc, LANES), F32)
        for k in range(per_device):
            v = v + cot[pl.ds(pl.multiple_of((k * grow + i) * rpc, rpc), rpc), :].astype(F32) * picks[k]
        graw[pl.ds(pl.multiple_of(i * rpc, rpc), rpc), :] = v
        return c

    lax.fori_loop(0, grow, pick, 0)

    pl.semaphore_wait(barrier, n_dev - 1)
    share_start(ar1, dp, n_dp, dp_peer, s1, r1)

    def by_image(q, first, second):
        def rows_of(b, t, o):
            return graw[pl.ds(o * rpc + t * n_img + b, 8, stride=rpc), :]

        for t in range(tiles):
            sl = slice(t * LANES, (t + 1) * LANES)
            for i, b in enumerate((first, second)):
                for h in range(2):
                    v = jnp.concatenate([rows_of(b, t, h * 16), rows_of(b, t, h * 16 + 8)], axis=0)
                    gsend[q, i * 32 + h * 16 : i * 32 + h * 16 + 16, sl] = v.astype(BF16)
            v = jnp.concatenate([rows_of(first, t, 32), rows_of(second, t, 32)], axis=0)
            gsend[q, 64:80, sl] = v.astype(BF16)

    by_image(0, sib, xs)
    g_sib = remote(gsend.at[0], gsx, sg.at[0], rg.at[0], {"chan": sib})
    g_sib.start()
    by_image(1, ch, xp)
    lane16 = iota((16, n_px), 1)
    row_of, col_of = lane16 >> 5, lane16 & (SIDE - 1)
    for b in range(n_img):
        mask[b] = jnp.where((row_of < side[b]) & (col_of < side[b]), 1.0, 0.0)

    out_x[pl.ds(n_rows, out_x.shape[0] - n_rows), :] = jnp.zeros((out_x.shape[0] - n_rows, LANES), F32)
    step_rows = 3 * rpc

    def widen(i, c):
        r = pl.ds(pl.multiple_of(i * step_rows, step_rows), step_rows)
        out_x[r, :] = feat[r, :].astype(F32)
        return c

    lax.fori_loop(0, n_rows // step_rows, widen, 0)

    g_sib.wait()
    gpair[...] = (gsend[1].astype(F32) + gsx[...].astype(F32)).astype(BF16)
    g_x = remote(gpair, grx, sg.at[1], rg.at[1], {"chan": xp})
    g_x.start()

    loads[7].wait()
    w2pad[...] = jnp.zeros(w2pad.shape, F32)
    w2wide[...] = jnp.zeros(w2wide.shape, F32)
    for t in range(9):
        w2pad[t, 0:grow, 0:grow] = w2v[t].astype(F32)
        tile, off = t * TAP // LANES, t * TAP % LANES
        v = pltpu.roll(w2pad[t], off, 1) if off else w2pad[t]
        lane = iota(v.shape, 1)
        here = slice(tile * LANES, (tile + 1) * LANES)
        w2wide[:, here] = w2wide[:, here] + jnp.where(lane >= off, v, 0.0)
        if off + grow > LANES:
            there = slice((tile + 1) * LANES, (tile + 2) * LANES)
            w2wide[:, there] = w2wide[:, there] + jnp.where(lane < off, v, 0.0)
    w2r[ch] = w2wide[...].astype(BF16)
    loads[5].wait()
    loads[6].wait()
    gsl[ch, 0:1, 0:grow] = gain2v[...]
    gsl[ch, 1:2, 0:grow] = bias2v[...]
    w_near = remote(w2r.at[ch], w2r.at[ch], sw.at[0], rw.at[0], {"chan": sib})
    w_far = remote(w2r.at[ch], w2r.at[ch], sw.at[1], rw.at[1], {"chan": xp})
    w_on = remote(w2r.at[xp], w2r.at[xp], sw.at[2], rw.at[2], {"chan": sib})
    w_far.start()
    w_near.start()
    share_start(gsl, ch, n_ch, ch_peer, sb, rb)

    loads[2].wait()
    w1s[...] = jnp.zeros(w1s.shape, BF16)
    w1s[0:n_d, 0:n_c] = w1v[...]
    rowbuf[...] = jnp.zeros(rowbuf.shape, F32)
    loads[3].wait()
    loads[4].wait()
    rowbuf[0:1, :] = gain1v[0:1, 0:LANES]
    rowbuf[1:2, 0 : n_c - LANES] = gain1v[0:1, LANES:n_c]
    rowbuf[2:3, :] = bias1v[0:1, 0:LANES]
    rowbuf[3:4, 0 : n_c - LANES] = bias1v[0:1, LANES:n_c]


    share_wait(ar1, dp, n_dp, dp_peer, s1, r1)
    tot1 = total(ar1)
    count = tot1[1:2, LANES - 1 : LANES]
    mean1, rstd1, scale1, keep1 = [], [], [], []
    for i in range(2):
        mean = tot1[i : i + 1] / count
        rstd = lax.rsqrt(tot1[2 + i : 3 + i] / count - mean * mean + EPS)
        here = lane1 + i * LANES
        ids = ch * n_c + here
        first = new_slot * grow
        keep = jnp.where(
            (here < n_c) & ((ids < first) | (ids >= first + grow)), 1.0, 0.0
        )
        scale = rstd * rowbuf[i : i + 1, :]
        shift = rowbuf[2 + i : 3 + i, :] - mean * scale
        size = c_sizes[i]
        r = pl.ds(i * LANES, size)
        col_a[r, :] = as_column(0.5 * scale * keep, size)
        col_b[r, :] = as_column(0.5 * shift * keep, size)
        mean1.append(mean)
        keep1.append(keep)
        rstd1.append(rstd)
        scale1.append(scale)

    def partial(j, first, n):
        def body(g, c):
            r = pl.ds(pl.multiple_of(g * 16, 16), 16)
            a, b = col_a[r, :], col_b[r, :]
            for t in range(first, first + n):
                sl = slice(t * LANES, (t + 1) * LANES)
                k = g * 16 * rpc + t * n_img + j
                v = jnp.concatenate([out_x[pl.ds(k + h * 8 * rpc, 8, stride=rpc), :] for h in range(2)], axis=0)
                xb[j, r, sl] = v.astype(BF16)
                v = v * a + b
                act[j, r, sl] = ((v * jnp.tanh(v) + v) * mask[j, :, sl]).astype(BF16)
            return c

        lax.fori_loop(0, cp // 16, body, 0)
        sl = slice(first * LANES, (first + n) * LANES)
        part[j, :, sl] = jnp.dot(w1s[...], act[j, :, sl], preferred_element_type=F32)

    rows_d = pl.ds(0, d8)
    unit = tiles // sum(SPANS)
    edges = [sum(SPANS[:p]) * unit for p in range(PIECES + 1)]

    def lanes_of(p):
        return pl.ds(edges[p] * LANES, (edges[p + 1] - edges[p]) * LANES)

    def tiles_of(p):
        return [slice(t * LANES, (t + 1) * LANES) for t in range(edges[p], edges[p + 1])]

    blocks, rest = d8 // 64, d8 // 64 * 64
    plain = blocks * 40

    def code(read, p, words, tops):
        top = jnp.maximum(jnp.max(row_top[...], axis=1, keepdims=True), 1e-30)
        tops[p, 0:1, :] = as_row(top[0:LANES])
        tops[p, 1:2, :] = as_row(top[LANES:d8])
        row_scale[...] = jnp.broadcast_to(LEVELS / top, (d8, LANES))

        def quantized(first, n, sl):
            r = pl.ds(pl.multiple_of(first, 8), n)
            return jnp.round(read(r, sl) * row_scale[r, :]).astype(jnp.int32)

        def block(i, c):
            for t, sl in enumerate(tiles_of(p), edges[p]):
                high = jnp.zeros((8, LANES), jnp.int32)
                for k in range(4):
                    first = quantized(i * 64 + k * 8, 8, sl)
                    second = quantized(i * 64 + 32 + k * 8, 8, sl)
                    words[t, pl.ds(pl.multiple_of(i * 40 + k * 8, 8), 8), :] = (first << 12) | (second & 0xFFF)
                    high = high | (((second >> 12) & 0xFF) << (8 * k))
                words[t, pl.ds(pl.multiple_of(i * 40 + 32, 8), 8), :] = high
            return c

        lax.fori_loop(0, blocks, block, 0)
        for t, sl in enumerate(tiles_of(p), edges[p]):
            words[t, plain : plain + d8 - rest, :] = quantized(rest, d8 - rest, sl)

    def unscale(tops, p):
        top = jnp.concatenate([as_column(tops[p, 0:1, :], LANES), as_column(tops[p, 1:2, :], d8 - LANES)], axis=0)
        row_scale[...] = top * (1.0 / LEVELS)

    def uncode(write, p, words):
        def put(first, n, sl, q):
            r = pl.ds(pl.multiple_of(first, 8), n)
            write(r, sl, q.astype(F32) * row_scale[r, :])

        def block(i, c):
            for t, sl in enumerate(tiles_of(p), edges[p]):
                high = words[t, pl.ds(pl.multiple_of(i * 40 + 32, 8), 8), :]
                for k in range(4):
                    low = words[t, pl.ds(pl.multiple_of(i * 40 + k * 8, 8), 8), :]
                    put(i * 64 + k * 8, 8, sl, low >> 12)
                    put(i * 64 + 32 + k * 8, 8, sl, (((high << (24 - 8 * k)) >> 24) << 12) | (low & 0xFFF))
            return c

        lax.fori_loop(0, blocks, block, 0)
        for t, sl in enumerate(tiles_of(p), edges[p]):
            put(rest, d8 - rest, sl, words[t, plain : plain + d8 - rest, :])

    def top_of(values):
        value = jnp.abs(values[0])
        for other in values[1:]:
            value = jnp.maximum(value, jnp.abs(other))
        return value

    def piece_of(j, p):
        partial(j, edges[p], edges[p + 1] - edges[p])

    def over(p):
        at = lanes_of(p)
        return remote(part.at[xs, rows_d, at], rx_a.at[rows_d, at], sp.at[p], rp.at[p], {"chan": sib})

    to_x = []
    piece_of(xs, 0)
    over(0).start()
    piece_of(xp, 0)
    for p in range(PIECES):
        if p + 1 < PIECES:
            piece_of(xs, p + 1)
            over(p + 1).start()
        over(p).wait()

        def add_a(g, c):
            r = pl.ds(pl.multiple_of(g * 8, 8), 8)
            values = [part[xp, r, sl] + rx_a[r, sl] for sl in tiles_of(p)]
            for sl, v in zip(tiles_of(p), values):
                part[xp, r, sl] = v
            row_top[r, :] = top_of(values)
            return c

        lax.fori_loop(0, d8 // 8, add_a, 0)
        code(lambda r, sl: part[xp, r, sl], p, px_out, tx_out)
        at = pl.ds(edges[p], edges[p + 1] - edges[p])
        copies = [
            remote(tx_out.at[p], tx_in.at[p], sq.at[0, p], rq.at[0, p], {"chan": xp}),
            remote(px_out.at[at], px_in.at[at], sq.at[1, p], rq.at[1, p], {"chan": xp}),
        ]
        for copy in copies:
            copy.start()
        to_x.append(copies)
        if p + 1 < PIECES:
            piece_of(xp, p + 1)
    for i in range(2):
        r = pl.ds(i * LANES, c_sizes[i])
        col_m[r, :] = as_column(mean1[i], c_sizes[i])
        col_k[r, :] = as_column(keep1[i], c_sizes[i])
    partial(sib, 0, tiles)
    to_sib_b = remote(part.at[sib, rows_d], rx_b.at[rows_d], sx.at[0], rxs.at[0], {"chan": sib})
    to_sib_b.start()
    partial(ch, 0, tiles)

    g_x.wait()
    px = iota((TAP, n_px), 1)
    py, pxx = px >> 5, px & (SIDE - 1)
    gcur[40:TAP, :] = jnp.zeros((TAP - 40, n_px), F32)
    for i in range(2):
        mine, theirs = slice(i * 32, i * 32 + 32), slice(32 - i * 32, 64 - i * 32)
        gcur[0:32, :] = gpair[mine, :].astype(F32) + grx[theirs, :].astype(F32)
        tails, others = gpair[64:80, :].astype(F32), grx[64:80, :].astype(F32)
        gcur[32:40, :] = tails[i * 8 : i * 8 + 8] + others[8 - i * 8 : 16 - i * 8]
        for ky in range(3):
            for kx in range(3):
                shift = (ky - 1) * SIDE + (kx - 1)
                t = ky * 3 + kx
                v = gcur[...]
                if shift != 0:
                    v = pltpu.roll(v, shift % n_px, 1)
                ok = None
                for off, pos in ((ky - 1, py), (kx - 1, pxx)):
                    if off == 1:
                        test = pos >= 1
                    elif off == -1:
                        test = pos <= SIDE - 2
                    else:
                        continue
                    ok = test if ok is None else ok & test
                if ok is not None:
                    v = jnp.where(ok, v, 0.0)
                g9[i, t * TAP : (t + 1) * TAP, :] = v.astype(BF16)
        g9[i, pl.ds(9 * TAP, TAPS - 9 * TAP), :] = jnp.zeros((TAPS - 9 * TAP, n_px), BF16)
    def slopes(j):
        def body(g, c):
            r = pl.ds(pl.multiple_of(g * 16, 16), 16)
            a, b = col_a[r, :], col_b[r, :]
            k = 0.5 * col_k[r, :]
            for t in range(tiles):
                sl = slice(t * LANES, (t + 1) * LANES)
                v = xb[j, r, sl].astype(F32) * a + b
                th = jnp.tanh(v)
                slope[j, r, sl] = ((1.0 + th) * (1.0 + v * (1.0 - th))) * (mask[j, :, sl] * k)
            return c

        lax.fori_loop(0, cp // 16, body, 0)

    slopes(xs)
    slopes(xp)

    to_sib_b.wait()
    sum_a[...] = jnp.zeros(sum_a.shape, F32)
    sum_b[...] = jnp.zeros(sum_b.shape, F32)
    hid[:, d8:dpad, :] = jnp.zeros((2, dpad - d8, n_px), F32)
    gp2[...] = jnp.zeros(gp2.shape, F32)

    def across(p):
        at = pl.ds(edges[p], edges[p + 1] - edges[p])
        return [
            remote(th_out.at[p], th_in.at[p], sh.at[0, p], rh.at[0, p], {"chan": xp}),
            remote(ph_out.at[at], ph_in.at[at], sh.at[1, p], rh.at[1, p], {"chan": xp}),
        ]

    def start_across(p):
        for copy in across(p):
            copy.start()

    for p in range(PIECES):
        for copy in to_x[p]:
            copy.wait()
        unscale(tx_in, p)

        def gather(r, sl, v):
            hid[0, r, sl] = (part[ch, r, sl] + rx_b[r, sl]) + v

        uncode(gather, p, px_in)

        def sums(g, c):
            r = pl.ds(pl.multiple_of(g * 8, 8), 8)
            s_acc, q_acc = sum_a[r, :], sum_b[r, :]
            values = [hid[0, r, sl] for sl in tiles_of(p)]
            for v in values:
                s_acc = s_acc + v
                q_acc = q_acc + v * v
            sum_a[r, :] = s_acc
            sum_b[r, :] = q_acc
            tops_h[p, r, :] = top_of(values)
            return c

        lax.fori_loop(0, d8 // 8, sums, 0)
        if p < AHEAD:
            row_top[...] = tops_h[p]
            code(lambda r, sl: hid[0, r, sl], p, ph_out, th_out)
            start_across(p)

    def pack(slots):
        s, q = as_rows(sum_a[0:d8, :], d_sizes), as_rows(sum_b[0:d8, :], d_sizes)
        slots[me, 0:1, :] = s[0]
        slots[me, 1:2, :] = s[1]
        slots[me, 2:3, :] = q[0]
        slots[me, 3:4, :] = q[1]

    def columns_d(row0, row1):
        tail = jnp.zeros((dpad - d8, LANES), F32)
        return jnp.concatenate(
            [as_column(row0, LANES), as_column(row1, d8 - LANES), tail], axis=0
        )

    pack(ar2)
    share_start(ar2, me, n_dev, dev_peer, s2, r2)
    for p in range(AHEAD, PIECES):
        row_top[...] = tops_h[p]
        code(lambda r, sl: hid[0, r, sl], p, ph_out, th_out)
        start_across(p)

    w_far.wait()
    w_on.start()
    slopes(sib)
    slopes(ch)
    w_near.wait()
    w_on.wait()
    share_wait(gsl, ch, n_ch, ch_peer, sb, rb)
    acc = jnp.zeros((dpad, w2b.shape[1]), F32)
    for j in range(n_ch):
        rows = iota((dpad, TAP), 0)
        cols = iota((dpad, TAP), 1)
        place = jnp.where((rows == cols + j * grow) & (cols < grow), 1.0, 0.0).astype(BF16)
        acc = acc + jnp.dot(place, w2r[j], preferred_element_type=F32)
    w2b[...] = acc.astype(BF16)
    for i in range(2):
        back[i] = jnp.dot(w2b[...], g9[i], preferred_element_type=F32)
    rows = iota((dpad, LANES), 0)
    cols = iota((dpad, LANES), 1)
    gain2c = jnp.zeros((dpad, 1), F32)
    bias2c = jnp.zeros((dpad, 1), F32)
    for j in range(n_ch):
        place = (rows == cols + j * grow) & (cols < grow)
        gain2c = gain2c + jnp.sum(jnp.where(place, gsl[j, 0:1, :], 0.0), axis=1, keepdims=True)
        bias2c = bias2c + jnp.sum(jnp.where(place, gsl[j, 1:2, :], 0.0), axis=1, keepdims=True)
    col_c[0] = jnp.broadcast_to(gain2c, (dpad, LANES))
    col_c[1] = jnp.broadcast_to(bias2c, (dpad, LANES))

    def widen_cot(i, c):
        r = pl.ds(pl.multiple_of(i * step_rows, step_rows), step_rows)
        k = [jnp.broadcast_to(col_k[pl.ds(i * 3 + n, 1), :], (rpc, LANES)) for n in range(3)]
        base[r, :] = cot[r, :].astype(F32) * jnp.concatenate(k, axis=0)
        return c

    lax.fori_loop(0, n_rows // step_rows, widen_cot, 0)

    share_wait(ar2, me, n_dev, dev_peer, s2, r2)
    tot2 = total(ar2)
    mean2 = [tot2[i : i + 1] / count for i in range(2)]
    rstd2 = [lax.rsqrt(tot2[2 + i : 3 + i] / count - mean2[i] * mean2[i] + EPS) for i in range(2)]
    mean2c = columns_d(*mean2)
    rstd2c = columns_d(*rstd2)
    scale2c = rstd2c * col_c[0]
    col_c[2] = mean2c
    col_c[3] = rstd2c
    col_c[4] = scale2c
    col_c[5] = 0.5 * scale2c
    col_c[6] = 0.5 * (col_c[1] - mean2c * scale2c)

    def second(g, c):
        r = pl.ds(pl.multiple_of(g * 16, 16), 16)
        a, b, m = col_c[5, r, :], col_c[6, r, :], col_c[2, r, :]
        s_acc = jnp.zeros((16, LANES), F32)
        q_acc = jnp.zeros((16, LANES), F32)
        for t in range(tiles):
            sl = slice(t * LANES, (t + 1) * LANES)
            h = hid[0, r, sl]
            mk = mask[ch, :, sl]
            v = h * a + b
            th = jnp.tanh(v)
            act2[r, sl] = ((v * th + v) * mk).astype(BF16)
            gp = (0.5 * mk) * ((1.0 + th) * (1.0 + v * (1.0 - th))) * back[0, r, sl]
            gp2[0, r, sl] = gp
            s_acc = s_acc + gp
            q_acc = q_acc + gp * (h - m)
        sum_a[r, :] = s_acc
        sum_b[r, :] = q_acc
        return c

    lax.fori_loop(0, dpad // 16, second, 0)
    pack(ar3)
    share_start(ar3, me, n_dev, dev_peer, s3, r3)

    w2acc[...] = lax.dot_general(
        act2[...], g9[0], (((1,), (1,)), ((), ())), preferred_element_type=F32
    )
    for j in range(n_ch):
        for lt in range(4):
            sl = slice(lt * LANES, (lt + 1) * LANES)
            cw[j, lt * 32 : lt * 32 + 32, :] = w2acc[j * grow : j * grow + 32, sl]
            cw[j, 128 + lt : 129 + lt, :] = w2acc[j * grow + 32 : j * grow + 33, sl]
        cw[j, 132:136, :] = jnp.zeros((4, LANES), F32)
    w_sib = [
        remote(cw.at[xs], cwr.at[1], sc.at[0], rc.at[0], {"chan": sib}),
        remote(cw.at[sib], cwr.at[0], sc.at[1], rc.at[1], {"chan": sib}),
    ]
    for copy in w_sib:
        copy.start()

    def second_other(p):
        for copy in across(p):
            copy.wait()
        unscale(th_in, p)

        def keep_hidden(r, sl, v):
            hid[1, r, sl] = v

        uncode(keep_hidden, p, ph_in)

        def body(g, c):
            r = pl.ds(pl.multiple_of(g * 16, 16), 16)
            a, b = col_c[5, r, :], col_c[6, r, :]
            for sl in tiles_of(p):
                v = hid[1, r, sl] * a + b
                th = jnp.tanh(v)
                gp2[1, r, sl] = (
                    (0.5 * mask[xp, :, sl]) * ((1.0 + th) * (1.0 + v * (1.0 - th))) * back[1, r, sl]
                )
            return c

        lax.fori_loop(0, dpad // 16, body, 0)

    zbuf[...] = lax.dot_general(
        w2b[...], act2[...], (((0,), (0,)), ((), ())), preferred_element_type=F32
    )
    new = jnp.zeros((TAP, n_px), F32)
    for ky in range(3):
        for kx in range(3):
            shift = (ky - 1) * SIDE + (kx - 1)
            t = ky * 3 + kx
            v = zbuf[t * TAP : (t + 1) * TAP, :]
            if shift != 0:
                v = pltpu.roll(v, (-shift) % n_px, 1)
            ok = None
            for off, pos in ((ky - 1, py), (kx - 1, pxx)):
                if off == -1:
                    test = pos >= 1
                elif off == 1:
                    test = pos <= SIDE - 2
                else:
                    continue
                ok = test if ok is None else ok & test
            if ok is not None:
                v = jnp.where(ok, v, 0.0)
            new = new + v
    new = new * jnp.concatenate([mask[ch]] * (TAP // 16), axis=0)
    gall[ch] = new[0 : gall.shape[1]]
    for copy in w_sib:
        copy.wait()
    cw[xp] = cw[xp] + cwr[1]
    cw[ch] = cw[ch] + cwr[0]
    w_x = remote(cw.at[xp], cwx, sc.at[2], rc.at[2], {"chan": xp})
    w_x.start()
    new_sib = remote(gall.at[ch], gall.at[ch], so.at[0], ro.at[0], {"chan": sib})
    new_xp = remote(gall.at[ch], gall.at[ch], so.at[1], ro.at[1], {"chan": xp})
    new_on = remote(gall.at[xp], gall.at[xp], so.at[2], ro.at[2], {"chan": sib})
    new_xp.start()
    new_sib.start()
    for p in range(PIECES):
        second_other(p)

    share_wait(ar3, me, n_dev, dev_peer, s3, r3)
    tot3 = total(ar3)
    gain_sum2 = [tot3[2 + i : 3 + i] * rstd2[i] for i in range(2)]
    bias_sum2 = [tot3[i : i + 1] for i in range(2)]
    gain_sum2c = columns_d(*gain_sum2)
    bias_sum2c = columns_d(*bias_sum2)
    col_c[7] = col_c[4] * bias_sum2c / count
    col_c[8] = col_c[4] * col_c[3] * gain_sum2c / count

    def third(i, j, k):
        def body(g, c):
            r = pl.ds(pl.multiple_of(g * 16, 16), 16)
            c1, c2, c3, m = col_c[4, r, :], col_c[7, r, :], col_c[8, r, :], col_c[2, r, :]
            for sl in [slice(t * LANES, (t + 1) * LANES) for t in range(k * tiles // 2, (k + 1) * tiles // 2)]:
                gha[j, r, sl] = (
                    c1 * gp2[i, r, sl] - mask[j, :, sl] * (c2 + c3 * (hid[i, r, sl] - m))
                ).astype(BF16)
            return c

        lax.fori_loop(0, dpad // 16, body, 0)

    grads = []
    for i, j in ((0, ch), (1, xp)):
        for k in range(2):
            third(i, j, k)
            at = pl.ds(k * (n_px // 2), n_px // 2)
            copy = remote(gha.at[j, :, at], gha.at[j, :, at], st.at[i, k], rt.at[i, k], {"chan": sib})
            copy.start()
            grads.append(copy)
    d_rows, d_cols = iota((dpad, LANES), 0), iota((dpad, LANES), 1)
    here_d = (d_rows == d_cols + ch * grow) & (d_cols < grow)
    out_g2[...] = jnp.sum(jnp.where(here_d, gain_sum2c, 0.0), axis=0, keepdims=True)[:, 0:grow]
    out_b2[...] = jnp.sum(jnp.where(here_d, bias_sum2c, 0.0), axis=0, keepdims=True)[:, 0:grow]

    w1acc[...] = jnp.zeros(w1acc.shape, F32)
    sum_a[...] = jnp.zeros(sum_a.shape, F32)
    sum_b[...] = jnp.zeros(sum_b.shape, F32)

    def weight_grad(j, k=None):
        at = slice(0, n_px) if k is None else slice(k * (n_px // 2), (k + 1) * (n_px // 2))
        w1acc[0:dpad, 0:cp] = w1acc[0:dpad, 0:cp] + lax.dot_general(
            gha[j, :, at], act[j, :, at], (((1,), (1,)), ((), ())), preferred_element_type=F32
        )

    def input_grad(j):
        gact[...] = lax.dot_general(
            w1s[...], gha[j], (((0,), (0,)), ((), ())), preferred_element_type=F32
        )

        def body(g, c):
            r = pl.ds(pl.multiple_of(g * 16, 16), 16)
            m = col_m[r, :]
            s_acc, q_acc = sum_a[r, :], sum_b[r, :]
            for t in range(tiles):
                sl = slice(t * LANES, (t + 1) * LANES)
                gp = gact[r, sl] * slope[j, r, sl]
                gp1[j, r, sl] = gp
                s_acc = s_acc + gp
                q_acc = q_acc + gp * (xb[j, r, sl].astype(F32) - m)
            sum_a[r, :] = s_acc
            sum_b[r, :] = q_acc
            return c

        lax.fori_loop(0, cp // 16, body, 0)

    weight_grad(ch)
    weight_grad(xp)
    w_x.wait()
    for i, j in ((0, sib), (1, xs)):
        for k in range(2):
            grads[2 * i + k].wait()
            weight_grad(j, k)

    for r in range(17):
        cb[r // 5, r % 5 * 8 : r % 5 * 8 + 8, :] = w1acc[r * 8 : r * 8 + 8, 0:LANES]
    for k in range(6):
        v = w1acc[k * 8 : k * 8 + 8, LANES : 2 * LANES]
        for i in range(1, 3):
            v = v + pltpu.roll(w1acc[i * 48 + k * 8 : i * 48 + k * 8 + 8, LANES : 2 * LANES], 40 * i, 1)
        r = 17 + k
        cb[r // 5, r % 5 * 8 : r % 5 * 8 + 8, :] = v
    for k in range(17):
        r = 23 + k
        cb[r // 5, r % 5 * 8 : r % 5 * 8 + 8, :] = cw[ch, k * 8 : k * 8 + 8, :] + cwx[k * 8 : k * 8 + 8, :]

    def encode(v):
        top = jnp.maximum(jnp.max(jnp.abs(v), axis=0, keepdims=True), 1e-30)
        power = jnp.floor(jnp.log2(top) + 1.0001)
        q = jnp.clip(jnp.round(v * jnp.exp2(15.0 - power)), -32767.0, 32767.0).astype(jnp.int32)
        low = jnp.concatenate([q[24:40], jnp.broadcast_to(power.astype(jnp.int32), (8, LANES))], axis=0)
        return (q[0:24] << 16) | (low & 0xFFFF)

    def decode(w):
        high, low = w >> 16, (w << 16) >> 16
        scale = jnp.exp2(low[16:24].astype(F32) - 15.0)
        q = jnp.concatenate([high, low[0:16]], axis=0).astype(F32)
        return q * jnp.concatenate([scale] * 5, axis=0)

    for q in range(OWNERS):
        coded[q] = encode(cb[q])
    stride = n_dp // OWNERS
    my_part = dp // stride
    is_owner = lax.rem(dp, stride) == 0

    def part_to(k):
        q = my_part ^ (OWNERS - 1 - k)
        return q, q * stride

    def push(k, c):
        q, to = part_to(k)

        @pl.when(to != dp)
        def _():
            remote(coded.at[q], rsl.at[dp], sr.at[k], rr.at[dp], {"dp": to}).start()

        return c

    lax.fori_loop(0, OWNERS, push, 0)
    for j in (ch, xp, sib, xs):
        input_grad(j)
    s4_, q4_ = as_rows(sum_a[...], c_sizes), as_rows(sum_b[...], c_sizes)
    for i in range(2):
        ar4[dp, i : i + 1, :] = s4_[i]
        ar4[dp, 2 + i : 3 + i, :] = q4_[i]
    share_start(ar4, dp, n_dp, dp_peer, s4, r4)
    new_xp.wait()
    new_on.start()

    def scatter(g, c):
        first = g * 16 * rpc
        r = pl.ds(pl.multiple_of(g * 16, 16), 16)
        for b in range(n_img):
            for t in range(tiles):
                v = gp1[b, r, t * LANES : (t + 1) * LANES]
                for h in range(2):
                    at = pl.ds(first + h * 8 * rpc + t * n_img + b, 8, stride=rpc)
                    out_g[at, :] = v[h * 8 : h * 8 + 8]
        return c

    lax.fori_loop(0, 5, scatter, 0)

    def push_wait(k, c):
        q, to = part_to(k)

        @pl.when(to != dp)
        def _():
            remote(coded.at[q], rsl.at[dp], sr.at[k], rr.at[dp], {"dp": to}).wait_send()

        return c

    def pull(k, c):
        src = lax.rem(dp + k, n_dp)
        remote(coded.at[0], rsl.at[src], sr.at[0], rr.at[src], {"dp": src}).wait_recv()
        return c

    @pl.when(is_owner)
    def _():
        lax.fori_loop(1, n_dp, pull, 0)
        v = cb[my_part]
        for k in range(1, n_dp):
            v = v + decode(rsl[lax.rem(dp + k, n_dp)])
        fin[my_part] = encode(v)

        def give(k):
            remote(fin.at[my_part], fin.at[my_part], sa.at[k], ra.at[my_part], dp_peer(k)).start()

        far_first(n_dp, give)

    lax.fori_loop(0, OWNERS, push_wait, 0)
    lax.fori_loop(5, cp // 16, scatter, 0)

    for i in range(2):
        col_a[pl.ds(i * LANES, c_sizes[i]), :] = as_column(scale1[i], c_sizes[i])

    new_sib.wait()
    new_on.wait()
    for b in range(n_img):
        for t in range(tiles):
            for h in range(gall.shape[1] // 8):
                out_new[pl.ds(h * 8 * rpc + t * n_img + b, 8, stride=rpc), :] = gall[
                    b, h * 8 : h * 8 + 8, t * LANES : (t + 1) * LANES
                ]
    out_slot[...] = (slot_of - ch * per_device)[0:8].astype(F32)

    share_wait(ar4, dp, n_dp, dp_peer, s4, r4)
    tot4 = total(ar4)
    for i in range(2):
        bias_sum = tot4[i : i + 1]
        gain_sum = tot4[2 + i : 3 + i] * rstd1[i]
        size = c_sizes[i]
        r = pl.ds(i * LANES, size)
        k1 = -scale1[i] * rstd1[i] * gain_sum / count
        k0 = -scale1[i] * bias_sum / count - k1 * mean1[i]
        col_b[r, :] = as_column(k0, size)
        col_m[r, :] = as_column(k1, size)
        width = min(LANES, n_c - i * LANES)
        out_g1[0:1, i * LANES : i * LANES + width] = gain_sum[:, 0:width]
        out_b1[0:1, i * LANES : i * LANES + width] = bias_sum[:, 0:width]
    mask_of = mask_raw[...]

    def last(i, c):
        for k in range(5):
            row = i * 5 + k
            at = pl.ds(pl.multiple_of(row * rpc, rpc), rpc)
            k0 = jnp.broadcast_to(col_b[pl.ds(row, 1), :], (rpc, LANES))
            k1 = jnp.broadcast_to(col_m[pl.ds(row, 1), :], (rpc, LANES))
            a = jnp.broadcast_to(col_a[pl.ds(row, 1), :], (rpc, LANES))
            out_g[at, :] = base[at, :] + a * out_g[at, :] + mask_of * (k0 + k1 * out_x[at, :])
        return c

    lax.fori_loop(0, n_c // 5, last, 0)

    @pl.when(is_owner)
    def _():
        def gave(k, c):
            remote(fin.at[my_part], fin.at[my_part], sa.at[k], ra.at[my_part], dp_peer(k)).wait_send()
            return c

        lax.fori_loop(1, n_dp, gave, 0)

    def take(q, c):
        @pl.when(q * stride != dp)
        def _():
            remote(fin.at[q], fin.at[q], sa.at[0], ra.at[q], {"dp": q * stride}).wait_recv()

        return c

    lax.fori_loop(0, OWNERS, take, 0)
    for q in range(OWNERS):
        cb[q] = decode(fin[q])
    for r in range(17):
        height = min(8, n_d - r * 8)
        out_w1[r * 8 : r * 8 + height, 0:LANES] = cb[r // 5, r % 5 * 8 : r % 5 * 8 + height, :]
    for k in range(6):
        r = 17 + k
        v = cb[r // 5, r % 5 * 8 : r % 5 * 8 + 8, :]
        for i in range(3):
            row = i * 48 + k * 8
            height = min(8, n_d - row)
            if height > 0:
                u = v if i == 0 else pltpu.roll(v, LANES - 40 * i, 1)
                out_w1[row : row + height, LANES:n_c] = u[0:height, 0 : n_c - LANES]
    for k in range(17):
        r = 23 + k
        v = cb[r // 5, r % 5 * 8 : r % 5 * 8 + 8, :]
        if k < 16:
            w2acc[k % 4 * 8 : k % 4 * 8 + 8, k // 4 * LANES : (k // 4 + 1) * LANES] = v
        else:
            for lt in range(4):
                w2acc[32:33, lt * LANES : (lt + 1) * LANES] = v[lt : lt + 1]
    v = w2acc[0:40, :]
    for t in range(9):
        u = v if t == 0 else pltpu.roll(v, TAPS - t * TAP, 1)
        out_w2[t] = u[0:grow, 0:grow]


def finish(n_rows, grow_rows, *refs):
    n = (len(refs) - 3) // 2
    new, slot = refs[n : n + 2]
    outs, sem = refs[n + 2 : -1], refs[-1]
    segments = n_rows // grow_rows
    copies = [pltpu.make_async_copy(refs[1].at[pl.ds(0, n_rows)], outs[1], sem.at[1])]
    copies += [pltpu.make_async_copy(refs[i], outs[i], sem.at[i]) for i in range(2, n)]
    for copy in copies:
        copy.start()
    here = jnp.max(slot[...])
    for k in range(segments):
        at = pl.ds(k * grow_rows, grow_rows)
        kept = pltpu.make_async_copy(refs[0].at[at], outs[0].at[at], sem.at[n + k])
        grown = pltpu.make_async_copy(new.at[pl.ds(0, grow_rows)], outs[0].at[at], sem.at[n + k])
        pl.when(here == k)(grown.start)
        pl.when(here != k)(kept.start)
        copies.append(kept)
    for copy in copies:
        copy.wait()


def flat(values):
    n, c, p = values.shape
    return (
        values.transpose(1, 0, 2).reshape(c, n, p // LANES, LANES).transpose(0, 2, 1, 3).reshape(-1, LANES)
    )


def unflat(rows, n, c, p):
    return rows.reshape(c, p // LANES, n, LANES).transpose(0, 2, 1, 3).reshape(c, n, p).transpose(1, 0, 2)


def on_device(
    n_dp, n_ch, features, gain1, bias1, weight1, gain2, bias2, weight2, cotangent, image_side, block_slot
):
    n_img, n_c, n_px = features.shape
    n_d = weight1.shape[1]
    grow = weight2.shape[3]
    cp = pad_to(n_c, 16)
    dpad = pad_to(n_d, 16)
    d8 = pad_to(n_d, 8)
    rpc = n_px // LANES * n_img
    n_rows, n_pad = n_c * rpc, cp * rpc
    n_dev = n_dp * n_ch
    words = d8 // 64 * 40 + d8 % 64
    cfg = (n_dp, n_ch, n_img, n_c, n_px, n_d, grow)
    args = (
        flat(features),
        flat(cotangent),
        weight1.T,
        gain1.reshape(1, -1),
        bias1.reshape(1, -1),
        gain2.reshape(1, -1),
        bias2.reshape(1, -1),
        weight2.reshape(9, grow, grow),
        image_side,
        block_slot,
    )
    args = [pltpu.with_memory_space_constraint(v, pltpu.HBM) for v in args]
    sd = jax.ShapeDtypeStruct
    in_vmem = pl.BlockSpec(memory_space=pltpu.VMEM)
    in_hbm = pl.BlockSpec(memory_space=pltpu.HBM)
    dma = pltpu.SemaphoreType.DMA
    v = pltpu.VMEM
    scratch = [
        v((n_rows, LANES), BF16), v((n_rows, LANES), BF16), v((n_d, n_c), BF16),
        v((1, n_c), F32), v((1, n_c), F32), v((1, grow), F32), v((1, grow), F32),
        v((9, grow, grow), BF16), pltpu.SMEM(image_side.shape, jnp.int32), pltpu.SMEM(block_slot.shape, jnp.int32),
        v((n_img, 16, n_px), F32), v((rpc, LANES), F32), v((n_rows, LANES), F32),
        v((n_img, cp, n_px), BF16), v((n_img, cp, n_px), BF16),
        v((n_img, cp, n_px), F32), v((n_img, cp, n_px), F32), v((cp, n_px), F32),
        v((cp, LANES), F32), v((cp, LANES), F32), v((cp, LANES), F32), v((cp, LANES), F32),
        v((9, dpad, LANES), F32), v((cp, LANES), F32), v((cp, LANES), F32),
        v((8, LANES), F32),
        v((dpad, cp), BF16), v((n_img, dpad, n_px), F32),
        v((dpad, n_px), F32), v((dpad, n_px), F32), v((2, dpad, n_px), F32),
        v((d8, LANES), F32), v((d8, LANES), F32), v((PIECES, d8, LANES), F32),
        v((n_px // LANES, words, LANES), jnp.int32), v((n_px // LANES, words, LANES), jnp.int32), v((PIECES, 2, LANES), F32), v((PIECES, 2, LANES), F32),
        v((n_px // LANES, words, LANES), jnp.int32), v((n_px // LANES, words, LANES), jnp.int32), v((PIECES, 2, LANES), F32), v((PIECES, 2, LANES), F32),
        v((40 * rpc, LANES), F32), v((2, 80, n_px), BF16),
        v((80, n_px), BF16), v((80, n_px), BF16), v((80, n_px), BF16), v((TAP, n_px), F32),
        v((2, TAPS, n_px), BF16), v((9, TAP, LANES), F32), v((TAP, TAPS), F32), v((n_ch, TAP, TAPS), BF16), v((dpad, TAPS), BF16),
        v((n_ch, 2, LANES), F32),
        v((dpad, n_px), BF16), v((2, dpad, n_px), F32), v((2, dpad, n_px), F32), v((TAPS, n_px), F32),
        v((n_ch, 40, n_px), F32), v((n_ch, dpad, n_px), BF16),
        v((n_ch, 136, LANES), F32), v((2, 136, LANES), F32), v((136, LANES), F32),
        v((OWNERS, 40, LANES), F32), v((OWNERS, 24, LANES), jnp.int32),
        v((n_dp, 24, LANES), jnp.int32), v((OWNERS, 24, LANES), jnp.int32), v((dpad, 256), F32), v((dpad, TAPS), F32),
        v((n_dp, 4, LANES), F32), v((n_dev, 4, LANES), F32), v((n_dev, 4, LANES), F32), v((n_dp, 4, LANES), F32),
        dma((13,)),
        dma((n_dp,)), dma((n_dp,)), dma((n_dev,)), dma((n_dev,)), dma((n_dev,)), dma((n_dev,)), dma((n_dp,)), dma((n_dp,)),
        dma((3,)), dma((3,)), dma((PIECES,)), dma((PIECES,)), dma((2, PIECES)), dma((2, PIECES)),
        dma((2,)), dma((2,)), dma((n_ch,)), dma((n_ch,)), dma((n_ch,)), dma((n_ch,)),
        dma((2, PIECES)), dma((2, PIECES)), dma((2, 2)), dma((2, 2)), dma((3,)), dma((3,)), dma((3,)), dma((3,)),
        dma((OWNERS,)), dma((n_dp,)), dma((n_dp,)), dma((OWNERS,)),
    ]
    out_shape = (
        sd((n_pad, LANES), F32), sd((n_pad, LANES), F32), sd((n_d, n_c), F32),
        sd((1, n_c), F32), sd((1, n_c), F32), sd((9, grow, grow), F32), sd((1, grow), F32), sd((1, grow), F32),
        sd((40 * rpc, LANES), F32), sd((8, LANES), F32),
    )
    outs = pl.pallas_call(
        functools.partial(layer, cfg),
        out_shape=out_shape,
        in_specs=[in_hbm] * len(args),
        out_specs=(in_vmem,) * len(out_shape),
        scratch_shapes=scratch,
        compiler_params=pltpu.CompilerParams(
            collective_id=0, has_side_effects=True, vmem_limit_bytes=40 << 20
        ),
    )(*args)
    final = (sd((n_rows, LANES), F32),) * 2 + out_shape[2:-2]
    o = pl.pallas_call(
        functools.partial(finish, n_rows, grow * rpc),
        out_shape=final,
        in_specs=[in_vmem] * len(outs),
        out_specs=(in_hbm,) * len(final),
        scratch_shapes=[dma((len(final) + n_c // grow,))],
        compiler_params=pltpu.CompilerParams(vmem_limit_bytes=8 << 20),
    )(*outs)
    return (
        unflat(o[0], n_img, n_c, n_px),
        unflat(o[1], n_img, n_c, n_px),
        o[2].T,
        o[3].reshape(-1),
        o[4].reshape(-1),
        o[5].reshape(3, 3, grow, grow),
        o[6].reshape(-1),
        o[7].reshape(-1),
    )


def solution(mesh):
    in_specs = (
        P("dp", "chan", None),
        P("chan"),
        P("chan"),
        P("chan", None),
        P("chan"),
        P("chan"),
        P(None, None, "chan", None),
        P("dp", "chan", None),
        P("dp"),
        P(),
    )
    out_specs = (
        P("dp", "chan", None),
        P("dp", "chan", None),
        P("chan", None),
        P("chan"),
        P("chan"),
        P(None, None, "chan", None),
        P("chan"),
        P("chan"),
    )
    body = functools.partial(on_device, mesh.shape["dp"], mesh.shape["chan"])
    return jax.shard_map(body, mesh=mesh, in_specs=in_specs, out_specs=out_specs, check_vma=False)
```

```python
import functools

import jax
import jax.numpy as jnp
from jax import lax
from jax.experimental import pallas as pl
from jax.experimental.pallas import tpu as pltpu
from jax.sharding import PartitionSpec as P

SIDE = 32
EPS = 1e-05
LANES = 128
TAP = 48
TAPS = 512
SPANS = (1, 2, 3, 2)
PIECES = len(SPANS)
AHEAD = 2
LEVELS = 524000.0
OWNERS = 8

MESH = pl.DeviceIdType.MESH
F32 = jnp.float32
BF16 = jnp.bfloat16


def pad_to(size, unit):
    return (size + unit - 1) // unit * unit


def iota(shape, axis):
    return lax.broadcasted_iota(jnp.int32, shape, axis)


def as_row(column):
    n = column.shape[0]
    eye = iota((n, LANES), 0) == iota((n, LANES), 1)
    return jnp.sum(jnp.where(eye, column, 0.0), axis=0, keepdims=True)


def as_column(row, n):
    eye = iota((n, LANES), 0) == iota((n, LANES), 1)
    return jnp.broadcast_to(jnp.sum(jnp.where(eye, row, 0.0), axis=1, keepdims=True), (n, LANES))


def as_rows(values, sizes):
    column = jnp.sum(values, axis=1, keepdims=True)
    rows, start = [], 0
    for size in sizes:
        rows.append(as_row(column[start : start + size]))
        start += size
    return rows


def layer(
    cfg,
    feat_h, cot_h, w1_h, gain1_h, bias1_h, gain2_h, bias2_h, w2_h, side_h, slot_h,
    out_x, out_g, out_w1, out_g1, out_b1, out_w2, out_g2, out_b2, out_new, out_slot,
    feat, cot, w1v, gain1v, bias1v, gain2v, bias2v, w2v, side, slot,
    mask, mask_raw, base, xb, act, slope, gp1, gact,
    col_a, col_b, col_m, col_k, col_c, sum_a, sum_b, rowbuf,
    w1s, part, rx_a, rx_b, hid, row_top, row_scale, tops_h,
    px_out, px_in, tx_out, tx_in, ph_out, ph_in, th_out, th_in,
    graw, gsend, gsx, gpair, grx, gcur, g9, w2pad, w2wide, w2r, w2b, gsl,
    act2, gp2, back, zbuf, gall, gha,
    cw, cwr, cwx, cb, coded, rsl, fin, w1acc, w2acc,
    ar1, ar2, ar3, ar4,
    load_sem, s1, r1, s2, r2, s3, r3, s4, r4, sx, rxs, sp, rp, sq, rq, sg, rg, sw, rw, sb, rb, sh, rh, st, rt, so, ro, sc, rc, sr, rr, sa, ra,
):
    n_dp, n_ch, n_img, n_c, n_px, n_d, grow = cfg
    n_dev = n_dp * n_ch
    cp = xb.shape[1]
    dpad = w1s.shape[0]
    d8 = pad_to(n_d, 8)
    tiles = n_px // LANES
    rpc = tiles * n_img
    c_sizes = (LANES, cp - LANES)
    d_sizes = (LANES, d8 - LANES)
    dp = lax.axis_index("dp")
    ch = lax.axis_index("chan")
    me = dp * n_ch + ch
    half = n_ch // 2
    cx, cc = ch // half, lax.rem(ch, half)
    sib = cx * half + (1 - cc)
    xp = (1 - cx) * half + cc
    xs = (1 - cx) * half + (1 - cc)

    def dev_peer(k):
        q = me ^ k
        return {"dp": q // n_ch, "chan": lax.rem(q, n_ch)}

    def dp_peer(k):
        return {"dp": dp ^ k}

    def ch_peer(k):
        return {"chan": ch ^ k}

    def far_first(count, step):
        if count <= 32:
            for k in range(count - 1, 0, -1):
                step(k)
        else:

            def body(i, c):
                step(count - 1 - i)
                return c

            lax.fori_loop(0, count - 1, body, 0)

    loads = {
        i: pltpu.make_async_copy(h, v, load_sem.at[i])
        for i, (h, v) in enumerate(
            (
                (cot_h, cot), (w1_h, w1v), (gain1_h, gain1v), (bias1_h, bias1v),
                (gain2_h, gain2v), (bias2_h, bias2v), (w2_h, w2v), (side_h, side), (slot_h, slot),
            ),
            1,
        )
    }
    feat_groups, feat_parts, start = [], [], 0
    for k in range(3):
        groups = pad_to(n_c, 8) // 8 * (k + 1) // 3 - sum(feat_groups)
        size = min(groups * 8, n_c - start) * rpc
        at = pl.ds(start * rpc, size)
        feat_parts.append(pltpu.make_async_copy(feat_h.at[at], feat.at[at], load_sem.at[10 + k]))
        feat_groups.append(groups)
        start += groups * 8
    for copy in [loads[8], loads[9], *feat_parts, *(loads[i] for i in range(1, 8))]:
        copy.start()
    barrier = pltpu.get_barrier_semaphore()

    def greet(k):
        pl.semaphore_signal(barrier, inc=1, device_id=dev_peer(k), device_id_type=MESH)

    far_first(n_dev, greet)

    def remote(src, dst, send, recv, device):
        return pltpu.make_async_remote_copy(
            src_ref=src, dst_ref=dst, send_sem=send, recv_sem=recv, device_id=device, device_id_type=MESH
        )

    still_sent = []

    def share_start(slots, mine, count, peer, send, recv):
        def step(k):
            remote(slots.at[mine], slots.at[mine], send.at[k], recv.at[k], peer(k)).start()

        far_first(count, step)

    def share_wait(slots, mine, count, peer, send, recv):
        def step(k):
            remote(slots.at[mine], slots.at[mine], send.at[k], recv.at[k], peer(k)).wait_recv()

        def sent(k):
            remote(slots.at[mine], slots.at[mine], send.at[k], recv.at[k], peer(k)).wait_send()

        far_first(count, step)
        still_sent.append(lambda: far_first(count, sent))

    def total(slots):
        if slots.shape[0] <= 32:
            value = slots[0]
            for i in range(1, slots.shape[0]):
                value = value + slots[i]
            return value
        return lax.fori_loop(1, slots.shape[0], lambda i, v: v + slots[i], slots[0])

    loads[8].wait()
    loads[9].wait()
    row_r, lane_r = iota((rpc, LANES), 0), iota((rpc, LANES), 1)
    tile_of, image_of = row_r // n_img, row_r % n_img
    count_here = jnp.int32(0)
    side_of = jnp.zeros((rpc, LANES), jnp.int32)
    for b in range(n_img):
        count_here = count_here + side[b] * side[b]
        side_of = jnp.where(image_of == b, side[b], side_of)
    pixel_of = tile_of * LANES + lane_r
    mask_raw[...] = jnp.where((pixel_of // SIDE < side_of) & (pixel_of % SIDE < side_of), 1.0, 0.0)
    mask_of = mask_raw[...]
    n_rows = feat.shape[0]

    def halves(v):
        while v.shape[0] > 8:
            n = v.shape[0] // 2
            v = v[0:n] + v[n:]
        return v

    sub = iota((8, LANES), 0)

    def fold(values):
        for d in (4, 2, 1):
            half_n = len(values) // 2
            values = [
                jnp.where((sub & d) == 0, u + pltpu.roll(u, 8 - d, 0), v + pltpu.roll(v, d, 0))
                for u, v in zip(values[:half_n], values[half_n:])
            ]
        return values[0]

    def first_sums(g, c, n=8):
        s, q = [], []
        for k in range(n):
            v = feat[pl.ds(pl.multiple_of((g * 8 + k) * rpc, rpc), rpc), :].astype(F32)
            w = v * mask_of
            s.append(halves(w))
            q.append(halves(w * v))
        none = [jnp.zeros((8, LANES), F32)] * (8 - n)
        at = pl.ds(pl.multiple_of(g * 8, 8), 8)
        sum_a[at, :] = fold(s + none)
        sum_b[at, :] = fold(q + none)
        return c

    whole, done = n_c // 8, 0
    for k, groups in enumerate(feat_groups):
        feat_parts[k].wait()
        lax.fori_loop(done, min(done + groups, whole), first_sums, 0)
        done += groups
    if n_c % 8:
        first_sums(whole, 0, n_c % 8)
    spare = pl.ds(pad_to(n_c, 8), cp - pad_to(n_c, 8))
    sum_a[spare, :] = jnp.zeros((cp - pad_to(n_c, 8), LANES), F32)
    sum_b[spare, :] = jnp.zeros((cp - pad_to(n_c, 8), LANES), F32)
    lane1 = iota((1, LANES), 1)
    s0, sq0 = as_rows(sum_a[...], c_sizes), as_rows(sum_b[...], c_sizes)
    ar1[dp, 0:1, :] = s0[0]
    ar1[dp, 1:2, :] = jnp.where(lane1 == LANES - 1, count_here.astype(F32), s0[1])
    ar1[dp, 2:3, :] = sq0[0]
    ar1[dp, 3:4, :] = sq0[1]

    new_slot = slot[slot.shape[0] - 1]
    per_device = n_c // grow
    slot_of = iota((rpc, LANES), 0) * 0 + new_slot
    loads[1].wait()
    graw[grow * rpc : 40 * rpc, :] = jnp.zeros(((40 - grow) * rpc, LANES), F32)
    picks = [jnp.where(slot_of == ch * per_device + i, mask_of, 0.0) for i in range(per_device)]

    def pick(i, c):
        v = jnp.zeros((rpc, LANES), F32)
        for k in range(per_device):
            v = v + cot[pl.ds(pl.multiple_of((k * grow + i) * rpc, rpc), rpc), :].astype(F32) * picks[k]
        graw[pl.ds(pl.multiple_of(i * rpc, rpc), rpc), :] = v
        return c

    lax.fori_loop(0, grow, pick, 0)

    pl.semaphore_wait(barrier, n_dev - 1)
    share_start(ar1, dp, n_dp, dp_peer, s1, r1)

    def by_image(q, first, second):
        def rows_of(b, t, o):
            return graw[pl.ds(o * rpc + t * n_img + b, 8, stride=rpc), :]

        for t in range(tiles):
            sl = slice(t * LANES, (t + 1) * LANES)
            for i, b in enumerate((first, second)):
                for h in range(2):
                    v = jnp.concatenate([rows_of(b, t, h * 16), rows_of(b, t, h * 16 + 8)], axis=0)
                    gsend[q, i * 32 + h * 16 : i * 32 + h * 16 + 16, sl] = v.astype(BF16)
            v = jnp.concatenate([rows_of(first, t, 32), rows_of(second, t, 32)], axis=0)
            gsend[q, 64:80, sl] = v.astype(BF16)

    by_image(0, sib, xs)
    g_sib = remote(gsend.at[0], gsx, sg.at[0], rg.at[0], {"chan": sib})
    g_sib.start()
    by_image(1, ch, xp)
    lane16 = iota((16, n_px), 1)
    row_of, col_of = lane16 >> 5, lane16 & (SIDE - 1)
    for b in range(n_img):
        mask[b] = jnp.where((row_of < side[b]) & (col_of < side[b]), 1.0, 0.0)

    out_x[pl.ds(n_rows, out_x.shape[0] - n_rows), :] = jnp.zeros((out_x.shape[0] - n_rows, LANES), F32)
    step_rows = 3 * rpc

    def widen(i, c):
        r = pl.ds(pl.multiple_of(i * step_rows, step_rows), step_rows)
        out_x[r, :] = feat[r, :].astype(F32)
        return c

    lax.fori_loop(0, n_rows // step_rows, widen, 0)

    g_sib.wait()
    gpair[...] = (gsend[1].astype(F32) + gsx[...].astype(F32)).astype(BF16)
    g_x = remote(gpair, grx, sg.at[1], rg.at[1], {"chan": xp})
    g_x.start()

    loads[7].wait()
    w2pad[...] = jnp.zeros(w2pad.shape, F32)
    w2wide[...] = jnp.zeros(w2wide.shape, F32)
    for t in range(9):
        w2pad[t, 0:grow, 0:grow] = w2v[t].astype(F32)
        tile, off = t * TAP // LANES, t * TAP % LANES
        v = pltpu.roll(w2pad[t], off, 1) if off else w2pad[t]
        lane = iota(v.shape, 1)
        here = slice(tile * LANES, (tile + 1) * LANES)
        w2wide[:, here] = w2wide[:, here] + jnp.where(lane >= off, v, 0.0)
        if off + grow > LANES:
            there = slice((tile + 1) * LANES, (tile + 2) * LANES)
            w2wide[:, there] = w2wide[:, there] + jnp.where(lane < off, v, 0.0)
    w2r[ch] = w2wide[...].astype(BF16)
    loads[5].wait()
    loads[6].wait()
    gsl[ch, 0:1, 0:grow] = gain2v[...]
    gsl[ch, 1:2, 0:grow] = bias2v[...]
    w_near = remote(w2r.at[ch], w2r.at[ch], sw.at[0], rw.at[0], {"chan": sib})
    w_far = remote(w2r.at[ch], w2r.at[ch], sw.at[1], rw.at[1], {"chan": xp})
    w_on = remote(w2r.at[xp], w2r.at[xp], sw.at[2], rw.at[2], {"chan": sib})
    w_far.start()
    w_near.start()
    share_start(gsl, ch, n_ch, ch_peer, sb, rb)

    loads[2].wait()
    w1s[...] = jnp.zeros(w1s.shape, BF16)
    w1s[0:n_d, 0:n_c] = w1v[...]
    rowbuf[...] = jnp.zeros(rowbuf.shape, F32)
    loads[3].wait()
    loads[4].wait()
    rowbuf[0:1, :] = gain1v[0:1, 0:LANES]
    rowbuf[1:2, 0 : n_c - LANES] = gain1v[0:1, LANES:n_c]
    rowbuf[2:3, :] = bias1v[0:1, 0:LANES]
    rowbuf[3:4, 0 : n_c - LANES] = bias1v[0:1, LANES:n_c]


    share_wait(ar1, dp, n_dp, dp_peer, s1, r1)
    tot1 = total(ar1)
    count = tot1[1:2, LANES - 1 : LANES]
    mean1, rstd1, scale1, keep1 = [], [], [], []
    for i in range(2):
        mean = tot1[i : i + 1] / count
        rstd = lax.rsqrt(tot1[2 + i : 3 + i] / count - mean * mean + EPS)
        here = lane1 + i * LANES
        ids = ch * n_c + here
        first = new_slot * grow
        keep = jnp.where(
            (here < n_c) & ((ids < first) | (ids >= first + grow)), 1.0, 0.0
        )
        scale = rstd * rowbuf[i : i + 1, :]
        shift = rowbuf[2 + i : 3 + i, :] - mean * scale
        size = c_sizes[i]
        r = pl.ds(i * LANES, size)
        col_a[r, :] = as_column(0.5 * scale * keep, size)
        col_b[r, :] = as_column(0.5 * shift * keep, size)
        mean1.append(mean)
        keep1.append(keep)
        rstd1.append(rstd)
        scale1.append(scale)

    def partial(j, first, n):
        def body(g, c):
            r = pl.ds(pl.multiple_of(g * 16, 16), 16)
            a, b = col_a[r, :], col_b[r, :]
            for t in range(first, first + n):
                sl = slice(t * LANES, (t + 1) * LANES)
                k = g * 16 * rpc + t * n_img + j
                v = jnp.concatenate([out_x[pl.ds(k + h * 8 * rpc, 8, stride=rpc), :] for h in range(2)], axis=0)
                xb[j, r, sl] = v.astype(BF16)
                v = v * a + b
                act[j, r, sl] = ((v * jnp.tanh(v) + v) * mask[j, :, sl]).astype(BF16)
            return c

        lax.fori_loop(0, cp // 16, body, 0)
        sl = slice(first * LANES, (first + n) * LANES)
        part[j, :, sl] = jnp.dot(w1s[...], act[j, :, sl], preferred_element_type=F32)

    rows_d = pl.ds(0, d8)
    unit = tiles // sum(SPANS)
    edges = [sum(SPANS[:p]) * unit for p in range(PIECES + 1)]

    def lanes_of(p):
        return pl.ds(edges[p] * LANES, (edges[p + 1] - edges[p]) * LANES)

    def tiles_of(p):
        return [slice(t * LANES, (t + 1) * LANES) for t in range(edges[p], edges[p + 1])]

    blocks, rest = d8 // 64, d8 // 64 * 64
    plain = blocks * 40

    def code(read, p, words, tops):
        top = jnp.maximum(jnp.max(row_top[...], axis=1, keepdims=True), 1e-30)
        row_scale[...] = jnp.broadcast_to(LEVELS / top, (d8, LANES))

        def quantized(first, n, sl):
            r = pl.ds(pl.multiple_of(first, 8), n)
            return jnp.round(read(r, sl) * row_scale[r, :]).astype(jnp.int32)

        def block(i, c):
            for t, sl in enumerate(tiles_of(p), edges[p]):
                high = jnp.zeros((8, LANES), jnp.int32)
                for k in range(4):
                    first = quantized(i * 64 + k * 8, 8, sl)
                    second = quantized(i * 64 + 32 + k * 8, 8, sl)
                    words[t, pl.ds(pl.multiple_of(i * 40 + k * 8, 8), 8), :] = (first << 12) | (second & 0xFFF)
                    high = high | (((second >> 12) & 0xFF) << (8 * k))
                words[t, pl.ds(pl.multiple_of(i * 40 + 32, 8), 8), :] = high
            return c

        lax.fori_loop(0, blocks, block, 0)
        for t, sl in enumerate(tiles_of(p), edges[p]):
            words[t, plain : plain + d8 - rest, :] = quantized(rest, d8 - rest, sl)
        tops[p, 0:1, :] = as_row(top[0:LANES])
        tops[p, 1:2, :] = as_row(top[LANES:d8])

    def unscale(tops, p):
        top = jnp.concatenate([as_column(tops[p, 0:1, :], LANES), as_column(tops[p, 1:2, :], d8 - LANES)], axis=0)
        row_scale[...] = top * (1.0 / LEVELS)

    def uncode(write, p, words):
        def put(first, n, sl, q):
            r = pl.ds(pl.multiple_of(first, 8), n)
            write(r, sl, q.astype(F32) * row_scale[r, :])

        def block(i, c):
            for t, sl in enumerate(tiles_of(p), edges[p]):
                high = words[t, pl.ds(pl.multiple_of(i * 40 + 32, 8), 8), :]
                for k in range(4):
                    low = words[t, pl.ds(pl.multiple_of(i * 40 + k * 8, 8), 8), :]
                    put(i * 64 + k * 8, 8, sl, low >> 12)
                    put(i * 64 + 32 + k * 8, 8, sl, (((high << (24 - 8 * k)) >> 24) << 12) | (low & 0xFFF))
            return c

        lax.fori_loop(0, blocks, block, 0)
        for t, sl in enumerate(tiles_of(p), edges[p]):
            put(rest, d8 - rest, sl, words[t, plain : plain + d8 - rest, :])

    def top_of(values):
        value = jnp.abs(values[0])
        for other in values[1:]:
            value = jnp.maximum(value, jnp.abs(other))
        return value

    def piece_of(j, p):
        partial(j, edges[p], edges[p + 1] - edges[p])

    def over(p):
        at = lanes_of(p)
        return remote(part.at[xs, rows_d, at], rx_a.at[rows_d, at], sp.at[p], rp.at[p], {"chan": sib})

    to_x = []
    piece_of(xs, 0)
    over(0).start()
    piece_of(xp, 0)
    for p in range(PIECES):
        if p + 1 < PIECES:
            piece_of(xs, p + 1)
            over(p + 1).start()
        over(p).wait()

        def add_a(g, c):
            r = pl.ds(pl.multiple_of(g * 8, 8), 8)
            values = [part[xp, r, sl] + rx_a[r, sl] for sl in tiles_of(p)]
            for sl, v in zip(tiles_of(p), values):
                part[xp, r, sl] = v
            row_top[r, :] = top_of(values)
            return c

        lax.fori_loop(0, d8 // 8, add_a, 0)
        code(lambda r, sl: part[xp, r, sl], p, px_out, tx_out)
        at = pl.ds(edges[p], edges[p + 1] - edges[p])
        copies = [
            remote(tx_out.at[p], tx_in.at[p], sq.at[0, p], rq.at[0, p], {"chan": xp}),
            remote(px_out.at[at], px_in.at[at], sq.at[1, p], rq.at[1, p], {"chan": xp}),
        ]
        for copy in copies:
            copy.start()
        to_x.append(copies)
        if p + 1 < PIECES:
            piece_of(xp, p + 1)
    for i in range(2):
        r = pl.ds(i * LANES, c_sizes[i])
        col_m[r, :] = as_column(mean1[i], c_sizes[i])
        col_k[r, :] = as_column(keep1[i], c_sizes[i])
    partial(sib, 0, tiles)
    to_sib_b = remote(part.at[sib, rows_d], rx_b.at[rows_d], sx.at[0], rxs.at[0], {"chan": sib})
    to_sib_b.start()
    partial(ch, 0, tiles)

    g_x.wait()
    px = iota((TAP, n_px), 1)
    py, pxx = px >> 5, px & (SIDE - 1)
    gcur[40:TAP, :] = jnp.zeros((TAP - 40, n_px), F32)
    for i in range(2):
        mine, theirs = slice(i * 32, i * 32 + 32), slice(32 - i * 32, 64 - i * 32)
        gcur[0:32, :] = gpair[mine, :].astype(F32) + grx[theirs, :].astype(F32)
        tails, others = gpair[64:80, :].astype(F32), grx[64:80, :].astype(F32)
        gcur[32:40, :] = tails[i * 8 : i * 8 + 8] + others[8 - i * 8 : 16 - i * 8]
        for ky in range(3):
            for kx in range(3):
                shift = (ky - 1) * SIDE + (kx - 1)
                t = ky * 3 + kx
                v = gcur[...]
                if shift != 0:
                    v = pltpu.roll(v, shift % n_px, 1)
                ok = None
                for off, pos in ((ky - 1, py), (kx - 1, pxx)):
                    if off == 1:
                        test = pos >= 1
                    elif off == -1:
                        test = pos <= SIDE - 2
                    else:
                        continue
                    ok = test if ok is None else ok & test
                if ok is not None:
                    v = jnp.where(ok, v, 0.0)
                g9[i, t * TAP : (t + 1) * TAP, :] = v.astype(BF16)
        g9[i, pl.ds(9 * TAP, TAPS - 9 * TAP), :] = jnp.zeros((TAPS - 9 * TAP, n_px), BF16)
    def slopes(j):
        def body(g, c):
            r = pl.ds(pl.multiple_of(g * 16, 16), 16)
            a, b = col_a[r, :], col_b[r, :]
            k = 0.5 * col_k[r, :]
            for t in range(tiles):
                sl = slice(t * LANES, (t + 1) * LANES)
                v = xb[j, r, sl].astype(F32) * a + b
                th = jnp.tanh(v)
                slope[j, r, sl] = ((1.0 + th) * (1.0 + v * (1.0 - th))) * (mask[j, :, sl] * k)
            return c

        lax.fori_loop(0, cp // 16, body, 0)


    to_sib_b.wait()
    sum_a[...] = jnp.zeros(sum_a.shape, F32)
    sum_b[...] = jnp.zeros(sum_b.shape, F32)
    hid[:, d8:dpad, :] = jnp.zeros((2, dpad - d8, n_px), F32)
    gp2[...] = jnp.zeros(gp2.shape, F32)

    def across(p):
        at = pl.ds(edges[p], edges[p + 1] - edges[p])
        return [
            remote(th_out.at[p], th_in.at[p], sh.at[0, p], rh.at[0, p], {"chan": xp}),
            remote(ph_out.at[at], ph_in.at[at], sh.at[1, p], rh.at[1, p], {"chan": xp}),
        ]

    def start_across(p):
        for copy in across(p):
            copy.start()

    for p in range(PIECES):
        for copy in to_x[p]:
            copy.wait()
        unscale(tx_in, p)

        def gather(r, sl, v):
            hid[0, r, sl] = (part[ch, r, sl] + rx_b[r, sl]) + v

        uncode(gather, p, px_in)

        def sums(g, c):
            r = pl.ds(pl.multiple_of(g * 8, 8), 8)
            s_acc, q_acc = sum_a[r, :], sum_b[r, :]
            values = [hid[0, r, sl] for sl in tiles_of(p)]
            for v in values:
                s_acc = s_acc + v
                q_acc = q_acc + v * v
            sum_a[r, :] = s_acc
            sum_b[r, :] = q_acc
            tops_h[p, r, :] = top_of(values)
            return c

        lax.fori_loop(0, d8 // 8, sums, 0)
        if p < AHEAD:
            row_top[...] = tops_h[p]
            code(lambda r, sl: hid[0, r, sl], p, ph_out, th_out)
            start_across(p)

    def pack(slots):
        s, q = as_rows(sum_a[0:d8, :], d_sizes), as_rows(sum_b[0:d8, :], d_sizes)
        slots[me, 0:1, :] = s[0]
        slots[me, 1:2, :] = s[1]
        slots[me, 2:3, :] = q[0]
        slots[me, 3:4, :] = q[1]

    def columns_d(row0, row1):
        tail = jnp.zeros((dpad - d8, LANES), F32)
        return jnp.concatenate(
            [as_column(row0, LANES), as_column(row1, d8 - LANES), tail], axis=0
        )

    pack(ar2)
    share_start(ar2, me, n_dev, dev_peer, s2, r2)
    for p in range(AHEAD, PIECES):
        row_top[...] = tops_h[p]
        code(lambda r, sl: hid[0, r, sl], p, ph_out, th_out)
        start_across(p)

    w_far.wait()
    w_on.start()
    slopes(xs)
    slopes(xp)
    w_near.wait()
    w_on.wait()
    share_wait(gsl, ch, n_ch, ch_peer, sb, rb)
    acc = jnp.zeros((dpad, w2b.shape[1]), F32)
    for j in range(n_ch):
        rows = iota((dpad, TAP), 0)
        cols = iota((dpad, TAP), 1)
        place = jnp.where((rows == cols + j * grow) & (cols < grow), 1.0, 0.0).astype(BF16)
        acc = acc + jnp.dot(place, w2r[j], preferred_element_type=F32)
    w2b[...] = acc.astype(BF16)
    for i in range(2):
        back[i] = jnp.dot(w2b[...], g9[i], preferred_element_type=F32)
    rows = iota((dpad, LANES), 0)
    cols = iota((dpad, LANES), 1)
    gain2c = jnp.zeros((dpad, 1), F32)
    bias2c = jnp.zeros((dpad, 1), F32)
    for j in range(n_ch):
        place = (rows == cols + j * grow) & (cols < grow)
        gain2c = gain2c + jnp.sum(jnp.where(place, gsl[j, 0:1, :], 0.0), axis=1, keepdims=True)
        bias2c = bias2c + jnp.sum(jnp.where(place, gsl[j, 1:2, :], 0.0), axis=1, keepdims=True)
    col_c[0] = jnp.broadcast_to(gain2c, (dpad, LANES))
    col_c[1] = jnp.broadcast_to(bias2c, (dpad, LANES))

    def widen_cot(i, c):
        r = pl.ds(pl.multiple_of(i * step_rows, step_rows), step_rows)
        k = [jnp.broadcast_to(col_k[pl.ds(i * 3 + n, 1), :], (rpc, LANES)) for n in range(3)]
        base[r, :] = cot[r, :].astype(F32) * jnp.concatenate(k, axis=0)
        return c

    lax.fori_loop(0, n_rows // step_rows, widen_cot, 0)

    share_wait(ar2, me, n_dev, dev_peer, s2, r2)
    tot2 = total(ar2)
    mean2 = [tot2[i : i + 1] / count for i in range(2)]
    rstd2 = [lax.rsqrt(tot2[2 + i : 3 + i] / count - mean2[i] * mean2[i] + EPS) for i in range(2)]
    mean2c = columns_d(*mean2)
    rstd2c = columns_d(*rstd2)
    scale2c = rstd2c * col_c[0]
    col_c[2] = mean2c
    col_c[3] = rstd2c
    col_c[4] = scale2c
    col_c[5] = 0.5 * scale2c
    col_c[6] = 0.5 * (col_c[1] - mean2c * scale2c)

    def second(g, c):
        r = pl.ds(pl.multiple_of(g * 16, 16), 16)
        a, b, m = col_c[5, r, :], col_c[6, r, :], col_c[2, r, :]
        s_acc = jnp.zeros((16, LANES), F32)
        q_acc = jnp.zeros((16, LANES), F32)
        for t in range(tiles):
            sl = slice(t * LANES, (t + 1) * LANES)
            h = hid[0, r, sl]
            mk = mask[ch, :, sl]
            v = h * a + b
            th = jnp.tanh(v)
            act2[r, sl] = ((v * th + v) * mk).astype(BF16)
            gp = (0.5 * mk) * ((1.0 + th) * (1.0 + v * (1.0 - th))) * back[0, r, sl]
            gp2[0, r, sl] = gp
            s_acc = s_acc + gp
            q_acc = q_acc + gp * (h - m)
        sum_a[r, :] = s_acc
        sum_b[r, :] = q_acc
        return c

    lax.fori_loop(0, dpad // 16, second, 0)
    pack(ar3)
    share_start(ar3, me, n_dev, dev_peer, s3, r3)

    w2acc[...] = lax.dot_general(
        act2[...], g9[0], (((1,), (1,)), ((), ())), preferred_element_type=F32
    )
    for j in range(n_ch):
        for lt in range(4):
            sl = slice(lt * LANES, (lt + 1) * LANES)
            cw[j, lt * 32 : lt * 32 + 32, :] = w2acc[j * grow : j * grow + 32, sl]
            cw[j, 128 + lt : 129 + lt, :] = w2acc[j * grow + 32 : j * grow + 33, sl]
        cw[j, 132:136, :] = jnp.zeros((4, LANES), F32)
    w_sib = [
        remote(cw.at[xs], cwr.at[1], sc.at[0], rc.at[0], {"chan": sib}),
        remote(cw.at[sib], cwr.at[0], sc.at[1], rc.at[1], {"chan": sib}),
    ]
    for copy in w_sib:
        copy.start()

    def second_other(p):
        for copy in across(p):
            copy.wait()
        unscale(th_in, p)

        def keep_hidden(r, sl, v):
            hid[1, r, sl] = v

        uncode(keep_hidden, p, ph_in)

        def body(g, c):
            r = pl.ds(pl.multiple_of(g * 16, 16), 16)
            a, b = col_c[5, r, :], col_c[6, r, :]
            for sl in tiles_of(p):
                v = hid[1, r, sl] * a + b
                th = jnp.tanh(v)
                gp2[1, r, sl] = (
                    (0.5 * mask[xp, :, sl]) * ((1.0 + th) * (1.0 + v * (1.0 - th))) * back[1, r, sl]
                )
            return c

        lax.fori_loop(0, dpad // 16, body, 0)

    zbuf[...] = lax.dot_general(
        w2b[...], act2[...], (((0,), (0,)), ((), ())), preferred_element_type=F32
    )
    new = jnp.zeros((TAP, n_px), F32)
    for ky in range(3):
        for kx in range(3):
            shift = (ky - 1) * SIDE + (kx - 1)
            t = ky * 3 + kx
            v = zbuf[t * TAP : (t + 1) * TAP, :]
            if shift != 0:
                v = pltpu.roll(v, (-shift) % n_px, 1)
            ok = None
            for off, pos in ((ky - 1, py), (kx - 1, pxx)):
                if off == -1:
                    test = pos >= 1
                elif off == 1:
                    test = pos <= SIDE - 2
                else:
                    continue
                ok = test if ok is None else ok & test
            if ok is not None:
                v = jnp.where(ok, v, 0.0)
            new = new + v
    new = new * jnp.concatenate([mask[ch]] * (TAP // 16), axis=0)
    gall[ch] = new[0 : gall.shape[1]]
    for copy in w_sib:
        copy.wait()
    cw[xp] = cw[xp] + cwr[1]
    cw[ch] = cw[ch] + cwr[0]
    w_x = remote(cw.at[xp], cwx, sc.at[2], rc.at[2], {"chan": xp})
    w_x.start()
    new_sib = remote(gall.at[ch], gall.at[ch], so.at[0], ro.at[0], {"chan": sib})
    new_xp = remote(gall.at[ch], gall.at[ch], so.at[1], ro.at[1], {"chan": xp})
    new_on = remote(gall.at[xp], gall.at[xp], so.at[2], ro.at[2], {"chan": sib})
    new_xp.start()
    new_sib.start()
    slopes(sib)
    slopes(ch)
    for p in range(PIECES):
        second_other(p)

    w1acc[...] = jnp.zeros(w1acc.shape, F32)
    sum_a[...] = jnp.zeros(sum_a.shape, F32)
    sum_b[...] = jnp.zeros(sum_b.shape, F32)
    share_wait(ar3, me, n_dev, dev_peer, s3, r3)
    tot3 = total(ar3)
    gain_sum2 = [tot3[2 + i : 3 + i] * rstd2[i] for i in range(2)]
    bias_sum2 = [tot3[i : i + 1] for i in range(2)]
    gain_sum2c = columns_d(*gain_sum2)
    bias_sum2c = columns_d(*bias_sum2)
    col_c[7] = col_c[4] * bias_sum2c / count
    col_c[8] = col_c[4] * col_c[3] * gain_sum2c / count

    def third(i, j, k):
        def body(g, c):
            r = pl.ds(pl.multiple_of(g * 16, 16), 16)
            c1, c2, c3, m = col_c[4, r, :], col_c[7, r, :], col_c[8, r, :], col_c[2, r, :]
            for sl in [slice(t * LANES, (t + 1) * LANES) for t in range(k * tiles // 2, (k + 1) * tiles // 2)]:
                gha[j, r, sl] = (
                    c1 * gp2[i, r, sl] - mask[j, :, sl] * (c2 + c3 * (hid[i, r, sl] - m))
                ).astype(BF16)
            return c

        lax.fori_loop(0, dpad // 16, body, 0)

    grads = []
    for i, j in ((0, ch), (1, xp)):
        for k in range(2):
            third(i, j, k)
            at = pl.ds(k * (n_px // 2), n_px // 2)
            copy = remote(gha.at[j, :, at], gha.at[j, :, at], st.at[i, k], rt.at[i, k], {"chan": sib})
            copy.start()
            grads.append(copy)


    def weight_grad(j, k=None):
        at = slice(0, n_px) if k is None else slice(k * (n_px // 2), (k + 1) * (n_px // 2))
        w1acc[0:dpad, 0:cp] = w1acc[0:dpad, 0:cp] + lax.dot_general(
            gha[j, :, at], act[j, :, at], (((1,), (1,)), ((), ())), preferred_element_type=F32
        )

    def input_grad(j):
        gact[...] = lax.dot_general(
            w1s[...], gha[j], (((0,), (0,)), ((), ())), preferred_element_type=F32
        )

        def body(g, c):
            r = pl.ds(pl.multiple_of(g * 16, 16), 16)
            m = col_m[r, :]
            s_acc, q_acc = sum_a[r, :], sum_b[r, :]
            for t in range(tiles):
                sl = slice(t * LANES, (t + 1) * LANES)
                gp = gact[r, sl] * slope[j, r, sl]
                gp1[j, r, sl] = gp
                s_acc = s_acc + gp
                q_acc = q_acc + gp * (xb[j, r, sl].astype(F32) - m)
            sum_a[r, :] = s_acc
            sum_b[r, :] = q_acc
            return c

        lax.fori_loop(0, cp // 16, body, 0)

    weight_grad(ch)
    weight_grad(xp)
    w_x.wait()
    for i, j in ((0, sib), (1, xs)):
        for k in range(2):
            grads[2 * i + k].wait()
            weight_grad(j, k)

    for r in range(17):
        cb[r // 5, r % 5 * 8 : r % 5 * 8 + 8, :] = w1acc[r * 8 : r * 8 + 8, 0:LANES]
    for k in range(6):
        v = w1acc[k * 8 : k * 8 + 8, LANES : 2 * LANES]
        for i in range(1, 3):
            v = v + pltpu.roll(w1acc[i * 48 + k * 8 : i * 48 + k * 8 + 8, LANES : 2 * LANES], 40 * i, 1)
        r = 17 + k
        cb[r // 5, r % 5 * 8 : r % 5 * 8 + 8, :] = v
    for k in range(17):
        r = 23 + k
        cb[r // 5, r % 5 * 8 : r % 5 * 8 + 8, :] = cw[ch, k * 8 : k * 8 + 8, :] + cwx[k * 8 : k * 8 + 8, :]

    def encode(v):
        top = jnp.maximum(jnp.max(jnp.abs(v), axis=0, keepdims=True), 1e-30)
        power = jnp.floor(jnp.log2(top) + 1.0001)
        q = jnp.clip(jnp.round(v * jnp.exp2(15.0 - power)), -32767.0, 32767.0).astype(jnp.int32)
        low = jnp.concatenate([q[24:40], jnp.broadcast_to(power.astype(jnp.int32), (8, LANES))], axis=0)
        return (q[0:24] << 16) | (low & 0xFFFF)

    def decode(w):
        high, low = w >> 16, (w << 16) >> 16
        scale = jnp.exp2(low[16:24].astype(F32) - 15.0)
        q = jnp.concatenate([high, low[0:16]], axis=0).astype(F32)
        return q * jnp.concatenate([scale] * 5, axis=0)

    for q in range(OWNERS):
        coded[q] = encode(cb[q])
    stride = n_dp // OWNERS
    my_part = dp // stride
    is_owner = lax.rem(dp, stride) == 0

    def part_to(k):
        q = my_part ^ (OWNERS - 1 - k)
        return q, q * stride

    def push(k, c):
        q, to = part_to(k)

        @pl.when(to != dp)
        def _():
            remote(coded.at[q], rsl.at[dp], sr.at[k], rr.at[dp], {"dp": to}).start()

        return c

    lax.fori_loop(0, OWNERS, push, 0)
    d_rows, d_cols = iota((dpad, LANES), 0), iota((dpad, LANES), 1)
    here_d = (d_rows == d_cols + ch * grow) & (d_cols < grow)
    out_g2[...] = jnp.sum(jnp.where(here_d, gain_sum2c, 0.0), axis=0, keepdims=True)[:, 0:grow]
    out_b2[...] = jnp.sum(jnp.where(here_d, bias_sum2c, 0.0), axis=0, keepdims=True)[:, 0:grow]
    for j in (ch, xp, sib, xs):
        input_grad(j)
    s4_, q4_ = as_rows(sum_a[...], c_sizes), as_rows(sum_b[...], c_sizes)
    for i in range(2):
        ar4[dp, i : i + 1, :] = s4_[i]
        ar4[dp, 2 + i : 3 + i, :] = q4_[i]
    share_start(ar4, dp, n_dp, dp_peer, s4, r4)

    def scatter(g, c):
        first = g * 16 * rpc
        r = pl.ds(pl.multiple_of(g * 16, 16), 16)
        for b in range(n_img):
            for t in range(tiles):
                v = gp1[b, r, t * LANES : (t + 1) * LANES]
                for h in range(2):
                    at = pl.ds(first + h * 8 * rpc + t * n_img + b, 8, stride=rpc)
                    out_g[at, :] = v[h * 8 : h * 8 + 8]
        return c

    lax.fori_loop(0, 5, scatter, 0)

    def push_wait(k, c):
        q, to = part_to(k)

        @pl.when(to != dp)
        def _():
            remote(coded.at[q], rsl.at[dp], sr.at[k], rr.at[dp], {"dp": to}).wait_send()

        return c

    def pull(k, c):
        src = lax.rem(dp + k, n_dp)
        remote(coded.at[0], rsl.at[src], sr.at[0], rr.at[src], {"dp": src}).wait_recv()
        return c

    @pl.when(is_owner)
    def _():
        lax.fori_loop(1, n_dp, pull, 0)
        v = cb[my_part]
        for k in range(1, n_dp):
            v = v + decode(rsl[lax.rem(dp + k, n_dp)])
        fin[my_part] = encode(v)

        def give(k):
            remote(fin.at[my_part], fin.at[my_part], sa.at[k], ra.at[my_part], dp_peer(k)).start()

        far_first(n_dp, give)

    lax.fori_loop(0, OWNERS, push_wait, 0)
    new_xp.wait()
    new_on.start()
    lax.fori_loop(5, cp // 16, scatter, 0)

    for i in range(2):
        col_a[pl.ds(i * LANES, c_sizes[i]), :] = as_column(scale1[i], c_sizes[i])

    new_sib.wait()
    new_on.wait()
    for b in range(n_img):
        for t in range(tiles):
            for h in range(gall.shape[1] // 8):
                out_new[pl.ds(h * 8 * rpc + t * n_img + b, 8, stride=rpc), :] = gall[
                    b, h * 8 : h * 8 + 8, t * LANES : (t + 1) * LANES
                ]
    out_slot[...] = (slot_of - ch * per_device)[0:8].astype(F32)

    share_wait(ar4, dp, n_dp, dp_peer, s4, r4)
    tot4 = total(ar4)
    for i in range(2):
        bias_sum = tot4[i : i + 1]
        gain_sum = tot4[2 + i : 3 + i] * rstd1[i]
        size = c_sizes[i]
        r = pl.ds(i * LANES, size)
        k1 = -scale1[i] * rstd1[i] * gain_sum / count
        k0 = -scale1[i] * bias_sum / count - k1 * mean1[i]
        col_b[r, :] = as_column(k0, size)
        col_m[r, :] = as_column(k1, size)
        width = min(LANES, n_c - i * LANES)
        out_g1[0:1, i * LANES : i * LANES + width] = gain_sum[:, 0:width]
        out_b1[0:1, i * LANES : i * LANES + width] = bias_sum[:, 0:width]
    mask_of = mask_raw[...]

    def last(i, c):
        for k in range(5):
            row = i * 5 + k
            at = pl.ds(pl.multiple_of(row * rpc, rpc), rpc)
            k0 = jnp.broadcast_to(col_b[pl.ds(row, 1), :], (rpc, LANES))
            k1 = jnp.broadcast_to(col_m[pl.ds(row, 1), :], (rpc, LANES))
            a = jnp.broadcast_to(col_a[pl.ds(row, 1), :], (rpc, LANES))
            out_g[at, :] = base[at, :] + a * out_g[at, :] + mask_of * (k0 + k1 * out_x[at, :])
        return c

    lax.fori_loop(0, n_c // 5, last, 0)

    for wait in still_sent:
        wait()

    @pl.when(is_owner)
    def _():
        def gave(k, c):
            remote(fin.at[my_part], fin.at[my_part], sa.at[k], ra.at[my_part], dp_peer(k)).wait_send()
            return c

        lax.fori_loop(1, n_dp, gave, 0)

    def take(q, c):
        @pl.when(q * stride != dp)
        def _():
            remote(fin.at[q], fin.at[q], sa.at[0], ra.at[q], {"dp": q * stride}).wait_recv()

        return c

    lax.fori_loop(0, OWNERS, take, 0)
    for q in range(OWNERS):
        cb[q] = decode(fin[q])
    for r in range(17):
        height = min(8, n_d - r * 8)
        out_w1[r * 8 : r * 8 + height, 0:LANES] = cb[r // 5, r % 5 * 8 : r % 5 * 8 + height, :]
    for k in range(6):
        r = 17 + k
        v = cb[r // 5, r % 5 * 8 : r % 5 * 8 + 8, :]
        for i in range(3):
            row = i * 48 + k * 8
            height = min(8, n_d - row)
            if height > 0:
                u = v if i == 0 else pltpu.roll(v, LANES - 40 * i, 1)
                out_w1[row : row + height, LANES:n_c] = u[0:height, 0 : n_c - LANES]
    for k in range(17):
        r = 23 + k
        v = cb[r // 5, r % 5 * 8 : r % 5 * 8 + 8, :]
        if k < 16:
            w2acc[k % 4 * 8 : k % 4 * 8 + 8, k // 4 * LANES : (k // 4 + 1) * LANES] = v
        else:
            for lt in range(4):
                w2acc[32:33, lt * LANES : (lt + 1) * LANES] = v[lt : lt + 1]
    v = w2acc[0:40, :]
    for t in range(9):
        u = v if t == 0 else pltpu.roll(v, TAPS - t * TAP, 1)
        out_w2[t] = u[0:grow, 0:grow]


def finish(n_rows, grow_rows, *refs):
    n = (len(refs) - 3) // 2
    new, slot = refs[n : n + 2]
    outs, sem = refs[n + 2 : -1], refs[-1]
    segments = n_rows // grow_rows
    copies = [pltpu.make_async_copy(refs[1].at[pl.ds(0, n_rows)], outs[1], sem.at[1])]
    copies += [pltpu.make_async_copy(refs[i], outs[i], sem.at[i]) for i in range(2, n)]
    for copy in copies:
        copy.start()
    here = jnp.max(slot[...])
    for k in range(segments):
        at = pl.ds(k * grow_rows, grow_rows)
        kept = pltpu.make_async_copy(refs[0].at[at], outs[0].at[at], sem.at[n + k])
        grown = pltpu.make_async_copy(new.at[pl.ds(0, grow_rows)], outs[0].at[at], sem.at[n + k])
        pl.when(here == k)(grown.start)
        pl.when(here != k)(kept.start)
        copies.append(kept)
    for copy in copies:
        copy.wait()


def flat(values):
    n, c, p = values.shape
    return (
        values.transpose(1, 0, 2).reshape(c, n, p // LANES, LANES).transpose(0, 2, 1, 3).reshape(-1, LANES)
    )


def unflat(rows, n, c, p):
    return rows.reshape(c, p // LANES, n, LANES).transpose(0, 2, 1, 3).reshape(c, n, p).transpose(1, 0, 2)


def on_device(
    n_dp, n_ch, features, gain1, bias1, weight1, gain2, bias2, weight2, cotangent, image_side, block_slot
):
    n_img, n_c, n_px = features.shape
    n_d = weight1.shape[1]
    grow = weight2.shape[3]
    cp = pad_to(n_c, 16)
    dpad = pad_to(n_d, 16)
    d8 = pad_to(n_d, 8)
    rpc = n_px // LANES * n_img
    n_rows, n_pad = n_c * rpc, cp * rpc
    n_dev = n_dp * n_ch
    words = d8 // 64 * 40 + d8 % 64
    cfg = (n_dp, n_ch, n_img, n_c, n_px, n_d, grow)
    args = (
        flat(features),
        flat(cotangent),
        weight1.T,
        gain1.reshape(1, -1),
        bias1.reshape(1, -1),
        gain2.reshape(1, -1),
        bias2.reshape(1, -1),
        weight2.reshape(9, grow, grow),
        image_side,
        block_slot,
    )
    args = [pltpu.with_memory_space_constraint(v, pltpu.HBM) for v in args]
    sd = jax.ShapeDtypeStruct
    in_vmem = pl.BlockSpec(memory_space=pltpu.VMEM)
    in_hbm = pl.BlockSpec(memory_space=pltpu.HBM)
    dma = pltpu.SemaphoreType.DMA
    v = pltpu.VMEM
    scratch = [
        v((n_rows, LANES), BF16), v((n_rows, LANES), BF16), v((n_d, n_c), BF16),
        v((1, n_c), F32), v((1, n_c), F32), v((1, grow), F32), v((1, grow), F32),
        v((9, grow, grow), BF16), pltpu.SMEM(image_side.shape, jnp.int32), pltpu.SMEM(block_slot.shape, jnp.int32),
        v((n_img, 16, n_px), F32), v((rpc, LANES), F32), v((n_rows, LANES), F32),
        v((n_img, cp, n_px), BF16), v((n_img, cp, n_px), BF16),
        v((n_img, cp, n_px), F32), v((n_img, cp, n_px), F32), v((cp, n_px), F32),
        v((cp, LANES), F32), v((cp, LANES), F32), v((cp, LANES), F32), v((cp, LANES), F32),
        v((9, dpad, LANES), F32), v((cp, LANES), F32), v((cp, LANES), F32),
        v((8, LANES), F32),
        v((dpad, cp), BF16), v((n_img, dpad, n_px), F32),
        v((dpad, n_px), F32), v((dpad, n_px), F32), v((2, dpad, n_px), F32),
        v((d8, LANES), F32), v((d8, LANES), F32), v((PIECES, d8, LANES), F32),
        v((n_px // LANES, words, LANES), jnp.int32), v((n_px // LANES, words, LANES), jnp.int32), v((PIECES, 2, LANES), F32), v((PIECES, 2, LANES), F32),
        v((n_px // LANES, words, LANES), jnp.int32), v((n_px // LANES, words, LANES), jnp.int32), v((PIECES, 2, LANES), F32), v((PIECES, 2, LANES), F32),
        v((40 * rpc, LANES), F32), v((2, 80, n_px), BF16),
        v((80, n_px), BF16), v((80, n_px), BF16), v((80, n_px), BF16), v((TAP, n_px), F32),
        v((2, TAPS, n_px), BF16), v((9, TAP, LANES), F32), v((TAP, TAPS), F32), v((n_ch, TAP, TAPS), BF16), v((dpad, TAPS), BF16),
        v((n_ch, 2, LANES), F32),
        v((dpad, n_px), BF16), v((2, dpad, n_px), F32), v((2, dpad, n_px), F32), v((TAPS, n_px), F32),
        v((n_ch, 40, n_px), F32), v((n_ch, dpad, n_px), BF16),
        v((n_ch, 136, LANES), F32), v((2, 136, LANES), F32), v((136, LANES), F32),
        v((OWNERS, 40, LANES), F32), v((OWNERS, 24, LANES), jnp.int32),
        v((n_dp, 24, LANES), jnp.int32), v((OWNERS, 24, LANES), jnp.int32), v((dpad, 256), F32), v((dpad, TAPS), F32),
        v((n_dp, 4, LANES), F32), v((n_dev, 4, LANES), F32), v((n_dev, 4, LANES), F32), v((n_dp, 4, LANES), F32),
        dma((13,)),
        dma((n_dp,)), dma((n_dp,)), dma((n_dev,)), dma((n_dev,)), dma((n_dev,)), dma((n_dev,)), dma((n_dp,)), dma((n_dp,)),
        dma((3,)), dma((3,)), dma((PIECES,)), dma((PIECES,)), dma((2, PIECES)), dma((2, PIECES)),
        dma((2,)), dma((2,)), dma((n_ch,)), dma((n_ch,)), dma((n_ch,)), dma((n_ch,)),
        dma((2, PIECES)), dma((2, PIECES)), dma((2, 2)), dma((2, 2)), dma((3,)), dma((3,)), dma((3,)), dma((3,)),
        dma((OWNERS,)), dma((n_dp,)), dma((n_dp,)), dma((OWNERS,)),
    ]
    out_shape = (
        sd((n_pad, LANES), F32), sd((n_pad, LANES), F32), sd((n_d, n_c), F32),
        sd((1, n_c), F32), sd((1, n_c), F32), sd((9, grow, grow), F32), sd((1, grow), F32), sd((1, grow), F32),
        sd((40 * rpc, LANES), F32), sd((8, LANES), F32),
    )
    outs = pl.pallas_call(
        functools.partial(layer, cfg),
        out_shape=out_shape,
        in_specs=[in_hbm] * len(args),
        out_specs=(in_vmem,) * len(out_shape),
        scratch_shapes=scratch,
        compiler_params=pltpu.CompilerParams(
            collective_id=0, has_side_effects=True, vmem_limit_bytes=40 << 20
        ),
    )(*args)
    final = (sd((n_rows, LANES), F32),) * 2 + out_shape[2:-2]
    o = pl.pallas_call(
        functools.partial(finish, n_rows, grow * rpc),
        out_shape=final,
        in_specs=[in_vmem] * len(outs),
        out_specs=(in_hbm,) * len(final),
        scratch_shapes=[dma((len(final) + n_c // grow,))],
        compiler_params=pltpu.CompilerParams(vmem_limit_bytes=8 << 20),
    )(*outs)
    return (
        unflat(o[0], n_img, n_c, n_px),
        unflat(o[1], n_img, n_c, n_px),
        o[2].T,
        o[3].reshape(-1),
        o[4].reshape(-1),
        o[5].reshape(3, 3, grow, grow),
        o[6].reshape(-1),
        o[7].reshape(-1),
    )


def solution(mesh):
    in_specs = (
        P("dp", "chan", None),
        P("chan"),
        P("chan"),
        P("chan", None),
        P("chan"),
        P("chan"),
        P(None, None, "chan", None),
        P("dp", "chan", None),
        P("dp"),
        P(),
    )
    out_specs = (
        P("dp", "chan", None),
        P("dp", "chan", None),
        P("chan", None),
        P("chan"),
        P("chan"),
        P(None, None, "chan", None),
        P("chan"),
        P("chan"),
    )
    body = functools.partial(on_device, mesh.shape["dp"], mesh.shape["chan"])
    return jax.shard_map(body, mesh=mesh, in_specs=in_specs, out_specs=out_specs, check_vma=False)
```

```python
import functools

import jax
import jax.numpy as jnp
from jax import lax
from jax.experimental import pallas as pl
from jax.experimental.pallas import tpu as pltpu
from jax.sharding import PartitionSpec as P

SIDE = 32
EPS = 1e-05
LANES = 128
TAP = 48
TAPS = 512
SPANS = (1, 2, 3, 2)
PIECES = len(SPANS)
AHEAD = 2
LEVELS = 524000.0
OWNERS = 8

MESH = pl.DeviceIdType.MESH
F32 = jnp.float32
BF16 = jnp.bfloat16


def pad_to(size, unit):
    return (size + unit - 1) // unit * unit


def iota(shape, axis):
    return lax.broadcasted_iota(jnp.int32, shape, axis)


def as_row(column):
    n = column.shape[0]
    eye = iota((n, LANES), 0) == iota((n, LANES), 1)
    return jnp.sum(jnp.where(eye, column, 0.0), axis=0, keepdims=True)


def as_column(row, n):
    eye = iota((n, LANES), 0) == iota((n, LANES), 1)
    return jnp.broadcast_to(jnp.sum(jnp.where(eye, row, 0.0), axis=1, keepdims=True), (n, LANES))


def as_rows(values, sizes):
    column = jnp.sum(values, axis=1, keepdims=True)
    rows, start = [], 0
    for size in sizes:
        rows.append(as_row(column[start : start + size]))
        start += size
    return rows


def layer(
    cfg,
    feat_h, cot_h, w1_h, gain1_h, bias1_h, gain2_h, bias2_h, w2_h, side_h, slot_h,
    out_x, out_g, out_w1, out_g1, out_b1, out_w2, out_g2, out_b2, out_new, out_slot,
    feat, cot, w1v, gain1v, bias1v, gain2v, bias2v, w2v, side, slot,
    mask, mask_raw, base, xb, act, slope, gp1, gact,
    col_a, col_b, col_m, col_k, col_c, sum_a, sum_b, rowbuf,
    w1s, part, rx_a, rx_b, hid, row_top, row_scale, tops_h,
    px_out, px_in, tx_out, tx_in, ph_out, ph_in, th_out, th_in,
    graw, gsend, gsx, gpair, grx, gcur, g9, w2pad, w2wide, w2r, w2b, gsl,
    act2, gp2, back, zbuf, gall, gha,
    cw, cwr, cwx, cb, coded, rsl, fin, w1acc, w2acc,
    ar1, ar2, ar3, ar4,
    load_sem, s1, r1, s2, r2, s3, r3, s4, r4, sx, rxs, sp, rp, sq, rq, sg, rg, sw, rw, sb, rb, sh, rh, st, rt, so, ro, sc, rc, sr, rr, sa, ra,
):
    n_dp, n_ch, n_img, n_c, n_px, n_d, grow = cfg
    n_dev = n_dp * n_ch
    cp = xb.shape[1]
    dpad = w1s.shape[0]
    d8 = pad_to(n_d, 8)
    tiles = n_px // LANES
    rpc = tiles * n_img
    c_sizes = (LANES, cp - LANES)
    d_sizes = (LANES, d8 - LANES)
    dp = lax.axis_index("dp")
    ch = lax.axis_index("chan")
    me = dp * n_ch + ch
    half = n_ch // 2
    cx, cc = ch // half, lax.rem(ch, half)
    sib = cx * half + (1 - cc)
    xp = (1 - cx) * half + cc
    xs = (1 - cx) * half + (1 - cc)

    def dev_peer(k):
        q = me ^ k
        return {"dp": q // n_ch, "chan": lax.rem(q, n_ch)}

    def dp_peer(k):
        return {"dp": dp ^ k}

    def ch_peer(k):
        return {"chan": ch ^ k}

    def far_first(count, step):
        if count <= 32:
            for k in range(count - 1, 0, -1):
                step(k)
        else:

            def body(i, c):
                step(count - 1 - i)
                return c

            lax.fori_loop(0, count - 1, body, 0)

    loads = {
        i: pltpu.make_async_copy(h, v, load_sem.at[i])
        for i, (h, v) in enumerate(
            (
                (cot_h, cot), (w1_h, w1v), (gain1_h, gain1v), (bias1_h, bias1v),
                (gain2_h, gain2v), (bias2_h, bias2v), (w2_h, w2v), (side_h, side), (slot_h, slot),
            ),
            1,
        )
    }
    feat_groups, feat_parts, start = [], [], 0
    for k in range(3):
        groups = pad_to(n_c, 8) // 8 * (k + 1) // 3 - sum(feat_groups)
        size = min(groups * 8, n_c - start) * rpc
        at = pl.ds(start * rpc, size)
        feat_parts.append(pltpu.make_async_copy(feat_h.at[at], feat.at[at], load_sem.at[10 + k]))
        feat_groups.append(groups)
        start += groups * 8
    for copy in [loads[8], loads[9], *feat_parts, *(loads[i] for i in range(1, 8))]:
        copy.start()
    barrier = pltpu.get_barrier_semaphore()

    def greet(k):
        pl.semaphore_signal(barrier, inc=1, device_id=dev_peer(k), device_id_type=MESH)

    far_first(n_dev, greet)

    def remote(src, dst, send, recv, device):
        return pltpu.make_async_remote_copy(
            src_ref=src, dst_ref=dst, send_sem=send, recv_sem=recv, device_id=device, device_id_type=MESH
        )

    still_sent = []

    def share_start(slots, mine, count, peer, send, recv):
        def step(k):
            remote(slots.at[mine], slots.at[mine], send.at[k], recv.at[k], peer(k)).start()

        far_first(count, step)

    def share_wait(slots, mine, count, peer, send, recv):
        def step(k):
            remote(slots.at[mine], slots.at[mine], send.at[k], recv.at[k], peer(k)).wait_recv()

        def sent(k):
            remote(slots.at[mine], slots.at[mine], send.at[k], recv.at[k], peer(k)).wait_send()

        far_first(count, step)
        still_sent.append(lambda: far_first(count, sent))

    def total(slots):
        if slots.shape[0] <= 32:
            value = slots[0]
            for i in range(1, slots.shape[0]):
                value = value + slots[i]
            return value
        return lax.fori_loop(1, slots.shape[0], lambda i, v: v + slots[i], slots[0])

    loads[8].wait()
    loads[9].wait()
    row_r, lane_r = iota((rpc, LANES), 0), iota((rpc, LANES), 1)
    tile_of, image_of = row_r // n_img, row_r % n_img
    count_here = jnp.int32(0)
    side_of = jnp.zeros((rpc, LANES), jnp.int32)
    for b in range(n_img):
        count_here = count_here + side[b] * side[b]
        side_of = jnp.where(image_of == b, side[b], side_of)
    pixel_of = tile_of * LANES + lane_r
    mask_raw[...] = jnp.where((pixel_of // SIDE < side_of) & (pixel_of % SIDE < side_of), 1.0, 0.0)
    mask_of = mask_raw[...]
    n_rows = feat.shape[0]

    def halves(v):
        while v.shape[0] > 8:
            n = v.shape[0] // 2
            v = v[0:n] + v[n:]
        return v

    sub = iota((8, LANES), 0)

    def fold(values):
        for d in (4, 2, 1):
            half_n = len(values) // 2
            values = [
                jnp.where((sub & d) == 0, u + pltpu.roll(u, 8 - d, 0), v + pltpu.roll(v, d, 0))
                for u, v in zip(values[:half_n], values[half_n:])
            ]
        return values[0]

    def first_sums(g, c, n=8):
        s, q = [], []
        for k in range(n):
            v = feat[pl.ds(pl.multiple_of((g * 8 + k) * rpc, rpc), rpc), :].astype(F32)
            w = v * mask_of
            s.append(halves(w))
            q.append(halves(w * v))
        none = [jnp.zeros((8, LANES), F32)] * (8 - n)
        at = pl.ds(pl.multiple_of(g * 8, 8), 8)
        sum_a[at, :] = fold(s + none)
        sum_b[at, :] = fold(q + none)
        return c

    whole, done = n_c // 8, 0
    for k, groups in enumerate(feat_groups):
        feat_parts[k].wait()
        lax.fori_loop(done, min(done + groups, whole), first_sums, 0)
        done += groups
    if n_c % 8:
        first_sums(whole, 0, n_c % 8)
    spare = pl.ds(pad_to(n_c, 8), cp - pad_to(n_c, 8))
    sum_a[spare, :] = jnp.zeros((cp - pad_to(n_c, 8), LANES), F32)
    sum_b[spare, :] = jnp.zeros((cp - pad_to(n_c, 8), LANES), F32)
    lane1 = iota((1, LANES), 1)
    s0, sq0 = as_rows(sum_a[...], c_sizes), as_rows(sum_b[...], c_sizes)
    ar1[dp, 0:1, :] = s0[0]
    ar1[dp, 1:2, :] = jnp.where(lane1 == LANES - 1, count_here.astype(F32), s0[1])
    ar1[dp, 2:3, :] = sq0[0]
    ar1[dp, 3:4, :] = sq0[1]

    new_slot = slot[slot.shape[0] - 1]
    per_device = n_c // grow
    slot_of = iota((rpc, LANES), 0) * 0 + new_slot
    loads[1].wait()
    graw[grow * rpc : 40 * rpc, :] = jnp.zeros(((40 - grow) * rpc, LANES), F32)
    picks = [jnp.where(slot_of == ch * per_device + i, mask_of, 0.0) for i in range(per_device)]

    def pick(i, c):
        v = jnp.zeros((rpc, LANES), F32)
        for k in range(per_device):
            v = v + cot[pl.ds(pl.multiple_of((k * grow + i) * rpc, rpc), rpc), :].astype(F32) * picks[k]
        graw[pl.ds(pl.multiple_of(i * rpc, rpc), rpc), :] = v
        return c

    lax.fori_loop(0, grow, pick, 0)

    pl.semaphore_wait(barrier, n_dev - 1)
    share_start(ar1, dp, n_dp, dp_peer, s1, r1)

    def by_image(q, first, second):
        def rows_of(b, t, o):
            return graw[pl.ds(o * rpc + t * n_img + b, 8, stride=rpc), :]

        for t in range(tiles):
            sl = slice(t * LANES, (t + 1) * LANES)
            for i, b in enumerate((first, second)):
                for h in range(2):
                    v = jnp.concatenate([rows_of(b, t, h * 16), rows_of(b, t, h * 16 + 8)], axis=0)
                    gsend[q, i * 32 + h * 16 : i * 32 + h * 16 + 16, sl] = v.astype(BF16)
            v = jnp.concatenate([rows_of(first, t, 32), rows_of(second, t, 32)], axis=0)
            gsend[q, 64:80, sl] = v.astype(BF16)

    by_image(0, sib, xs)
    g_sib = remote(gsend.at[0], gsx, sg.at[0], rg.at[0], {"chan": sib})
    g_sib.start()
    by_image(1, ch, xp)
    lane16 = iota((16, n_px), 1)
    row_of, col_of = lane16 >> 5, lane16 & (SIDE - 1)
    for b in range(n_img):
        mask[b] = jnp.where((row_of < side[b]) & (col_of < side[b]), 1.0, 0.0)

    out_x[pl.ds(n_rows, out_x.shape[0] - n_rows), :] = jnp.zeros((out_x.shape[0] - n_rows, LANES), F32)
    step_rows = 3 * rpc

    def widen(i, c):
        r = pl.ds(pl.multiple_of(i * step_rows, step_rows), step_rows)
        out_x[r, :] = feat[r, :].astype(F32)
        return c

    lax.fori_loop(0, n_rows // step_rows, widen, 0)

    g_sib.wait()
    gpair[...] = (gsend[1].astype(F32) + gsx[...].astype(F32)).astype(BF16)
    g_x = remote(gpair, grx, sg.at[1], rg.at[1], {"chan": xp})
    g_x.start()

    loads[7].wait()
    w2pad[...] = jnp.zeros(w2pad.shape, F32)
    w2wide[...] = jnp.zeros(w2wide.shape, F32)
    for t in range(9):
        w2pad[t, 0:grow, 0:grow] = w2v[t].astype(F32)
        tile, off = t * TAP // LANES, t * TAP % LANES
        v = pltpu.roll(w2pad[t], off, 1) if off else w2pad[t]
        lane = iota(v.shape, 1)
        here = slice(tile * LANES, (tile + 1) * LANES)
        w2wide[:, here] = w2wide[:, here] + jnp.where(lane >= off, v, 0.0)
        if off + grow > LANES:
            there = slice((tile + 1) * LANES, (tile + 2) * LANES)
            w2wide[:, there] = w2wide[:, there] + jnp.where(lane < off, v, 0.0)
    w2r[ch] = w2wide[...].astype(BF16)
    loads[5].wait()
    loads[6].wait()
    gsl[ch, 0:1, 0:grow] = gain2v[...]
    gsl[ch, 1:2, 0:grow] = bias2v[...]
    w_near = remote(w2r.at[ch], w2r.at[ch], sw.at[0], rw.at[0], {"chan": sib})
    w_far = remote(w2r.at[ch], w2r.at[ch], sw.at[1], rw.at[1], {"chan": xp})
    w_on = remote(w2r.at[xp], w2r.at[xp], sw.at[2], rw.at[2], {"chan": sib})
    w_far.start()
    w_near.start()
    share_start(gsl, ch, n_ch, ch_peer, sb, rb)

    loads[2].wait()
    w1s[...] = jnp.zeros(w1s.shape, BF16)
    w1s[0:n_d, 0:n_c] = w1v[...]
    rowbuf[...] = jnp.zeros(rowbuf.shape, F32)
    loads[3].wait()
    loads[4].wait()
    rowbuf[0:1, :] = gain1v[0:1, 0:LANES]
    rowbuf[1:2, 0 : n_c - LANES] = gain1v[0:1, LANES:n_c]
    rowbuf[2:3, :] = bias1v[0:1, 0:LANES]
    rowbuf[3:4, 0 : n_c - LANES] = bias1v[0:1, LANES:n_c]


    share_wait(ar1, dp, n_dp, dp_peer, s1, r1)
    tot1 = total(ar1)
    count = tot1[1:2, LANES - 1 : LANES]
    mean1, rstd1, scale1, keep1 = [], [], [], []
    for i in range(2):
        mean = tot1[i : i + 1] / count
        rstd = lax.rsqrt(tot1[2 + i : 3 + i] / count - mean * mean + EPS)
        here = lane1 + i * LANES
        ids = ch * n_c + here
        first = new_slot * grow
        keep = jnp.where(
            (here < n_c) & ((ids < first) | (ids >= first + grow)), 1.0, 0.0
        )
        scale = rstd * rowbuf[i : i + 1, :]
        shift = rowbuf[2 + i : 3 + i, :] - mean * scale
        size = c_sizes[i]
        r = pl.ds(i * LANES, size)
        col_a[r, :] = as_column(0.5 * scale * keep, size)
        col_b[r, :] = as_column(0.5 * shift * keep, size)
        mean1.append(mean)
        keep1.append(keep)
        rstd1.append(rstd)
        scale1.append(scale)

    def partial(j, first, n):
        def body(g, c):
            r = pl.ds(pl.multiple_of(g * 16, 16), 16)
            a, b = col_a[r, :], col_b[r, :]
            for t in range(first, first + n):
                sl = slice(t * LANES, (t + 1) * LANES)
                k = g * 16 * rpc + t * n_img + j
                v = jnp.concatenate([out_x[pl.ds(k + h * 8 * rpc, 8, stride=rpc), :] for h in range(2)], axis=0)
                xb[j, r, sl] = v.astype(BF16)
                v = v * a + b
                act[j, r, sl] = ((v * jnp.tanh(v) + v) * mask[j, :, sl]).astype(BF16)
            return c

        lax.fori_loop(0, cp // 16, body, 0)
        sl = slice(first * LANES, (first + n) * LANES)
        part[j, :, sl] = jnp.dot(w1s[...], act[j, :, sl], preferred_element_type=F32)

    rows_d = pl.ds(0, d8)
    unit = tiles // sum(SPANS)
    edges = [sum(SPANS[:p]) * unit for p in range(PIECES + 1)]

    def lanes_of(p):
        return pl.ds(edges[p] * LANES, (edges[p + 1] - edges[p]) * LANES)

    def tiles_of(p):
        return [slice(t * LANES, (t + 1) * LANES) for t in range(edges[p], edges[p + 1])]

    blocks, rest = d8 // 64, d8 // 64 * 64
    plain = blocks * 40

    def code(read, p, words, tops):
        top = jnp.maximum(jnp.max(row_top[...], axis=1, keepdims=True), 1e-30)
        row_scale[...] = jnp.broadcast_to(LEVELS / top, (d8, LANES))

        def quantized(first, n, sl):
            r = pl.ds(pl.multiple_of(first, 8), n)
            return jnp.round(read(r, sl) * row_scale[r, :]).astype(jnp.int32)

        def block(i, c):
            for t, sl in enumerate(tiles_of(p), edges[p]):
                high = jnp.zeros((8, LANES), jnp.int32)
                for k in range(4):
                    first = quantized(i * 64 + k * 8, 8, sl)
                    second = quantized(i * 64 + 32 + k * 8, 8, sl)
                    words[t, pl.ds(pl.multiple_of(i * 40 + k * 8, 8), 8), :] = (first << 12) | (second & 0xFFF)
                    high = high | (((second >> 12) & 0xFF) << (8 * k))
                words[t, pl.ds(pl.multiple_of(i * 40 + 32, 8), 8), :] = high
            return c

        lax.fori_loop(0, blocks, block, 0)
        for t, sl in enumerate(tiles_of(p), edges[p]):
            words[t, plain : plain + d8 - rest, :] = quantized(rest, d8 - rest, sl)
        tops[p, 0:1, :] = as_row(top[0:LANES])
        tops[p, 1:2, :] = as_row(top[LANES:d8])

    def unscale(tops, p):
        top = jnp.concatenate([as_column(tops[p, 0:1, :], LANES), as_column(tops[p, 1:2, :], d8 - LANES)], axis=0)
        row_scale[...] = top * (1.0 / LEVELS)

    def uncode(write, p, words):
        def put(first, n, sl, q):
            r = pl.ds(pl.multiple_of(first, 8), n)
            write(r, sl, q.astype(F32) * row_scale[r, :])

        def block(i, c):
            for t, sl in enumerate(tiles_of(p), edges[p]):
                high = words[t, pl.ds(pl.multiple_of(i * 40 + 32, 8), 8), :]
                for k in range(4):
                    low = words[t, pl.ds(pl.multiple_of(i * 40 + k * 8, 8), 8), :]
                    put(i * 64 + k * 8, 8, sl, low >> 12)
                    put(i * 64 + 32 + k * 8, 8, sl, (((high << (24 - 8 * k)) >> 24) << 12) | (low & 0xFFF))
            return c

        lax.fori_loop(0, blocks, block, 0)
        for t, sl in enumerate(tiles_of(p), edges[p]):
            put(rest, d8 - rest, sl, words[t, plain : plain + d8 - rest, :])

    def top_of(values):
        value = jnp.abs(values[0])
        for other in values[1:]:
            value = jnp.maximum(value, jnp.abs(other))
        return value

    def piece_of(j, p):
        partial(j, edges[p], edges[p + 1] - edges[p])

    def over(p):
        at = lanes_of(p)
        return remote(part.at[xs, rows_d, at], rx_a.at[rows_d, at], sp.at[p], rp.at[p], {"chan": sib})

    to_x = []
    piece_of(xs, 0)
    over(0).start()
    piece_of(xp, 0)
    for p in range(PIECES):
        if p + 1 < PIECES:
            piece_of(xs, p + 1)
            over(p + 1).start()
        over(p).wait()

        def add_a(g, c):
            r = pl.ds(pl.multiple_of(g * 8, 8), 8)
            values = [part[xp, r, sl] + rx_a[r, sl] for sl in tiles_of(p)]
            for sl, v in zip(tiles_of(p), values):
                part[xp, r, sl] = v
            row_top[r, :] = top_of(values)
            return c

        lax.fori_loop(0, d8 // 8, add_a, 0)
        code(lambda r, sl: part[xp, r, sl], p, px_out, tx_out)
        at = pl.ds(edges[p], edges[p + 1] - edges[p])
        copies = [
            remote(tx_out.at[p], tx_in.at[p], sq.at[0, p], rq.at[0, p], {"chan": xp}),
            remote(px_out.at[at], px_in.at[at], sq.at[1, p], rq.at[1, p], {"chan": xp}),
        ]
        for copy in copies:
            copy.start()
        to_x.append(copies)
        if p + 1 < PIECES:
            piece_of(xp, p + 1)
    for i in range(2):
        r = pl.ds(i * LANES, c_sizes[i])
        col_m[r, :] = as_column(mean1[i], c_sizes[i])
        col_k[r, :] = as_column(keep1[i], c_sizes[i])
    partial(sib, 0, tiles)
    to_sib_b = remote(part.at[sib, rows_d], rx_b.at[rows_d], sx.at[0], rxs.at[0], {"chan": sib})
    to_sib_b.start()
    partial(ch, 0, tiles)

    g_x.wait()
    px = iota((TAP, n_px), 1)
    py, pxx = px >> 5, px & (SIDE - 1)
    gcur[40:TAP, :] = jnp.zeros((TAP - 40, n_px), F32)
    for i in range(2):
        mine, theirs = slice(i * 32, i * 32 + 32), slice(32 - i * 32, 64 - i * 32)
        gcur[0:32, :] = gpair[mine, :].astype(F32) + grx[theirs, :].astype(F32)
        tails, others = gpair[64:80, :].astype(F32), grx[64:80, :].astype(F32)
        gcur[32:40, :] = tails[i * 8 : i * 8 + 8] + others[8 - i * 8 : 16 - i * 8]
        for ky in range(3):
            for kx in range(3):
                shift = (ky - 1) * SIDE + (kx - 1)
                t = ky * 3 + kx
                v = gcur[...]
                if shift != 0:
                    v = pltpu.roll(v, shift % n_px, 1)
                ok = None
                for off, pos in ((ky - 1, py), (kx - 1, pxx)):
                    if off == 1:
                        test = pos >= 1
                    elif off == -1:
                        test = pos <= SIDE - 2
                    else:
                        continue
                    ok = test if ok is None else ok & test
                if ok is not None:
                    v = jnp.where(ok, v, 0.0)
                g9[i, t * TAP : (t + 1) * TAP, :] = v.astype(BF16)
        g9[i, pl.ds(9 * TAP, TAPS - 9 * TAP), :] = jnp.zeros((TAPS - 9 * TAP, n_px), BF16)
    def slopes(j):
        def body(g, c):
            r = pl.ds(pl.multiple_of(g * 16, 16), 16)
            a, b = col_a[r, :], col_b[r, :]
            k = 0.5 * col_k[r, :]
            for t in range(tiles):
                sl = slice(t * LANES, (t + 1) * LANES)
                v = xb[j, r, sl].astype(F32) * a + b
                th = jnp.tanh(v)
                slope[j, r, sl] = ((1.0 + th) * (1.0 + v * (1.0 - th))) * (mask[j, :, sl] * k)
            return c

        lax.fori_loop(0, cp // 16, body, 0)


    to_sib_b.wait()
    sum_a[...] = jnp.zeros(sum_a.shape, F32)
    sum_b[...] = jnp.zeros(sum_b.shape, F32)
    hid[:, d8:dpad, :] = jnp.zeros((2, dpad - d8, n_px), F32)
    gp2[...] = jnp.zeros(gp2.shape, F32)

    def across(p):
        at = pl.ds(edges[p], edges[p + 1] - edges[p])
        return [
            remote(th_out.at[p], th_in.at[p], sh.at[0, p], rh.at[0, p], {"chan": xp}),
            remote(ph_out.at[at], ph_in.at[at], sh.at[1, p], rh.at[1, p], {"chan": xp}),
        ]

    def start_across(p):
        for copy in across(p):
            copy.start()

    for p in range(PIECES):
        for copy in to_x[p]:
            copy.wait()
        unscale(tx_in, p)

        def gather(r, sl, v):
            hid[0, r, sl] = (part[ch, r, sl] + rx_b[r, sl]) + v

        uncode(gather, p, px_in)

        def sums(g, c):
            r = pl.ds(pl.multiple_of(g * 8, 8), 8)
            s_acc, q_acc = sum_a[r, :], sum_b[r, :]
            values = [hid[0, r, sl] for sl in tiles_of(p)]
            for v in values:
                s_acc = s_acc + v
                q_acc = q_acc + v * v
            sum_a[r, :] = s_acc
            sum_b[r, :] = q_acc
            tops_h[p, r, :] = top_of(values)
            return c

        lax.fori_loop(0, d8 // 8, sums, 0)
        if p < AHEAD:
            row_top[...] = tops_h[p]
            code(lambda r, sl: hid[0, r, sl], p, ph_out, th_out)
            start_across(p)

    def pack(slots):
        s, q = as_rows(sum_a[0:d8, :], d_sizes), as_rows(sum_b[0:d8, :], d_sizes)
        slots[me, 0:1, :] = s[0]
        slots[me, 1:2, :] = s[1]
        slots[me, 2:3, :] = q[0]
        slots[me, 3:4, :] = q[1]

    def columns_d(row0, row1):
        tail = jnp.zeros((dpad - d8, LANES), F32)
        return jnp.concatenate(
            [as_column(row0, LANES), as_column(row1, d8 - LANES), tail], axis=0
        )

    pack(ar2)
    share_start(ar2, me, n_dev, dev_peer, s2, r2)
    for p in range(AHEAD, PIECES):
        row_top[...] = tops_h[p]
        code(lambda r, sl: hid[0, r, sl], p, ph_out, th_out)
        start_across(p)

    w_far.wait()
    w_on.start()
    slopes(xs)
    slopes(xp)
    w_near.wait()
    w_on.wait()
    share_wait(gsl, ch, n_ch, ch_peer, sb, rb)
    acc = jnp.zeros((dpad, w2b.shape[1]), F32)
    for j in range(n_ch):
        rows = iota((dpad, TAP), 0)
        cols = iota((dpad, TAP), 1)
        place = jnp.where((rows == cols + j * grow) & (cols < grow), 1.0, 0.0).astype(BF16)
        acc = acc + jnp.dot(place, w2r[j], preferred_element_type=F32)
    w2b[...] = acc.astype(BF16)
    for i in range(2):
        back[i] = jnp.dot(w2b[...], g9[i], preferred_element_type=F32)
    rows = iota((dpad, LANES), 0)
    cols = iota((dpad, LANES), 1)
    gain2c = jnp.zeros((dpad, 1), F32)
    bias2c = jnp.zeros((dpad, 1), F32)
    for j in range(n_ch):
        place = (rows == cols + j * grow) & (cols < grow)
        gain2c = gain2c + jnp.sum(jnp.where(place, gsl[j, 0:1, :], 0.0), axis=1, keepdims=True)
        bias2c = bias2c + jnp.sum(jnp.where(place, gsl[j, 1:2, :], 0.0), axis=1, keepdims=True)
    col_c[0] = jnp.broadcast_to(gain2c, (dpad, LANES))
    col_c[1] = jnp.broadcast_to(bias2c, (dpad, LANES))

    def widen_cot(i, c):
        r = pl.ds(pl.multiple_of(i * step_rows, step_rows), step_rows)
        k = [jnp.broadcast_to(col_k[pl.ds(i * 3 + n, 1), :], (rpc, LANES)) for n in range(3)]
        base[r, :] = cot[r, :].astype(F32) * jnp.concatenate(k, axis=0)
        return c

    lax.fori_loop(0, n_rows // step_rows, widen_cot, 0)

    share_wait(ar2, me, n_dev, dev_peer, s2, r2)
    tot2 = total(ar2)
    mean2 = [tot2[i : i + 1] / count for i in range(2)]
    rstd2 = [lax.rsqrt(tot2[2 + i : 3 + i] / count - mean2[i] * mean2[i] + EPS) for i in range(2)]
    mean2c = columns_d(*mean2)
    rstd2c = columns_d(*rstd2)
    scale2c = rstd2c * col_c[0]
    col_c[2] = mean2c
    col_c[3] = rstd2c
    col_c[4] = scale2c
    col_c[5] = 0.5 * scale2c
    col_c[6] = 0.5 * (col_c[1] - mean2c * scale2c)

    def second(g, c):
        r = pl.ds(pl.multiple_of(g * 16, 16), 16)
        a, b, m = col_c[5, r, :], col_c[6, r, :], col_c[2, r, :]
        s_acc = jnp.zeros((16, LANES), F32)
        q_acc = jnp.zeros((16, LANES), F32)
        for t in range(tiles):
            sl = slice(t * LANES, (t + 1) * LANES)
            h = hid[0, r, sl]
            mk = mask[ch, :, sl]
            v = h * a + b
            th = jnp.tanh(v)
            act2[r, sl] = ((v * th + v) * mk).astype(BF16)
            gp = (0.5 * mk) * ((1.0 + th) * (1.0 + v * (1.0 - th))) * back[0, r, sl]
            gp2[0, r, sl] = gp
            s_acc = s_acc + gp
            q_acc = q_acc + gp * (h - m)
        sum_a[r, :] = s_acc
        sum_b[r, :] = q_acc
        return c

    lax.fori_loop(0, dpad // 16, second, 0)
    pack(ar3)
    share_start(ar3, me, n_dev, dev_peer, s3, r3)

    w2acc[...] = lax.dot_general(
        act2[...], g9[0], (((1,), (1,)), ((), ())), preferred_element_type=F32
    )
    for j in range(n_ch):
        for lt in range(4):
            sl = slice(lt * LANES, (lt + 1) * LANES)
            cw[j, lt * 32 : lt * 32 + 32, :] = w2acc[j * grow : j * grow + 32, sl]
            cw[j, 128 + lt : 129 + lt, :] = w2acc[j * grow + 32 : j * grow + 33, sl]
        cw[j, 132:136, :] = jnp.zeros((4, LANES), F32)
    w_sib = [
        remote(cw.at[xs], cwr.at[1], sc.at[0], rc.at[0], {"chan": sib}),
        remote(cw.at[sib], cwr.at[0], sc.at[1], rc.at[1], {"chan": sib}),
    ]
    for copy in w_sib:
        copy.start()

    def second_other(p):
        for copy in across(p):
            copy.wait()
        unscale(th_in, p)

        def keep_hidden(r, sl, v):
            hid[1, r, sl] = v

        uncode(keep_hidden, p, ph_in)

        def body(g, c):
            r = pl.ds(pl.multiple_of(g * 16, 16), 16)
            a, b = col_c[5, r, :], col_c[6, r, :]
            for sl in tiles_of(p):
                v = hid[1, r, sl] * a + b
                th = jnp.tanh(v)
                gp2[1, r, sl] = (
                    (0.5 * mask[xp, :, sl]) * ((1.0 + th) * (1.0 + v * (1.0 - th))) * back[1, r, sl]
                )
            return c

        lax.fori_loop(0, dpad // 16, body, 0)

    zbuf[...] = lax.dot_general(
        w2b[...], act2[...], (((0,), (0,)), ((), ())), preferred_element_type=F32
    )
    new = jnp.zeros((TAP, n_px), F32)
    for ky in range(3):
        for kx in range(3):
            shift = (ky - 1) * SIDE + (kx - 1)
            t = ky * 3 + kx
            v = zbuf[t * TAP : (t + 1) * TAP, :]
            if shift != 0:
                v = pltpu.roll(v, (-shift) % n_px, 1)
            ok = None
            for off, pos in ((ky - 1, py), (kx - 1, pxx)):
                if off == -1:
                    test = pos >= 1
                elif off == 1:
                    test = pos <= SIDE - 2
                else:
                    continue
                ok = test if ok is None else ok & test
            if ok is not None:
                v = jnp.where(ok, v, 0.0)
            new = new + v
    new = new * jnp.concatenate([mask[ch]] * (TAP // 16), axis=0)
    gall[ch] = new[0 : gall.shape[1]]
    for copy in w_sib:
        copy.wait()
    cw[xp] = cw[xp] + cwr[1]
    cw[ch] = cw[ch] + cwr[0]
    w_x = remote(cw.at[xp], cwx, sc.at[2], rc.at[2], {"chan": xp})
    w_x.start()
    new_sib = remote(gall.at[ch], gall.at[ch], so.at[0], ro.at[0], {"chan": sib})
    new_xp = remote(gall.at[ch], gall.at[ch], so.at[1], ro.at[1], {"chan": xp})
    new_on = remote(gall.at[xp], gall.at[xp], so.at[2], ro.at[2], {"chan": sib})
    new_xp.start()
    new_sib.start()
    slopes(sib)
    slopes(ch)
    for p in range(PIECES):
        second_other(p)

    w1acc[...] = jnp.zeros(w1acc.shape, F32)
    sum_a[...] = jnp.zeros(sum_a.shape, F32)
    sum_b[...] = jnp.zeros(sum_b.shape, F32)
    share_wait(ar3, me, n_dev, dev_peer, s3, r3)
    tot3 = total(ar3)
    gain_sum2 = [tot3[2 + i : 3 + i] * rstd2[i] for i in range(2)]
    bias_sum2 = [tot3[i : i + 1] for i in range(2)]
    gain_sum2c = columns_d(*gain_sum2)
    bias_sum2c = columns_d(*bias_sum2)
    col_c[7] = col_c[4] * bias_sum2c / count
    col_c[8] = col_c[4] * col_c[3] * gain_sum2c / count

    def third(i, j, k):
        def body(g, c):
            r = pl.ds(pl.multiple_of(g * 16, 16), 16)
            c1, c2, c3, m = col_c[4, r, :], col_c[7, r, :], col_c[8, r, :], col_c[2, r, :]
            for sl in [slice(t * LANES, (t + 1) * LANES) for t in range(k * tiles // 2, (k + 1) * tiles // 2)]:
                gha[j, r, sl] = (
                    c1 * gp2[i, r, sl] - mask[j, :, sl] * (c2 + c3 * (hid[i, r, sl] - m))
                ).astype(BF16)
            return c

        lax.fori_loop(0, dpad // 16, body, 0)

    grads = []
    for i, j in ((0, ch), (1, xp)):
        for k in range(2):
            third(i, j, k)
            at = pl.ds(k * (n_px // 2), n_px // 2)
            copy = remote(gha.at[j, :, at], gha.at[j, :, at], st.at[i, k], rt.at[i, k], {"chan": sib})
            copy.start()
            grads.append(copy)


    def weight_grad(j, k=None):
        at = slice(0, n_px) if k is None else slice(k * (n_px // 2), (k + 1) * (n_px // 2))
        w1acc[0:dpad, 0:cp] = w1acc[0:dpad, 0:cp] + lax.dot_general(
            gha[j, :, at], act[j, :, at], (((1,), (1,)), ((), ())), preferred_element_type=F32
        )

    def input_grad(j):
        gact[...] = lax.dot_general(
            w1s[...], gha[j], (((0,), (0,)), ((), ())), preferred_element_type=F32
        )

        def body(g, c):
            r = pl.ds(pl.multiple_of(g * 16, 16), 16)
            m = col_m[r, :]
            s_acc, q_acc = sum_a[r, :], sum_b[r, :]
            for t in range(tiles):
                sl = slice(t * LANES, (t + 1) * LANES)
                gp = gact[r, sl] * slope[j, r, sl]
                gp1[j, r, sl] = gp
                s_acc = s_acc + gp
                q_acc = q_acc + gp * (xb[j, r, sl].astype(F32) - m)
            sum_a[r, :] = s_acc
            sum_b[r, :] = q_acc
            return c

        lax.fori_loop(0, cp // 16, body, 0)

    weight_grad(ch)
    weight_grad(xp)
    w_x.wait()
    for i, j in ((0, sib), (1, xs)):
        for k in range(2):
            grads[2 * i + k].wait()
            weight_grad(j, k)

    for r in range(17):
        cb[r // 5, r % 5 * 8 : r % 5 * 8 + 8, :] = w1acc[r * 8 : r * 8 + 8, 0:LANES]
    for k in range(6):
        v = w1acc[k * 8 : k * 8 + 8, LANES : 2 * LANES]
        for i in range(1, 3):
            v = v + pltpu.roll(w1acc[i * 48 + k * 8 : i * 48 + k * 8 + 8, LANES : 2 * LANES], 40 * i, 1)
        r = 17 + k
        cb[r // 5, r % 5 * 8 : r % 5 * 8 + 8, :] = v
    for k in range(17):
        r = 23 + k
        cb[r // 5, r % 5 * 8 : r % 5 * 8 + 8, :] = cw[ch, k * 8 : k * 8 + 8, :] + cwx[k * 8 : k * 8 + 8, :]

    def encode(v):
        top = jnp.maximum(jnp.max(jnp.abs(v), axis=0, keepdims=True), 1e-30)
        power = jnp.floor(jnp.log2(top) + 1.0001)
        q = jnp.clip(jnp.round(v * jnp.exp2(15.0 - power)), -32767.0, 32767.0).astype(jnp.int32)
        low = jnp.concatenate([q[24:40], jnp.broadcast_to(power.astype(jnp.int32), (8, LANES))], axis=0)
        return (q[0:24] << 16) | (low & 0xFFFF)

    def decode(w):
        high, low = w >> 16, (w << 16) >> 16
        scale = jnp.exp2(low[16:24].astype(F32) - 15.0)
        q = jnp.concatenate([high, low[0:16]], axis=0).astype(F32)
        return q * jnp.concatenate([scale] * 5, axis=0)

    def encode_part(v):
        top = jnp.maximum(jnp.max(jnp.abs(v), axis=0, keepdims=True), 1e-30)
        power = jnp.floor(jnp.log2(top) + 1.0001)
        q = jnp.clip(jnp.round(v * jnp.exp2(23.0 - power)), -8388607.0, 8388607.0).astype(jnp.int32)
        extra = q[32:40]
        power = jnp.broadcast_to(jnp.clip(power, -127.0, 127.0).astype(jnp.int32), (8, LANES))
        spare = jnp.concatenate([extra, extra >> 8, extra >> 16, power], axis=0) & 0xFF
        return (q[0:32] << 8) | spare

    def decode_part(w):
        spare = w & 0xFF
        extra = spare[0:8] | (spare[8:16] << 8) | (((w[16:24] << 24) >> 24) << 16)
        scale = jnp.exp2(((w[24:32] << 24) >> 24).astype(F32) - 23.0)
        return jnp.concatenate([w >> 8, extra], axis=0).astype(F32) * jnp.concatenate([scale] * 5, axis=0)

    for q in range(OWNERS):
        coded[q] = encode_part(cb[q])
    stride = n_dp // OWNERS
    my_part = dp // stride
    is_owner = lax.rem(dp, stride) == 0

    def part_to(k):
        q = my_part ^ (OWNERS - 1 - k)
        return q, q * stride

    def push(k, c):
        q, to = part_to(k)

        @pl.when(to != dp)
        def _():
            remote(coded.at[q], rsl.at[dp], sr.at[k], rr.at[dp], {"dp": to}).start()

        return c

    lax.fori_loop(0, OWNERS, push, 0)
    d_rows, d_cols = iota((dpad, LANES), 0), iota((dpad, LANES), 1)
    here_d = (d_rows == d_cols + ch * grow) & (d_cols < grow)
    out_g2[...] = jnp.sum(jnp.where(here_d, gain_sum2c, 0.0), axis=0, keepdims=True)[:, 0:grow]
    out_b2[...] = jnp.sum(jnp.where(here_d, bias_sum2c, 0.0), axis=0, keepdims=True)[:, 0:grow]
    for j in (ch, xp, sib, xs):
        input_grad(j)
    s4_, q4_ = as_rows(sum_a[...], c_sizes), as_rows(sum_b[...], c_sizes)
    for i in range(2):
        ar4[dp, i : i + 1, :] = s4_[i]
        ar4[dp, 2 + i : 3 + i, :] = q4_[i]
    share_start(ar4, dp, n_dp, dp_peer, s4, r4)

    def scatter(g, c):
        first = g * 16 * rpc
        r = pl.ds(pl.multiple_of(g * 16, 16), 16)
        for b in range(n_img):
            for t in range(tiles):
                v = gp1[b, r, t * LANES : (t + 1) * LANES]
                for h in range(2):
                    at = pl.ds(first + h * 8 * rpc + t * n_img + b, 8, stride=rpc)
                    out_g[at, :] = v[h * 8 : h * 8 + 8]
        return c

    lax.fori_loop(0, 5, scatter, 0)

    def push_wait(k, c):
        q, to = part_to(k)

        @pl.when(to != dp)
        def _():
            remote(coded.at[q], rsl.at[dp], sr.at[k], rr.at[dp], {"dp": to}).wait_send()

        return c

    def pull(k, c):
        src = lax.rem(dp + k, n_dp)
        remote(coded.at[0], rsl.at[src], sr.at[0], rr.at[src], {"dp": src}).wait_recv()
        return c

    @pl.when(is_owner)
    def _():
        lax.fori_loop(1, n_dp, pull, 0)
        v = cb[my_part]
        for k in range(1, n_dp):
            v = v + decode_part(rsl[lax.rem(dp + k, n_dp)])
        fin[my_part] = encode(v)

        def give(k):
            remote(fin.at[my_part], fin.at[my_part], sa.at[k], ra.at[my_part], dp_peer(k)).start()

        far_first(n_dp, give)

    lax.fori_loop(0, OWNERS, push_wait, 0)
    new_xp.wait()
    new_on.start()
    lax.fori_loop(5, cp // 16, scatter, 0)

    for i in range(2):
        col_a[pl.ds(i * LANES, c_sizes[i]), :] = as_column(scale1[i], c_sizes[i])

    new_sib.wait()
    new_on.wait()
    for b in range(n_img):
        for t in range(tiles):
            for h in range(gall.shape[1] // 8):
                out_new[pl.ds(h * 8 * rpc + t * n_img + b, 8, stride=rpc), :] = gall[
                    b, h * 8 : h * 8 + 8, t * LANES : (t + 1) * LANES
                ]
    out_slot[...] = (slot_of - ch * per_device)[0:8].astype(F32)

    share_wait(ar4, dp, n_dp, dp_peer, s4, r4)
    tot4 = total(ar4)
    for i in range(2):
        bias_sum = tot4[i : i + 1]
        gain_sum = tot4[2 + i : 3 + i] * rstd1[i]
        size = c_sizes[i]
        r = pl.ds(i * LANES, size)
        k1 = -scale1[i] * rstd1[i] * gain_sum / count
        k0 = -scale1[i] * bias_sum / count - k1 * mean1[i]
        col_b[r, :] = as_column(k0, size)
        col_m[r, :] = as_column(k1, size)
        width = min(LANES, n_c - i * LANES)
        out_g1[0:1, i * LANES : i * LANES + width] = gain_sum[:, 0:width]
        out_b1[0:1, i * LANES : i * LANES + width] = bias_sum[:, 0:width]
    mask_of = mask_raw[...]

    def last(i, c):
        for k in range(5):
            row = i * 5 + k
            at = pl.ds(pl.multiple_of(row * rpc, rpc), rpc)
            k0 = jnp.broadcast_to(col_b[pl.ds(row, 1), :], (rpc, LANES))
            k1 = jnp.broadcast_to(col_m[pl.ds(row, 1), :], (rpc, LANES))
            a = jnp.broadcast_to(col_a[pl.ds(row, 1), :], (rpc, LANES))
            out_g[at, :] = base[at, :] + a * out_g[at, :] + mask_of * (k0 + k1 * out_x[at, :])
        return c

    lax.fori_loop(0, n_c // 5, last, 0)

    for wait in still_sent:
        wait()

    @pl.when(is_owner)
    def _():
        def gave(k, c):
            remote(fin.at[my_part], fin.at[my_part], sa.at[k], ra.at[my_part], dp_peer(k)).wait_send()
            return c

        lax.fori_loop(1, n_dp, gave, 0)

    def take(q, c):
        @pl.when(q * stride != dp)
        def _():
            remote(fin.at[q], fin.at[q], sa.at[0], ra.at[q], {"dp": q * stride}).wait_recv()

        return c

    lax.fori_loop(0, OWNERS, take, 0)
    for q in range(OWNERS):
        cb[q] = decode(fin[q])
    for r in range(17):
        height = min(8, n_d - r * 8)
        out_w1[r * 8 : r * 8 + height, 0:LANES] = cb[r // 5, r % 5 * 8 : r % 5 * 8 + height, :]
    for k in range(6):
        r = 17 + k
        v = cb[r // 5, r % 5 * 8 : r % 5 * 8 + 8, :]
        for i in range(3):
            row = i * 48 + k * 8
            height = min(8, n_d - row)
            if height > 0:
                u = v if i == 0 else pltpu.roll(v, LANES - 40 * i, 1)
                out_w1[row : row + height, LANES:n_c] = u[0:height, 0 : n_c - LANES]
    for k in range(17):
        r = 23 + k
        v = cb[r // 5, r % 5 * 8 : r % 5 * 8 + 8, :]
        if k < 16:
            w2acc[k % 4 * 8 : k % 4 * 8 + 8, k // 4 * LANES : (k // 4 + 1) * LANES] = v
        else:
            for lt in range(4):
                w2acc[32:33, lt * LANES : (lt + 1) * LANES] = v[lt : lt + 1]
    v = w2acc[0:40, :]
    for t in range(9):
        u = v if t == 0 else pltpu.roll(v, TAPS - t * TAP, 1)
        out_w2[t] = u[0:grow, 0:grow]


def finish(n_rows, grow_rows, *refs):
    n = (len(refs) - 3) // 2
    new, slot = refs[n : n + 2]
    outs, sem = refs[n + 2 : -1], refs[-1]
    segments = n_rows // grow_rows
    copies = [pltpu.make_async_copy(refs[1].at[pl.ds(0, n_rows)], outs[1], sem.at[1])]
    copies += [pltpu.make_async_copy(refs[i], outs[i], sem.at[i]) for i in range(2, n)]
    for copy in copies:
        copy.start()
    here = jnp.max(slot[...])
    for k in range(segments):
        at = pl.ds(k * grow_rows, grow_rows)
        kept = pltpu.make_async_copy(refs[0].at[at], outs[0].at[at], sem.at[n + k])
        grown = pltpu.make_async_copy(new.at[pl.ds(0, grow_rows)], outs[0].at[at], sem.at[n + k])
        pl.when(here == k)(grown.start)
        pl.when(here != k)(kept.start)
        copies.append(kept)
    for copy in copies:
        copy.wait()


def flat(values):
    n, c, p = values.shape
    return (
        values.transpose(1, 0, 2).reshape(c, n, p // LANES, LANES).transpose(0, 2, 1, 3).reshape(-1, LANES)
    )


def unflat(rows, n, c, p):
    return rows.reshape(c, p // LANES, n, LANES).transpose(0, 2, 1, 3).reshape(c, n, p).transpose(1, 0, 2)


def on_device(
    n_dp, n_ch, features, gain1, bias1, weight1, gain2, bias2, weight2, cotangent, image_side, block_slot
):
    n_img, n_c, n_px = features.shape
    n_d = weight1.shape[1]
    grow = weight2.shape[3]
    cp = pad_to(n_c, 16)
    dpad = pad_to(n_d, 16)
    d8 = pad_to(n_d, 8)
    rpc = n_px // LANES * n_img
    n_rows, n_pad = n_c * rpc, cp * rpc
    n_dev = n_dp * n_ch
    words = d8 // 64 * 40 + d8 % 64
    cfg = (n_dp, n_ch, n_img, n_c, n_px, n_d, grow)
    args = (
        flat(features),
        flat(cotangent),
        weight1.T,
        gain1.reshape(1, -1),
        bias1.reshape(1, -1),
        gain2.reshape(1, -1),
        bias2.reshape(1, -1),
        weight2.reshape(9, grow, grow),
        image_side,
        block_slot,
    )
    args = [pltpu.with_memory_space_constraint(v, pltpu.HBM) for v in args]
    sd = jax.ShapeDtypeStruct
    in_vmem = pl.BlockSpec(memory_space=pltpu.VMEM)
    in_hbm = pl.BlockSpec(memory_space=pltpu.HBM)
    dma = pltpu.SemaphoreType.DMA
    v = pltpu.VMEM
    scratch = [
        v((n_rows, LANES), BF16), v((n_rows, LANES), BF16), v((n_d, n_c), BF16),
        v((1, n_c), F32), v((1, n_c), F32), v((1, grow), F32), v((1, grow), F32),
        v((9, grow, grow), BF16), pltpu.SMEM(image_side.shape, jnp.int32), pltpu.SMEM(block_slot.shape, jnp.int32),
        v((n_img, 16, n_px), F32), v((rpc, LANES), F32), v((n_rows, LANES), F32),
        v((n_img, cp, n_px), BF16), v((n_img, cp, n_px), BF16),
        v((n_img, cp, n_px), F32), v((n_img, cp, n_px), F32), v((cp, n_px), F32),
        v((cp, LANES), F32), v((cp, LANES), F32), v((cp, LANES), F32), v((cp, LANES), F32),
        v((9, dpad, LANES), F32), v((cp, LANES), F32), v((cp, LANES), F32),
        v((8, LANES), F32),
        v((dpad, cp), BF16), v((n_img, dpad, n_px), F32),
        v((dpad, n_px), F32), v((dpad, n_px), F32), v((2, dpad, n_px), F32),
        v((d8, LANES), F32), v((d8, LANES), F32), v((PIECES, d8, LANES), F32),
        v((n_px // LANES, words, LANES), jnp.int32), v((n_px // LANES, words, LANES), jnp.int32), v((PIECES, 2, LANES), F32), v((PIECES, 2, LANES), F32),
        v((n_px // LANES, words, LANES), jnp.int32), v((n_px // LANES, words, LANES), jnp.int32), v((PIECES, 2, LANES), F32), v((PIECES, 2, LANES), F32),
        v((40 * rpc, LANES), F32), v((2, 80, n_px), BF16),
        v((80, n_px), BF16), v((80, n_px), BF16), v((80, n_px), BF16), v((TAP, n_px), F32),
        v((2, TAPS, n_px), BF16), v((9, TAP, LANES), F32), v((TAP, TAPS), F32), v((n_ch, TAP, TAPS), BF16), v((dpad, TAPS), BF16),
        v((n_ch, 2, LANES), F32),
        v((dpad, n_px), BF16), v((2, dpad, n_px), F32), v((2, dpad, n_px), F32), v((TAPS, n_px), F32),
        v((n_ch, 40, n_px), F32), v((n_ch, dpad, n_px), BF16),
        v((n_ch, 136, LANES), F32), v((2, 136, LANES), F32), v((136, LANES), F32),
        v((OWNERS, 40, LANES), F32), v((OWNERS, 32, LANES), jnp.int32),
        v((n_dp, 32, LANES), jnp.int32), v((OWNERS, 24, LANES), jnp.int32), v((dpad, 256), F32), v((dpad, TAPS), F32),
        v((n_dp, 4, LANES), F32), v((n_dev, 4, LANES), F32), v((n_dev, 4, LANES), F32), v((n_dp, 4, LANES), F32),
        dma((13,)),
        dma((n_dp,)), dma((n_dp,)), dma((n_dev,)), dma((n_dev,)), dma((n_dev,)), dma((n_dev,)), dma((n_dp,)), dma((n_dp,)),
        dma((3,)), dma((3,)), dma((PIECES,)), dma((PIECES,)), dma((2, PIECES)), dma((2, PIECES)),
        dma((2,)), dma((2,)), dma((n_ch,)), dma((n_ch,)), dma((n_ch,)), dma((n_ch,)),
        dma((2, PIECES)), dma((2, PIECES)), dma((2, 2)), dma((2, 2)), dma((3,)), dma((3,)), dma((3,)), dma((3,)),
        dma((OWNERS,)), dma((n_dp,)), dma((n_dp,)), dma((OWNERS,)),
    ]
    out_shape = (
        sd((n_pad, LANES), F32), sd((n_pad, LANES), F32), sd((n_d, n_c), F32),
        sd((1, n_c), F32), sd((1, n_c), F32), sd((9, grow, grow), F32), sd((1, grow), F32), sd((1, grow), F32),
        sd((40 * rpc, LANES), F32), sd((8, LANES), F32),
    )
    outs = pl.pallas_call(
        functools.partial(layer, cfg),
        out_shape=out_shape,
        in_specs=[in_hbm] * len(args),
        out_specs=(in_vmem,) * len(out_shape),
        scratch_shapes=scratch,
        compiler_params=pltpu.CompilerParams(
            collective_id=0, has_side_effects=True, vmem_limit_bytes=40 << 20
        ),
    )(*args)
    final = (sd((n_rows, LANES), F32),) * 2 + out_shape[2:-2]
    o = pl.pallas_call(
        functools.partial(finish, n_rows, grow * rpc),
        out_shape=final,
        in_specs=[in_vmem] * len(outs),
        out_specs=(in_hbm,) * len(final),
        scratch_shapes=[dma((len(final) + n_c // grow,))],
        compiler_params=pltpu.CompilerParams(vmem_limit_bytes=8 << 20),
    )(*outs)
    return (
        unflat(o[0], n_img, n_c, n_px),
        unflat(o[1], n_img, n_c, n_px),
        o[2].T,
        o[3].reshape(-1),
        o[4].reshape(-1),
        o[5].reshape(3, 3, grow, grow),
        o[6].reshape(-1),
        o[7].reshape(-1),
    )


def solution(mesh):
    in_specs = (
        P("dp", "chan", None),
        P("chan"),
        P("chan"),
        P("chan", None),
        P("chan"),
        P("chan"),
        P(None, None, "chan", None),
        P("dp", "chan", None),
        P("dp"),
        P(),
    )
    out_specs = (
        P("dp", "chan", None),
        P("dp", "chan", None),
        P("chan", None),
        P("chan"),
        P("chan"),
        P(None, None, "chan", None),
        P("chan"),
        P("chan"),
    )
    body = functools.partial(on_device, mesh.shape["dp"], mesh.shape["chan"])
    return jax.shard_map(body, mesh=mesh, in_specs=in_specs, out_specs=out_specs, check_vma=False)
```

```python
import functools

import jax
import jax.numpy as jnp
from jax import lax
from jax.experimental import pallas as pl
from jax.experimental.pallas import tpu as pltpu
from jax.sharding import PartitionSpec as P

SIDE = 32
EPS = 1e-05
LANES = 128
TAP = 48
TAPS = 512
SPANS = (1, 2, 3, 2)
PIECES = len(SPANS)
AHEAD = 2
LEVELS = 524000.0
OWNERS = 8

MESH = pl.DeviceIdType.MESH
F32 = jnp.float32
BF16 = jnp.bfloat16


def pad_to(size, unit):
    return (size + unit - 1) // unit * unit


def iota(shape, axis):
    return lax.broadcasted_iota(jnp.int32, shape, axis)


def as_row(column):
    n = column.shape[0]
    eye = iota((n, LANES), 0) == iota((n, LANES), 1)
    return jnp.sum(jnp.where(eye, column, 0.0), axis=0, keepdims=True)


def as_column(row, n):
    eye = iota((n, LANES), 0) == iota((n, LANES), 1)
    return jnp.broadcast_to(jnp.sum(jnp.where(eye, row, 0.0), axis=1, keepdims=True), (n, LANES))


def as_rows(values, sizes):
    column = jnp.sum(values, axis=1, keepdims=True)
    rows, start = [], 0
    for size in sizes:
        rows.append(as_row(column[start : start + size]))
        start += size
    return rows


def layer(
    cfg,
    feat_h, cot_h, w1_h, gain1_h, bias1_h, gain2_h, bias2_h, w2_h, side_h, slot_h,
    out_x, out_g, out_w1, out_g1, out_b1, out_w2, out_g2, out_b2, out_new, out_slot,
    feat, cot, w1v, gain1v, bias1v, gain2v, bias2v, w2v, side, slot,
    mask, mask_raw, base, xb, act, slope, gp1, gact,
    col_a, col_b, col_m, col_k, col_c, sum_a, sum_b, rowbuf,
    w1s, part, rx_a, rx_b, hid, row_top, row_scale, tops_h,
    px_out, px_in, tx_out, tx_in, ph_out, ph_in, th_out, th_in,
    graw, gsend, gsx, gpair, grx, gcur, g9, w2pad, w2wide, w2r, w2b, gsl,
    act2, gp2, back, zbuf, gall, gha,
    cw, cwr, cwx, cb, coded, rsl, fin, w1acc, w2acc,
    ar1, ar2, ar3, ar4,
    load_sem, s1, r1, s2, r2, s3, r3, s4, r4, sx, rxs, sp, rp, sq, rq, sg, rg, sw, rw, sb, rb, sh, rh, st, rt, so, ro, sc, rc, sr, rr, sa, ra,
):
    n_dp, n_ch, n_img, n_c, n_px, n_d, grow = cfg
    n_dev = n_dp * n_ch
    cp = xb.shape[1]
    dpad = w1s.shape[0]
    d8 = pad_to(n_d, 8)
    tiles = n_px // LANES
    rpc = tiles * n_img
    c_sizes = (LANES, cp - LANES)
    d_sizes = (LANES, d8 - LANES)
    dp = lax.axis_index("dp")
    ch = lax.axis_index("chan")
    me = dp * n_ch + ch
    half = n_ch // 2
    cx, cc = ch // half, lax.rem(ch, half)
    sib = cx * half + (1 - cc)
    xp = (1 - cx) * half + cc
    xs = (1 - cx) * half + (1 - cc)

    def dev_peer(k):
        q = me ^ k
        return {"dp": q // n_ch, "chan": lax.rem(q, n_ch)}

    def dp_peer(k):
        return {"dp": dp ^ k}

    def ch_peer(k):
        return {"chan": ch ^ k}

    def far_first(count, step):
        if count <= 32:
            for k in range(count - 1, 0, -1):
                step(k)
        else:

            def body(i, c):
                step(count - 1 - i)
                return c

            lax.fori_loop(0, count - 1, body, 0)

    loads = {
        i: pltpu.make_async_copy(h, v, load_sem.at[i])
        for i, (h, v) in enumerate(
            (
                (cot_h, cot), (w1_h, w1v), (gain1_h, gain1v), (bias1_h, bias1v),
                (gain2_h, gain2v), (bias2_h, bias2v), (w2_h, w2v), (side_h, side), (slot_h, slot),
            ),
            1,
        )
    }
    feat_groups, feat_parts, start = [], [], 0
    for k in range(3):
        groups = pad_to(n_c, 8) // 8 * (k + 1) // 3 - sum(feat_groups)
        size = min(groups * 8, n_c - start) * rpc
        at = pl.ds(start * rpc, size)
        feat_parts.append(pltpu.make_async_copy(feat_h.at[at], feat.at[at], load_sem.at[10 + k]))
        feat_groups.append(groups)
        start += groups * 8
    for copy in [loads[8], loads[9], *feat_parts, *(loads[i] for i in range(1, 8))]:
        copy.start()
    barrier = pltpu.get_barrier_semaphore()

    def greet(k):
        pl.semaphore_signal(barrier, inc=1, device_id=dev_peer(k), device_id_type=MESH)

    far_first(n_dev, greet)

    def remote(src, dst, send, recv, device):
        return pltpu.make_async_remote_copy(
            src_ref=src, dst_ref=dst, send_sem=send, recv_sem=recv, device_id=device, device_id_type=MESH
        )

    still_sent = []

    def share_start(slots, mine, count, peer, send, recv):
        def step(k):
            remote(slots.at[mine], slots.at[mine], send.at[k], recv.at[k], peer(k)).start()

        far_first(count, step)

    def share_wait(slots, mine, count, peer, send, recv):
        def step(k):
            remote(slots.at[mine], slots.at[mine], send.at[k], recv.at[k], peer(k)).wait_recv()

        def sent(k):
            remote(slots.at[mine], slots.at[mine], send.at[k], recv.at[k], peer(k)).wait_send()

        far_first(count, step)
        still_sent.append(lambda: far_first(count, sent))

    def total(slots):
        if slots.shape[0] <= 32:
            value = slots[0]
            for i in range(1, slots.shape[0]):
                value = value + slots[i]
            return value
        return lax.fori_loop(1, slots.shape[0], lambda i, v: v + slots[i], slots[0])

    loads[8].wait()
    loads[9].wait()
    row_r, lane_r = iota((rpc, LANES), 0), iota((rpc, LANES), 1)
    tile_of, image_of = row_r // n_img, row_r % n_img
    count_here = jnp.int32(0)
    side_of = jnp.zeros((rpc, LANES), jnp.int32)
    for b in range(n_img):
        count_here = count_here + side[b] * side[b]
        side_of = jnp.where(image_of == b, side[b], side_of)
    pixel_of = tile_of * LANES + lane_r
    mask_raw[...] = jnp.where((pixel_of // SIDE < side_of) & (pixel_of % SIDE < side_of), 1.0, 0.0)
    mask_of = mask_raw[...]
    n_rows = feat.shape[0]

    def halves(v):
        while v.shape[0] > 8:
            n = v.shape[0] // 2
            v = v[0:n] + v[n:]
        return v

    sub = iota((8, LANES), 0)

    def fold(values):
        for d in (4, 2, 1):
            half_n = len(values) // 2
            values = [
                jnp.where((sub & d) == 0, u + pltpu.roll(u, 8 - d, 0), v + pltpu.roll(v, d, 0))
                for u, v in zip(values[:half_n], values[half_n:])
            ]
        return values[0]

    def first_sums(g, c, n=8):
        s, q = [], []
        for k in range(n):
            v = feat[pl.ds(pl.multiple_of((g * 8 + k) * rpc, rpc), rpc), :].astype(F32)
            w = v * mask_of
            s.append(halves(w))
            q.append(halves(w * v))
        none = [jnp.zeros((8, LANES), F32)] * (8 - n)
        at = pl.ds(pl.multiple_of(g * 8, 8), 8)
        sum_a[at, :] = fold(s + none)
        sum_b[at, :] = fold(q + none)
        return c

    whole, done = n_c // 8, 0
    for k, groups in enumerate(feat_groups):
        feat_parts[k].wait()
        lax.fori_loop(done, min(done + groups, whole), first_sums, 0)
        done += groups
    if n_c % 8:
        first_sums(whole, 0, n_c % 8)
    spare = pl.ds(pad_to(n_c, 8), cp - pad_to(n_c, 8))
    sum_a[spare, :] = jnp.zeros((cp - pad_to(n_c, 8), LANES), F32)
    sum_b[spare, :] = jnp.zeros((cp - pad_to(n_c, 8), LANES), F32)
    lane1 = iota((1, LANES), 1)
    s0, sq0 = as_rows(sum_a[...], c_sizes), as_rows(sum_b[...], c_sizes)
    ar1[dp, 0:1, :] = s0[0]
    ar1[dp, 1:2, :] = jnp.where(lane1 == LANES - 1, count_here.astype(F32), s0[1])
    ar1[dp, 2:3, :] = sq0[0]
    ar1[dp, 3:4, :] = sq0[1]

    new_slot = slot[slot.shape[0] - 1]
    per_device = n_c // grow
    slot_of = iota((rpc, LANES), 0) * 0 + new_slot
    loads[1].wait()
    graw[grow * rpc : 40 * rpc, :] = jnp.zeros(((40 - grow) * rpc, LANES), F32)
    picks = [jnp.where(slot_of == ch * per_device + i, mask_of, 0.0) for i in range(per_device)]

    def pick(i, c):
        v = jnp.zeros((rpc, LANES), F32)
        for k in range(per_device):
            v = v + cot[pl.ds(pl.multiple_of((k * grow + i) * rpc, rpc), rpc), :].astype(F32) * picks[k]
        graw[pl.ds(pl.multiple_of(i * rpc, rpc), rpc), :] = v
        return c

    lax.fori_loop(0, grow, pick, 0)

    pl.semaphore_wait(barrier, n_dev - 1)
    share_start(ar1, dp, n_dp, dp_peer, s1, r1)

    def by_image(q, first, second):
        def rows_of(b, t, o):
            return graw[pl.ds(o * rpc + t * n_img + b, 8, stride=rpc), :]

        for t in range(tiles):
            sl = slice(t * LANES, (t + 1) * LANES)
            for i, b in enumerate((first, second)):
                for h in range(2):
                    v = jnp.concatenate([rows_of(b, t, h * 16), rows_of(b, t, h * 16 + 8)], axis=0)
                    gsend[q, i * 32 + h * 16 : i * 32 + h * 16 + 16, sl] = v.astype(BF16)
            v = jnp.concatenate([rows_of(first, t, 32), rows_of(second, t, 32)], axis=0)
            gsend[q, 64:80, sl] = v.astype(BF16)

    by_image(0, sib, xs)
    g_sib = remote(gsend.at[0], gsx, sg.at[0], rg.at[0], {"chan": sib})
    g_sib.start()
    by_image(1, ch, xp)
    lane16 = iota((16, n_px), 1)
    row_of, col_of = lane16 >> 5, lane16 & (SIDE - 1)
    for b in range(n_img):
        mask[b] = jnp.where((row_of < side[b]) & (col_of < side[b]), 1.0, 0.0)

    out_x[pl.ds(n_rows, out_x.shape[0] - n_rows), :] = jnp.zeros((out_x.shape[0] - n_rows, LANES), F32)
    step_rows = 3 * rpc

    def widen(i, c):
        r = pl.ds(pl.multiple_of(i * step_rows, step_rows), step_rows)
        out_x[r, :] = feat[r, :].astype(F32)
        return c

    lax.fori_loop(0, n_rows // step_rows, widen, 0)

    g_sib.wait()
    gpair[...] = (gsend[1].astype(F32) + gsx[...].astype(F32)).astype(BF16)
    g_x = remote(gpair, grx, sg.at[1], rg.at[1], {"chan": xp})
    g_x.start()

    loads[7].wait()
    w2pad[...] = jnp.zeros(w2pad.shape, F32)
    w2wide[...] = jnp.zeros(w2wide.shape, F32)
    for t in range(9):
        w2pad[t, 0:grow, 0:grow] = w2v[t].astype(F32)
        tile, off = t * TAP // LANES, t * TAP % LANES
        v = pltpu.roll(w2pad[t], off, 1) if off else w2pad[t]
        lane = iota(v.shape, 1)
        here = slice(tile * LANES, (tile + 1) * LANES)
        w2wide[:, here] = w2wide[:, here] + jnp.where(lane >= off, v, 0.0)
        if off + grow > LANES:
            there = slice((tile + 1) * LANES, (tile + 2) * LANES)
            w2wide[:, there] = w2wide[:, there] + jnp.where(lane < off, v, 0.0)
    w2r[ch] = w2wide[...].astype(BF16)
    loads[5].wait()
    loads[6].wait()
    gsl[ch, 0:1, 0:grow] = gain2v[...]
    gsl[ch, 1:2, 0:grow] = bias2v[...]
    w_near = remote(w2r.at[ch], w2r.at[ch], sw.at[0], rw.at[0], {"chan": sib})
    w_far = remote(w2r.at[ch], w2r.at[ch], sw.at[1], rw.at[1], {"chan": xp})
    w_on = remote(w2r.at[xp], w2r.at[xp], sw.at[2], rw.at[2], {"chan": sib})
    w_far.start()
    w_near.start()
    share_start(gsl, ch, n_ch, ch_peer, sb, rb)

    loads[2].wait()
    w1s[...] = jnp.zeros(w1s.shape, BF16)
    w1s[0:n_d, 0:n_c] = w1v[...]
    rowbuf[...] = jnp.zeros(rowbuf.shape, F32)
    loads[3].wait()
    loads[4].wait()
    rowbuf[0:1, :] = gain1v[0:1, 0:LANES]
    rowbuf[1:2, 0 : n_c - LANES] = gain1v[0:1, LANES:n_c]
    rowbuf[2:3, :] = bias1v[0:1, 0:LANES]
    rowbuf[3:4, 0 : n_c - LANES] = bias1v[0:1, LANES:n_c]


    share_wait(ar1, dp, n_dp, dp_peer, s1, r1)
    tot1 = total(ar1)
    count = tot1[1:2, LANES - 1 : LANES]
    mean1, rstd1, scale1, keep1 = [], [], [], []
    for i in range(2):
        mean = tot1[i : i + 1] / count
        rstd = lax.rsqrt(tot1[2 + i : 3 + i] / count - mean * mean + EPS)
        here = lane1 + i * LANES
        ids = ch * n_c + here
        first = new_slot * grow
        keep = jnp.where(
            (here < n_c) & ((ids < first) | (ids >= first + grow)), 1.0, 0.0
        )
        scale = rstd * rowbuf[i : i + 1, :]
        shift = rowbuf[2 + i : 3 + i, :] - mean * scale
        size = c_sizes[i]
        r = pl.ds(i * LANES, size)
        col_a[r, :] = as_column(0.5 * scale * keep, size)
        col_b[r, :] = as_column(0.5 * shift * keep, size)
        mean1.append(mean)
        keep1.append(keep)
        rstd1.append(rstd)
        scale1.append(scale)

    def partial(j, first, n):
        def body(g, c):
            r = pl.ds(pl.multiple_of(g * 16, 16), 16)
            a, b = col_a[r, :], col_b[r, :]
            for t in range(first, first + n):
                sl = slice(t * LANES, (t + 1) * LANES)
                k = g * 16 * rpc + t * n_img + j
                v = jnp.concatenate([out_x[pl.ds(k + h * 8 * rpc, 8, stride=rpc), :] for h in range(2)], axis=0)
                xb[j, r, sl] = v.astype(BF16)
                v = v * a + b
                act[j, r, sl] = ((v * jnp.tanh(v) + v) * mask[j, :, sl]).astype(BF16)
            return c

        lax.fori_loop(0, cp // 16, body, 0)
        sl = slice(first * LANES, (first + n) * LANES)
        part[j, :, sl] = jnp.dot(w1s[...], act[j, :, sl], preferred_element_type=F32)

    rows_d = pl.ds(0, d8)
    unit = tiles // sum(SPANS)
    edges = [sum(SPANS[:p]) * unit for p in range(PIECES + 1)]

    def lanes_of(p):
        return pl.ds(edges[p] * LANES, (edges[p + 1] - edges[p]) * LANES)

    def tiles_of(p):
        return [slice(t * LANES, (t + 1) * LANES) for t in range(edges[p], edges[p + 1])]

    blocks, rest = d8 // 64, d8 // 64 * 64
    plain = blocks * 40

    def code(read, p, words, tops):
        top = jnp.maximum(jnp.max(row_top[...], axis=1, keepdims=True), 1e-30)
        row_scale[...] = jnp.broadcast_to(LEVELS / top, (d8, LANES))

        def quantized(first, n, sl):
            r = pl.ds(pl.multiple_of(first, 8), n)
            return jnp.round(read(r, sl) * row_scale[r, :]).astype(jnp.int32)

        def block(i, c):
            for t, sl in enumerate(tiles_of(p), edges[p]):
                high = jnp.zeros((8, LANES), jnp.int32)
                for k in range(4):
                    first = quantized(i * 64 + k * 8, 8, sl)
                    second = quantized(i * 64 + 32 + k * 8, 8, sl)
                    words[t, pl.ds(pl.multiple_of(i * 40 + k * 8, 8), 8), :] = (first << 12) | (second & 0xFFF)
                    high = high | (((second >> 12) & 0xFF) << (8 * k))
                words[t, pl.ds(pl.multiple_of(i * 40 + 32, 8), 8), :] = high
            return c

        lax.fori_loop(0, blocks, block, 0)
        for t, sl in enumerate(tiles_of(p), edges[p]):
            words[t, plain : plain + d8 - rest, :] = quantized(rest, d8 - rest, sl)
        tops[p, 0:1, :] = as_row(top[0:LANES])
        tops[p, 1:2, :] = as_row(top[LANES:d8])

    def unscale(tops, p):
        top = jnp.concatenate([as_column(tops[p, 0:1, :], LANES), as_column(tops[p, 1:2, :], d8 - LANES)], axis=0)
        row_scale[...] = top * (1.0 / LEVELS)

    def uncode(write, p, words):
        def put(first, n, sl, q):
            r = pl.ds(pl.multiple_of(first, 8), n)
            write(r, sl, q.astype(F32) * row_scale[r, :])

        def block(i, c):
            for t, sl in enumerate(tiles_of(p), edges[p]):
                high = words[t, pl.ds(pl.multiple_of(i * 40 + 32, 8), 8), :]
                for k in range(4):
                    low = words[t, pl.ds(pl.multiple_of(i * 40 + k * 8, 8), 8), :]
                    put(i * 64 + k * 8, 8, sl, low >> 12)
                    put(i * 64 + 32 + k * 8, 8, sl, (((high << (24 - 8 * k)) >> 24) << 12) | (low & 0xFFF))
            return c

        lax.fori_loop(0, blocks, block, 0)
        for t, sl in enumerate(tiles_of(p), edges[p]):
            put(rest, d8 - rest, sl, words[t, plain : plain + d8 - rest, :])

    def top_of(values):
        value = jnp.abs(values[0])
        for other in values[1:]:
            value = jnp.maximum(value, jnp.abs(other))
        return value

    def piece_of(j, p):
        partial(j, edges[p], edges[p + 1] - edges[p])

    def over(p):
        at = lanes_of(p)
        return remote(part.at[xs, rows_d, at], rx_a.at[rows_d, at], sp.at[p], rp.at[p], {"chan": sib})

    to_x = []
    piece_of(xs, 0)
    over(0).start()
    piece_of(xp, 0)
    for p in range(PIECES):
        if p + 1 < PIECES:
            piece_of(xs, p + 1)
            over(p + 1).start()
        over(p).wait()

        def add_a(g, c):
            r = pl.ds(pl.multiple_of(g * 8, 8), 8)
            values = [part[xp, r, sl] + rx_a[r, sl] for sl in tiles_of(p)]
            for sl, v in zip(tiles_of(p), values):
                part[xp, r, sl] = v
            row_top[r, :] = top_of(values)
            return c

        lax.fori_loop(0, d8 // 8, add_a, 0)
        code(lambda r, sl: part[xp, r, sl], p, px_out, tx_out)
        at = pl.ds(edges[p], edges[p + 1] - edges[p])
        copies = [
            remote(tx_out.at[p], tx_in.at[p], sq.at[0, p], rq.at[0, p], {"chan": xp}),
            remote(px_out.at[at], px_in.at[at], sq.at[1, p], rq.at[1, p], {"chan": xp}),
        ]
        for copy in copies:
            copy.start()
        to_x.append(copies)
        if p + 1 < PIECES:
            piece_of(xp, p + 1)
    for i in range(2):
        r = pl.ds(i * LANES, c_sizes[i])
        col_m[r, :] = as_column(mean1[i], c_sizes[i])
        col_k[r, :] = as_column(keep1[i], c_sizes[i])
    partial(sib, 0, tiles)
    to_sib_b = remote(part.at[sib, rows_d], rx_b.at[rows_d], sx.at[0], rxs.at[0], {"chan": sib})
    to_sib_b.start()
    partial(ch, 0, tiles)

    g_x.wait()
    px = iota((TAP, n_px), 1)
    py, pxx = px >> 5, px & (SIDE - 1)
    gcur[40:TAP, :] = jnp.zeros((TAP - 40, n_px), F32)
    for i in range(2):
        mine, theirs = slice(i * 32, i * 32 + 32), slice(32 - i * 32, 64 - i * 32)
        gcur[0:32, :] = gpair[mine, :].astype(F32) + grx[theirs, :].astype(F32)
        tails, others = gpair[64:80, :].astype(F32), grx[64:80, :].astype(F32)
        gcur[32:40, :] = tails[i * 8 : i * 8 + 8] + others[8 - i * 8 : 16 - i * 8]
        for ky in range(3):
            for kx in range(3):
                shift = (ky - 1) * SIDE + (kx - 1)
                t = ky * 3 + kx
                v = gcur[...]
                if shift != 0:
                    v = pltpu.roll(v, shift % n_px, 1)
                ok = None
                for off, pos in ((ky - 1, py), (kx - 1, pxx)):
                    if off == 1:
                        test = pos >= 1
                    elif off == -1:
                        test = pos <= SIDE - 2
                    else:
                        continue
                    ok = test if ok is None else ok & test
                if ok is not None:
                    v = jnp.where(ok, v, 0.0)
                g9[i, t * TAP : (t + 1) * TAP, :] = v.astype(BF16)
        g9[i, pl.ds(9 * TAP, TAPS - 9 * TAP), :] = jnp.zeros((TAPS - 9 * TAP, n_px), BF16)
    def slopes(j):
        def body(g, c):
            r = pl.ds(pl.multiple_of(g * 16, 16), 16)
            a, b = col_a[r, :], col_b[r, :]
            k = 0.5 * col_k[r, :]
            for t in range(tiles):
                sl = slice(t * LANES, (t + 1) * LANES)
                v = xb[j, r, sl].astype(F32) * a + b
                th = jnp.tanh(v)
                slope[j, r, sl] = ((1.0 + th) * (1.0 + v * (1.0 - th))) * (mask[j, :, sl] * k)
            return c

        lax.fori_loop(0, cp // 16, body, 0)


    to_sib_b.wait()
    sum_a[...] = jnp.zeros(sum_a.shape, F32)
    sum_b[...] = jnp.zeros(sum_b.shape, F32)
    hid[:, d8:dpad, :] = jnp.zeros((2, dpad - d8, n_px), F32)
    gp2[...] = jnp.zeros(gp2.shape, F32)

    def across(p):
        at = pl.ds(edges[p], edges[p + 1] - edges[p])
        return [
            remote(th_out.at[p], th_in.at[p], sh.at[0, p], rh.at[0, p], {"chan": xp}),
            remote(ph_out.at[at], ph_in.at[at], sh.at[1, p], rh.at[1, p], {"chan": xp}),
        ]

    def start_across(p):
        for copy in across(p):
            copy.start()

    for p in range(PIECES):
        for copy in to_x[p]:
            copy.wait()
        unscale(tx_in, p)

        def gather(r, sl, v):
            hid[0, r, sl] = (part[ch, r, sl] + rx_b[r, sl]) + v

        uncode(gather, p, px_in)

        def sums(g, c):
            r = pl.ds(pl.multiple_of(g * 8, 8), 8)
            s_acc, q_acc = sum_a[r, :], sum_b[r, :]
            values = [hid[0, r, sl] for sl in tiles_of(p)]
            for v in values:
                s_acc = s_acc + v
                q_acc = q_acc + v * v
            sum_a[r, :] = s_acc
            sum_b[r, :] = q_acc
            tops_h[p, r, :] = top_of(values)
            return c

        lax.fori_loop(0, d8 // 8, sums, 0)
        if p < AHEAD:
            row_top[...] = tops_h[p]
            code(lambda r, sl: hid[0, r, sl], p, ph_out, th_out)
            start_across(p)

    def pack(slots):
        s, q = as_rows(sum_a[0:d8, :], d_sizes), as_rows(sum_b[0:d8, :], d_sizes)
        slots[me, 0:1, :] = s[0]
        slots[me, 1:2, :] = s[1]
        slots[me, 2:3, :] = q[0]
        slots[me, 3:4, :] = q[1]

    def columns_d(row0, row1):
        tail = jnp.zeros((dpad - d8, LANES), F32)
        return jnp.concatenate(
            [as_column(row0, LANES), as_column(row1, d8 - LANES), tail], axis=0
        )

    pack(ar2)
    share_start(ar2, me, n_dev, dev_peer, s2, r2)
    for p in range(AHEAD, PIECES):
        row_top[...] = tops_h[p]
        code(lambda r, sl: hid[0, r, sl], p, ph_out, th_out)
        start_across(p)

    w_far.wait()
    w_on.start()
    slopes(xs)
    slopes(xp)
    w_near.wait()
    w_on.wait()
    share_wait(gsl, ch, n_ch, ch_peer, sb, rb)
    acc = jnp.zeros((dpad, w2b.shape[1]), F32)
    for j in range(n_ch):
        rows = iota((dpad, TAP), 0)
        cols = iota((dpad, TAP), 1)
        place = jnp.where((rows == cols + j * grow) & (cols < grow), 1.0, 0.0).astype(BF16)
        acc = acc + jnp.dot(place, w2r[j], preferred_element_type=F32)
    w2b[...] = acc.astype(BF16)
    for i in range(2):
        back[i] = jnp.dot(w2b[...], g9[i], preferred_element_type=F32)
    rows = iota((dpad, LANES), 0)
    cols = iota((dpad, LANES), 1)
    gain2c = jnp.zeros((dpad, 1), F32)
    bias2c = jnp.zeros((dpad, 1), F32)
    for j in range(n_ch):
        place = (rows == cols + j * grow) & (cols < grow)
        gain2c = gain2c + jnp.sum(jnp.where(place, gsl[j, 0:1, :], 0.0), axis=1, keepdims=True)
        bias2c = bias2c + jnp.sum(jnp.where(place, gsl[j, 1:2, :], 0.0), axis=1, keepdims=True)
    col_c[0] = jnp.broadcast_to(gain2c, (dpad, LANES))
    col_c[1] = jnp.broadcast_to(bias2c, (dpad, LANES))

    def widen_cot(i, c):
        r = pl.ds(pl.multiple_of(i * step_rows, step_rows), step_rows)
        k = [jnp.broadcast_to(col_k[pl.ds(i * 3 + n, 1), :], (rpc, LANES)) for n in range(3)]
        base[r, :] = cot[r, :].astype(F32) * jnp.concatenate(k, axis=0)
        return c

    lax.fori_loop(0, n_rows // step_rows, widen_cot, 0)

    share_wait(ar2, me, n_dev, dev_peer, s2, r2)
    tot2 = total(ar2)
    mean2 = [tot2[i : i + 1] / count for i in range(2)]
    rstd2 = [lax.rsqrt(tot2[2 + i : 3 + i] / count - mean2[i] * mean2[i] + EPS) for i in range(2)]
    mean2c = columns_d(*mean2)
    rstd2c = columns_d(*rstd2)
    scale2c = rstd2c * col_c[0]
    col_c[2] = mean2c
    col_c[3] = rstd2c
    col_c[4] = scale2c
    col_c[5] = 0.5 * scale2c
    col_c[6] = 0.5 * (col_c[1] - mean2c * scale2c)

    def second(g, c):
        r = pl.ds(pl.multiple_of(g * 16, 16), 16)
        a, b, m = col_c[5, r, :], col_c[6, r, :], col_c[2, r, :]
        s_acc = jnp.zeros((16, LANES), F32)
        q_acc = jnp.zeros((16, LANES), F32)
        for t in range(tiles):
            sl = slice(t * LANES, (t + 1) * LANES)
            h = hid[0, r, sl]
            mk = mask[ch, :, sl]
            v = h * a + b
            th = jnp.tanh(v)
            act2[r, sl] = ((v * th + v) * mk).astype(BF16)
            gp = (0.5 * mk) * ((1.0 + th) * (1.0 + v * (1.0 - th))) * back[0, r, sl]
            gp2[0, r, sl] = gp
            s_acc = s_acc + gp
            q_acc = q_acc + gp * (h - m)
        sum_a[r, :] = s_acc
        sum_b[r, :] = q_acc
        return c

    lax.fori_loop(0, dpad // 16, second, 0)
    pack(ar3)
    share_start(ar3, me, n_dev, dev_peer, s3, r3)

    w2acc[...] = lax.dot_general(
        act2[...], g9[0], (((1,), (1,)), ((), ())), preferred_element_type=F32
    )
    for j in range(n_ch):
        for lt in range(4):
            sl = slice(lt * LANES, (lt + 1) * LANES)
            cw[j, lt * 32 : lt * 32 + 32, :] = w2acc[j * grow : j * grow + 32, sl]
            cw[j, 128 + lt : 129 + lt, :] = w2acc[j * grow + 32 : j * grow + 33, sl]
        cw[j, 132:136, :] = jnp.zeros((4, LANES), F32)
    w_sib = [
        remote(cw.at[xs], cwr.at[1], sc.at[0], rc.at[0], {"chan": sib}),
        remote(cw.at[sib], cwr.at[0], sc.at[1], rc.at[1], {"chan": sib}),
    ]
    for copy in w_sib:
        copy.start()

    def second_other(p):
        for copy in across(p):
            copy.wait()
        unscale(th_in, p)

        def keep_hidden(r, sl, v):
            hid[1, r, sl] = v

        uncode(keep_hidden, p, ph_in)

        def body(g, c):
            r = pl.ds(pl.multiple_of(g * 16, 16), 16)
            a, b = col_c[5, r, :], col_c[6, r, :]
            for sl in tiles_of(p):
                v = hid[1, r, sl] * a + b
                th = jnp.tanh(v)
                gp2[1, r, sl] = (
                    (0.5 * mask[xp, :, sl]) * ((1.0 + th) * (1.0 + v * (1.0 - th))) * back[1, r, sl]
                )
            return c

        lax.fori_loop(0, dpad // 16, body, 0)

    zbuf[...] = lax.dot_general(
        w2b[...], act2[...], (((0,), (0,)), ((), ())), preferred_element_type=F32
    )
    new = jnp.zeros((TAP, n_px), F32)
    for ky in range(3):
        for kx in range(3):
            shift = (ky - 1) * SIDE + (kx - 1)
            t = ky * 3 + kx
            v = zbuf[t * TAP : (t + 1) * TAP, :]
            if shift != 0:
                v = pltpu.roll(v, (-shift) % n_px, 1)
            ok = None
            for off, pos in ((ky - 1, py), (kx - 1, pxx)):
                if off == -1:
                    test = pos >= 1
                elif off == 1:
                    test = pos <= SIDE - 2
                else:
                    continue
                ok = test if ok is None else ok & test
            if ok is not None:
                v = jnp.where(ok, v, 0.0)
            new = new + v
    new = new * jnp.concatenate([mask[ch]] * (TAP // 16), axis=0)
    gall[ch] = new[0 : gall.shape[1]]
    for copy in w_sib:
        copy.wait()
    cw[xp] = cw[xp] + cwr[1]
    cw[ch] = cw[ch] + cwr[0]
    w_x = remote(cw.at[xp], cwx, sc.at[2], rc.at[2], {"chan": xp})
    w_x.start()
    new_sib = remote(gall.at[ch], gall.at[ch], so.at[0], ro.at[0], {"chan": sib})
    new_xp = remote(gall.at[ch], gall.at[ch], so.at[1], ro.at[1], {"chan": xp})
    new_on = remote(gall.at[xp], gall.at[xp], so.at[2], ro.at[2], {"chan": sib})
    new_xp.start()
    new_sib.start()
    slopes(sib)
    slopes(ch)
    for p in range(PIECES):
        second_other(p)

    w1acc[...] = jnp.zeros(w1acc.shape, F32)
    sum_a[...] = jnp.zeros(sum_a.shape, F32)
    sum_b[...] = jnp.zeros(sum_b.shape, F32)
    share_wait(ar3, me, n_dev, dev_peer, s3, r3)
    tot3 = total(ar3)
    gain_sum2 = [tot3[2 + i : 3 + i] * rstd2[i] for i in range(2)]
    bias_sum2 = [tot3[i : i + 1] for i in range(2)]
    gain_sum2c = columns_d(*gain_sum2)
    bias_sum2c = columns_d(*bias_sum2)
    col_c[7] = col_c[4] * bias_sum2c / count
    col_c[8] = col_c[4] * col_c[3] * gain_sum2c / count

    def third(i, j, k):
        def body(g, c):
            r = pl.ds(pl.multiple_of(g * 16, 16), 16)
            c1, c2, c3, m = col_c[4, r, :], col_c[7, r, :], col_c[8, r, :], col_c[2, r, :]
            for sl in [slice(t * LANES, (t + 1) * LANES) for t in range(k * tiles // 2, (k + 1) * tiles // 2)]:
                gha[j, r, sl] = (
                    c1 * gp2[i, r, sl] - mask[j, :, sl] * (c2 + c3 * (hid[i, r, sl] - m))
                ).astype(BF16)
            return c

        lax.fori_loop(0, dpad // 16, body, 0)

    grads = []
    for i, j in ((0, ch), (1, xp)):
        for k in range(2):
            third(i, j, k)
            at = pl.ds(k * (n_px // 2), n_px // 2)
            copy = remote(gha.at[j, :, at], gha.at[j, :, at], st.at[i, k], rt.at[i, k], {"chan": sib})
            copy.start()
            grads.append(copy)


    def weight_grad(j, k=None):
        at = slice(0, n_px) if k is None else slice(k * (n_px // 2), (k + 1) * (n_px // 2))
        w1acc[0:dpad, 0:cp] = w1acc[0:dpad, 0:cp] + lax.dot_general(
            gha[j, :, at], act[j, :, at], (((1,), (1,)), ((), ())), preferred_element_type=F32
        )

    def input_grad(j):
        gact[...] = lax.dot_general(
            w1s[...], gha[j], (((0,), (0,)), ((), ())), preferred_element_type=F32
        )

        def body(g, c):
            r = pl.ds(pl.multiple_of(g * 16, 16), 16)
            m = col_m[r, :]
            s_acc, q_acc = sum_a[r, :], sum_b[r, :]
            for t in range(tiles):
                sl = slice(t * LANES, (t + 1) * LANES)
                gp = gact[r, sl] * slope[j, r, sl]
                gp1[j, r, sl] = gp
                s_acc = s_acc + gp
                q_acc = q_acc + gp * (xb[j, r, sl].astype(F32) - m)
            sum_a[r, :] = s_acc
            sum_b[r, :] = q_acc
            return c

        lax.fori_loop(0, cp // 16, body, 0)

    weight_grad(ch)
    weight_grad(xp)
    w_x.wait()
    for i, j in ((0, sib), (1, xs)):
        for k in range(2):
            grads[2 * i + k].wait()
            weight_grad(j, k)

    for r in range(17):
        cb[r // 5, r % 5 * 8 : r % 5 * 8 + 8, :] = w1acc[r * 8 : r * 8 + 8, 0:LANES]
    for k in range(6):
        v = w1acc[k * 8 : k * 8 + 8, LANES : 2 * LANES]
        for i in range(1, 3):
            v = v + pltpu.roll(w1acc[i * 48 + k * 8 : i * 48 + k * 8 + 8, LANES : 2 * LANES], 40 * i, 1)
        r = 17 + k
        cb[r // 5, r % 5 * 8 : r % 5 * 8 + 8, :] = v
    for k in range(17):
        r = 23 + k
        cb[r // 5, r % 5 * 8 : r % 5 * 8 + 8, :] = cw[ch, k * 8 : k * 8 + 8, :] + cwx[k * 8 : k * 8 + 8, :]

    def encode(v):
        top = jnp.maximum(jnp.max(jnp.abs(v), axis=0, keepdims=True), 1e-30)
        power = jnp.floor(jnp.log2(top) + 1.0001)
        q = jnp.clip(jnp.round(v * jnp.exp2(15.0 - power)), -32767.0, 32767.0).astype(jnp.int32)
        low = jnp.concatenate([q[24:40], jnp.broadcast_to(power.astype(jnp.int32), (8, LANES))], axis=0)
        return (q[0:24] << 16) | (low & 0xFFFF)

    def decode(w):
        high, low = w >> 16, (w << 16) >> 16
        scale = jnp.exp2(low[16:24].astype(F32) - 15.0)
        q = jnp.concatenate([high, low[0:16]], axis=0).astype(F32)
        return q * jnp.concatenate([scale] * 5, axis=0)

    def encode_part(v):
        top = jnp.maximum(jnp.max(jnp.abs(v), axis=0, keepdims=True), 1e-30)
        power = jnp.floor(jnp.log2(top) + 1.0001)
        q = jnp.clip(jnp.round(v * jnp.exp2(23.0 - power)), -8388607.0, 8388607.0).astype(jnp.int32)
        extra = q[32:40]
        power = jnp.broadcast_to(jnp.clip(power, -127.0, 127.0).astype(jnp.int32), (8, LANES))
        spare = jnp.concatenate([extra, extra >> 8, extra >> 16, power], axis=0) & 0xFF
        return (q[0:32] << 8) | spare

    def decode_part(w):
        spare = w & 0xFF
        extra = spare[0:8] | (spare[8:16] << 8) | (((w[16:24] << 24) >> 24) << 16)
        scale = jnp.exp2(((w[24:32] << 24) >> 24).astype(F32) - 23.0)
        return jnp.concatenate([w >> 8, extra], axis=0).astype(F32) * jnp.concatenate([scale] * 5, axis=0)

    for q in range(OWNERS):
        coded[q] = encode_part(cb[q])
    stride = n_dp // OWNERS
    my_part = dp // stride
    is_owner = lax.rem(dp, stride) == 0

    def part_to(k):
        q = my_part ^ (OWNERS - 1 - k)
        return q, q * stride

    def push(k, c):
        q, to = part_to(k)

        @pl.when(to != dp)
        def _():
            remote(coded.at[q], rsl.at[dp], sr.at[k], rr.at[dp], {"dp": to}).start()

        return c

    lax.fori_loop(0, OWNERS, push, 0)
    d_rows, d_cols = iota((dpad, LANES), 0), iota((dpad, LANES), 1)
    here_d = (d_rows == d_cols + ch * grow) & (d_cols < grow)
    out_g2[...] = jnp.sum(jnp.where(here_d, gain_sum2c, 0.0), axis=0, keepdims=True)[:, 0:grow]
    out_b2[...] = jnp.sum(jnp.where(here_d, bias_sum2c, 0.0), axis=0, keepdims=True)[:, 0:grow]
    for j in (ch, xp, sib, xs):
        input_grad(j)
    s4_, q4_ = as_rows(sum_a[...], c_sizes), as_rows(sum_b[...], c_sizes)
    for i in range(2):
        ar4[dp, i : i + 1, :] = s4_[i]
        ar4[dp, 2 + i : 3 + i, :] = q4_[i]
    share_start(ar4, dp, n_dp, dp_peer, s4, r4)

    def scatter(g, c):
        first = g * 16 * rpc
        r = pl.ds(pl.multiple_of(g * 16, 16), 16)
        for b in range(n_img):
            for t in range(tiles):
                v = gp1[b, r, t * LANES : (t + 1) * LANES]
                for h in range(2):
                    at = pl.ds(first + h * 8 * rpc + t * n_img + b, 8, stride=rpc)
                    out_g[at, :] = v[h * 8 : h * 8 + 8]
        return c

    lax.fori_loop(0, 5, scatter, 0)

    def push_wait(k, c):
        q, to = part_to(k)

        @pl.when(to != dp)
        def _():
            remote(coded.at[q], rsl.at[dp], sr.at[k], rr.at[dp], {"dp": to}).wait_send()

        return c

    def pull(k, c):
        src = lax.rem(dp + k, n_dp)
        remote(coded.at[0], rsl.at[src], sr.at[0], rr.at[src], {"dp": src}).wait_recv()
        return c

    @pl.when(is_owner)
    def _():
        lax.fori_loop(1, n_dp, pull, 0)
        v = cb[my_part]
        for k in range(1, n_dp):
            v = v + decode_part(rsl[lax.rem(dp + k, n_dp)])
        fin[my_part] = encode(v)

        def give(k):
            remote(fin.at[my_part], fin.at[my_part], sa.at[k], ra.at[my_part], dp_peer(k)).start()

        far_first(n_dp, give)

    lax.fori_loop(0, OWNERS, push_wait, 0)
    new_xp.wait()
    new_on.start()
    lax.fori_loop(5, cp // 16, scatter, 0)

    for i in range(2):
        col_a[pl.ds(i * LANES, c_sizes[i]), :] = as_column(scale1[i], c_sizes[i])

    new_sib.wait()
    new_on.wait()
    for b in range(n_img):
        for t in range(tiles):
            for h in range(gall.shape[1] // 8):
                out_new[pl.ds(h * 8 * rpc + t * n_img + b, 8, stride=rpc), :] = gall[
                    b, h * 8 : h * 8 + 8, t * LANES : (t + 1) * LANES
                ]
    out_slot[...] = (slot_of - ch * per_device)[0:8].astype(F32)

    share_wait(ar4, dp, n_dp, dp_peer, s4, r4)
    tot4 = total(ar4)
    for i in range(2):
        bias_sum = tot4[i : i + 1]
        gain_sum = tot4[2 + i : 3 + i] * rstd1[i]
        size = c_sizes[i]
        r = pl.ds(i * LANES, size)
        k1 = -scale1[i] * rstd1[i] * gain_sum / count
        k0 = -scale1[i] * bias_sum / count - k1 * mean1[i]
        col_b[r, :] = as_column(k0, size)
        col_m[r, :] = as_column(k1, size)
        width = min(LANES, n_c - i * LANES)
        out_g1[0:1, i * LANES : i * LANES + width] = gain_sum[:, 0:width]
        out_b1[0:1, i * LANES : i * LANES + width] = bias_sum[:, 0:width]
    mask_of = mask_raw[...]

    def last(i, c):
        for k in range(5):
            row = i * 5 + k
            at = pl.ds(pl.multiple_of(row * rpc, rpc), rpc)
            k0 = jnp.broadcast_to(col_b[pl.ds(row, 1), :], (rpc, LANES))
            k1 = jnp.broadcast_to(col_m[pl.ds(row, 1), :], (rpc, LANES))
            a = jnp.broadcast_to(col_a[pl.ds(row, 1), :], (rpc, LANES))
            out_g[at, :] = base[at, :] + a * out_g[at, :] + mask_of * (k0 + k1 * out_x[at, :])
        return c

    lax.fori_loop(0, n_c // 5, last, 0)

    for wait in still_sent:
        wait()

    @pl.when(is_owner)
    def _():
        def gave(k, c):
            remote(fin.at[my_part], fin.at[my_part], sa.at[k], ra.at[my_part], dp_peer(k)).wait_send()
            return c

        lax.fori_loop(1, n_dp, gave, 0)

    def take(q, c):
        @pl.when(q * stride != dp)
        def _():
            remote(fin.at[q], fin.at[q], sa.at[0], ra.at[q], {"dp": q * stride}).wait_recv()

        return c

    lax.fori_loop(0, OWNERS, take, 0)
    for q in range(OWNERS):
        cb[q] = decode(fin[q])
    for r in range(17):
        height = min(8, n_d - r * 8)
        out_w1[r * 8 : r * 8 + height, 0:LANES] = cb[r // 5, r % 5 * 8 : r % 5 * 8 + height, :]
    for k in range(6):
        r = 17 + k
        v = cb[r // 5, r % 5 * 8 : r % 5 * 8 + 8, :]
        for i in range(3):
            row = i * 48 + k * 8
            height = min(8, n_d - row)
            if height > 0:
                u = v if i == 0 else pltpu.roll(v, LANES - 40 * i, 1)
                out_w1[row : row + height, LANES:n_c] = u[0:height, 0 : n_c - LANES]
    for k in range(17):
        r = 23 + k
        v = cb[r // 5, r % 5 * 8 : r % 5 * 8 + 8, :]
        if k < 16:
            w2acc[k % 4 * 8 : k % 4 * 8 + 8, k // 4 * LANES : (k // 4 + 1) * LANES] = v
        else:
            for lt in range(4):
                w2acc[32:33, lt * LANES : (lt + 1) * LANES] = v[lt : lt + 1]
    lane40 = iota((40, LANES), 1)
    for t in range(9):
        tile, off = t * TAP // LANES, t * TAP % LANES
        v = w2acc[0:40, tile * LANES : (tile + 1) * LANES]
        if off + grow > LANES:
            v = jnp.where(lane40 >= off, v, w2acc[0:40, (tile + 1) * LANES : (tile + 2) * LANES])
        if off:
            v = pltpu.roll(v, LANES - off, 1)
        out_w2[t] = v[0:grow, 0:grow]


def finish(n_rows, grow_rows, *refs):
    n = (len(refs) - 3) // 2
    new, slot = refs[n : n + 2]
    outs, sem = refs[n + 2 : -1], refs[-1]
    segments = n_rows // grow_rows
    copies = [pltpu.make_async_copy(refs[1].at[pl.ds(0, n_rows)], outs[1], sem.at[1])]
    copies += [pltpu.make_async_copy(refs[i], outs[i], sem.at[i]) for i in range(2, n)]
    for copy in copies:
        copy.start()
    here = jnp.max(slot[...])
    for k in range(segments):
        at = pl.ds(k * grow_rows, grow_rows)
        kept = pltpu.make_async_copy(refs[0].at[at], outs[0].at[at], sem.at[n + k])
        grown = pltpu.make_async_copy(new.at[pl.ds(0, grow_rows)], outs[0].at[at], sem.at[n + k])
        pl.when(here == k)(grown.start)
        pl.when(here != k)(kept.start)
        copies.append(kept)
    for copy in copies:
        copy.wait()


def flat(values):
    n, c, p = values.shape
    return (
        values.transpose(1, 0, 2).reshape(c, n, p // LANES, LANES).transpose(0, 2, 1, 3).reshape(-1, LANES)
    )


def unflat(rows, n, c, p):
    return rows.reshape(c, p // LANES, n, LANES).transpose(0, 2, 1, 3).reshape(c, n, p).transpose(1, 0, 2)


def on_device(
    n_dp, n_ch, features, gain1, bias1, weight1, gain2, bias2, weight2, cotangent, image_side, block_slot
):
    n_img, n_c, n_px = features.shape
    n_d = weight1.shape[1]
    grow = weight2.shape[3]
    cp = pad_to(n_c, 16)
    dpad = pad_to(n_d, 16)
    d8 = pad_to(n_d, 8)
    rpc = n_px // LANES * n_img
    n_rows, n_pad = n_c * rpc, cp * rpc
    n_dev = n_dp * n_ch
    words = d8 // 64 * 40 + d8 % 64
    cfg = (n_dp, n_ch, n_img, n_c, n_px, n_d, grow)
    args = (
        flat(features),
        flat(cotangent),
        weight1.T,
        gain1.reshape(1, -1),
        bias1.reshape(1, -1),
        gain2.reshape(1, -1),
        bias2.reshape(1, -1),
        weight2.reshape(9, grow, grow),
        image_side,
        block_slot,
    )
    args = [pltpu.with_memory_space_constraint(v, pltpu.HBM) for v in args]
    sd = jax.ShapeDtypeStruct
    in_vmem = pl.BlockSpec(memory_space=pltpu.VMEM)
    in_hbm = pl.BlockSpec(memory_space=pltpu.HBM)
    dma = pltpu.SemaphoreType.DMA
    v = pltpu.VMEM
    scratch = [
        v((n_rows, LANES), BF16), v((n_rows, LANES), BF16), v((n_d, n_c), BF16),
        v((1, n_c), F32), v((1, n_c), F32), v((1, grow), F32), v((1, grow), F32),
        v((9, grow, grow), BF16), pltpu.SMEM(image_side.shape, jnp.int32), pltpu.SMEM(block_slot.shape, jnp.int32),
        v((n_img, 16, n_px), F32), v((rpc, LANES), F32), v((n_rows, LANES), F32),
        v((n_img, cp, n_px), BF16), v((n_img, cp, n_px), BF16),
        v((n_img, cp, n_px), F32), v((n_img, cp, n_px), F32), v((cp, n_px), F32),
        v((cp, LANES), F32), v((cp, LANES), F32), v((cp, LANES), F32), v((cp, LANES), F32),
        v((9, dpad, LANES), F32), v((cp, LANES), F32), v((cp, LANES), F32),
        v((8, LANES), F32),
        v((dpad, cp), BF16), v((n_img, dpad, n_px), F32),
        v((dpad, n_px), F32), v((dpad, n_px), F32), v((2, dpad, n_px), F32),
        v((d8, LANES), F32), v((d8, LANES), F32), v((PIECES, d8, LANES), F32),
        v((n_px // LANES, words, LANES), jnp.int32), v((n_px // LANES, words, LANES), jnp.int32), v((PIECES, 2, LANES), F32), v((PIECES, 2, LANES), F32),
        v((n_px // LANES, words, LANES), jnp.int32), v((n_px // LANES, words, LANES), jnp.int32), v((PIECES, 2, LANES), F32), v((PIECES, 2, LANES), F32),
        v((40 * rpc, LANES), F32), v((2, 80, n_px), BF16),
        v((80, n_px), BF16), v((80, n_px), BF16), v((80, n_px), BF16), v((TAP, n_px), F32),
        v((2, TAPS, n_px), BF16), v((9, TAP, LANES), F32), v((TAP, TAPS), F32), v((n_ch, TAP, TAPS), BF16), v((dpad, TAPS), BF16),
        v((n_ch, 2, LANES), F32),
        v((dpad, n_px), BF16), v((2, dpad, n_px), F32), v((2, dpad, n_px), F32), v((TAPS, n_px), F32),
        v((n_ch, 40, n_px), F32), v((n_ch, dpad, n_px), BF16),
        v((n_ch, 136, LANES), F32), v((2, 136, LANES), F32), v((136, LANES), F32),
        v((OWNERS, 40, LANES), F32), v((OWNERS, 32, LANES), jnp.int32),
        v((n_dp, 32, LANES), jnp.int32), v((OWNERS, 24, LANES), jnp.int32), v((dpad, 256), F32), v((dpad, TAPS), F32),
        v((n_dp, 4, LANES), F32), v((n_dev, 4, LANES), F32), v((n_dev, 4, LANES), F32), v((n_dp, 4, LANES), F32),
        dma((13,)),
        dma((n_dp,)), dma((n_dp,)), dma((n_dev,)), dma((n_dev,)), dma((n_dev,)), dma((n_dev,)), dma((n_dp,)), dma((n_dp,)),
        dma((3,)), dma((3,)), dma((PIECES,)), dma((PIECES,)), dma((2, PIECES)), dma((2, PIECES)),
        dma((2,)), dma((2,)), dma((n_ch,)), dma((n_ch,)), dma((n_ch,)), dma((n_ch,)),
        dma((2, PIECES)), dma((2, PIECES)), dma((2, 2)), dma((2, 2)), dma((3,)), dma((3,)), dma((3,)), dma((3,)),
        dma((OWNERS,)), dma((n_dp,)), dma((n_dp,)), dma((OWNERS,)),
    ]
    out_shape = (
        sd((n_pad, LANES), F32), sd((n_pad, LANES), F32), sd((n_d, n_c), F32),
        sd((1, n_c), F32), sd((1, n_c), F32), sd((9, grow, grow), F32), sd((1, grow), F32), sd((1, grow), F32),
        sd((40 * rpc, LANES), F32), sd((8, LANES), F32),
    )
    outs = pl.pallas_call(
        functools.partial(layer, cfg),
        out_shape=out_shape,
        in_specs=[in_hbm] * len(args),
        out_specs=(in_vmem,) * len(out_shape),
        scratch_shapes=scratch,
        compiler_params=pltpu.CompilerParams(
            collective_id=0, has_side_effects=True, vmem_limit_bytes=40 << 20
        ),
    )(*args)
    final = (sd((n_rows, LANES), F32),) * 2 + out_shape[2:-2]
    o = pl.pallas_call(
        functools.partial(finish, n_rows, grow * rpc),
        out_shape=final,
        in_specs=[in_vmem] * len(outs),
        out_specs=(in_hbm,) * len(final),
        scratch_shapes=[dma((len(final) + n_c // grow,))],
        compiler_params=pltpu.CompilerParams(vmem_limit_bytes=8 << 20),
    )(*outs)
    return (
        unflat(o[0], n_img, n_c, n_px),
        unflat(o[1], n_img, n_c, n_px),
        o[2].T,
        o[3].reshape(-1),
        o[4].reshape(-1),
        o[5].reshape(3, 3, grow, grow),
        o[6].reshape(-1),
        o[7].reshape(-1),
    )


def solution(mesh):
    in_specs = (
        P("dp", "chan", None),
        P("chan"),
        P("chan"),
        P("chan", None),
        P("chan"),
        P("chan"),
        P(None, None, "chan", None),
        P("dp", "chan", None),
        P("dp"),
        P(),
    )
    out_specs = (
        P("dp", "chan", None),
        P("dp", "chan", None),
        P("chan", None),
        P("chan"),
        P("chan"),
        P(None, None, "chan", None),
        P("chan"),
        P("chan"),
    )
    body = functools.partial(on_device, mesh.shape["dp"], mesh.shape["chan"])
    return jax.shard_map(body, mesh=mesh, in_specs=in_specs, out_specs=out_specs, check_vma=False)
```
